128 devices in a mesh: gx: 16 (over x, y), gy: 8 (over z, core).
Axes of the slice: x: 4, y: 4, z: 4, core: 2. Of those that a mesh axis runs over, the one named last changes fastest.
Arguments:
- features: bfloat16 [32, 32, 256, 128], P(None, 'gx', 'gy'), may hold values from -80 to 80
- kernel_one: bfloat16 [32, 32, 3, 3, 3], replicated, may hold values from -0.21875 to 0.21875
- gain_one: float32 [32], replicated, may hold values from 0.5 to 1.5
- bias_one: float32 [32], replicated, may hold values from -0.5 to 0.5
- kernel_two: bfloat16 [32, 32, 3, 3, 3], replicated, may hold values from -0.21875 to 0.21875
- gain_two: float32 [32], replicated, may hold values from 0.5 to 1.5
- bias_two: float32 [32], replicated, may hold values from -0.5 to 0.5
- cotangent: bfloat16 [32, 32, 256, 128], P(None, 'gx', 'gy'), may hold values from -80 to 80
Outputs:
- output: bfloat16 [32, 32, 256, 128], P(None, 'gx', 'gy')
- features_grad: bfloat16 [32, 32, 256, 128], P(None, 'gx', 'gy')
- kernel_one_grad: float32 [32, 32, 3, 3, 3], replicated
- kernel_two_grad: float32 [32, 32, 3, 3, 3], replicated
- norm_grads: float32 [4, 32], replicated
The draws below stay inside these ranges and needn't reach their ends.
All inputs are finite; a program needn't handle non-finite values.
Results may differ from the reference program's by a relative error of at most 0.0078.
Values may be sent and summed in bfloat16 or wider, within the bound.
No kernel may reach another device: no remote copies, remote signals or barrier semaphores. Data moves between devices by JAX's collectives and lax.ppermute only.
A program may use at most 192 MiB of HBM per device.

```python
import jax
import jax.numpy as jnp
from jax import lax

C = 32
NX = 32
NY = 256
NZ = 128


def scaled_volume(key, salt):
    key = jax.random.fold_in(key, salt)
    noise_key, offset_key, rough_key = jax.random.split(key, 3)
    offsets = jax.random.uniform(offset_key, (C, 1, 1, 1), jnp.float32, -1.0, 1.0)
    rough = jnp.exp(jax.random.uniform(rough_key, (C, NX, NY, NZ), jnp.float32, jnp.log(0.5), jnp.log(2.0)))
    place_x = jnp.arange(NX, dtype=jnp.float32) / NX
    place_y = jnp.arange(NY, dtype=jnp.float32) / NY
    noise = jnp.clip(jax.random.normal(noise_key, (C, NX, NY, NZ), jnp.float32), -4.0, 4.0)
    ramp = jnp.exp(jnp.log(3.0) * place_x)[:, None] * jnp.exp(jnp.log(2.0) * place_y)[None, :]
    return (noise + offsets) * rough * ramp[None, :, :, None]


def draw_features(key, part):
    return scaled_volume(key, 11).astype(jnp.bfloat16)


def draw_cotangent(key, part):
    return scaled_volume(key, 23).astype(jnp.bfloat16)


def scatter_about(stream_key, extent, width, limit, kind=jnp.bfloat16):
    drawn = width * jax.random.normal(stream_key, extent, jnp.float32)
    return jnp.clip(drawn, min=-limit, max=limit).astype(kind)


def setup_inputs(seed: int = 0) -> dict:
    keys = jax.random.split(jax.random.key(seed), 9)
    return {
        "features": draw_features(jax.random.fold_in(keys[8], 71), 0),
        "kernel_one": scatter_about(keys[1], (C, C, 3, 3, 3), (C * 27) ** -0.5, 0.21875),
        "gain_one": jnp.clip(1.0 + 0.1 * jax.random.normal(keys[2], (C,), jnp.float32), 0.5, 1.5),
        "bias_one": jnp.clip(jax.random.uniform(keys[3], (C,), jnp.float32, -0.5, 0.5), -0.5, 0.5),
        "kernel_two": scatter_about(keys[4], (C, C, 3, 3, 3), (C * 27) ** -0.5, 0.21875),
        "gain_two": jnp.clip(1.0 + 0.1 * jax.random.normal(keys[5], (C,), jnp.float32), 0.5, 1.5),
        "bias_two": jnp.clip(jax.random.uniform(keys[6], (C,), jnp.float32, -0.5, 0.5), -0.5, 0.5),
        "cotangent": draw_cotangent(jax.random.fold_in(keys[8], 71), 0),
    }


EPSILON = 1e-05
SLOPE = 0.01
SHARPNESS = 8.0

def activate(shifted):
    return SLOPE * shifted + (1.0 - SLOPE) * jax.nn.softplus(SHARPNESS * shifted) / SHARPNESS

def activate_slope(shifted):
    return SLOPE + (1.0 - SLOPE) * jax.nn.sigmoid(SHARPNESS * shifted)

def column(values):
    return values[:, None, None, None]

def pad_all(values):
    return jnp.pad(values, ((0, 0), (1, 1), (1, 1), (1, 1)))

def conv_valid(padded, kernel):
    result = lax.conv_general_dilated(padded[None], kernel, (1, 1, 1), 'VALID', dimension_numbers=('NCDHW', 'OIDHW', 'NCDHW'), preferred_element_type=jnp.float32)
    return result[0]

def flip_kernel(kernel):
    return jnp.transpose(kernel[:, :, ::-1, ::-1, ::-1], (1, 0, 2, 3, 4))

def weight_grad(padded, gradient):
    result = lax.conv_general_dilated(padded[:, None], gradient[:, None], (1, 1, 1), 'VALID', dimension_numbers=('NCDHW', 'OIDHW', 'NCDHW'), preferred_element_type=jnp.float32)
    return jnp.transpose(result, (1, 0, 2, 3, 4))

def normalize(hidden, total_cells):
    center = lax.optimization_barrier(jnp.sum(hidden, axis=(1, 2, 3))) / total_cells
    spread = lax.optimization_barrier(jnp.sum(jnp.square(hidden - column(center)), axis=(1, 2, 3))) / total_cells
    inverse_std = lax.rsqrt(spread + EPSILON)
    return ((hidden - column(center)) * column(inverse_std), inverse_std)

def norm_backward(slope, normed, gain, inverse_std, total_cells):
    sum_plain = lax.optimization_barrier(jnp.sum(slope, axis=(1, 2, 3)))
    sum_normed = lax.optimization_barrier(jnp.sum(slope * normed, axis=(1, 2, 3)))
    gradient = column(gain * inverse_std) * (slope - column(sum_plain / total_cells) - normed * column(sum_normed / total_cells))
    return (gradient.astype(jnp.bfloat16), sum_plain, sum_normed)

def reference(features, kernel_one, gain_one, bias_one, kernel_two, gain_two, bias_two, cotangent):
    total_cells = float(NX * NY * NZ)
    x_pad = pad_all(features)
    normed_one, inv_one = normalize(conv_valid(x_pad, kernel_one), total_cells)
    shifted_one = normed_one * column(gain_one) + column(bias_one)
    active = activate(shifted_one).astype(jnp.bfloat16)
    a_pad = pad_all(active)
    normed_two, inv_two = normalize(conv_valid(a_pad, kernel_two), total_cells)
    shifted_two = normed_two * column(gain_two) + column(bias_two)
    output = activate(shifted_two).astype(jnp.bfloat16)
    slope_two = cotangent.astype(jnp.float32) * activate_slope(shifted_two)
    grad_two, plain_two, nsum_two = norm_backward(slope_two, normed_two, gain_two, inv_two, total_cells)
    scale = 1.0 / jnp.sqrt(jnp.float32(total_cells))
    kernel_two_grad = weight_grad(a_pad, grad_two) * scale
    back_one = conv_valid(pad_all(grad_two), flip_kernel(kernel_two))
    slope_one = back_one * activate_slope(shifted_one)
    grad_one, plain_one, nsum_one = norm_backward(slope_one, normed_one, gain_one, inv_one, total_cells)
    kernel_one_grad = weight_grad(x_pad, grad_one) * scale
    features_grad = conv_valid(pad_all(grad_one), flip_kernel(kernel_one)).astype(jnp.bfloat16)
    norm_grads = jnp.stack([nsum_one, plain_one, nsum_two, plain_two]) * scale
    return (output, features_grad, kernel_one_grad, kernel_two_grad, norm_grads)
```

```python
import jax
import jax.numpy as jnp
from jax import lax
from jax.experimental import pallas as pl
from jax.experimental.pallas import tpu as pltpu
from jax.sharding import Mesh
from jax.sharding import PartitionSpec as P

GX = ("gx_0", "gx_1")
GY = ("gy_0", "gy_1")
ALL = GX + GY

EPSILON = 1e-05
C = 32
ROWS = 32
F32 = jnp.float32
BF16 = jnp.bfloat16
LN2 = 0.6931471805599453
VM = pl.BlockSpec(memory_space=pltpu.VMEM)
SM = pl.BlockSpec(memory_space=pltpu.SMEM)


def sh(shape, kind):
    return jax.ShapeDtypeStruct(shape, kind)


def from_below(values, lane):
    return jnp.where(lane == 0, 0.0, pltpu.roll(values, 1, 1))


def from_above(values, lane):
    return jnp.where(lane == 127, 0.0, pltpu.roll(values, 127, 1))


def lanes(rows):
    return lax.broadcasted_iota(jnp.int32, (rows, 128), 1)


def conv_rows(v_ref, w_ref, rows, emit):
    lane = lanes(64)
    weights = w_ref[...]
    for y in range(0, rows, 2):
        first = v_ref[y : y + 3].reshape(384, 128)
        second = v_ref[y + 1 : y + 4].reshape(384, 128)
        product = jnp.dot(
            weights, jnp.concatenate([first, second], axis=1), preferred_element_type=F32
        )
        for k in range(2):
            part = product[:, k * 128 : (k + 1) * 128]
            emit(
                y + k,
                part[64:128] + from_below(part[0:64], lane) + from_above(part[128:192], lane),
            )


def fold(column):
    return column[0:C] + column[C : 2 * C]


def total(values):
    return jnp.sum(values, axis=1, keepdims=True)


def twice(column):
    return jnp.concatenate([column, column], axis=0)


def message(columns, msg_ref):
    count = msg_ref.shape[0]
    spare = jnp.zeros((128 - C * len(columns), 1), F32)
    column = jnp.concatenate([*columns, spare], axis=0)
    msg_ref[...] = jnp.transpose(jnp.broadcast_to(column, (128, count)))


def stats_out(h_ref, acc, start, low_ref, high_ref, msg_ref):
    center = fold(total(acc)) / (2 * ROWS * 128)
    both = twice(center)
    spread = jnp.zeros((64, 128), F32)
    for y in range(h_ref.shape[0]):
        off = h_ref[y] - both
        if start <= y < start + ROWS:
            spread = spread + off * off
        low_ref[y] = off[0:C].astype(BF16)
        high_ref[y] = off[C:].astype(BF16)
    message((center, fold(total(spread))), msg_ref)


def read_stats(r_ref, place_ref, cells):
    parts = jnp.transpose(r_ref[...])
    centers = parts[0:C]
    count = parts.shape[1]
    mean = total(centers) / count
    off = centers - mean
    spread = (total(parts[C : 2 * C]) + (2 * ROWS * 128) * total(off * off)) / cells
    at = lax.broadcasted_iota(jnp.int32, centers.shape, 1)
    low = total(jnp.where(at == place_ref[0], off, 0.0))
    high = total(jnp.where(at == place_ref[1], off, 0.0))
    return mean, lax.rsqrt(spread + EPSILON), low, high


def read_sums(r_ref):
    parts = jnp.transpose(r_ref[...])
    return total(parts[0:C]), total(parts[C : 2 * C])


def act(z):
    e = jnp.exp2(jnp.abs(z) * (-8.0 / LN2))
    soft = jnp.maximum(z, 0.0) * 0.99 + jnp.log2(1.0 + e) * (0.99 * LN2 / 8.0)
    return 0.01 * z + soft


def act_slope(z):
    return 0.505 + 0.495 * jnp.tanh(4.0 * z)


def kept(place_ref, y, rows, margin):
    low = place_ref[2].astype(F32)
    high = place_ref[3].astype(F32)
    if y < margin:
        edge = place_ref[4].astype(F32)
    elif y >= rows - margin:
        edge = place_ref[5].astype(F32)
    else:
        return low, None, high
    return low * edge, edge, high * edge


def masked(low, own, high, factors):
    f_low, f_own, f_high = factors
    own = own if f_own is None else own * f_own
    return jnp.concatenate([low * f_low, own, high * f_high], axis=0).astype(BF16)


def weight_sums(g_ref, v_ref, first, acc_ref, out_ref):
    step = 4
    for y in range(0, ROWS, step):
        right = jnp.concatenate(
            [v_ref[first + y + k : first + y + k + 3].reshape(384, 128) for k in range(step)], axis=1
        )
        left = g_ref[:, y * 128 : (y + step) * 128]
        product = lax.dot_general(
            left, right, (((1,), (1,)), ((), ())), preferred_element_type=F32
        )
        if y == 0:
            acc_ref[...] = product
        else:
            acc_ref[...] += product
    for dz in range(3):
        for dy in range(3):
            tile = acc_ref[dz * 64 : dz * 64 + 64, dy * 128 : dy * 128 + 128]
            out_ref[dz * 3 + dy] = tile[0:C] + pltpu.roll(tile[C:], 96, 1)


def put_shifted(g_ref, y, values, lane):
    at = slice(y * 128, (y + 1) * 128)
    g_ref[0:64, at] = from_above(values, lane).astype(BF16)
    g_ref[64:128, at] = values.astype(BF16)
    g_ref[128:192, at] = from_below(values, lane).astype(BF16)


def first_kernel(own, y_low, y_high, x_low, x_high, c_low, c_high, w, v, h, low, high, msg):
    for part, (rows, at) in (
        ((y_low, c_low, c_high, 0), (4, 0)),
        ((own, x_low, x_high, 0), (ROWS, 4)),
        ((y_high, c_low, c_high, 4), (4, ROWS + 4)),
    ):
        middle, left, right, offset = part
        for y in range(rows):
            v[at + y] = jnp.concatenate([left[offset + y], middle[y], right[offset + y]], axis=0)
    acc = [jnp.zeros((64, 128), F32)]

    def emit(y, values):
        h[y] = values
        if 3 <= y < 3 + ROWS:
            acc[0] = acc[0] + values

    conv_rows(v, w, ROWS + 6, emit)
    stats_out(h, acc[0], 3, low, high, msg)


def second_kernel(cells, place, h1, x_low, x_high, r1, gb, w, v, h, low, high, msg):
    mean, inverse, o_low, o_high = read_stats(r1, place, cells)
    scale = inverse * gb[:, 0:1]
    shift = gb[:, 1:2]
    mean2, scale2, shift2 = twice(mean), twice(scale), twice(shift)
    b_low, b_high = shift + o_low * scale, shift + o_high * scale
    rows = ROWS + 6
    for y in range(rows):
        a_low = act(x_low[y].astype(F32) * scale + b_low)
        a_own = act((h1[y] - mean2) * scale2 + shift2)
        a_high = act(x_high[y].astype(F32) * scale + b_high)
        v[y] = masked(a_low, a_own, a_high, kept(place, y, rows, 3))
    acc = [jnp.zeros((64, 128), F32)]

    def emit(y, values):
        h[y] = values
        if 2 <= y < 2 + ROWS:
            acc[0] = acc[0] + values

    conv_rows(v, w, ROWS + 4, emit)
    stats_out(h, acc[0], 2, low, high, msg)


def third_kernel(cells, place, h2, cot, r2, gb, out, msg):
    mean, inverse, _, _ = read_stats(r2, place, cells)
    mean2, inverse2 = twice(mean), twice(inverse)
    gain2, bias2 = twice(gb[:, 2:3]), twice(gb[:, 3:4])
    plain = jnp.zeros((64, 128), F32)
    both = jnp.zeros((64, 128), F32)
    for y in range(ROWS):
        normed = (h2[y + 2] - mean2) * inverse2
        z = normed * gain2 + bias2
        out[y] = act(z).astype(BF16)
        slope = cot[y + 2].astype(F32) * act_slope(z)
        plain = plain + slope
        both = both + slope * normed
    message((fold(total(both)), fold(total(plain))), msg)


def fourth_kernel(
    cells, place, h2, x_low, x_high, cot, t_low, t_high, r2, r3, h1, r1, gb, v2, w,
    slope1, low, high, msg, wg, v, g, acc,
):
    mean, inverse, o_low, o_high = read_stats(r2, place, cells)
    nsum, plain = read_sums(r3)
    gain, bias = gb[:, 2:3], gb[:, 3:4]
    lead = gain * inverse
    p_mean, n_mean = plain / cells, nsum / cells

    def grad(normed, c, gain, bias, lead, p_mean, n_mean):
        slope = c.astype(F32) * act_slope(normed * gain + bias)
        return lead * (slope - p_mean - normed * n_mean)

    one = (gain, bias, lead, p_mean, n_mean)
    two = tuple(twice(a) for a in one)
    mean2, inverse2 = twice(mean), twice(inverse)
    lane = lanes(64)
    rows = ROWS + 4
    for y in range(rows):
        g_low = grad((x_low[y].astype(F32) + o_low) * inverse, t_low[y], *one)
        g_own = grad((h2[y] - mean2) * inverse2, cot[y], *two)
        g_high = grad((x_high[y].astype(F32) + o_high) * inverse, t_high[y], *one)
        v[y] = masked(g_low, g_own, g_high, kept(place, y, rows, 2))
        if 2 <= y < 2 + ROWS:
            put_shifted(g, y - 2, g_own, lane)

    mean, inverse, _, _ = read_stats(r1, place, cells)
    mean2, inverse2 = twice(mean), twice(inverse)
    gain2, bias2 = twice(gb[:, 0:1]), twice(gb[:, 1:2])
    sums = [jnp.zeros((64, 128), F32), jnp.zeros((64, 128), F32)]

    def emit(y, values):
        normed = (h1[y + 2] - mean2) * inverse2
        slope = values * act_slope(normed * gain2 + bias2)
        slope1[y] = slope
        low[y] = slope[0:C].astype(BF16)
        high[y] = slope[C:].astype(BF16)
        if 1 <= y < 1 + ROWS:
            sums[0] = sums[0] + slope * normed
            sums[1] = sums[1] + slope

    conv_rows(v, w, ROWS + 2, emit)
    message((fold(total(sums[0])), fold(total(sums[1]))), msg)
    weight_sums(g, v2, 2, acc, wg)


def fifth_kernel(
    cells, place, slope1, s_low, s_high, h1, x_low, x_high, r1, r4, gb, v1, w, out, wg, v, g, acc
):
    mean, inverse, o_low, o_high = read_stats(r1, place, cells)
    nsum, plain = read_sums(r4)
    lead = gb[:, 0:1] * inverse
    p_mean, n_mean = plain / cells, nsum / cells
    mean2, inverse2, lead2 = twice(mean), twice(inverse), twice(lead)
    p_mean2, n_mean2 = twice(p_mean), twice(n_mean)
    lane = lanes(64)
    rows = ROWS + 2
    for y in range(rows):
        n_low = (x_low[y + 2].astype(F32) + o_low) * inverse
        n_own = (h1[y + 2] - mean2) * inverse2
        n_high = (x_high[y + 2].astype(F32) + o_high) * inverse
        g_low = lead * (s_low[y].astype(F32) - p_mean - n_low * n_mean)
        g_own = lead2 * (slope1[y] - p_mean2 - n_own * n_mean2)
        g_high = lead * (s_high[y].astype(F32) - p_mean - n_high * n_mean)
        v[y] = masked(g_low, g_own, g_high, kept(place, y, rows, 1))
        if 1 <= y < 1 + ROWS:
            put_shifted(g, y - 1, g_own, lane)

    def emit(y, values):
        out[y] = values.astype(BF16)

    conv_rows(v, w, ROWS, emit)
    weight_sums(g, v1, 3, acc, wg)


def call(kernel, ins, outs, name, scratch=(), smem_first=True):
    specs = [SM if (k == 0 and smem_first) else VM for k in range(len(ins))]
    return pl.pallas_call(
        kernel,
        out_shape=outs,
        in_specs=specs,
        out_specs=[VM] * len(outs),
        scratch_shapes=list(scratch),
        compiler_params=pltpu.CompilerParams(vmem_limit_bytes=40 * 1024 * 1024),
        cost_estimate=pl.CostEstimate(
            flops=2_000_000_000, bytes_accessed=6_000_000, transcendentals=0
        ),
        name=name,
    )(*ins)


def up(values, axes):
    count = lax.axis_size(axes)
    return lax.ppermute(values, axes, [(i, i + 1) for i in range(count - 1)])


def down(values, axes):
    count = lax.axis_size(axes)
    return lax.ppermute(values, axes, [(i + 1, i) for i in range(count - 1)])


def share(msg):
    return lax.all_to_all(msg, ALL, 0, 0, tiled=True)


def summed(pieces, count):
    rows = pieces.reshape(-1, 128)
    spare = -rows.shape[0] % count
    rows = jnp.pad(rows, ((0, spare), (0, 0))).reshape(count, -1, 128)
    own = share(rows).sum(axis=0)
    whole = share(jnp.broadcast_to(own[None], rows.shape))
    return whole.reshape(-1, 128)[: rows.shape[0] * rows.shape[1] - spare]


def kernel_matrix(kernel):
    first = jnp.pad(kernel, ((0, 0), (0, 0), (0, 1), (0, 0), (0, 0)))
    second = jnp.pad(kernel, ((0, 0), (0, 0), (1, 0), (0, 0), (0, 0)))
    both = jnp.stack([first, second])
    return jnp.transpose(both, (5, 0, 1, 4, 3, 2)).reshape(192, 384)


def flip_kernel(kernel):
    return jnp.transpose(kernel[:, :, ::-1, ::-1, ::-1], (1, 0, 2, 3, 4))


def unfolded(rows):
    tiles = rows.reshape(3, 3, C, 128)[..., :96].reshape(3, 3, C, 3, C)
    return jnp.transpose(tiles, (2, 4, 3, 1, 0))


def local(features, kernel_one, gain_one, bias_one, kernel_two, gain_two, bias_two, cotangent):
    count_x, count_y = lax.axis_size(GX), lax.axis_size(GY)
    count = count_x * count_y
    cells = float(count * 2 * ROWS * 128)
    gx, gy = lax.axis_index(GX), lax.axis_index(GY)
    at = gx * count_y + gy
    place = jnp.stack(
        [at - count_y, at + count_y, gx > 0, gx < count_x - 1, gy > 0, gy < count_y - 1]
    ).astype(jnp.int32)
    gb = jnp.stack([gain_one, bias_one, gain_two, bias_two], axis=1)

    own = jnp.transpose(features, (2, 1, 0, 3)).reshape(ROWS, 64, 128)
    cot = jnp.transpose(cotangent, (2, 1, 0, 3)).reshape(ROWS, 64, 128)
    x_low = up(own[:, C:], GX)
    x_high = down(own[:, :C], GX)
    y_low = up(jnp.concatenate([own[-4:], cot[-2:]]), GY)
    y_high = down(jnp.concatenate([own[:4], cot[:2]]), GY)
    corner = jnp.concatenate([y_low[:4], y_high[:4]])
    c_low = up(corner[:, C:], GX)
    c_high = down(corner[:, :C], GX)
    w1, w2 = kernel_matrix(kernel_one), kernel_matrix(kernel_two)
    b1, b2 = kernel_matrix(flip_kernel(kernel_one)), kernel_matrix(flip_kernel(kernel_two))

    def rims(rows):
        return [sh((rows, C, 128), BF16)] * 2

    msg = sh((count, 128), F32)
    work = (pltpu.VMEM((192, ROWS * 128), BF16), pltpu.VMEM((192, 384), F32))

    v1, h1, low, high, m1 = call(
        first_kernel,
        (own, y_low[:4], y_high[:4], x_low, x_high, c_low, c_high, w1),
        [sh((40, 128, 128), BF16), sh((38, 64, 128), F32), *rims(38), msg],
        "conv_one",
        smem_first=False,
    )
    h1_low, h1_high = up(high, GX), down(low, GX)
    cot = jnp.concatenate([y_low[4:], cot, y_high[4:]])
    t_low, t_high = up(cot[:, C:], GX), down(cot[:, :C], GX)
    r1 = share(m1)

    v2, h2, low, high, m2 = call(
        lambda *refs: second_kernel(cells, *refs),
        (place, h1, h1_low, h1_high, r1, gb, w2),
        [sh((38, 128, 128), BF16), sh((36, 64, 128), F32), *rims(36), msg],
        "conv_two",
    )
    h2_low, h2_high = up(high, GX), down(low, GX)
    r2 = share(m2)

    output, m3 = call(
        lambda *refs: third_kernel(cells, *refs),
        (place, h2, cot, r2, gb),
        [sh((ROWS, 64, 128), BF16), msg],
        "slope_two",
    )
    r3 = share(m3)

    slope1, low, high, m4, wg2 = call(
        lambda *refs: fourth_kernel(cells, *refs),
        (place, h2, h2_low, h2_high, cot, t_low, t_high, r2, r3, h1, r1, gb, v2, b2),
        [sh((34, 64, 128), F32), *rims(34), msg, sh((9, C, 128), F32)],
        "back_two",
        scratch=(pltpu.VMEM((36, 128, 128), BF16), *work),
    )
    s_low, s_high = up(high, GX), down(low, GX)
    r4 = share(m4)

    grad, wg1 = call(
        lambda *refs: fifth_kernel(cells, *refs),
        (place, slope1, s_low, s_high, h1, h1_low, h1_high, r1, r4, gb, v1, b1),
        [sh((ROWS, 64, 128), BF16), sh((9, C, 128), F32)],
        "back_one",
        scratch=(pltpu.VMEM((34, 128, 128), BF16), *work),
    )
    scale = 1.0 / jnp.sqrt(jnp.float32(cells))
    whole = summed(jnp.concatenate([wg1, wg2]), count) * scale
    half = whole.shape[0] // 2
    norm_grads = jnp.concatenate(
        [r4[:, : 2 * C].sum(axis=0).reshape(2, C), r3[:, : 2 * C].sum(axis=0).reshape(2, C)]
    )

    def back(rows):
        return jnp.transpose(rows.reshape(ROWS, 2, C, 128), (2, 1, 0, 3))

    return (
        back(output),
        back(grad),
        unfolded(whole[:half]),
        unfolded(whole[half:]),
        norm_grads * scale,
    )


def solution(mesh):
    nx, ny = mesh.devices.shape
    parts = (4, nx // 4, ny // 2, 2)
    split = Mesh(mesh.devices.reshape(parts), ALL)
    spec = P(None, GX, GY, None)
    in_specs = (spec, P(), P(), P(), P(), P(), P(), spec)
    out_specs = (spec, spec, P(), P(), P())
    return jax.shard_map(local, mesh=split, in_specs=in_specs, out_specs=out_specs, check_vma=False)
```

```python
import jax
import jax.numpy as jnp
from jax import lax
from jax.experimental import pallas as pl
from jax.experimental.pallas import tpu as pltpu
from jax.sharding import Mesh
from jax.sharding import PartitionSpec as P

GX = ("gx_0", "gx_1")
GY = ("gy_0", "gy_1")
ALL = GX + GY

EPSILON = 1e-05
C = 32
ROWS = 32
F32 = jnp.float32
BF16 = jnp.bfloat16
LN2 = 0.6931471805599453
VM = pl.BlockSpec(memory_space=pltpu.VMEM)
SM = pl.BlockSpec(memory_space=pltpu.SMEM)


def sh(shape, kind):
    return jax.ShapeDtypeStruct(shape, kind)


def from_below(values, lane):
    return jnp.where(lane == 0, 0.0, pltpu.roll(values, 1, 1))


def from_above(values, lane):
    return jnp.where(lane == 127, 0.0, pltpu.roll(values, 127, 1))


def lanes(rows):
    return lax.broadcasted_iota(jnp.int32, (rows, 128), 1)


def conv_rows(v_ref, w_ref, rows, emit):
    lane = lanes(64)
    weights = w_ref[...]
    for y in range(0, rows, 2):
        first = v_ref[y : y + 3].reshape(384, 128)
        second = v_ref[y + 1 : y + 4].reshape(384, 128)
        product = jnp.dot(
            weights, jnp.concatenate([first, second], axis=1), preferred_element_type=F32
        )
        for k in range(2):
            part = product[:, k * 128 : (k + 1) * 128]
            emit(
                y + k,
                part[64:128] + from_below(part[0:64], lane) + from_above(part[128:192], lane),
            )


def fold(column):
    return column[0:C] + column[C : 2 * C]


def total(values):
    return jnp.sum(values, axis=1, keepdims=True)


def twice(column):
    return jnp.concatenate([column, column], axis=0)


def message(columns, msg_ref):
    count = msg_ref.shape[0]
    spare = jnp.zeros((128 - C * len(columns), 1), F32)
    column = jnp.concatenate([*columns, spare], axis=0)
    msg_ref[...] = jnp.transpose(jnp.broadcast_to(column, (128, count)))


def as_row(column):
    return jnp.transpose(jnp.broadcast_to(column, (128, 128)))[0:1]


def rows_message(columns, groups, msg_ref):
    spare = jnp.zeros((128 - C * len(columns), 1), F32)
    row = as_row(jnp.concatenate([*columns, spare], axis=0))
    at = lax.broadcasted_iota(jnp.int32, (8, 128), 0)
    tile = jnp.where(at == 0, jnp.broadcast_to(row, (8, 128)), 0.0)
    msg_ref[...] = jnp.broadcast_to(tile[None], msg_ref.shape)
    for k, group in enumerate(groups):
        for dz in range(3):
            for dy in range(3):
                msg_ref[dz * C : (dz + 1) * C, 1 + 3 * k + dy, :] = group(dz, dy)


def stats_out(h_ref, acc, start, low_ref, high_ref, msg_ref):
    center = fold(total(acc)) / (2 * ROWS * 128)
    both = twice(center)
    spread = jnp.zeros((64, 128), F32)
    for y in range(h_ref.shape[0]):
        off = h_ref[y] - both
        if start <= y < start + ROWS:
            spread = spread + off * off
        low_ref[y] = off[0:C].astype(BF16)
        high_ref[y] = off[C:].astype(BF16)
    message((center, fold(total(spread))), msg_ref)


def read_stats(r_ref, place_ref, cells):
    parts = jnp.transpose(r_ref[...])
    centers = parts[0:C]
    count = parts.shape[1]
    mean = total(centers) / count
    off = centers - mean
    spread = (total(parts[C : 2 * C]) + (2 * ROWS * 128) * total(off * off)) / cells
    at = lax.broadcasted_iota(jnp.int32, centers.shape, 1)
    low = total(jnp.where(at == place_ref[0], off, 0.0))
    high = total(jnp.where(at == place_ref[1], off, 0.0))
    return mean, lax.rsqrt(spread + EPSILON), low, high


def read_sums(r_ref):
    parts = jnp.transpose(jnp.broadcast_to(jnp.sum(r_ref[...], axis=0)[0:1], (128, 128)))[:, 0:1]
    return parts[0:C], parts[C : 2 * C]


def act(z):
    e = jnp.exp2(jnp.abs(z) * (-8.0 / LN2))
    soft = jnp.maximum(z, 0.0) * 0.99 + jnp.log2(1.0 + e) * (0.99 * LN2 / 8.0)
    return 0.01 * z + soft


def act_slope(z):
    return 0.505 + 0.495 * jnp.tanh(4.0 * z)


def kept(place_ref, y, rows, margin):
    low = place_ref[2].astype(F32)
    high = place_ref[3].astype(F32)
    if y < margin:
        edge = place_ref[4].astype(F32)
    elif y >= rows - margin:
        edge = place_ref[5].astype(F32)
    else:
        return low, None, high
    return low * edge, edge, high * edge


def masked(low, own, high, factors):
    f_low, f_own, f_high = factors
    own = own if f_own is None else own * f_own
    return jnp.concatenate([low * f_low, own, high * f_high], axis=0).astype(BF16)


def weight_sums(g_ref, v_ref, first, acc_ref):
    step = 4
    for y in range(0, ROWS, step):
        right = jnp.concatenate(
            [v_ref[first + y + k : first + y + k + 3].reshape(384, 128) for k in range(step)], axis=1
        )
        left = g_ref[:, y * 128 : (y + step) * 128]
        product = lax.dot_general(
            left, right, (((1,), (1,)), ((), ())), preferred_element_type=F32
        )
        if y == 0:
            acc_ref[...] = product
        else:
            acc_ref[...] += product


def folded(acc_ref):
    def tile(dz, dy):
        both = acc_ref[dz * 64 : dz * 64 + 64, dy * 128 : dy * 128 + 128]
        return both[0:C] + pltpu.roll(both[C:], 96, 1)

    return tile


def put_shifted(g_ref, y, values, lane):
    at = slice(y * 128, (y + 1) * 128)
    g_ref[0:64, at] = from_above(values, lane).astype(BF16)
    g_ref[64:128, at] = values.astype(BF16)
    g_ref[128:192, at] = from_below(values, lane).astype(BF16)


def pack_kernel(own, cot, up_ref, down_ref):
    up_ref[0:4] = own[ROWS - 4 : ROWS]
    up_ref[4:6] = cot[ROWS - 2 : ROWS]
    down_ref[0:4] = own[0:4]
    down_ref[4:6] = cot[0:2]


def planes_kernel(own, y_low, y_high, up_ref, down_ref):
    for part, rows, at in ((y_low, 4, 0), (own, ROWS, 4), (y_high, 4, ROWS + 4)):
        down_ref[at : at + rows] = part[0:rows, 0:C]
        up_ref[at : at + rows] = part[0:rows, C : 2 * C]


def weights_kernel(k1, k2, w1, w2, b1, b2):
    row = lax.broadcasted_iota(jnp.int32, (C, 128), 0)
    col = lax.broadcasted_iota(jnp.int32, (C, 128), 1)
    eye = jnp.where(row == col, 1.0, 0.0)[:, 0:C].astype(BF16)
    zero = jnp.zeros((C, C), BF16)
    for k_ref, w_ref, b_ref in ((k1, w1, b1), (k2, w2, b2)):
        lined = jnp.zeros((9 * C, 128), F32)
        for dx in range(3):
            spot = jnp.where(row + dx * C == col, 1.0, 0.0).astype(BF16)
            lined = lined + jnp.dot(
                k_ref[dx * 9 : dx * 9 + 9].reshape(9 * C, C), spot, preferred_element_type=F32
            )
        stack = []
        for t in range(9):
            stack += [k_ref[18 + t], k_ref[9 + t], k_ref[t], zero]
        turned = lax.dot_general(
            eye,
            jnp.concatenate(stack, axis=0),
            (((1,), (1,)), ((), ())),
            preferred_element_type=F32,
        )
        for dy in range(3):
            for dz in range(3):
                here = slice(dy * 128, dy * 128 + 128)
                t = dy * 3 + dz
                tile = lined[t * C : t * C + C]
                w_ref[dz * 64 : dz * 64 + C, here] = tile.astype(BF16)
                w_ref[dz * 64 + C : dz * 64 + 64, here] = pltpu.roll(tile, C, 1).astype(BF16)
                t = 8 - t
                tile = turned[:, t * 128 : t * 128 + 128]
                b_ref[dz * 64 : dz * 64 + C, here] = tile.astype(BF16)
                b_ref[dz * 64 + C : dz * 64 + 64, here] = pltpu.roll(tile, C, 1).astype(BF16)


def first_kernel(own, y_low, y_high, x_low, x_high, w, v, h, low, high, msg):
    for middle, rows, at in ((y_low, 4, 0), (own, ROWS, 4), (y_high, 4, ROWS + 4)):
        for y in range(rows):
            v[at + y] = jnp.concatenate([x_low[at + y], middle[y], x_high[at + y]], axis=0)
    acc = [jnp.zeros((64, 128), F32)]

    def emit(y, values):
        h[y] = values
        if 3 <= y < 3 + ROWS:
            acc[0] = acc[0] + values

    conv_rows(v, w, ROWS + 6, emit)
    stats_out(h, acc[0], 3, low, high, msg)


def second_kernel(cells, place, h1, x_low, x_high, r1, gb, w, v, h, low, high, msg):
    mean, inverse, o_low, o_high = read_stats(r1, place, cells)
    scale = inverse * gb[:, 0:1]
    shift = gb[:, 1:2]
    mean2, scale2, shift2 = twice(mean), twice(scale), twice(shift)
    b_low, b_high = shift + o_low * scale, shift + o_high * scale
    rows = ROWS + 6
    for y in range(rows):
        a_low = act(x_low[y].astype(F32) * scale + b_low)
        a_own = act((h1[y] - mean2) * scale2 + shift2)
        a_high = act(x_high[y].astype(F32) * scale + b_high)
        v[y] = masked(a_low, a_own, a_high, kept(place, y, rows, 3))
    acc = [jnp.zeros((64, 128), F32)]

    def emit(y, values):
        h[y] = values
        if 2 <= y < 2 + ROWS:
            acc[0] = acc[0] + values

    conv_rows(v, w, ROWS + 4, emit)
    stats_out(h, acc[0], 2, low, high, msg)


def side_kernel(cells, place, h1, r1, v1, xn, x1, g, acc):
    mean, inverse, _, _ = read_stats(r1, place, cells)
    mean2, inverse2 = twice(mean), twice(inverse)
    lane = lanes(64)
    for y in range(ROWS):
        put_shifted(g, y, (h1[y + 3] - mean2) * inverse2, lane)
    weight_sums(g, v1, 3, acc)
    tile = folded(acc)
    for dz in range(3):
        for dy in range(3):
            xn[dz * 3 + dy] = tile(dz, dy)
    lane = lanes(128)
    inner = v1[5].astype(F32)
    for y in range(6, 3 + ROWS):
        inner = inner + v1[y].astype(F32)
    ends = [v1[y].astype(F32) for y in (3, 4, 3 + ROWS, 4 + ROWS)]
    windows = (inner + ends[0] + ends[1], inner + ends[1] + ends[2], inner + ends[2] + ends[3])
    columns = []
    for dz in range(3):
        for dy in range(3):
            values = windows[dy]
            if dz == 0:
                values = jnp.where(lane == 127, 0.0, values)
            if dz == 2:
                values = jnp.where(lane == 0, 0.0, values)
            column = total(values)
            column = column + jnp.concatenate([column[C:], column[:C]], axis=0)
            columns.append(column)
    wide = jnp.concatenate(columns + [jnp.zeros((128, 119), F32)], axis=1)
    x1[...] = jnp.transpose(wide)[0:16]


def cot_row(cot, y_low, y_high, y):
    if y < 2:
        return y_low[4 + y]
    if y < 2 + ROWS:
        return cot[y - 2]
    return y_high[2 + y - ROWS]


def third_kernel(cells, place, h2, cot, y_low, y_high, r2, gb, xn, x1, out, t_low, t_high, msg):
    mean, inverse, _, _ = read_stats(r2, place, cells)
    mean2, inverse2 = twice(mean), twice(inverse)
    gain2, bias2 = twice(gb[:, 2:3]), twice(gb[:, 3:4])
    plain = jnp.zeros((64, 128), F32)
    both = jnp.zeros((64, 128), F32)
    for y in range(ROWS):
        normed = (h2[y + 2] - mean2) * inverse2
        z = normed * gain2 + bias2
        out[y] = act(z).astype(BF16)
        slope = cot[y].astype(F32) * act_slope(z)
        plain = plain + slope
        both = both + slope * normed
    for y in range(ROWS + 4):
        values = cot_row(cot, y_low, y_high, y)
        t_low[y] = values[0:C]
        t_high[y] = values[C:]

    def ones(dz, dy):
        return jnp.broadcast_to(x1[dz * 3 + dy : dz * 3 + dy + 1, :], (C, 128))

    rows_message(
        (fold(total(both)), fold(total(plain))), (lambda dz, dy: xn[dz * 3 + dy], ones), msg
    )


def fourth_kernel(
    cells, place, h2, x_low, x_high, cot, y_low, y_high, t_low, t_high, r2, r3, h1, r1, gb,
    v1, v2, w, slope1, low, high, msg, v, g, acc, acc1,
):
    mean, inverse, o_low, o_high = read_stats(r2, place, cells)
    nsum, plain = read_sums(r3)
    gain, bias = gb[:, 2:3], gb[:, 3:4]
    lead = gain * inverse
    p_mean, n_mean = plain / cells, nsum / cells

    def grad(normed, c, gain, bias, lead, p_mean, n_mean):
        slope = c.astype(F32) * act_slope(normed * gain + bias)
        return lead * (slope - p_mean - normed * n_mean)

    one = (gain, bias, lead, p_mean, n_mean)
    two = tuple(twice(a) for a in one)
    mean2, inverse2 = twice(mean), twice(inverse)
    lane = lanes(64)
    rows = ROWS + 4
    for y in range(rows):
        g_low = grad((x_low[y].astype(F32) + o_low) * inverse, t_low[y], *one)
        g_own = grad((h2[y] - mean2) * inverse2, cot_row(cot, y_low, y_high, y), *two)
        g_high = grad((x_high[y].astype(F32) + o_high) * inverse, t_high[y], *one)
        v[y] = masked(g_low, g_own, g_high, kept(place, y, rows, 2))
        if 2 <= y < 2 + ROWS:
            put_shifted(g, y - 2, g_own, lane)
    weight_sums(g, v2, 2, acc)

    mean, inverse, _, _ = read_stats(r1, place, cells)
    mean2, inverse2 = twice(mean), twice(inverse)
    gain2, bias2 = twice(gb[:, 0:1]), twice(gb[:, 1:2])
    sums = [jnp.zeros((64, 128), F32), jnp.zeros((64, 128), F32)]

    def emit(y, values):
        normed = (h1[y + 2] - mean2) * inverse2
        slope = values * act_slope(normed * gain2 + bias2)
        slope1[y] = slope
        low[y] = slope[0:C].astype(BF16)
        high[y] = slope[C:].astype(BF16)
        if 1 <= y < 1 + ROWS:
            sums[0] = sums[0] + slope * normed
            sums[1] = sums[1] + slope
            put_shifted(g, y - 1, slope, lane)

    conv_rows(v, w, ROWS + 2, emit)
    weight_sums(g, v1, 3, acc1)
    rows_message(
        (fold(total(sums[0])), fold(total(sums[1]))), (folded(acc1), folded(acc)), msg
    )


def owner_kernel(cells, place, r1, r3, r4, gb, msg, norms):
    _, inverse, _, _ = read_stats(r1, place, cells)
    nsum, plain = read_sums(r4)
    mine = lax.broadcasted_iota(jnp.int32, (C, 1), 0) == place[6]

    def picked(column):
        return jnp.sum(jnp.where(mine, column, 0.0), axis=0, keepdims=True)

    scale = cells**-0.5
    lead = picked(gb[:, 0:1] * inverse) * scale
    third, fourth = jnp.sum(r3[...], axis=0), jnp.sum(r4[...], axis=0)
    xn, x1 = third[1:4], third[4:7]
    one = lead * (fourth[1:4] - picked(plain) * (x1 / cells) - picked(nsum) * (xn / cells))
    two = fourth[4:7] * scale
    tile = jnp.concatenate([one, two, jnp.zeros((2, 128), F32)], axis=0)
    msg[...] = jnp.broadcast_to(tile[None], msg.shape)
    for k, row in enumerate((fourth[0:1], third[0:1])):
        norms[2 * k : 2 * k + 1] = row[:, 0:C] * scale
        norms[2 * k + 1 : 2 * k + 2] = row[:, C : 2 * C] * scale


def finish_kernel(parts, one, two):
    for dz in range(3):
        for dy in range(3):
            for k, out in enumerate((one, two)):
                tile = parts[dz * C : (dz + 1) * C, 3 * k + dy, :]
                for dx in range(3):
                    out[dx * 9 + dy * 3 + dz] = tile[:, dx * C : (dx + 1) * C]


def fifth_kernel(
    cells, place, slope1, s_low, s_high, h1, x_low, x_high, r1, r4, gb, w, out, v
):
    mean, inverse, o_low, o_high = read_stats(r1, place, cells)
    nsum, plain = read_sums(r4)
    lead = gb[:, 0:1] * inverse
    p_mean, n_mean = plain / cells, nsum / cells
    mean2, inverse2, lead2 = twice(mean), twice(inverse), twice(lead)
    p_mean2, n_mean2 = twice(p_mean), twice(n_mean)
    rows = ROWS + 2
    for y in range(rows):
        n_low = (x_low[y + 2].astype(F32) + o_low) * inverse
        n_own = (h1[y + 2] - mean2) * inverse2
        n_high = (x_high[y + 2].astype(F32) + o_high) * inverse
        g_low = lead * (s_low[y].astype(F32) - p_mean - n_low * n_mean)
        g_own = lead2 * (slope1[y] - p_mean2 - n_own * n_mean2)
        g_high = lead * (s_high[y].astype(F32) - p_mean - n_high * n_mean)
        v[y] = masked(g_low, g_own, g_high, kept(place, y, rows, 1))

    def emit(y, values):
        out[y] = values.astype(BF16)

    conv_rows(v, w, ROWS, emit)


def call(kernel, ins, outs, name, scratch=(), smem_first=True):
    specs = [SM if (k == 0 and smem_first) else VM for k in range(len(ins))]
    return pl.pallas_call(
        kernel,
        out_shape=outs,
        in_specs=specs,
        out_specs=[VM] * len(outs),
        scratch_shapes=list(scratch),
        compiler_params=pltpu.CompilerParams(vmem_limit_bytes=24 * 1024 * 1024),
        cost_estimate=pl.CostEstimate(
            flops=2_000_000_000, bytes_accessed=6_000_000, transcendentals=0
        ),
        name=name,
    )(*ins)


def up(values, axes):
    count = lax.axis_size(axes)
    return lax.ppermute(values, axes, [(i, i + 1) for i in range(count - 1)])


def down(values, axes):
    count = lax.axis_size(axes)
    return lax.ppermute(values, axes, [(i + 1, i) for i in range(count - 1)])


def share(msg):
    return lax.all_to_all(msg, ALL, 0, 0, tiled=True)


def local(features, kernel_one, gain_one, bias_one, kernel_two, gain_two, bias_two, cotangent):
    count_x, count_y = lax.axis_size(GX), lax.axis_size(GY)
    count = count_x * count_y
    cells = float(count * 2 * ROWS * 128)
    gx, gy = lax.axis_index(GX), lax.axis_index(GY)
    at = gx * count_y + gy
    place = jnp.stack(
        [at - count_y, at + count_y, gx > 0, gx < count_x - 1, gy > 0, gy < count_y - 1, at % C]
    ).astype(jnp.int32)
    gb = jnp.stack([gain_one, bias_one, gain_two, bias_two], axis=1)

    own = jnp.transpose(features, (2, 1, 0, 3)).reshape(ROWS, 64, 128)
    cot = jnp.transpose(cotangent, (2, 1, 0, 3)).reshape(ROWS, 64, 128)

    def rims(rows):
        return [sh((rows, C, 128), BF16)] * 2

    msg, wide = sh((count, 128), F32), sh((count, 8, 128), F32)
    corr = (pltpu.VMEM((192, ROWS * 128), BF16), pltpu.VMEM((192, 384), F32))

    y_up, y_down = call(
        pack_kernel, (own, cot), [sh((6, 64, 128), BF16)] * 2, "pack", smem_first=False
    )
    y_low, y_high = up(y_up, GY), down(y_down, GY)
    x_up, x_down = call(planes_kernel, (own, y_low, y_high), rims(40), "planes", smem_first=False)
    x_low, x_high = up(x_up, GX), down(x_down, GX)
    taps = [
        jnp.transpose(k, (2, 3, 4, 0, 1)).reshape(27, C, C) for k in (kernel_one, kernel_two)
    ]
    w1, w2, b1, b2 = call(
        weights_kernel, taps, [sh((192, 384), BF16)] * 4, "weights", smem_first=False
    )

    v1, h1, low, high, m1 = call(
        first_kernel,
        (own, y_low, y_high, x_low, x_high, w1),
        [sh((40, 128, 128), BF16), sh((38, 64, 128), F32), *rims(38), msg],
        "conv_one",
        smem_first=False,
    )
    h1_low, h1_high = up(high, GX), down(low, GX)
    r1 = share(m1)

    v2, h2, low, high, m2 = call(
        lambda *refs: second_kernel(cells, *refs),
        (place, h1, h1_low, h1_high, r1, gb, w2),
        [sh((38, 128, 128), BF16), sh((36, 64, 128), F32), *rims(36), msg],
        "conv_two",
    )
    h2_low, h2_high = up(high, GX), down(low, GX)
    r2 = share(m2)
    xn, x1 = call(
        lambda *refs: side_kernel(cells, *refs),
        (place, h1, r1, v1),
        [sh((9, C, 128), F32), sh((16, 128), F32)],
        "normed_features",
        scratch=corr,
    )

    output, low, high, m3 = call(
        lambda *refs: third_kernel(cells, *refs),
        (place, h2, cot, y_low, y_high, r2, gb, xn, x1),
        [sh((ROWS, 64, 128), BF16), *rims(36), wide],
        "slope_two",
    )
    t_low, t_high = up(high, GX), down(low, GX)
    r3 = share(m3)

    slope1, low, high, m4 = call(
        lambda *refs: fourth_kernel(cells, *refs),
        (
            place, h2, h2_low, h2_high, cot, y_low, y_high, t_low, t_high, r2, r3, h1, r1, gb,
            v1, v2, b2,
        ),
        [sh((34, 64, 128), F32), *rims(34), wide],
        "back_two",
        scratch=(pltpu.VMEM((36, 128, 128), BF16), *corr, corr[1]),
    )
    s_low, s_high = up(high, GX), down(low, GX)
    r4 = share(m4)

    m5, norm_grads = call(
        lambda *refs: owner_kernel(cells, *refs),
        (place, r1, r3, r4, gb),
        [wide, sh((4, C), F32)],
        "own_rows",
    )
    r5 = share(m5)
    (grad,) = call(
        lambda *refs: fifth_kernel(cells, *refs),
        (place, slope1, s_low, s_high, h1, h1_low, h1_high, r1, r4, gb, b1),
        [sh((ROWS, 64, 128), BF16)],
        "back_one",
        scratch=(pltpu.VMEM((34, 128, 128), BF16),),
    )
    grads = call(finish_kernel, (r5,), [sh((27, C, C), F32)] * 2, "finish", smem_first=False)
    one, two = [jnp.transpose(k.reshape(3, 3, 3, C, C), (3, 4, 0, 1, 2)) for k in grads]

    def back(rows):
        return jnp.transpose(rows.reshape(ROWS, 2, C, 128), (2, 1, 0, 3))

    return back(output), back(grad), one, two, norm_grads


def solution(mesh):
    nx, ny = mesh.devices.shape
    parts = (4, nx // 4, ny // 2, 2)
    split = Mesh(mesh.devices.reshape(parts), ALL)
    spec = P(None, GX, GY, None)
    in_specs = (spec, P(), P(), P(), P(), P(), P(), spec)
    out_specs = (spec, spec, P(), P(), P())
    return jax.shard_map(local, mesh=split, in_specs=in_specs, out_specs=out_specs, check_vma=False)
```

```python
import jax
import jax.numpy as jnp
from jax import lax
from jax.experimental import pallas as pl
from jax.experimental.pallas import tpu as pltpu
from jax.sharding import Mesh
from jax.sharding import PartitionSpec as P

GX = ("gx_0", "gx_1")
GY = ("gy_0", "gy_1")
ALL = GX + GY

EPSILON = 1e-05
C = 32
ROWS = 32
F32 = jnp.float32
BF16 = jnp.bfloat16
LN2 = 0.6931471805599453
SM = pl.BlockSpec(memory_space=pltpu.SMEM)


def sh(shape, kind):
    return jax.ShapeDtypeStruct(shape, kind)


def from_below(values, lane):
    return jnp.where(lane == 0, 0.0, pltpu.roll(values, 1, 1))


def from_above(values, lane):
    return jnp.where(lane == 127, 0.0, pltpu.roll(values, 127, 1))


def lanes(rows):
    return lax.broadcasted_iota(jnp.int32, (rows, 128), 1)


def conv_rows(v_ref, w_ref, rows, emit):
    lane = lanes(64)
    weights = w_ref[...]
    for y in range(0, rows, 2):
        first = v_ref[y : y + 3].reshape(384, 128)
        second = v_ref[y + 1 : y + 4].reshape(384, 128)
        product = jnp.dot(
            weights, jnp.concatenate([first, second], axis=1), preferred_element_type=F32
        )
        for k in range(2):
            part = product[:, k * 128 : (k + 1) * 128]
            emit(
                y + k,
                part[64:128] + from_below(part[0:64], lane) + from_above(part[128:192], lane),
            )


def fold(column):
    return column[0:C] + column[C : 2 * C]


def total(values):
    return jnp.sum(values, axis=1, keepdims=True)


def twice(column):
    return jnp.concatenate([column, column], axis=0)


def message(columns, msg_ref):
    count = msg_ref.shape[0]
    spare = jnp.zeros((128 - C * len(columns), 1), F32)
    column = jnp.concatenate([*columns, spare], axis=0)
    msg_ref[...] = jnp.transpose(jnp.broadcast_to(column, (128, count)))


def as_row(column):
    return jnp.transpose(jnp.broadcast_to(column, (128, 128)))[0:1]


def rows_message(columns, groups, msg_ref):
    spare = jnp.zeros((128 - C * len(columns), 1), F32)
    row = as_row(jnp.concatenate([*columns, spare], axis=0))
    at = lax.broadcasted_iota(jnp.int32, (8, 128), 0)
    tile = jnp.where(at == 0, jnp.broadcast_to(row, (8, 128)), 0.0)
    msg_ref[...] = jnp.broadcast_to(tile[None], msg_ref.shape)
    for k, group in enumerate(groups):
        for dz in range(3):
            for dy in range(3):
                msg_ref[dz * C : (dz + 1) * C, 1 + 3 * k + dy, :] = group(dz, dy)


def stats_out(send, h_ref, acc, start, low_ref, high_ref, msg_ref):
    center = fold(total(acc)) / (2 * ROWS * 128)
    both = twice(center)
    spread = jnp.zeros((64, 128), F32)
    for y in range(h_ref.shape[0]):
        off = h_ref[y] - both
        if start <= y < start + ROWS:
            spread = spread + off * off
        low_ref[y] = off[0:C].astype(BF16)
        high_ref[y] = off[C:].astype(BF16)
    send(low_ref, high_ref)
    message((center, fold(total(spread))), msg_ref)


def read_stats(r_ref, place_ref, cells):
    parts = jnp.transpose(r_ref[...])
    centers = parts[0:C]
    count = parts.shape[1]
    mean = total(centers) / count
    off = centers - mean
    spread = (total(parts[C : 2 * C]) + (2 * ROWS * 128) * total(off * off)) / cells
    at = lax.broadcasted_iota(jnp.int32, centers.shape, 1)
    low = total(jnp.where(at == place_ref[0], off, 0.0))
    high = total(jnp.where(at == place_ref[1], off, 0.0))
    return mean, lax.rsqrt(spread + EPSILON), low, high


def read_sums(r_ref):
    parts = jnp.transpose(jnp.broadcast_to(jnp.sum(r_ref[...], axis=0)[0:1], (128, 128)))[:, 0:1]
    return parts[0:C], parts[C : 2 * C]


def act(z):
    e = jnp.exp2(jnp.abs(z) * (-8.0 / LN2))
    soft = jnp.maximum(z, 0.0) * 0.99 + jnp.log2(1.0 + e) * (0.99 * LN2 / 8.0)
    return 0.01 * z + soft


def act_slope(z):
    return 0.505 + 0.495 * jnp.tanh(4.0 * z)


def kept(place_ref, y, rows, margin):
    low = place_ref[2].astype(F32)
    high = place_ref[3].astype(F32)
    if y < margin:
        edge = place_ref[4].astype(F32)
    elif y >= rows - margin:
        edge = place_ref[5].astype(F32)
    else:
        return low, None, high
    return low * edge, edge, high * edge


def masked(low, own, high, factors):
    f_low, f_own, f_high = factors
    own = own if f_own is None else own * f_own
    return jnp.concatenate([low * f_low, own, high * f_high], axis=0).astype(BF16)


def weight_sums(g_ref, v_ref, first, acc_ref):
    step = 4
    for y in range(0, ROWS, step):
        right = jnp.concatenate(
            [v_ref[first + y + k : first + y + k + 3].reshape(384, 128) for k in range(step)], axis=1
        )
        left = g_ref[:, y * 128 : (y + step) * 128]
        product = lax.dot_general(
            left, right, (((1,), (1,)), ((), ())), preferred_element_type=F32
        )
        if y == 0:
            acc_ref[...] = product
        else:
            acc_ref[...] += product


def folded(acc_ref):
    def tile(dz, dy):
        both = acc_ref[dz * 64 : dz * 64 + 64, dy * 128 : dy * 128 + 128]
        return both[0:C] + pltpu.roll(both[C:], 96, 1)

    return tile


def put_shifted(g_ref, y, values, lane):
    at = slice(y * 128, (y + 1) * 128)
    g_ref[0:64, at] = from_above(values, lane).astype(BF16)
    g_ref[64:128, at] = values.astype(BF16)
    g_ref[128:192, at] = from_below(values, lane).astype(BF16)


def pack_kernel(need, send, own, cot, up_ref, down_ref):
    need(own, cot)
    up_ref[0:4] = own[ROWS - 4 : ROWS]
    up_ref[4:6] = cot[ROWS - 2 : ROWS]
    down_ref[0:4] = own[0:4]
    down_ref[4:6] = cot[0:2]


def planes_kernel(need, send, own, y_low, y_high, up_ref, down_ref):
    need(own, y_low, y_high)
    for part, rows, at in ((y_low, 4, 0), (own, ROWS, 4), (y_high, 4, ROWS + 4)):
        down_ref[at : at + rows] = part[0:rows, 0:C]
        up_ref[at : at + rows] = part[0:rows, C : 2 * C]


def weights_kernel(need, send, k1, k2, w1, w2, b1, b2):
    need(k1, k2)
    row = lax.broadcasted_iota(jnp.int32, (C, 128), 0)
    col = lax.broadcasted_iota(jnp.int32, (C, 128), 1)
    eye = jnp.where(row == col, 1.0, 0.0)[:, 0:C].astype(BF16)
    zero = jnp.zeros((C, C), BF16)
    for k_ref, w_ref, b_ref in ((k1, w1, b1), (k2, w2, b2)):
        lined = jnp.zeros((9 * C, 128), F32)
        for dx in range(3):
            spot = jnp.where(row + dx * C == col, 1.0, 0.0).astype(BF16)
            lined = lined + jnp.dot(
                k_ref[dx * 9 : dx * 9 + 9].reshape(9 * C, C), spot, preferred_element_type=F32
            )
        stack = []
        for t in range(9):
            stack += [k_ref[18 + t], k_ref[9 + t], k_ref[t], zero]
        turned = lax.dot_general(
            eye,
            jnp.concatenate(stack, axis=0),
            (((1,), (1,)), ((), ())),
            preferred_element_type=F32,
        )
        for dy in range(3):
            for dz in range(3):
                here = slice(dy * 128, dy * 128 + 128)
                t = dy * 3 + dz
                tile = lined[t * C : t * C + C]
                w_ref[dz * 64 : dz * 64 + C, here] = tile.astype(BF16)
                w_ref[dz * 64 + C : dz * 64 + 64, here] = pltpu.roll(tile, C, 1).astype(BF16)
                t = 8 - t
                tile = turned[:, t * 128 : t * 128 + 128]
                b_ref[dz * 64 : dz * 64 + C, here] = tile.astype(BF16)
                b_ref[dz * 64 + C : dz * 64 + 64, here] = pltpu.roll(tile, C, 1).astype(BF16)


def first_kernel(need, send, own, y_low, y_high, x_low, x_high, w, v, h, low, high, msg):
    need(own, y_low, y_high, x_low, x_high)
    for middle, rows, at in ((y_low, 4, 0), (own, ROWS, 4), (y_high, 4, ROWS + 4)):
        for y in range(rows):
            v[at + y] = jnp.concatenate([x_low[at + y], middle[y], x_high[at + y]], axis=0)
    send(v)
    need(w)
    acc = [jnp.zeros((64, 128), F32)]

    def emit(y, values):
        h[y] = values
        if 3 <= y < 3 + ROWS:
            acc[0] = acc[0] + values

    conv_rows(v, w, ROWS + 6, emit)
    send(h)
    stats_out(send, h, acc[0], 3, low, high, msg)


def second_kernel(cells, need, send, place, h1, x_low, x_high, r1, gb, w, v, h, low, high, msg):
    need(r1, gb)
    mean, inverse, o_low, o_high = read_stats(r1, place, cells)
    need(h1, x_low, x_high)
    scale = inverse * gb[:, 0:1]
    shift = gb[:, 1:2]
    mean2, scale2, shift2 = twice(mean), twice(scale), twice(shift)
    b_low, b_high = shift + o_low * scale, shift + o_high * scale
    rows = ROWS + 6
    for y in range(rows):
        a_low = act(x_low[y].astype(F32) * scale + b_low)
        a_own = act((h1[y] - mean2) * scale2 + shift2)
        a_high = act(x_high[y].astype(F32) * scale + b_high)
        v[y] = masked(a_low, a_own, a_high, kept(place, y, rows, 3))
    send(v)
    need(w)
    acc = [jnp.zeros((64, 128), F32)]

    def emit(y, values):
        h[y] = values
        if 2 <= y < 2 + ROWS:
            acc[0] = acc[0] + values

    conv_rows(v, w, ROWS + 4, emit)
    send(h)
    stats_out(send, h, acc[0], 2, low, high, msg)


def side_kernel(cells, need, send, place, h1, r1, v1, xn, x1, g, acc):
    need(h1, r1, v1)
    mean, inverse, _, _ = read_stats(r1, place, cells)
    mean2, inverse2 = twice(mean), twice(inverse)
    lane = lanes(64)
    for y in range(ROWS):
        put_shifted(g, y, (h1[y + 3] - mean2) * inverse2, lane)
    weight_sums(g, v1, 3, acc)
    tile = folded(acc)
    for dz in range(3):
        for dy in range(3):
            xn[dz * 3 + dy] = tile(dz, dy)
    lane = lanes(128)
    inner = v1[5].astype(F32)
    for y in range(6, 3 + ROWS):
        inner = inner + v1[y].astype(F32)
    ends = [v1[y].astype(F32) for y in (3, 4, 3 + ROWS, 4 + ROWS)]
    windows = (inner + ends[0] + ends[1], inner + ends[1] + ends[2], inner + ends[2] + ends[3])
    columns = []
    for dz in range(3):
        for dy in range(3):
            values = windows[dy]
            if dz == 0:
                values = jnp.where(lane == 127, 0.0, values)
            if dz == 2:
                values = jnp.where(lane == 0, 0.0, values)
            column = total(values)
            column = column + jnp.concatenate([column[C:], column[:C]], axis=0)
            columns.append(column)
    wide = jnp.concatenate(columns + [jnp.zeros((128, 119), F32)], axis=1)
    x1[...] = jnp.transpose(wide)[0:16]


def cot_row(cot, y_low, y_high, y):
    if y < 2:
        return y_low[4 + y]
    if y < 2 + ROWS:
        return cot[y - 2]
    return y_high[2 + y - ROWS]


def third_kernel(cells, need, send, place, h2, cot, y_low, y_high, r2, gb, xn, x1, out, t_low, t_high, msg):
    need(r2, gb)
    mean, inverse, _, _ = read_stats(r2, place, cells)
    need(h2, cot, y_low, y_high)
    mean2, inverse2 = twice(mean), twice(inverse)
    gain2, bias2 = twice(gb[:, 2:3]), twice(gb[:, 3:4])
    plain = jnp.zeros((64, 128), F32)
    both = jnp.zeros((64, 128), F32)
    for y in range(ROWS):
        normed = (h2[y + 2] - mean2) * inverse2
        z = normed * gain2 + bias2
        out[y] = act(z).astype(BF16)
        slope = cot[y].astype(F32) * act_slope(z)
        plain = plain + slope
        both = both + slope * normed
    send(out)
    for y in range(ROWS + 4):
        values = cot_row(cot, y_low, y_high, y)
        t_low[y] = values[0:C]
        t_high[y] = values[C:]
    send(t_low, t_high)
    need(xn, x1)

    def ones(dz, dy):
        return jnp.broadcast_to(x1[dz * 3 + dy : dz * 3 + dy + 1, :], (C, 128))

    rows_message(
        (fold(total(both)), fold(total(plain))), (lambda dz, dy: xn[dz * 3 + dy], ones), msg
    )


def fourth_kernel(
    cells, need, send, place, h2, x_low, x_high, cot, y_low, y_high, t_low, t_high, r2, r3, h1, r1, gb,
    v1, v2, w, slope1, low, high, msg, v, g, acc, acc1,
):
    need(r2, r3, gb)
    mean, inverse, o_low, o_high = read_stats(r2, place, cells)
    nsum, plain = read_sums(r3)
    need(h2, x_low, x_high, cot, y_low, y_high, t_low, t_high)
    gain, bias = gb[:, 2:3], gb[:, 3:4]
    lead = gain * inverse
    p_mean, n_mean = plain / cells, nsum / cells

    def grad(normed, c, gain, bias, lead, p_mean, n_mean):
        slope = c.astype(F32) * act_slope(normed * gain + bias)
        return lead * (slope - p_mean - normed * n_mean)

    one = (gain, bias, lead, p_mean, n_mean)
    two = tuple(twice(a) for a in one)
    mean2, inverse2 = twice(mean), twice(inverse)
    lane = lanes(64)
    rows = ROWS + 4
    for y in range(rows):
        g_low = grad((x_low[y].astype(F32) + o_low) * inverse, t_low[y], *one)
        g_own = grad((h2[y] - mean2) * inverse2, cot_row(cot, y_low, y_high, y), *two)
        g_high = grad((x_high[y].astype(F32) + o_high) * inverse, t_high[y], *one)
        v[y] = masked(g_low, g_own, g_high, kept(place, y, rows, 2))
        if 2 <= y < 2 + ROWS:
            put_shifted(g, y - 2, g_own, lane)
    need(v2)
    weight_sums(g, v2, 2, acc)

    need(h1, r1, w)
    mean, inverse, _, _ = read_stats(r1, place, cells)
    mean2, inverse2 = twice(mean), twice(inverse)
    gain2, bias2 = twice(gb[:, 0:1]), twice(gb[:, 1:2])
    sums = [jnp.zeros((64, 128), F32), jnp.zeros((64, 128), F32)]

    def emit(y, values):
        normed = (h1[y + 2] - mean2) * inverse2
        slope = values * act_slope(normed * gain2 + bias2)
        slope1[y] = slope
        low[y] = slope[0:C].astype(BF16)
        high[y] = slope[C:].astype(BF16)
        if 1 <= y < 1 + ROWS:
            sums[0] = sums[0] + slope * normed
            sums[1] = sums[1] + slope
            put_shifted(g, y - 1, slope, lane)

    conv_rows(v, w, ROWS + 2, emit)
    send(slope1, low, high)
    need(v1)
    weight_sums(g, v1, 3, acc1)
    rows_message(
        (fold(total(sums[0])), fold(total(sums[1]))), (folded(acc1), folded(acc)), msg
    )


def owner_kernel(cells, need, send, place, r1, r3, r4, gb, msg, norms):
    need(r1, r3, r4, gb)
    _, inverse, _, _ = read_stats(r1, place, cells)
    nsum, plain = read_sums(r4)
    mine = lax.broadcasted_iota(jnp.int32, (C, 1), 0) == place[6]

    def picked(column):
        return jnp.sum(jnp.where(mine, column, 0.0), axis=0, keepdims=True)

    scale = cells**-0.5
    lead = picked(gb[:, 0:1] * inverse) * scale
    third, fourth = jnp.sum(r3[...], axis=0), jnp.sum(r4[...], axis=0)
    xn, x1 = third[1:4], third[4:7]
    one = lead * (fourth[1:4] - picked(plain) * (x1 / cells) - picked(nsum) * (xn / cells))
    two = fourth[4:7] * scale
    tile = jnp.concatenate([one, two, jnp.zeros((2, 128), F32)], axis=0)
    msg[...] = jnp.broadcast_to(tile[None], msg.shape)
    for k, row in enumerate((fourth[0:1], third[0:1])):
        norms[2 * k : 2 * k + 1] = row[:, 0:C] * scale
        norms[2 * k + 1 : 2 * k + 2] = row[:, C : 2 * C] * scale


def finish_kernel(need, send, parts, one, two):
    need(parts)
    for dz in range(3):
        for dy in range(3):
            for k, out in enumerate((one, two)):
                tile = parts[dz * C : (dz + 1) * C, 3 * k + dy, :]
                for dx in range(3):
                    out[dx * 9 + dy * 3 + dz] = tile[:, dx * C : (dx + 1) * C]


def fifth_kernel(
    cells, need, send, place, slope1, s_low, s_high, h1, x_low, x_high, r1, r4, gb, w, out, v
):
    need(r1, r4, gb)
    mean, inverse, o_low, o_high = read_stats(r1, place, cells)
    nsum, plain = read_sums(r4)
    need(slope1, s_low, s_high, h1, x_low, x_high)
    lead = gb[:, 0:1] * inverse
    p_mean, n_mean = plain / cells, nsum / cells
    mean2, inverse2, lead2 = twice(mean), twice(inverse), twice(lead)
    p_mean2, n_mean2 = twice(p_mean), twice(n_mean)
    rows = ROWS + 2
    for y in range(rows):
        n_low = (x_low[y + 2].astype(F32) + o_low) * inverse
        n_own = (h1[y + 2] - mean2) * inverse2
        n_high = (x_high[y + 2].astype(F32) + o_high) * inverse
        g_low = lead * (s_low[y].astype(F32) - p_mean - n_low * n_mean)
        g_own = lead2 * (slope1[y] - p_mean2 - n_own * n_mean2)
        g_high = lead * (s_high[y].astype(F32) - p_mean - n_high * n_mean)
        v[y] = masked(g_low, g_own, g_high, kept(place, y, rows, 1))

    need(w)

    def emit(y, values):
        out[y] = values.astype(BF16)

    conv_rows(v, w, ROWS, emit)


def call(kernel, ins, outs, name, scratch=(), smem_first=True):
    lead = 1 if smem_first else 0
    count_in, count_out = len(ins) - lead, len(outs)

    def body(*refs):
        first, rest = refs[:lead], refs[lead:]
        parts = []
        for size in (count_in, count_out, count_in, count_out, 2):
            parts.append(rest[:size])
            rest = rest[size:]
        sources, targets, in_bufs, out_bufs, (in_sems, out_sems) = parts
        arriving = [
            pltpu.make_async_copy(a, b, in_sems.at[k])
            for k, (a, b) in enumerate(zip(sources, in_bufs))
        ]
        leaving = [
            pltpu.make_async_copy(a, b, out_sems.at[k])
            for k, (a, b) in enumerate(zip(out_bufs, targets))
        ]
        waiting, held = list(range(count_in)), list(range(count_out))
        for copy in arriving:
            copy.start()

        def need(*wanted):
            for k in list(waiting):
                if any(in_bufs[k] is ref for ref in wanted):
                    arriving[k].wait()
                    waiting.remove(k)

        def send(*ready):
            for k in list(held):
                if any(out_bufs[k] is ref for ref in ready):
                    leaving[k].start()
                    held.remove(k)

        kernel(need, send, *first, *in_bufs, *out_bufs, *rest)
        send(*out_bufs)
        need(*in_bufs)
        for copy in leaving:
            copy.wait()

    far = pl.BlockSpec(memory_space=pltpu.HBM)
    return pl.pallas_call(
        body,
        out_shape=outs,
        in_specs=[SM] * lead + [far] * count_in,
        out_specs=[far] * count_out,
        scratch_shapes=[
            *[pltpu.VMEM(a.shape, a.dtype) for a in ins[lead:]],
            *[pltpu.VMEM(a.shape, a.dtype) for a in outs],
            pltpu.SemaphoreType.DMA((count_in,)),
            pltpu.SemaphoreType.DMA((count_out,)),
            *scratch,
        ],
        compiler_params=pltpu.CompilerParams(vmem_limit_bytes=56 * 1024 * 1024),
        cost_estimate=pl.CostEstimate(
            flops=2_000_000_000, bytes_accessed=6_000_000, transcendentals=0
        ),
        name=name,
    )(*ins)


def up(values, axes):
    count = lax.axis_size(axes)
    return lax.ppermute(values, axes, [(i, i + 1) for i in range(count - 1)])


def down(values, axes):
    count = lax.axis_size(axes)
    return lax.ppermute(values, axes, [(i + 1, i) for i in range(count - 1)])


def share(msg):
    return lax.all_to_all(msg, ALL, 0, 0, tiled=True)


def local(features, kernel_one, gain_one, bias_one, kernel_two, gain_two, bias_two, cotangent):
    count_x, count_y = lax.axis_size(GX), lax.axis_size(GY)
    count = count_x * count_y
    cells = float(count * 2 * ROWS * 128)
    gx, gy = lax.axis_index(GX), lax.axis_index(GY)
    at = gx * count_y + gy
    place = jnp.stack(
        [at - count_y, at + count_y, gx > 0, gx < count_x - 1, gy > 0, gy < count_y - 1, at % C]
    ).astype(jnp.int32)
    gb = jnp.stack([gain_one, bias_one, gain_two, bias_two], axis=1)

    own = jnp.transpose(features, (2, 1, 0, 3)).reshape(ROWS, 64, 128)
    cot = jnp.transpose(cotangent, (2, 1, 0, 3)).reshape(ROWS, 64, 128)

    def rims(rows):
        return [sh((rows, C, 128), BF16)] * 2

    msg, wide = sh((count, 128), F32), sh((count, 8, 128), F32)
    corr = (pltpu.VMEM((192, ROWS * 128), BF16), pltpu.VMEM((192, 384), F32))

    y_up, y_down = call(
        pack_kernel, (own, cot), [sh((6, 64, 128), BF16)] * 2, "pack", smem_first=False
    )
    y_low, y_high = up(y_up, GY), down(y_down, GY)
    x_up, x_down = call(planes_kernel, (own, y_low, y_high), rims(40), "planes", smem_first=False)
    x_low, x_high = up(x_up, GX), down(x_down, GX)
    taps = [
        jnp.transpose(k, (2, 3, 4, 0, 1)).reshape(27, C, C) for k in (kernel_one, kernel_two)
    ]
    w1, w2, b1, b2 = call(
        weights_kernel, taps, [sh((192, 384), BF16)] * 4, "weights", smem_first=False
    )

    v1, h1, low, high, m1 = call(
        first_kernel,
        (own, y_low, y_high, x_low, x_high, w1),
        [sh((40, 128, 128), BF16), sh((38, 64, 128), F32), *rims(38), msg],
        "conv_one",
        smem_first=False,
    )
    h1_low, h1_high = up(high, GX), down(low, GX)
    r1 = share(m1)

    v2, h2, low, high, m2 = call(
        lambda *refs: second_kernel(cells, *refs),
        (place, h1, h1_low, h1_high, r1, gb, w2),
        [sh((38, 128, 128), BF16), sh((36, 64, 128), F32), *rims(36), msg],
        "conv_two",
    )
    h2_low, h2_high = up(high, GX), down(low, GX)
    r2 = share(m2)
    xn, x1 = call(
        lambda *refs: side_kernel(cells, *refs),
        (place, h1, r1, v1),
        [sh((9, C, 128), F32), sh((16, 128), F32)],
        "normed_features",
        scratch=corr,
    )

    output, low, high, m3 = call(
        lambda *refs: third_kernel(cells, *refs),
        (place, h2, cot, y_low, y_high, r2, gb, xn, x1),
        [sh((ROWS, 64, 128), BF16), *rims(36), wide],
        "slope_two",
    )
    t_low, t_high = up(high, GX), down(low, GX)
    r3 = share(m3)

    slope1, low, high, m4 = call(
        lambda *refs: fourth_kernel(cells, *refs),
        (
            place, h2, h2_low, h2_high, cot, y_low, y_high, t_low, t_high, r2, r3, h1, r1, gb,
            v1, v2, b2,
        ),
        [sh((34, 64, 128), F32), *rims(34), wide],
        "back_two",
        scratch=(pltpu.VMEM((36, 128, 128), BF16), *corr, corr[1]),
    )
    s_low, s_high = up(high, GX), down(low, GX)
    r4 = share(m4)

    m5, norm_grads = call(
        lambda *refs: owner_kernel(cells, *refs),
        (place, r1, r3, r4, gb),
        [wide, sh((4, C), F32)],
        "own_rows",
    )
    r5 = share(m5)
    (grad,) = call(
        lambda *refs: fifth_kernel(cells, *refs),
        (place, slope1, s_low, s_high, h1, h1_low, h1_high, r1, r4, gb, b1),
        [sh((ROWS, 64, 128), BF16)],
        "back_one",
        scratch=(pltpu.VMEM((34, 128, 128), BF16),),
    )
    grads = call(finish_kernel, (r5,), [sh((27, C, C), F32)] * 2, "finish", smem_first=False)
    one, two = [jnp.transpose(k.reshape(3, 3, 3, C, C), (3, 4, 0, 1, 2)) for k in grads]

    def back(rows):
        return jnp.transpose(rows.reshape(ROWS, 2, C, 128), (2, 1, 0, 3))

    return back(output), back(grad), one, two, norm_grads


def solution(mesh):
    nx, ny = mesh.devices.shape
    parts = (4, nx // 4, ny // 2, 2)
    split = Mesh(mesh.devices.reshape(parts), ALL)
    spec = P(None, GX, GY, None)
    in_specs = (spec, P(), P(), P(), P(), P(), P(), spec)
    out_specs = (spec, spec, P(), P(), P())
    return jax.shard_map(local, mesh=split, in_specs=in_specs, out_specs=out_specs, check_vma=False)
```

```python
import jax
import jax.numpy as jnp
from jax import lax
from jax.experimental import pallas as pl
from jax.experimental.pallas import tpu as pltpu
from jax.sharding import Mesh
from jax.sharding import PartitionSpec as P

GX = ("gx_0", "gx_1")
GY = ("gy_0", "gy_1")
ALL = GX + GY

EPSILON = 1e-05
C = 32
ROWS = 32
F32 = jnp.float32
BF16 = jnp.bfloat16
LN2 = 0.6931471805599453
SM = pl.BlockSpec(memory_space=pltpu.SMEM)


def sh(shape, kind):
    return jax.ShapeDtypeStruct(shape, kind)


def from_below(values, lane):
    return jnp.where(lane == 0, 0.0, pltpu.roll(values, 1, 1))


def from_above(values, lane):
    return jnp.where(lane == 127, 0.0, pltpu.roll(values, 127, 1))


def lanes(rows):
    return lax.broadcasted_iota(jnp.int32, (rows, 128), 1)


def conv_rows(v_ref, w_ref, rows, emit):
    lane = lanes(64)
    weights = w_ref[...]
    for y in range(0, rows, 2):
        first = v_ref[y : y + 3].reshape(384, 128)
        second = v_ref[y + 1 : y + 4].reshape(384, 128)
        product = jnp.dot(
            weights, jnp.concatenate([first, second], axis=1), preferred_element_type=F32
        )
        for k in range(2):
            part = product[:, k * 128 : (k + 1) * 128]
            emit(
                y + k,
                part[64:128] + from_below(part[0:64], lane) + from_above(part[128:192], lane),
            )


def fold(column):
    return column[0:C] + column[C : 2 * C]


def total(values):
    return jnp.sum(values, axis=1, keepdims=True)


def twice(column):
    return jnp.concatenate([column, column], axis=0)


def message(columns, msg_ref):
    count = msg_ref.shape[0]
    spare = jnp.zeros((128 - C * len(columns), 1), F32)
    column = jnp.concatenate([*columns, spare], axis=0)
    msg_ref[...] = jnp.transpose(jnp.broadcast_to(column, (128, count)))


def as_row(column):
    return jnp.transpose(jnp.broadcast_to(column, (128, 128)))[0:1]


def rows_message(columns, groups, msg_ref):
    spare = jnp.zeros((128 - C * len(columns), 1), F32)
    row = as_row(jnp.concatenate([*columns, spare], axis=0))
    height = msg_ref.shape[1]
    at = lax.broadcasted_iota(jnp.int32, (height, 128), 0)
    tile = jnp.where(at == 0, jnp.broadcast_to(row, (height, 128)), 0.0)
    msg_ref[...] = jnp.broadcast_to(tile[None], msg_ref.shape)
    for k, group in enumerate(groups):
        for dz in range(3):
            for dy in range(3):
                msg_ref[dz * C : (dz + 1) * C, 1 + 3 * k + dy, :] = group(dz, dy)


def stats_out(send, h_ref, acc, start, low_ref, high_ref):
    center = fold(total(acc)) / (2 * ROWS * 128)
    both = twice(center)
    spread = jnp.zeros((64, 128), F32)
    for y in range(h_ref.shape[0]):
        off = h_ref[y] - both
        if start <= y < start + ROWS:
            spread = spread + off * off
        low_ref[y] = off[0:C].astype(BF16)
        high_ref[y] = off[C:].astype(BF16)
    send(low_ref, high_ref)
    return center, fold(total(spread))


def stats_of(rows, place_ref, cells, st_ref):
    parts = jnp.transpose(rows)
    centers = parts[0:C]
    count = parts.shape[1]
    mean = total(centers) / count
    off = centers - mean
    spread = (total(parts[C : 2 * C]) + (2 * ROWS * 128) * total(off * off)) / cells
    at = lax.broadcasted_iota(jnp.int32, centers.shape, 1)
    low = total(jnp.where(at == place_ref[0], off, 0.0))
    high = total(jnp.where(at == place_ref[1], off, 0.0))
    found = (mean, lax.rsqrt(spread + EPSILON), low, high)
    st_ref[...] = jnp.concatenate([*found, jnp.zeros((C, 124), F32)], axis=1)
    return found


def kept_stats(st_ref):
    return tuple(st_ref[:, k : k + 1] for k in range(4))


def sums_of(row):
    parts = jnp.transpose(jnp.broadcast_to(row, (128, 128)))[:, 0:1]
    return parts[0:C], parts[C : 2 * C]


def feature_sums(v):
    lane = lanes(128)
    inner = v[5].astype(F32)
    for y in range(6, 3 + ROWS):
        inner = inner + v[y].astype(F32)
    ends = [v[y].astype(F32) for y in (3, 4, 3 + ROWS, 4 + ROWS)]
    windows = (inner + ends[0] + ends[1], inner + ends[1] + ends[2], inner + ends[2] + ends[3])
    columns = []
    for dz in range(3):
        for dy in range(3):
            values = windows[dy]
            if dz == 0:
                values = jnp.where(lane == 127, 0.0, values)
            if dz == 2:
                values = jnp.where(lane == 0, 0.0, values)
            column = total(values)
            columns.append(column + jnp.concatenate([column[C:], column[:C]], axis=0))
    rows = jnp.transpose(jnp.concatenate(columns + [jnp.zeros((128, 119), F32)], axis=1))
    return lambda dz, dy: jnp.broadcast_to(rows[dz * 3 + dy : dz * 3 + dy + 1], (C, 128))


def act(z):
    e = jnp.exp2(jnp.abs(z) * (-8.0 / LN2))
    soft = jnp.maximum(z, 0.0) * 0.99 + jnp.log2(1.0 + e) * (0.99 * LN2 / 8.0)
    return 0.01 * z + soft


def act_slope(z):
    return 0.505 + 0.495 * jnp.tanh(4.0 * z)


def kept(place_ref, y, rows, margin):
    low = place_ref[2].astype(F32)
    high = place_ref[3].astype(F32)
    if y < margin:
        edge = place_ref[4].astype(F32)
    elif y >= rows - margin:
        edge = place_ref[5].astype(F32)
    else:
        return low, None, high
    return low * edge, edge, high * edge


def masked(low, own, high, factors):
    f_low, f_own, f_high = factors
    own = own if f_own is None else own * f_own
    return jnp.concatenate([low * f_low, own, high * f_high], axis=0).astype(BF16)


def weight_sums(g_ref, v_ref, first, acc_ref):
    step = 4
    for y in range(0, ROWS, step):
        right = jnp.concatenate(
            [v_ref[first + y + k : first + y + k + 3].reshape(384, 128) for k in range(step)], axis=1
        )
        left = g_ref[:, y * 128 : (y + step) * 128]
        product = lax.dot_general(
            left, right, (((1,), (1,)), ((), ())), preferred_element_type=F32
        )
        if y == 0:
            acc_ref[...] = product
        else:
            acc_ref[...] += product


def folded(acc_ref):
    def tile(dz, dy):
        both = acc_ref[dz * 64 : dz * 64 + 64, dy * 128 : dy * 128 + 128]
        return both[0:C] + pltpu.roll(both[C:], 96, 1)

    return tile


def put_shifted(g_ref, y, values, lane):
    at = slice(y * 128, (y + 1) * 128)
    g_ref[0:64, at] = from_above(values, lane).astype(BF16)
    g_ref[64:128, at] = values.astype(BF16)
    g_ref[128:192, at] = from_below(values, lane).astype(BF16)


def pack_kernel(need, send, own, cot, up_ref, down_ref):
    need(own, cot)
    up_ref[0:4] = own[ROWS - 4 : ROWS]
    up_ref[4:6] = cot[ROWS - 2 : ROWS]
    down_ref[0:4] = own[0:4]
    down_ref[4:6] = cot[0:2]


def planes_kernel(need, send, own, cot, y_low, y_high, up_ref, down_ref, t_up, t_down):
    need(own, cot, y_low, y_high)
    for part, rows, at in ((y_low, 4, 0), (own, ROWS, 4), (y_high, 4, ROWS + 4)):
        down_ref[at : at + rows] = part[0:rows, 0:C]
        up_ref[at : at + rows] = part[0:rows, C : 2 * C]
    send(up_ref, down_ref)
    for part, first, rows, at in ((y_low, 4, 2, 0), (cot, 0, ROWS, 2), (y_high, 4, 2, ROWS + 2)):
        t_down[at : at + rows] = part[first : first + rows, 0:C]
        t_up[at : at + rows] = part[first : first + rows, C : 2 * C]


def weights_kernel(need, send, k1, k2, w1, w2, b1, b2):
    need(k1, k2)
    row = lax.broadcasted_iota(jnp.int32, (C, 128), 0)
    col = lax.broadcasted_iota(jnp.int32, (C, 128), 1)
    eye = jnp.where(row == col, 1.0, 0.0)[:, 0:C].astype(BF16)
    zero = jnp.zeros((C, C), BF16)
    for k_ref, w_ref, b_ref in ((k1, w1, b1), (k2, w2, b2)):
        lined = jnp.zeros((9 * C, 128), F32)
        for dx in range(3):
            spot = jnp.where(row + dx * C == col, 1.0, 0.0).astype(BF16)
            lined = lined + jnp.dot(
                k_ref[dx * 9 : dx * 9 + 9].reshape(9 * C, C), spot, preferred_element_type=F32
            )
        stack = []
        for t in range(9):
            stack += [k_ref[18 + t], k_ref[9 + t], k_ref[t], zero]
        turned = lax.dot_general(
            eye,
            jnp.concatenate(stack, axis=0),
            (((1,), (1,)), ((), ())),
            preferred_element_type=F32,
        )
        for dy in range(3):
            for dz in range(3):
                here = slice(dy * 128, dy * 128 + 128)
                t = dy * 3 + dz
                tile = lined[t * C : t * C + C]
                w_ref[dz * 64 : dz * 64 + C, here] = tile.astype(BF16)
                w_ref[dz * 64 + C : dz * 64 + 64, here] = pltpu.roll(tile, C, 1).astype(BF16)
                t = 8 - t
                tile = turned[:, t * 128 : t * 128 + 128]
                b_ref[dz * 64 : dz * 64 + C, here] = tile.astype(BF16)
                b_ref[dz * 64 + C : dz * 64 + 64, here] = pltpu.roll(tile, C, 1).astype(BF16)


def first_kernel(need, send, own, y_low, y_high, x_low, x_high, w, v, h, low, high, msg):
    need(own, y_low, y_high, x_low, x_high)
    for middle, rows, at in ((y_low, 4, 0), (own, ROWS, 4), (y_high, 4, ROWS + 4)):
        for y in range(rows):
            v[at + y] = jnp.concatenate([x_low[at + y], middle[y], x_high[at + y]], axis=0)
    send(v)
    need(w)
    acc = [jnp.zeros((64, 128), F32)]

    def emit(y, values):
        h[y] = values
        if 3 <= y < 3 + ROWS:
            acc[0] = acc[0] + values

    conv_rows(v, w, ROWS + 6, emit)
    send(h)
    columns = stats_out(send, h, acc[0], 3, low, high)
    rows_message(columns, (feature_sums(v),), msg)


def second_kernel(cells, need, send, place, r1, gb, h1, x_low, x_high, w, v, h, low, high, msg, st1, x1):
    need(r1, gb)
    mean, inverse, o_low, o_high = stats_of(r1[:, 0, :], place, cells, st1)
    x1[...] = jnp.sum(r1[...], axis=0)
    send(st1, x1)
    need(h1, x_low, x_high)
    scale = inverse * gb[:, 0:1]
    shift = gb[:, 1:2]
    mean2, scale2, shift2 = twice(mean), twice(scale), twice(shift)
    b_low, b_high = shift + o_low * scale, shift + o_high * scale
    rows = ROWS + 6
    for y in range(rows):
        a_low = act(x_low[y].astype(F32) * scale + b_low)
        a_own = act((h1[y] - mean2) * scale2 + shift2)
        a_high = act(x_high[y].astype(F32) * scale + b_high)
        v[y] = masked(a_low, a_own, a_high, kept(place, y, rows, 3))
    send(v)
    need(w)
    acc = [jnp.zeros((64, 128), F32)]

    def emit(y, values):
        h[y] = values
        if 2 <= y < 2 + ROWS:
            acc[0] = acc[0] + values

    conv_rows(v, w, ROWS + 4, emit)
    send(h)
    message(stats_out(send, h, acc[0], 2, low, high), msg)


def side_kernel(need, send, st1, h1, v1, xn, g, acc):
    need(st1, h1)
    mean, inverse, _, _ = kept_stats(st1)
    mean2, inverse2 = twice(mean), twice(inverse)
    lane = lanes(64)
    for y in range(ROWS):
        put_shifted(g, y, (h1[y + 3] - mean2) * inverse2, lane)
    need(v1)
    weight_sums(g, v1, 3, acc)
    tile = folded(acc)
    for dz in range(3):
        for dy in range(3):
            xn[dz * 3 + dy] = tile(dz, dy)


def cot_row(cot, y_low, y_high, y):
    if y < 2:
        return y_low[4 + y]
    if y < 2 + ROWS:
        return cot[y - 2]
    return y_high[2 + y - ROWS]


def third_kernel(cells, need, send, place, r2, gb, cot, h2, xn, out, msg, st2):
    need(r2, gb)
    mean, inverse, _, _ = stats_of(r2[...], place, cells, st2)
    need(h2, cot)
    mean2, inverse2 = twice(mean), twice(inverse)
    gain2, bias2 = twice(gb[:, 2:3]), twice(gb[:, 3:4])
    plain = jnp.zeros((64, 128), F32)
    both = jnp.zeros((64, 128), F32)
    for y in range(ROWS):
        normed = (h2[y + 2] - mean2) * inverse2
        z = normed * gain2 + bias2
        out[y] = act(z).astype(BF16)
        slope = cot[y].astype(F32) * act_slope(z)
        plain = plain + slope
        both = both + slope * normed
    send(out)
    need(xn)

    rows_message((fold(total(both)), fold(total(plain))), (lambda dz, dy: xn[dz * 3 + dy],), msg)


def fourth_kernel(
    cells, need, send, place, r3, st2, gb, h2, x_low, x_high, cot, y_low, y_high, t_low, t_high,
    w, st1, h1, v2, v1, slope1, low, high, msg, t3, v, g, acc, acc1,
):
    need(r3, st2, gb)
    mean, inverse, o_low, o_high = kept_stats(st2)
    t3[...] = jnp.sum(r3[...], axis=0)
    send(t3)
    nsum, plain = sums_of(t3[0:1])
    need(h2, x_low, x_high, cot, y_low, y_high, t_low, t_high)
    gain, bias = gb[:, 2:3], gb[:, 3:4]
    lead = gain * inverse
    p_mean, n_mean = plain / cells, nsum / cells

    def grad(normed, c, gain, bias, lead, p_mean, n_mean):
        slope = c.astype(F32) * act_slope(normed * gain + bias)
        return lead * (slope - p_mean - normed * n_mean)

    one = (gain, bias, lead, p_mean, n_mean)
    two = tuple(twice(a) for a in one)
    mean2, inverse2 = twice(mean), twice(inverse)
    lane = lanes(64)
    rows = ROWS + 4
    for y in range(rows):
        g_low = grad((x_low[y].astype(F32) + o_low) * inverse, t_low[y], *one)
        g_own = grad((h2[y] - mean2) * inverse2, cot_row(cot, y_low, y_high, y), *two)
        g_high = grad((x_high[y].astype(F32) + o_high) * inverse, t_high[y], *one)
        v[y] = masked(g_low, g_own, g_high, kept(place, y, rows, 2))
        if 2 <= y < 2 + ROWS:
            put_shifted(g, y - 2, g_own, lane)
    need(v2)
    weight_sums(g, v2, 2, acc)

    need(h1, st1, w)
    mean, inverse, _, _ = kept_stats(st1)
    mean2, inverse2 = twice(mean), twice(inverse)
    gain2, bias2 = twice(gb[:, 0:1]), twice(gb[:, 1:2])
    sums = [jnp.zeros((64, 128), F32), jnp.zeros((64, 128), F32)]

    def emit(y, values):
        normed = (h1[y + 2] - mean2) * inverse2
        slope = values * act_slope(normed * gain2 + bias2)
        slope1[y] = slope
        low[y] = slope[0:C].astype(BF16)
        high[y] = slope[C:].astype(BF16)
        if 1 <= y < 1 + ROWS:
            sums[0] = sums[0] + slope * normed
            sums[1] = sums[1] + slope
            put_shifted(g, y - 1, slope, lane)

    conv_rows(v, w, ROWS + 2, emit)
    send(slope1, low, high)
    need(v1)
    weight_sums(g, v1, 3, acc1)
    rows_message(
        (fold(total(sums[0])), fold(total(sums[1]))), (folded(acc1), folded(acc)), msg
    )


def owner_kernel(cells, need, send, place, r4, st1, gb, t3, x1, msg, norms, t4):
    need(r4, st1, gb, t3, x1)
    _, inverse, _, _ = kept_stats(st1)
    t4[...] = jnp.sum(r4[...], axis=0)
    nsum, plain = sums_of(t4[0:1])
    mine = lax.broadcasted_iota(jnp.int32, (C, 1), 0) == place[6]

    def picked(column):
        return jnp.sum(jnp.where(mine, column, 0.0), axis=0, keepdims=True)

    scale = cells**-0.5
    lead = picked(gb[:, 0:1] * inverse) * scale
    third, fourth = t3[...], t4[...]
    one = fourth[1:4] - picked(plain) * (x1[1:4] / cells) - picked(nsum) * (third[1:4] / cells)
    one = lead * one
    two = fourth[4:7] * scale
    tile = jnp.concatenate([one, two, jnp.zeros((2, 128), F32)], axis=0)
    msg[...] = jnp.broadcast_to(tile[None], msg.shape)
    for k, row in enumerate((fourth[0:1], third[0:1])):
        norms[2 * k : 2 * k + 1] = row[:, 0:C] * scale
        norms[2 * k + 1 : 2 * k + 2] = row[:, C : 2 * C] * scale


def finish_kernel(need, send, parts, one, two):
    need(parts)
    for dz in range(3):
        for dy in range(3):
            for k, out in enumerate((one, two)):
                tile = parts[dz * C : (dz + 1) * C, 3 * k + dy, :]
                for dx in range(3):
                    out[dx * 9 + dy * 3 + dz] = tile[:, dx * C : (dx + 1) * C]


def fifth_kernel(
    cells, need, send, place, t4, st1, gb, slope1, s_low, s_high, h1, x_low, x_high, w, out, v
):
    need(t4, st1, gb)
    mean, inverse, o_low, o_high = kept_stats(st1)
    nsum, plain = sums_of(t4[0:1])
    need(slope1, s_low, s_high, h1, x_low, x_high)
    lead = gb[:, 0:1] * inverse
    p_mean, n_mean = plain / cells, nsum / cells
    mean2, inverse2, lead2 = twice(mean), twice(inverse), twice(lead)
    p_mean2, n_mean2 = twice(p_mean), twice(n_mean)
    rows = ROWS + 2
    for y in range(rows):
        n_low = (x_low[y + 2].astype(F32) + o_low) * inverse
        n_own = (h1[y + 2] - mean2) * inverse2
        n_high = (x_high[y + 2].astype(F32) + o_high) * inverse
        g_low = lead * (s_low[y].astype(F32) - p_mean - n_low * n_mean)
        g_own = lead2 * (slope1[y] - p_mean2 - n_own * n_mean2)
        g_high = lead * (s_high[y].astype(F32) - p_mean - n_high * n_mean)
        v[y] = masked(g_low, g_own, g_high, kept(place, y, rows, 1))

    need(w)

    def emit(y, values):
        out[y] = values.astype(BF16)

    conv_rows(v, w, ROWS, emit)


def call(kernel, ins, outs, name, scratch=(), smem_first=True, after=()):
    lead = 1 if smem_first else 0
    count_in, count_out = len(ins) - lead, len(outs)

    def body(*refs):
        first, rest = refs[:lead], refs[lead:]
        parts = []
        for size in (count_in, len(after), count_out, count_in, count_out, 2):
            parts.append(rest[:size])
            rest = rest[size:]
        sources, _, targets, in_bufs, out_bufs, (in_sems, out_sems) = parts
        arriving = [
            pltpu.make_async_copy(a, b, in_sems.at[k])
            for k, (a, b) in enumerate(zip(sources, in_bufs))
        ]
        leaving = [
            pltpu.make_async_copy(a, b, out_sems.at[k])
            for k, (a, b) in enumerate(zip(out_bufs, targets))
        ]
        waiting, held = list(range(count_in)), list(range(count_out))
        for copy in arriving:
            copy.start()

        def need(*wanted):
            for k in list(waiting):
                if any(in_bufs[k] is ref for ref in wanted):
                    arriving[k].wait()
                    waiting.remove(k)

        def send(*ready):
            for k in list(held):
                if any(out_bufs[k] is ref for ref in ready):
                    leaving[k].start()
                    held.remove(k)

        kernel(need, send, *first, *in_bufs, *out_bufs, *rest)
        send(*out_bufs)
        need(*in_bufs)
        for copy in leaving:
            copy.wait()

    far = pl.BlockSpec(memory_space=pltpu.HBM)
    return pl.pallas_call(
        body,
        out_shape=outs,
        in_specs=[SM] * lead + [far] * (count_in + len(after)),
        out_specs=[far] * count_out,
        scratch_shapes=[
            *[pltpu.VMEM(a.shape, a.dtype) for a in ins[lead:]],
            *[pltpu.VMEM(a.shape, a.dtype) for a in outs],
            pltpu.SemaphoreType.DMA((count_in,)),
            pltpu.SemaphoreType.DMA((count_out,)),
            *scratch,
        ],
        compiler_params=pltpu.CompilerParams(vmem_limit_bytes=56 * 1024 * 1024),
        cost_estimate=pl.CostEstimate(
            flops=2_000_000_000, bytes_accessed=6_000_000, transcendentals=0
        ),
        name=name,
    )(*ins, *after)


def up(values, axes):
    count = lax.axis_size(axes)
    return lax.ppermute(values, axes, [(i, i + 1) for i in range(count - 1)])


def down(values, axes):
    count = lax.axis_size(axes)
    return lax.ppermute(values, axes, [(i + 1, i) for i in range(count - 1)])


def share(msg):
    return lax.all_to_all(msg, ALL, 0, 0, tiled=True)


def local(features, kernel_one, gain_one, bias_one, kernel_two, gain_two, bias_two, cotangent):
    count_x, count_y = lax.axis_size(GX), lax.axis_size(GY)
    count = count_x * count_y
    cells = float(count * 2 * ROWS * 128)
    gx, gy = lax.axis_index(GX), lax.axis_index(GY)
    at = gx * count_y + gy
    place = jnp.stack(
        [at - count_y, at + count_y, gx > 0, gx < count_x - 1, gy > 0, gy < count_y - 1, at % C]
    ).astype(jnp.int32)
    gb = jnp.stack([gain_one, bias_one, gain_two, bias_two], axis=1)

    own = jnp.transpose(features, (2, 1, 0, 3)).reshape(ROWS, 64, 128)
    cot = jnp.transpose(cotangent, (2, 1, 0, 3)).reshape(ROWS, 64, 128)

    def rims(rows):
        return [sh((rows, C, 128), BF16)] * 2

    msg, four, five, wide = (
        sh((count, *tile), F32) for tile in ((128,), (4, 128), (5, 128), (8, 128))
    )
    stats = sh((C, 128), F32)
    corr = (pltpu.VMEM((192, ROWS * 128), BF16), pltpu.VMEM((192, 384), F32))

    y_up, y_down = call(
        pack_kernel, (own, cot), [sh((6, 64, 128), BF16)] * 2, "pack", smem_first=False
    )
    y_low, y_high = up(y_up, GY), down(y_down, GY)
    x_up, x_down, t_up, t_down = call(
        planes_kernel, (own, cot, y_low, y_high), rims(40) + rims(36), "planes", smem_first=False
    )
    x_low, x_high = up(x_up, GX), down(x_down, GX)
    taps = [
        jnp.transpose(k, (2, 3, 4, 0, 1)).reshape(27, C, C) for k in (kernel_one, kernel_two)
    ]
    w1, w2, b1, b2 = call(
        weights_kernel, taps, [sh((192, 384), BF16)] * 4, "weights", smem_first=False
    )

    v1, h1, low, high, m1 = call(
        first_kernel,
        (own, y_low, y_high, x_low, x_high, w1),
        [sh((40, 128, 128), BF16), sh((38, 64, 128), F32), *rims(38), five],
        "conv_one",
        smem_first=False,
    )
    h1_low, h1_high = up(high, GX), down(low, GX)
    r1 = share(m1)

    v2, h2, low, high, m2, st1, x1 = call(
        lambda *refs: second_kernel(cells, *refs),
        (place, r1, gb, h1, h1_low, h1_high, w2),
        [
            sh((38, 128, 128), BF16), sh((36, 64, 128), F32), *rims(36), msg, stats,
            sh((5, 128), F32),
        ],
        "conv_two",
    )
    h2_low, h2_high = up(high, GX), down(low, GX)
    t_low, t_high = up(t_up, GX), down(t_down, GX)
    r2 = share(m2)
    (xn,) = call(
        side_kernel,
        (st1, h1, v1),
        [sh((9, C, 128), F32)],
        "normed_features",
        scratch=corr,
        smem_first=False,
    )

    output, m3, st2 = call(
        lambda *refs: third_kernel(cells, *refs),
        (place, r2, gb, cot, h2, xn),
        [sh((ROWS, 64, 128), BF16), four, stats],
        "slope_two",
    )
    r3 = share(m3)

    slope1, low, high, m4, t3 = call(
        lambda *refs: fourth_kernel(cells, *refs),
        (
            place, r3, st2, gb, h2, h2_low, h2_high, cot, y_low, y_high, t_low, t_high,
            b2, st1, h1, v2, v1,
        ),
        [sh((34, 64, 128), F32), *rims(34), wide, sh((4, 128), F32)],
        "back_two",
        scratch=(pltpu.VMEM((36, 128, 128), BF16), *corr, corr[1]),
    )
    s_low, s_high = up(high, GX), down(low, GX)
    r4 = share(m4)

    m5, norm_grads, t4 = call(
        lambda *refs: owner_kernel(cells, *refs),
        (place, r4, st1, gb, t3, x1),
        [wide, sh((4, C), F32), sh((8, 128), F32)],
        "own_rows",
        after=(s_low, s_high),
    )
    r5 = share(m5)
    (grad,) = call(
        lambda *refs: fifth_kernel(cells, *refs),
        (place, t4, st1, gb, slope1, s_low, s_high, h1, h1_low, h1_high, b1),
        [sh((ROWS, 64, 128), BF16)],
        "back_one",
        scratch=(pltpu.VMEM((34, 128, 128), BF16),),
    )
    grads = call(finish_kernel, (r5,), [sh((27, C, C), F32)] * 2, "finish", smem_first=False)
    one, two = [jnp.transpose(k.reshape(3, 3, 3, C, C), (3, 4, 0, 1, 2)) for k in grads]

    def back(rows):
        return jnp.transpose(rows.reshape(ROWS, 2, C, 128), (2, 1, 0, 3))

    return back(output), back(grad), one, two, norm_grads


def solution(mesh):
    nx, ny = mesh.devices.shape
    parts = (4, nx // 4, ny // 2, 2)
    split = Mesh(mesh.devices.reshape(parts), ALL)
    spec = P(None, GX, GY, None)
    in_specs = (spec, P(), P(), P(), P(), P(), P(), spec)
    out_specs = (spec, spec, P(), P(), P())
    return jax.shard_map(local, mesh=split, in_specs=in_specs, out_specs=out_specs, check_vma=False)
```

```python
import jax
import jax.numpy as jnp
from jax import lax
from jax.experimental import pallas as pl
from jax.experimental.pallas import tpu as pltpu
from jax.sharding import Mesh
from jax.sharding import PartitionSpec as P

GX = ("gx_0", "gx_1")
GY = ("gy_0", "gy_1")
ALL = GX + GY

EPSILON = 1e-05
C = 32
ROWS = 32
F32 = jnp.float32
BF16 = jnp.bfloat16
LN2 = 0.6931471805599453
SM = pl.BlockSpec(memory_space=pltpu.SMEM)


def sh(shape, kind):
    return jax.ShapeDtypeStruct(shape, kind)


def from_below(values, lane):
    return jnp.where(lane == 0, 0.0, pltpu.roll(values, 1, 1))


def from_above(values, lane):
    return jnp.where(lane == 127, 0.0, pltpu.roll(values, 127, 1))


def lanes(rows):
    return lax.broadcasted_iota(jnp.int32, (rows, 128), 1)


def windows_of(*refs):
    if len(refs) == 1:
        return lambda y: refs[0][y : y + 3].reshape(384, 128)
    return lambda y: jnp.concatenate([ref[y + k] for k in range(3) for ref in refs], axis=0)


def conv_rows(window, w_ref, rows, emit):
    lane = lanes(64)
    weights = w_ref[...]
    for y in range(0, rows, 2):
        both = jnp.concatenate([window(y), window(y + 1)], axis=1)
        product = jnp.dot(weights, both, preferred_element_type=F32)
        for k in range(2):
            part = product[:, k * 128 : (k + 1) * 128]
            emit(
                y + k,
                part[64:128] + from_below(part[0:64], lane) + from_above(part[128:192], lane),
            )


def fold(column):
    return column[0:C] + column[C : 2 * C]


def total(values):
    return jnp.sum(values, axis=1, keepdims=True)


def twice(column):
    return jnp.concatenate([column, column], axis=0)


def fourfold(column):
    return twice(twice(column))


def message(columns, msg_ref):
    count = msg_ref.shape[0]
    spare = jnp.zeros((128 - C * len(columns), 1), F32)
    column = jnp.concatenate([*columns, spare], axis=0)
    msg_ref[...] = jnp.transpose(jnp.broadcast_to(column, (128, count)))


def as_row(column):
    return jnp.transpose(jnp.broadcast_to(column, (128, 128)))[0:1]


def rows_message(columns, groups, msg_ref):
    spare = jnp.zeros((128 - C * len(columns), 1), F32)
    row = as_row(jnp.concatenate([*columns, spare], axis=0))
    height = msg_ref.shape[1]
    at = lax.broadcasted_iota(jnp.int32, (height, 128), 0)
    tile = jnp.where(at == 0, jnp.broadcast_to(row, (height, 128)), 0.0)
    msg_ref[...] = jnp.broadcast_to(tile[None], msg_ref.shape)
    for k, group in enumerate(groups):
        for dz in range(3):
            for dy in range(3):
                msg_ref[dz * C : (dz + 1) * C, 1 + 3 * k + dy, :] = group(dz, dy)


def center_of(acc):
    return fold(total(acc)) / (2 * ROWS * 128)


def stats_of(rows, place_ref, cells, st_ref):
    parts = jnp.transpose(rows)
    centers = parts[0:C]
    count = parts.shape[1]
    mean = total(centers) / count
    off = centers - mean
    spread = (total(parts[C : 2 * C]) + (2 * ROWS * 128) * total(off * off)) / cells
    at = lax.broadcasted_iota(jnp.int32, centers.shape, 1)
    low = total(jnp.where(at == place_ref[0], off, 0.0))
    high = total(jnp.where(at == place_ref[1], off, 0.0))
    found = (mean, lax.rsqrt(spread + EPSILON), low, high)
    st_ref[...] = jnp.concatenate([*found, jnp.zeros((C, 124), F32)], axis=1)
    return found


def kept_stats(st_ref):
    return tuple(st_ref[:, k : k + 1] for k in range(4))


def sums_of(row):
    parts = jnp.transpose(jnp.broadcast_to(row, (128, 128)))[:, 0:1]
    return parts[0:C], parts[C : 2 * C]


def feature_sums(v):
    lane = lanes(128)
    inner = v[5].astype(F32)
    for y in range(6, 3 + ROWS):
        inner = inner + v[y].astype(F32)
    ends = [v[y].astype(F32) for y in (3, 4, 3 + ROWS, 4 + ROWS)]
    windows = (inner + ends[0] + ends[1], inner + ends[1] + ends[2], inner + ends[2] + ends[3])
    columns = []
    for dz in range(3):
        for dy in range(3):
            values = windows[dy]
            if dz == 0:
                values = jnp.where(lane == 127, 0.0, values)
            if dz == 2:
                values = jnp.where(lane == 0, 0.0, values)
            column = total(values)
            columns.append(column + jnp.concatenate([column[C:], column[:C]], axis=0))
    rows = jnp.transpose(jnp.concatenate(columns + [jnp.zeros((128, 119), F32)], axis=1))
    return lambda dz, dy: jnp.broadcast_to(rows[dz * 3 + dy : dz * 3 + dy + 1], (C, 128))


def act(z):
    e = jnp.exp2(jnp.abs(z) * (-8.0 / LN2))
    soft = jnp.maximum(z, 0.0) * 0.99 + jnp.log2(1.0 + e) * (0.99 * LN2 / 8.0)
    return 0.01 * z + soft


def act_slope(z):
    return 0.505 + 0.495 * jnp.tanh(4.0 * z)


def kept(place_ref, y, rows, margin):
    low = place_ref[2].astype(F32)
    high = place_ref[3].astype(F32)
    if y < margin:
        edge = place_ref[4].astype(F32)
    elif y >= rows - margin:
        edge = place_ref[5].astype(F32)
    else:
        return low, None, high
    return low * edge, edge, high * edge


def masked(values, factors):
    f_low, f_own, f_high = factors
    own = values[C : 3 * C]
    own = own if f_own is None else own * f_own
    return jnp.concatenate([values[0:C] * f_low, own, values[3 * C :] * f_high], axis=0).astype(
        BF16
    )


def weight_sums(g_ref, v_ref, first, acc_ref):
    step = 4
    for y in range(0, ROWS, step):
        right = jnp.concatenate(
            [v_ref[first + y + k : first + y + k + 3].reshape(384, 128) for k in range(step)], axis=1
        )
        left = g_ref[:, y * 128 : (y + step) * 128]
        product = lax.dot_general(
            left, right, (((1,), (1,)), ((), ())), preferred_element_type=F32
        )
        if y == 0:
            acc_ref[...] = product
        else:
            acc_ref[...] += product


def folded(acc_ref):
    def tile(dz, dy):
        both = acc_ref[dz * 64 : dz * 64 + 64, dy * 128 : dy * 128 + 128]
        return both[0:C] + pltpu.roll(both[C:], 96, 1)

    return tile


def put_shifted(g_ref, y, values, lane):
    at = slice(y * 128, (y + 1) * 128)
    g_ref[0:64, at] = from_above(values, lane).astype(BF16)
    g_ref[64:128, at] = values.astype(BF16)
    g_ref[128:192, at] = from_below(values, lane).astype(BF16)


def pack_kernel(need, send, own, cot, up_ref, down_ref):
    need(own, cot)
    up_ref[0:4] = own[ROWS - 4 : ROWS]
    up_ref[4:6] = cot[ROWS - 2 : ROWS]
    down_ref[0:4] = own[0:4]
    down_ref[4:6] = cot[0:2]


def planes_kernel(need, send, own, y_low, y_high, ext):
    need(own, y_low, y_high)
    ext[0:4] = y_low[0:4]
    ext[4 : 4 + ROWS] = own[...]
    ext[4 + ROWS : 8 + ROWS] = y_high[0:4]


def weights_kernel(need, send, k1, k2, w1, w2, b1, b2):
    need(k1, k2)
    row = lax.broadcasted_iota(jnp.int32, (C, 128), 0)
    col = lax.broadcasted_iota(jnp.int32, (C, 128), 1)
    eye = jnp.where(row == col, 1.0, 0.0)[:, 0:C].astype(BF16)
    zero = jnp.zeros((C, C), BF16)
    for k_ref, w_ref, b_ref in ((k1, w1, b1), (k2, w2, b2)):
        lined = jnp.zeros((9 * C, 128), F32)
        for dx in range(3):
            spot = jnp.where(row + dx * C == col, 1.0, 0.0).astype(BF16)
            lined = lined + jnp.dot(
                k_ref[dx * 9 : dx * 9 + 9].reshape(9 * C, C), spot, preferred_element_type=F32
            )
        stack = []
        for t in range(9):
            stack += [k_ref[18 + t], k_ref[9 + t], k_ref[t], zero]
        turned = lax.dot_general(
            eye,
            jnp.concatenate(stack, axis=0),
            (((1,), (1,)), ((), ())),
            preferred_element_type=F32,
        )
        for dy in range(3):
            for dz in range(3):
                here = slice(dy * 128, dy * 128 + 128)
                t = dy * 3 + dz
                tile = lined[t * C : t * C + C]
                w_ref[dz * 64 : dz * 64 + C, here] = tile.astype(BF16)
                w_ref[dz * 64 + C : dz * 64 + 64, here] = pltpu.roll(tile, C, 1).astype(BF16)
                t = 8 - t
                tile = turned[:, t * 128 : t * 128 + 128]
                b_ref[dz * 64 : dz * 64 + C, here] = tile.astype(BF16)
                b_ref[dz * 64 + C : dz * 64 + 64, here] = pltpu.roll(tile, C, 1).astype(BF16)


def first_kernel(need, send, low, high, own, w, v, h, msg):
    need(own, w)
    acc = [jnp.zeros((64, 128), F32), jnp.zeros((64, 128), F32)]
    for k, pair in enumerate(((low, own), (own, high))):

        def emit(y, values, k=k):
            h[y, 64 * k : 64 * k + 64] = values
            if 3 <= y < 3 + ROWS:
                acc[k] = acc[k] + values

        conv_rows(windows_of(*pair), w, ROWS + 6, emit)
    send(h)
    for y in range(ROWS + 8):
        v[y] = jnp.concatenate([low[y][C:], own[y], high[y][0:C]], axis=0)
    send(v)
    center = center_of(jnp.concatenate([acc[0][C:], acc[1][0:C]], axis=0))
    both = twice(center)
    spread = jnp.zeros((64, 128), F32)
    for y in range(3, 3 + ROWS):
        off = h[y, C : 3 * C] - both
        spread = spread + off * off
    rows_message((center, fold(total(spread))), (feature_sums(v),), msg)


def second_kernel(
    cells, need, send, place, r1, gb, h1, cot, y_low, y_high, w, v, h, low, high, msg, st1, x1
):
    need(gb)
    mean, inverse, _, _ = stats_of(r1[:, 0, :], place, cells, st1)
    x1[...] = jnp.sum(r1[...], axis=0)
    send(st1, x1)
    mean4, scale4 = fourfold(mean), fourfold(inverse * gb[:, 0:1])
    shift4 = fourfold(gb[:, 1:2])
    rows = ROWS + 6
    need(h1)
    for y in range(rows):
        v[y] = masked(act((h1[y] - mean4) * scale4 + shift4), kept(place, y, rows, 3))
    send(v)
    need(w, cot, y_low, y_high)
    acc = [jnp.zeros((64, 128), F32)]

    def emit(y, values):
        h[y] = values
        if 2 <= y < 2 + ROWS:
            acc[0] = acc[0] + values

    rows = ROWS + 4
    conv_rows(windows_of(v), w, rows, emit)
    send(h)
    center = center_of(acc[0])
    both = twice(center)
    spread = jnp.zeros((64, 128), F32)
    for y in range(rows):
        off = h[y] - both
        if 2 <= y < 2 + ROWS:
            spread = spread + off * off
        low[y] = off[0:C].astype(BF16)
        high[y] = off[C:].astype(BF16)
        values = cot_row(cot, y_low, y_high, y)
        low[rows + y] = values[0:C]
        high[rows + y] = values[C:]
    send(low, high)
    message((center, fold(total(spread))), msg)


def side_kernel(need, send, st1, h1, v1, xn, g, acc):
    need(st1, h1)
    mean, inverse, _, _ = kept_stats(st1)
    mean2, inverse2 = twice(mean), twice(inverse)
    lane = lanes(64)
    for y in range(ROWS):
        put_shifted(g, y, (h1[y + 3] - mean2) * inverse2, lane)
    need(v1)
    weight_sums(g, v1, 3, acc)
    tile = folded(acc)
    for dz in range(3):
        for dy in range(3):
            xn[dz * 3 + dy] = tile(dz, dy)


def cot_row(cot, y_low, y_high, y):
    if y < 2:
        return y_low[4 + y]
    if y < 2 + ROWS:
        return cot[y - 2]
    return y_high[2 + y - ROWS]


def third_kernel(cells, need, send, place, r2, gb, cot, h2, xn, out, msg, st2):
    need(gb)
    mean, inverse, _, _ = stats_of(r2[...], place, cells, st2)
    need(h2, cot)
    mean2, inverse2 = twice(mean), twice(inverse)
    gain2, bias2 = twice(gb[:, 2:3]), twice(gb[:, 3:4])
    plain = jnp.zeros((64, 128), F32)
    both = jnp.zeros((64, 128), F32)
    for y in range(ROWS):
        normed = (h2[y + 2] - mean2) * inverse2
        z = normed * gain2 + bias2
        out[y] = act(z).astype(BF16)
        slope = cot[y].astype(F32) * act_slope(z)
        plain = plain + slope
        both = both + slope * normed
    send(out)
    need(xn)

    rows_message((fold(total(both)), fold(total(plain))), (lambda dz, dy: xn[dz * 3 + dy],), msg)


def fourth_kernel(
    cells, need, send, place, r3, st2, gb, h2, x_low, x_high, cot, y_low, y_high, w, st1, h1, v2, v1, slope1, low, high, msg, t3, v, g, acc, acc1,
):
    need(st2, gb)
    mean, inverse, o_low, o_high = kept_stats(st2)
    t3[...] = jnp.sum(r3[...], axis=0)
    send(t3)
    nsum, plain = sums_of(t3[0:1])
    need(h2, x_low, x_high, cot, y_low, y_high)
    gain, bias = gb[:, 2:3], gb[:, 3:4]
    lead = gain * inverse
    p_mean, n_mean = plain / cells, nsum / cells

    def grad(normed, c, gain, bias, lead, p_mean, n_mean):
        slope = c.astype(F32) * act_slope(normed * gain + bias)
        return lead * (slope - p_mean - normed * n_mean)

    one = (gain, bias, lead, p_mean, n_mean)
    two = tuple(twice(a) for a in one)
    mean2, inverse2 = twice(mean), twice(inverse)
    lane = lanes(64)
    rows = ROWS + 4
    for y in range(rows):
        g_low = grad((x_low[y].astype(F32) + o_low) * inverse, x_low[rows + y], *one)
        g_own = grad((h2[y] - mean2) * inverse2, cot_row(cot, y_low, y_high, y), *two)
        g_high = grad((x_high[y].astype(F32) + o_high) * inverse, x_high[rows + y], *one)
        both = jnp.concatenate([g_low, g_own, g_high], axis=0)
        v[y] = masked(both, kept(place, y, rows, 2))
        if 2 <= y < 2 + ROWS:
            put_shifted(g, y - 2, g_own, lane)
    need(v2)
    weight_sums(g, v2, 2, acc)

    need(h1, st1, w)
    mean, inverse, _, _ = kept_stats(st1)
    mean2, inverse2 = twice(mean), twice(inverse)
    gain2, bias2 = twice(gb[:, 0:1]), twice(gb[:, 1:2])
    sums = [jnp.zeros((64, 128), F32), jnp.zeros((64, 128), F32)]

    def emit(y, values):
        normed = (h1[y + 2] - mean2) * inverse2
        slope = values * act_slope(normed * gain2 + bias2)
        slope1[y] = slope
        low[y] = slope[0:C].astype(BF16)
        high[y] = slope[C:].astype(BF16)
        if 1 <= y < 1 + ROWS:
            sums[0] = sums[0] + slope * normed
            sums[1] = sums[1] + slope
            put_shifted(g, y - 1, slope, lane)

    conv_rows(windows_of(v), w, ROWS + 2, emit)
    send(slope1, low, high)
    need(v1)
    weight_sums(g, v1, 3, acc1)
    rows_message(
        (fold(total(sums[0])), fold(total(sums[1]))), (folded(acc1), folded(acc)), msg
    )


def owner_kernel(cells, need, send, place, r4, st1, gb, t3, x1, msg, norms, t4):
    need(st1, gb, t3, x1)
    _, inverse, _, _ = kept_stats(st1)
    t4[...] = jnp.sum(r4[...], axis=0)
    nsum, plain = sums_of(t4[0:1])
    mine = lax.broadcasted_iota(jnp.int32, (C, 1), 0) == place[6]

    def picked(column):
        return jnp.sum(jnp.where(mine, column, 0.0), axis=0, keepdims=True)

    scale = cells**-0.5
    lead = picked(gb[:, 0:1] * inverse) * scale
    third, fourth = t3[...], t4[...]
    one = fourth[1:4] - picked(plain) * (x1[1:4] / cells) - picked(nsum) * (third[1:4] / cells)
    one = lead * one
    two = fourth[4:7] * scale
    tile = jnp.concatenate([one, two, jnp.zeros((2, 128), F32)], axis=0)
    msg[...] = jnp.broadcast_to(tile[None], msg.shape)
    for k, row in enumerate((fourth[0:1], third[0:1])):
        norms[2 * k : 2 * k + 1] = row[:, 0:C] * scale
        norms[2 * k + 1 : 2 * k + 2] = row[:, C : 2 * C] * scale


def finish_kernel(need, send, parts, one, two):
    for dz in range(3):
        for dy in range(3):
            for k, out in enumerate((one, two)):
                tile = parts[dz * C : (dz + 1) * C, 3 * k + dy, :]
                for dx in range(3):
                    out[dx * 9 + dy * 3 + dz] = tile[:, dx * C : (dx + 1) * C]


def fifth_kernel(cells, need, send, place, t4, st1, gb, h1, slope1, s_low, s_high, w, out, v):
    need(t4, st1, gb)
    mean, inverse, _, _ = kept_stats(st1)
    nsum, plain = sums_of(t4[0:1])
    mean4, inverse4 = fourfold(mean), fourfold(inverse)
    lead4 = fourfold(gb[:, 0:1] * inverse)
    p_mean4, n_mean4 = fourfold(plain / cells), fourfold(nsum / cells)
    rows = ROWS + 2
    need(slope1, s_low, s_high, h1)
    for y in range(rows):
        slope = jnp.concatenate(
            [s_low[y].astype(F32), slope1[y], s_high[y].astype(F32)], axis=0
        )
        normed = (h1[y + 2] - mean4) * inverse4
        v[y] = masked(lead4 * (slope - p_mean4 - normed * n_mean4), kept(place, y, rows, 1))
    need(w)

    def emit(y, values):
        out[y] = values.astype(BF16)

    conv_rows(windows_of(v), w, ROWS, emit)


def call(kernel, ins, outs, name, scratch=(), smem_first=True, after=(), near=0, cut=()):
    lead = 1 if smem_first else 0
    count_in, count_out = len(ins) - lead - near, len(outs)
    far_ins = ins[lead + near :]
    own = [any(a is b for b in cut) for a in far_ins]
    shapes = [(a.shape[0], 2 * C, 128) if c else a.shape for a, c in zip(far_ins, own)]

    def body(*refs):
        first, rest = refs[: lead + near], refs[lead + near :]
        parts = []
        for size in (count_in, len(after), count_out, count_in, count_out, 2):
            parts.append(rest[:size])
            rest = rest[size:]
        sources, _, targets, in_bufs, out_bufs, (in_sems, out_sems) = parts
        arriving = [
            pltpu.make_async_copy(a.at[:, C : 3 * C] if c else a, b, in_sems.at[k])
            for k, (a, b, c) in enumerate(zip(sources, in_bufs, own))
        ]
        leaving = [
            pltpu.make_async_copy(a, b, out_sems.at[k])
            for k, (a, b) in enumerate(zip(out_bufs, targets))
        ]
        waiting, held = list(range(count_in)), list(range(count_out))
        for copy in arriving:
            copy.start()

        def need(*wanted):
            for k in list(waiting):
                if any(in_bufs[k] is ref for ref in wanted):
                    arriving[k].wait()
                    waiting.remove(k)

        def send(*ready):
            for k in list(held):
                if any(out_bufs[k] is ref for ref in ready):
                    leaving[k].start()
                    held.remove(k)

        kernel(need, send, *first, *in_bufs, *out_bufs, *rest)
        send(*out_bufs)
        need(*in_bufs)
        for copy in leaving:
            copy.wait()

    far = pl.BlockSpec(memory_space=pltpu.HBM)
    return pl.pallas_call(
        body,
        out_shape=outs,
        in_specs=[SM] * lead
        + [pl.BlockSpec(memory_space=pltpu.VMEM)] * near
        + [far] * (count_in + len(after)),
        out_specs=[far] * count_out,
        scratch_shapes=[
            *[pltpu.VMEM(shape, a.dtype) for shape, a in zip(shapes, far_ins)],
            *[pltpu.VMEM(a.shape, a.dtype) for a in outs],
            pltpu.SemaphoreType.DMA((max(count_in, 1),)),
            pltpu.SemaphoreType.DMA((count_out,)),
            *scratch,
        ],
        compiler_params=pltpu.CompilerParams(vmem_limit_bytes=56 * 1024 * 1024),
        cost_estimate=pl.CostEstimate(
            flops=2_000_000_000, bytes_accessed=6_000_000, transcendentals=0
        ),
        name=name,
    )(*ins, *after)


def up(values, axes):
    count = lax.axis_size(axes)
    return lax.ppermute(values, axes, [(i, i + 1) for i in range(count - 1)])


def down(values, axes):
    count = lax.axis_size(axes)
    return lax.ppermute(values, axes, [(i + 1, i) for i in range(count - 1)])


def share(msg):
    return lax.all_to_all(msg, ALL, 0, 0, tiled=True)


def local(features, kernel_one, gain_one, bias_one, kernel_two, gain_two, bias_two, cotangent):
    count_x, count_y = lax.axis_size(GX), lax.axis_size(GY)
    count = count_x * count_y
    cells = float(count * 2 * ROWS * 128)
    gx, gy = lax.axis_index(GX), lax.axis_index(GY)
    at = gx * count_y + gy
    place = jnp.stack(
        [at - count_y, at + count_y, gx > 0, gx < count_x - 1, gy > 0, gy < count_y - 1, at % C]
    ).astype(jnp.int32)
    gb = jnp.stack([gain_one, bias_one, gain_two, bias_two], axis=1)

    own = jnp.transpose(features, (2, 1, 0, 3)).reshape(ROWS, 64, 128)
    cot = jnp.transpose(cotangent, (2, 1, 0, 3)).reshape(ROWS, 64, 128)

    def rims(rows):
        return [sh((rows, C, 128), BF16)] * 2

    msg, four, wide = (sh((count, *tile), F32) for tile in ((128,), (4, 128), (8, 128)))
    stats = sh((C, 128), F32)
    corr = (pltpu.VMEM((192, ROWS * 128), BF16), pltpu.VMEM((192, 384), F32))

    y_up, y_down = call(
        pack_kernel, (own, cot), [sh((6, 64, 128), BF16)] * 2, "pack", smem_first=False
    )
    y_low, y_high = up(y_up, GY), down(y_down, GY)
    (ext,) = call(
        planes_kernel, (own, y_low, y_high), [sh((40, 64, 128), BF16)], "planes", smem_first=False
    )
    x_low, x_high = up(ext, GX), down(ext, GX)
    taps = [
        jnp.transpose(k, (2, 3, 4, 0, 1)).reshape(27, C, C) for k in (kernel_one, kernel_two)
    ]
    w1, w2, b1, b2 = call(
        weights_kernel, taps, [sh((192, 384), BF16)] * 4, "weights", smem_first=False
    )

    v1, h1, m1 = call(
        first_kernel,
        (x_low, x_high, ext, w1),
        [sh((40, 128, 128), BF16), sh((38, 128, 128), F32), four],
        "conv_one",
        smem_first=False,
        near=2,
    )
    r1 = share(m1)

    v2, h2, low, high, m2, st1, x1 = call(
        lambda *refs: second_kernel(cells, *refs),
        (place, r1, gb, h1, cot, y_low, y_high, w2),
        [
            sh((38, 128, 128), BF16), sh((36, 64, 128), F32), *rims(72), msg, stats,
            sh((4, 128), F32),
        ],
        "conv_two",
        near=1,
    )
    h2_low, h2_high = up(high, GX), down(low, GX)
    r2 = share(m2)
    (xn,) = call(
        side_kernel,
        (st1, h1, v1),
        [sh((9, C, 128), F32)],
        "normed_features",
        scratch=corr,
        smem_first=False,
        cut=(h1,),
    )

    output, m3, st2 = call(
        lambda *refs: third_kernel(cells, *refs),
        (place, r2, gb, cot, h2, xn),
        [sh((ROWS, 64, 128), BF16), four, stats],
        "slope_two",
        near=1,
    )
    r3 = share(m3)

    slope1, low, high, m4, t3 = call(
        lambda *refs: fourth_kernel(cells, *refs),
        (
            place, r3, st2, gb, h2, h2_low, h2_high, cot, y_low, y_high,
            b2, st1, h1, v2, v1,
        ),
        [sh((34, 64, 128), F32), *rims(34), wide, sh((4, 128), F32)],
        "back_two",
        near=1,
        cut=(h1,),
        scratch=(pltpu.VMEM((36, 128, 128), BF16), *corr, corr[1]),
    )
    s_low, s_high = up(high, GX), down(low, GX)
    r4 = share(m4)

    m5, norm_grads, t4 = call(
        lambda *refs: owner_kernel(cells, *refs),
        (place, r4, st1, gb, t3, x1),
        [wide, sh((4, C), F32), sh((8, 128), F32)],
        "own_rows",
        near=1,
        after=(s_low, s_high),
    )
    r5 = share(m5)
    (grad,) = call(
        lambda *refs: fifth_kernel(cells, *refs),
        (place, t4, st1, gb, h1, slope1, s_low, s_high, b1),
        [sh((ROWS, 64, 128), BF16)],
        "back_one",
        scratch=(pltpu.VMEM((34, 128, 128), BF16),),
    )
    grads = call(finish_kernel, (r5,), [sh((27, C, C), F32)] * 2, "finish", smem_first=False, near=1)
    one, two = [jnp.transpose(k.reshape(3, 3, 3, C, C), (3, 4, 0, 1, 2)) for k in grads]

    def back(rows):
        return jnp.transpose(rows.reshape(ROWS, 2, C, 128), (2, 1, 0, 3))

    return back(output), back(grad), one, two, norm_grads


def solution(mesh):
    nx, ny = mesh.devices.shape
    parts = (4, nx // 4, ny // 2, 2)
    split = Mesh(mesh.devices.reshape(parts), ALL)
    spec = P(None, GX, GY, None)
    in_specs = (spec, P(), P(), P(), P(), P(), P(), spec)
    out_specs = (spec, spec, P(), P(), P())
    return jax.shard_map(local, mesh=split, in_specs=in_specs, out_specs=out_specs, check_vma=False)
```

```python
import jax
import jax.numpy as jnp
from jax import lax
from jax.experimental import pallas as pl
from jax.experimental.pallas import tpu as pltpu
from jax.sharding import Mesh
from jax.sharding import PartitionSpec as P

GX = ("gx_0", "gx_1")
GY = ("gy_0", "gy_1")
ALL = GX + GY

EPSILON = 1e-05
C = 32
ROWS = 32
F32 = jnp.float32
BF16 = jnp.bfloat16
LN2 = 0.6931471805599453
SM = pl.BlockSpec(memory_space=pltpu.SMEM)


def sh(shape, kind):
    return jax.ShapeDtypeStruct(shape, kind)


def from_below(values, lane):
    return jnp.where(lane == 0, 0.0, pltpu.roll(values, 1, 1))


def from_above(values, lane):
    return jnp.where(lane == 127, 0.0, pltpu.roll(values, 127, 1))


def lanes(rows):
    return lax.broadcasted_iota(jnp.int32, (rows, 128), 1)


def windows_of(*refs):
    if len(refs) == 1:
        return lambda y: refs[0][y : y + 3].reshape(384, 128)
    return lambda y: jnp.concatenate([rows(y + k) for k in range(3) for rows in refs], axis=0)


def joined(margin, middle, below, above, first):
    def row(y):
        if y < margin:
            return below[y]
        if y < margin + ROWS:
            return middle[y - margin]
        return above[first + y - margin - ROWS]

    return row


def conv_rows(window, w_ref, rows, emit):
    lane = lanes(64)
    weights = w_ref[...]
    for y in range(0, rows, 2):
        both = jnp.concatenate([window(y), window(y + 1)], axis=1)
        product = jnp.dot(weights, both, preferred_element_type=F32)
        for k in range(2):
            part = product[:, k * 128 : (k + 1) * 128]
            emit(
                y + k,
                part[64:128] + from_below(part[0:64], lane) + from_above(part[128:192], lane),
            )


def fold(column):
    return column[0:C] + column[C : 2 * C]


def total(values):
    return jnp.sum(values, axis=1, keepdims=True)


def twice(column):
    return jnp.concatenate([column, column], axis=0)


def fourfold(column):
    return twice(twice(column))


def message(columns, msg_ref):
    count = msg_ref.shape[0]
    spare = jnp.zeros((128 - C * len(columns), 1), F32)
    column = jnp.concatenate([*columns, spare], axis=0)
    msg_ref[...] = jnp.transpose(jnp.broadcast_to(column, (128, count)))


def as_row(column):
    return jnp.transpose(jnp.broadcast_to(column, (128, 128)))[0:1]


def rows_message(columns, groups, msg_ref):
    spare = jnp.zeros((128 - C * len(columns), 1), F32)
    row = as_row(jnp.concatenate([*columns, spare], axis=0))
    height = msg_ref.shape[1]
    at = lax.broadcasted_iota(jnp.int32, (height, 128), 0)
    tile = jnp.where(at == 0, jnp.broadcast_to(row, (height, 128)), 0.0)
    msg_ref[...] = jnp.broadcast_to(tile[None], msg_ref.shape)
    for k, group in enumerate(groups):
        for dz in range(3):
            for dy in range(3):
                msg_ref[dz * C : (dz + 1) * C, 1 + 3 * k + dy, :] = group(dz, dy)


def center_of(acc):
    return fold(total(acc)) / (2 * ROWS * 128)


def stats_of(rows, place_ref, cells, st_ref):
    parts = jnp.transpose(rows)
    centers = parts[0:C]
    count = parts.shape[1]
    mean = total(centers) / count
    off = centers - mean
    spread = (total(parts[C : 2 * C]) + (2 * ROWS * 128) * total(off * off)) / cells
    at = lax.broadcasted_iota(jnp.int32, centers.shape, 1)
    low = total(jnp.where(at == place_ref[0], off, 0.0))
    high = total(jnp.where(at == place_ref[1], off, 0.0))
    own = total(jnp.where(at == place_ref[7], off, 0.0))
    found = (mean, lax.rsqrt(spread + EPSILON), low, high)
    st_ref[...] = jnp.concatenate([*found, own, jnp.zeros((C, 123), F32)], axis=1)
    return found


def kept_stats(st_ref):
    return tuple(st_ref[:, k : k + 1] for k in range(4))


def sums_of(row):
    parts = jnp.transpose(jnp.broadcast_to(row, (128, 128)))[:, 0:1]
    return parts[0:C], parts[C : 2 * C]


def feature_sums(v):
    lane = lanes(128)
    inner = v[5].astype(F32)
    for y in range(6, 3 + ROWS):
        inner = inner + v[y].astype(F32)
    ends = [v[y].astype(F32) for y in (3, 4, 3 + ROWS, 4 + ROWS)]
    windows = (inner + ends[0] + ends[1], inner + ends[1] + ends[2], inner + ends[2] + ends[3])
    columns = []
    for dz in range(3):
        for dy in range(3):
            values = windows[dy]
            if dz == 0:
                values = jnp.where(lane == 127, 0.0, values)
            if dz == 2:
                values = jnp.where(lane == 0, 0.0, values)
            column = total(values)
            columns.append(column + jnp.concatenate([column[C:], column[:C]], axis=0))
    return jnp.transpose(jnp.concatenate(columns + [jnp.zeros((128, 119), F32)], axis=1))[0:16]


def ones_of(x1):
    return lambda dz, dy: jnp.broadcast_to(x1[dz * 3 + dy : dz * 3 + dy + 1], (C, 128))


def act(z):
    e = jnp.exp2(jnp.abs(z) * (-8.0 / LN2))
    soft = jnp.maximum(z, 0.0) * 0.99 + jnp.log2(1.0 + e) * (0.99 * LN2 / 8.0)
    return 0.01 * z + soft


def act_slope(z):
    return 0.505 + 0.495 * jnp.tanh(4.0 * z)


def kept(place_ref, y, rows, margin):
    low = place_ref[2].astype(F32)
    high = place_ref[3].astype(F32)
    if y < margin:
        edge = place_ref[4].astype(F32)
    elif y >= rows - margin:
        edge = place_ref[5].astype(F32)
    else:
        return low, None, high
    return low * edge, edge, high * edge


def masked(values, factors):
    f_low, f_own, f_high = factors
    own = values[C : 3 * C]
    own = own if f_own is None else own * f_own
    return jnp.concatenate([values[0:C] * f_low, own, values[3 * C :] * f_high], axis=0).astype(
        BF16
    )


def weight_sums(g_ref, v_ref, first, acc_ref):
    step = 4
    for y in range(0, ROWS, step):
        right = jnp.concatenate(
            [v_ref[first + y + k : first + y + k + 3].reshape(384, 128) for k in range(step)], axis=1
        )
        left = g_ref[:, y * 128 : (y + step) * 128]
        product = lax.dot_general(
            left, right, (((1,), (1,)), ((), ())), preferred_element_type=F32
        )
        if y == 0:
            acc_ref[...] = product
        else:
            acc_ref[...] += product


def folded(acc_ref):
    def tile(dz, dy):
        both = acc_ref[dz * 64 : dz * 64 + 64, dy * 128 : dy * 128 + 128]
        return both[0:C] + pltpu.roll(both[C:], 96, 1)

    return tile


def put_shifted(g_ref, y, values, lane):
    at = slice(y * 128, (y + 1) * 128)
    g_ref[0:64, at] = from_above(values, lane).astype(BF16)
    g_ref[64:128, at] = values.astype(BF16)
    g_ref[128:192, at] = from_below(values, lane).astype(BF16)


def pack_kernel(need, send, own, cot, up_ref, down_ref):
    need(own, cot)
    up_ref[0:4] = own[ROWS - 4 : ROWS]
    up_ref[4:6] = cot[ROWS - 2 : ROWS]
    down_ref[0:4] = own[0:4]
    down_ref[4:6] = cot[0:2]


def corner_kernel(need, send, y_low, y_high, rows):
    need(y_low, y_high)
    rows[0:4] = y_low[0:4]
    rows[4:8] = y_high[0:4]


def weights_kernel(need, send, k1, k2, w1, w2, b1, b2):
    need(k1, k2)
    row = lax.broadcasted_iota(jnp.int32, (C, 128), 0)
    col = lax.broadcasted_iota(jnp.int32, (C, 128), 1)
    eye = jnp.where(row == col, 1.0, 0.0)[:, 0:C].astype(BF16)
    zero = jnp.zeros((C, C), BF16)
    for k_ref, w_ref, b_ref in ((k1, w1, b1), (k2, w2, b2)):
        lined = jnp.zeros((9 * C, 128), F32)
        for dx in range(3):
            spot = jnp.where(row + dx * C == col, 1.0, 0.0).astype(BF16)
            lined = lined + jnp.dot(
                k_ref[dx * 9 : dx * 9 + 9].reshape(9 * C, C), spot, preferred_element_type=F32
            )
        stack = []
        for t in range(9):
            stack += [k_ref[18 + t], k_ref[9 + t], k_ref[t], zero]
        turned = lax.dot_general(
            eye,
            jnp.concatenate(stack, axis=0),
            (((1,), (1,)), ((), ())),
            preferred_element_type=F32,
        )
        for dy in range(3):
            for dz in range(3):
                here = slice(dy * 128, dy * 128 + 128)
                t = dy * 3 + dz
                tile = lined[t * C : t * C + C]
                w_ref[dz * 64 : dz * 64 + C, here] = tile.astype(BF16)
                w_ref[dz * 64 + C : dz * 64 + 64, here] = pltpu.roll(tile, C, 1).astype(BF16)
                t = 8 - t
                tile = turned[:, t * 128 : t * 128 + 128]
                b_ref[dz * 64 : dz * 64 + C, here] = tile.astype(BF16)
                b_ref[dz * 64 + C : dz * 64 + 64, here] = pltpu.roll(tile, C, 1).astype(BF16)


def first_kernel(
    need, send, own, x_low, x_high, y_low, y_high, c_low, c_high, w, v, h, msg, x1, center_out
):
    need(own, x_low, x_high, y_low, y_high, c_low, c_high, w)
    low = joined(4, x_low, c_low, c_low, 4)
    high = joined(4, x_high, c_high, c_high, 4)
    own = joined(4, own, y_low, y_high, 0)
    acc = [jnp.zeros((64, 128), F32), jnp.zeros((64, 128), F32)]
    for k, pair in enumerate(((low, own), (own, high))):

        def emit(y, values, k=k):
            h[y, 64 * k : 64 * k + 64] = values
            if 3 <= y < 3 + ROWS:
                acc[k] = acc[k] + values

        conv_rows(windows_of(*pair), w, ROWS + 6, emit)
    send(h)
    for y in range(ROWS + 8):
        v[y] = jnp.concatenate([low(y)[C:], own(y), high(y)[0:C]], axis=0)
    send(v)
    center = center_of(jnp.concatenate([acc[0][C:], acc[1][0:C]], axis=0))
    both = twice(center)
    spread = jnp.zeros((64, 128), F32)
    for y in range(3, 3 + ROWS):
        off = h[y, C : 3 * C] - both
        spread = spread + off * off
    center_out[...] = jnp.broadcast_to(center, (C, 128))
    x1[...] = feature_sums(v)
    send(center_out, x1)
    rows_message((center, fold(total(spread))), (ones_of(x1),), msg)


def second_kernel(
    cells, need, send, place, r1, gb, h1, cot, y_low, y_high, w, v, h, low, high, msg, st1, x1
):
    need(gb)
    mean, inverse, _, _ = stats_of(r1[:, 0, :], place, cells, st1)
    x1[...] = jnp.sum(r1[...], axis=0)
    send(st1, x1)
    mean4, scale4 = fourfold(mean), fourfold(inverse * gb[:, 0:1])
    shift4 = fourfold(gb[:, 1:2])
    rows = ROWS + 6
    need(h1)
    for y in range(rows):
        v[y] = masked(act((h1[y] - mean4) * scale4 + shift4), kept(place, y, rows, 3))
    send(v)
    need(w, cot, y_low, y_high)
    acc = [jnp.zeros((64, 128), F32)]

    def emit(y, values):
        h[y] = values
        if 2 <= y < 2 + ROWS:
            acc[0] = acc[0] + values

    rows = ROWS + 4
    conv_rows(windows_of(v), w, rows, emit)
    send(h)
    center = center_of(acc[0])
    both = twice(center)
    spread = jnp.zeros((64, 128), F32)
    for y in range(rows):
        off = h[y] - both
        if 2 <= y < 2 + ROWS:
            spread = spread + off * off
        low[y] = off[0:C].astype(BF16)
        high[y] = off[C:].astype(BF16)
        values = cot_row(cot, y_low, y_high, y)
        low[rows + y] = values[0:C]
        high[rows + y] = values[C:]
    send(low, high)
    message((center, fold(total(spread))), msg)


def side_kernel(need, send, center, h1, v1, xh, g, acc):
    need(center, h1)
    both = twice(center[...])
    lane = lanes(64)
    for y in range(ROWS):
        put_shifted(g, y, h1[y + 3] - both, lane)
    need(v1)
    weight_sums(g, v1, 3, acc)
    tile = folded(acc)
    for dz in range(3):
        for dy in range(3):
            xh[dz * 3 + dy] = tile(dz, dy)


def cot_row(cot, y_low, y_high, y):
    if y < 2:
        return y_low[4 + y]
    if y < 2 + ROWS:
        return cot[y - 2]
    return y_high[2 + y - ROWS]


def third_kernel(cells, need, send, place, r2, gb, cot, h2, st1, x1, xh, out, msg, st2):
    need(gb)
    mean, inverse, _, _ = stats_of(r2[...], place, cells, st2)
    need(h2, cot)
    mean2, inverse2 = twice(mean), twice(inverse)
    gain2, bias2 = twice(gb[:, 2:3]), twice(gb[:, 3:4])
    plain = jnp.zeros((64, 128), F32)
    both = jnp.zeros((64, 128), F32)
    for y in range(ROWS):
        normed = (h2[y + 2] - mean2) * inverse2
        z = normed * gain2 + bias2
        out[y] = act(z).astype(BF16)
        slope = cot[y].astype(F32) * act_slope(z)
        plain = plain + slope
        both = both + slope * normed
    send(out)
    need(st1, x1, xh)
    inverse1, own1 = st1[:, 1:2], st1[:, 4:5]
    ones = ones_of(x1)

    def xn(dz, dy):
        return inverse1 * (xh[dz * 3 + dy] + own1 * ones(dz, dy))


    rows_message((fold(total(both)), fold(total(plain))), (xn,), msg)


def fourth_kernel(
    cells, need, send, place, r3, st2, gb, h2, x_low, x_high, cot, y_low, y_high, w, st1, h1, v2, v1, slope1, low, high, msg, t3, v, g, acc, acc1,
):
    need(st2, gb)
    mean, inverse, o_low, o_high = kept_stats(st2)
    t3[...] = jnp.sum(r3[...], axis=0)
    send(t3)
    nsum, plain = sums_of(t3[0:1])
    need(h2, x_low, x_high, cot, y_low, y_high)
    gain, bias = gb[:, 2:3], gb[:, 3:4]
    lead = gain * inverse
    p_mean, n_mean = plain / cells, nsum / cells

    def grad(normed, c, gain, bias, lead, p_mean, n_mean):
        slope = c.astype(F32) * act_slope(normed * gain + bias)
        return lead * (slope - p_mean - normed * n_mean)

    one = (gain, bias, lead, p_mean, n_mean)
    two = tuple(twice(a) for a in one)
    mean2, inverse2 = twice(mean), twice(inverse)
    lane = lanes(64)
    rows = ROWS + 4
    for y in range(rows):
        g_low = grad((x_low[y].astype(F32) + o_low) * inverse, x_low[rows + y], *one)
        g_own = grad((h2[y] - mean2) * inverse2, cot_row(cot, y_low, y_high, y), *two)
        g_high = grad((x_high[y].astype(F32) + o_high) * inverse, x_high[rows + y], *one)
        both = jnp.concatenate([g_low, g_own, g_high], axis=0)
        v[y] = masked(both, kept(place, y, rows, 2))
        if 2 <= y < 2 + ROWS:
            put_shifted(g, y - 2, g_own, lane)
    need(v2)
    weight_sums(g, v2, 2, acc)

    need(h1, st1, w)
    mean, inverse, _, _ = kept_stats(st1)
    mean2, inverse2 = twice(mean), twice(inverse)
    gain2, bias2 = twice(gb[:, 0:1]), twice(gb[:, 1:2])
    sums = [jnp.zeros((64, 128), F32), jnp.zeros((64, 128), F32)]

    def emit(y, values):
        normed = (h1[y + 2] - mean2) * inverse2
        slope = values * act_slope(normed * gain2 + bias2)
        slope1[y] = slope
        low[y] = slope[0:C].astype(BF16)
        high[y] = slope[C:].astype(BF16)
        if 1 <= y < 1 + ROWS:
            sums[0] = sums[0] + slope * normed
            sums[1] = sums[1] + slope
            put_shifted(g, y - 1, slope, lane)

    conv_rows(windows_of(v), w, ROWS + 2, emit)
    send(slope1, low, high)
    need(v1)
    weight_sums(g, v1, 3, acc1)
    rows_message(
        (fold(total(sums[0])), fold(total(sums[1]))), (folded(acc1), folded(acc)), msg
    )


def owner_kernel(cells, need, send, place, r4, st1, gb, t3, x1, msg, norms, t4):
    need(st1, gb, t3, x1)
    _, inverse, _, _ = kept_stats(st1)
    t4[...] = jnp.sum(r4[...], axis=0)
    nsum, plain = sums_of(t4[0:1])
    mine = lax.broadcasted_iota(jnp.int32, (C, 1), 0) == place[6]

    def picked(column):
        return jnp.sum(jnp.where(mine, column, 0.0), axis=0, keepdims=True)

    scale = cells**-0.5
    lead = picked(gb[:, 0:1] * inverse) * scale
    third, fourth = t3[...], t4[...]
    one = fourth[1:4] - picked(plain) * (x1[1:4] / cells) - picked(nsum) * (third[1:4] / cells)
    one = lead * one
    two = fourth[4:7] * scale
    tile = jnp.concatenate([one, two, jnp.zeros((2, 128), F32)], axis=0)
    msg[...] = jnp.broadcast_to(tile[None], msg.shape)
    for k, row in enumerate((fourth[0:1], third[0:1])):
        norms[2 * k : 2 * k + 1] = row[:, 0:C] * scale
        norms[2 * k + 1 : 2 * k + 2] = row[:, C : 2 * C] * scale


def finish_kernel(need, send, parts, one, two):
    for dz in range(3):
        for dy in range(3):
            for k, out in enumerate((one, two)):
                tile = parts[dz * C : (dz + 1) * C, 3 * k + dy, :]
                for dx in range(3):
                    out[dx * 9 + dy * 3 + dz] = tile[:, dx * C : (dx + 1) * C]


def fifth_kernel(cells, need, send, place, t4, st1, gb, h1, slope1, s_low, s_high, w, out, v):
    need(t4, st1, gb)
    mean, inverse, _, _ = kept_stats(st1)
    nsum, plain = sums_of(t4[0:1])
    mean4, inverse4 = fourfold(mean), fourfold(inverse)
    lead4 = fourfold(gb[:, 0:1] * inverse)
    p_mean4, n_mean4 = fourfold(plain / cells), fourfold(nsum / cells)
    rows = ROWS + 2
    need(slope1, s_low, s_high, h1)
    for y in range(rows):
        slope = jnp.concatenate(
            [s_low[y].astype(F32), slope1[y], s_high[y].astype(F32)], axis=0
        )
        normed = (h1[y + 2] - mean4) * inverse4
        v[y] = masked(lead4 * (slope - p_mean4 - normed * n_mean4), kept(place, y, rows, 1))
    need(w)

    def emit(y, values):
        out[y] = values.astype(BF16)

    conv_rows(windows_of(v), w, ROWS, emit)


def call(kernel, ins, outs, name, scratch=(), smem_first=True, after=(), near=0, cut=()):
    lead = 1 if smem_first else 0
    count_in, count_out = len(ins) - lead - near, len(outs)
    far_ins = ins[lead + near :]
    own = [any(a is b for b in cut) for a in far_ins]
    shapes = [(a.shape[0], 2 * C, 128) if c else a.shape for a, c in zip(far_ins, own)]

    def body(*refs):
        first, rest = refs[: lead + near], refs[lead + near :]
        parts = []
        for size in (count_in, len(after), count_out, count_in, count_out, 2):
            parts.append(rest[:size])
            rest = rest[size:]
        sources, _, targets, in_bufs, out_bufs, (in_sems, out_sems) = parts
        arriving = [
            pltpu.make_async_copy(a.at[:, C : 3 * C] if c else a, b, in_sems.at[k])
            for k, (a, b, c) in enumerate(zip(sources, in_bufs, own))
        ]
        leaving = [
            pltpu.make_async_copy(a, b, out_sems.at[k])
            for k, (a, b) in enumerate(zip(out_bufs, targets))
        ]
        waiting, held = list(range(count_in)), list(range(count_out))
        for copy in arriving:
            copy.start()

        def need(*wanted):
            for k in list(waiting):
                if any(in_bufs[k] is ref for ref in wanted):
                    arriving[k].wait()
                    waiting.remove(k)

        def send(*ready):
            for k in list(held):
                if any(out_bufs[k] is ref for ref in ready):
                    leaving[k].start()
                    held.remove(k)

        kernel(need, send, *first, *in_bufs, *out_bufs, *rest)
        send(*out_bufs)
        need(*in_bufs)
        for copy in leaving:
            copy.wait()

    far = pl.BlockSpec(memory_space=pltpu.HBM)
    return pl.pallas_call(
        body,
        out_shape=outs,
        in_specs=[SM] * lead
        + [pl.BlockSpec(memory_space=pltpu.VMEM)] * near
        + [far] * (count_in + len(after)),
        out_specs=[far] * count_out,
        scratch_shapes=[
            *[pltpu.VMEM(shape, a.dtype) for shape, a in zip(shapes, far_ins)],
            *[pltpu.VMEM(a.shape, a.dtype) for a in outs],
            pltpu.SemaphoreType.DMA((max(count_in, 1),)),
            pltpu.SemaphoreType.DMA((count_out,)),
            *scratch,
        ],
        compiler_params=pltpu.CompilerParams(vmem_limit_bytes=56 * 1024 * 1024),
        cost_estimate=pl.CostEstimate(
            flops=2_000_000_000, bytes_accessed=6_000_000, transcendentals=0
        ),
        name=name,
    )(*ins, *after)


def up(values, axes):
    count = lax.axis_size(axes)
    return lax.ppermute(values, axes, [(i, i + 1) for i in range(count - 1)])


def down(values, axes):
    count = lax.axis_size(axes)
    return lax.ppermute(values, axes, [(i + 1, i) for i in range(count - 1)])


def share(msg):
    return lax.all_to_all(msg, ALL, 0, 0, tiled=True)


def local(features, kernel_one, gain_one, bias_one, kernel_two, gain_two, bias_two, cotangent):
    count_x, count_y = lax.axis_size(GX), lax.axis_size(GY)
    count = count_x * count_y
    cells = float(count * 2 * ROWS * 128)
    gx, gy = lax.axis_index(GX), lax.axis_index(GY)
    at = gx * count_y + gy
    place = jnp.stack(
        [at - count_y, at + count_y, gx > 0, gx < count_x - 1, gy > 0, gy < count_y - 1, at % C, at]
    ).astype(jnp.int32)
    gb = jnp.stack([gain_one, bias_one, gain_two, bias_two], axis=1)

    own = jnp.transpose(features, (2, 1, 0, 3)).reshape(ROWS, 64, 128)
    cot = jnp.transpose(cotangent, (2, 1, 0, 3)).reshape(ROWS, 64, 128)

    def rims(rows):
        return [sh((rows, C, 128), BF16)] * 2

    msg, four, wide = (sh((count, *tile), F32) for tile in ((128,), (4, 128), (8, 128)))
    stats = sh((C, 128), F32)
    corr = (pltpu.VMEM((192, ROWS * 128), BF16), pltpu.VMEM((192, 384), F32))

    x_low, x_high = up(own, GX), down(own, GX)
    y_up, y_down = call(
        pack_kernel, (own, cot), [sh((6, 64, 128), BF16)] * 2, "pack", smem_first=False
    )
    y_low, y_high = up(y_up, GY), down(y_down, GY)
    (corner,) = call(
        corner_kernel, (y_low, y_high), [sh((8, 64, 128), BF16)], "corner", smem_first=False
    )
    c_low, c_high = up(corner, GX), down(corner, GX)
    taps = [
        jnp.transpose(k, (2, 3, 4, 0, 1)).reshape(27, C, C) for k in (kernel_one, kernel_two)
    ]
    w1, w2, b1, b2 = call(
        weights_kernel, taps, [sh((192, 384), BF16)] * 4, "weights", smem_first=False
    )

    v1, h1, m1, x1_own, center = call(
        first_kernel,
        (own, x_low, x_high, y_low, y_high, c_low, c_high, w1),
        [sh((40, 128, 128), BF16), sh((38, 128, 128), F32), four, sh((16, 128), F32), stats],
        "conv_one",
        smem_first=False,
    )
    r1 = share(m1)

    (xh,) = call(
        side_kernel,
        (center, h1, v1),
        [sh((9, C, 128), F32)],
        "hidden_features",
        scratch=corr,
        smem_first=False,
        cut=(h1,),
    )

    v2, h2, low, high, m2, st1, x1 = call(
        lambda *refs: second_kernel(cells, *refs),
        (place, r1, gb, h1, cot, y_low, y_high, w2),
        [
            sh((38, 128, 128), BF16), sh((36, 64, 128), F32), *rims(72), msg, stats,
            sh((4, 128), F32),
        ],
        "conv_two",
        near=1,
        after=(xh,),
    )
    h2_low, h2_high = up(high, GX), down(low, GX)
    r2 = share(m2)
    output, m3, st2 = call(
        lambda *refs: third_kernel(cells, *refs),
        (place, r2, gb, cot, h2, st1, x1_own, xh),
        [sh((ROWS, 64, 128), BF16), four, stats],
        "slope_two",
        near=1,
    )
    r3 = share(m3)

    def back(rows):
        return jnp.transpose(rows.reshape(ROWS, 2, C, 128), (2, 1, 0, 3))

    output = back(output)

    slope1, low, high, m4, t3 = call(
        lambda *refs: fourth_kernel(cells, *refs),
        (
            place, r3, st2, gb, h2, h2_low, h2_high, cot, y_low, y_high,
            b2, st1, h1, v2, v1,
        ),
        [sh((34, 64, 128), F32), *rims(34), wide, sh((4, 128), F32)],
        "back_two",
        near=1,
        cut=(h1,),
        scratch=(pltpu.VMEM((36, 128, 128), BF16), *corr, corr[1]),
    )
    s_low, s_high = up(high, GX), down(low, GX)
    r4 = share(m4)

    m5, norm_grads, t4 = call(
        lambda *refs: owner_kernel(cells, *refs),
        (place, r4, st1, gb, t3, x1),
        [wide, sh((4, C), F32), sh((8, 128), F32)],
        "own_rows",
        near=1,
        after=(s_low, s_high, output),
    )
    r5 = share(m5)
    (grad,) = call(
        lambda *refs: fifth_kernel(cells, *refs),
        (place, t4, st1, gb, h1, slope1, s_low, s_high, b1),
        [sh((ROWS, 64, 128), BF16)],
        "back_one",
        scratch=(pltpu.VMEM((34, 128, 128), BF16),),
    )
    grads = call(finish_kernel, (r5,), [sh((27, C, C), F32)] * 2, "finish", smem_first=False, near=1)
    one, two = [jnp.transpose(k.reshape(3, 3, 3, C, C), (3, 4, 0, 1, 2)) for k in grads]

    return output, back(grad), one, two, norm_grads


def solution(mesh):
    nx, ny = mesh.devices.shape
    parts = (4, nx // 4, ny // 2, 2)
    split = Mesh(mesh.devices.reshape(parts), ALL)
    spec = P(None, GX, GY, None)
    in_specs = (spec, P(), P(), P(), P(), P(), P(), spec)
    out_specs = (spec, spec, P(), P(), P())
    return jax.shard_map(local, mesh=split, in_specs=in_specs, out_specs=out_specs, check_vma=False)
```

```python
import jax
import jax.numpy as jnp
from jax import lax
from jax.experimental import pallas as pl
from jax.experimental.pallas import tpu as pltpu
from jax.sharding import Mesh
from jax.sharding import PartitionSpec as P

GX = ("gx_0", "gx_1")
GY = ("gy_0", "gy_1")
ALL = GX + GY

EPSILON = 1e-05
C = 32
ROWS = 32
F32 = jnp.float32
BF16 = jnp.bfloat16
LN2 = 0.6931471805599453
SM = pl.BlockSpec(memory_space=pltpu.SMEM)


def sh(shape, kind):
    return jax.ShapeDtypeStruct(shape, kind)


def from_below(values, lane):
    return jnp.where(lane == 0, 0.0, pltpu.roll(values, 1, 1))


def from_above(values, lane):
    return jnp.where(lane == 127, 0.0, pltpu.roll(values, 127, 1))


def lanes(rows):
    return lax.broadcasted_iota(jnp.int32, (rows, 128), 1)


def windows_of(*refs):
    if len(refs) == 1:
        return lambda y: refs[0][y : y + 3].reshape(384, 128)
    return lambda y: jnp.concatenate([rows(y + k) for k in range(3) for rows in refs], axis=0)


def joined(margin, middle, below, above, first):
    def row(y):
        if y < margin:
            return below[y]
        if y < margin + ROWS:
            return middle[y - margin]
        return above[first + y - margin - ROWS]

    return row


def conv_rows(window, w_ref, rows, emit):
    lane = lanes(64)
    weights = w_ref[...]
    for y in range(0, rows, 2):
        both = jnp.concatenate([window(y), window(y + 1)], axis=1)
        product = jnp.dot(weights, both, preferred_element_type=F32)
        for k in range(2):
            part = product[:, k * 128 : (k + 1) * 128]
            emit(
                y + k,
                part[64:128] + from_below(part[0:64], lane) + from_above(part[128:192], lane),
            )


def fold(column):
    return column[0:C] + column[C : 2 * C]


def total(values):
    return jnp.sum(values, axis=1, keepdims=True)


def twice(column):
    return jnp.concatenate([column, column], axis=0)


def fourfold(column):
    return twice(twice(column))


def message(columns, msg_ref):
    count = msg_ref.shape[0]
    spare = jnp.zeros((128 - C * len(columns), 1), F32)
    column = jnp.concatenate([*columns, spare], axis=0)
    msg_ref[...] = jnp.transpose(jnp.broadcast_to(column, (128, count)))


def as_row(column):
    return jnp.transpose(jnp.broadcast_to(column, (128, 128)))[0:1]


def rows_message(columns, groups, msg_ref):
    spare = jnp.zeros((128 - C * len(columns), 1), F32)
    row = as_row(jnp.concatenate([*columns, spare], axis=0))
    height = msg_ref.shape[1]
    at = lax.broadcasted_iota(jnp.int32, (height, 128), 0)
    tile = jnp.where(at == 0, jnp.broadcast_to(row, (height, 128)), 0.0)
    msg_ref[...] = jnp.broadcast_to(tile[None], msg_ref.shape)
    for k, group in enumerate(groups):
        for dz in range(3):
            for dy in range(3):
                msg_ref[dz * C : (dz + 1) * C, 1 + 3 * k + dy, :] = group(dz, dy)


def center_of(acc):
    return fold(total(acc)) / (2 * ROWS * 128)


def stats_of(rows, place_ref, cells, st_ref):
    parts = jnp.transpose(rows)
    centers = parts[0:C]
    count = parts.shape[1]
    mean = total(centers) / count
    off = centers - mean
    spread = (total(parts[C : 2 * C]) + (2 * ROWS * 128) * total(off * off)) / cells
    at = lax.broadcasted_iota(jnp.int32, centers.shape, 1)
    low = total(jnp.where(at == place_ref[0], off, 0.0))
    high = total(jnp.where(at == place_ref[1], off, 0.0))
    own = total(jnp.where(at == place_ref[7], off, 0.0))
    found = (mean, lax.rsqrt(spread + EPSILON), low, high)
    st_ref[...] = jnp.concatenate([*found, own, jnp.zeros((C, 123), F32)], axis=1)
    return found


def kept_stats(st_ref):
    return tuple(st_ref[:, k : k + 1] for k in range(4))


def sums_of(row):
    parts = jnp.transpose(jnp.broadcast_to(row, (128, 128)))[:, 0:1]
    return parts[0:C], parts[C : 2 * C]


def feature_sums(v):
    lane = lanes(128)
    inner = v[5].astype(F32)
    for y in range(6, 3 + ROWS):
        inner = inner + v[y].astype(F32)
    ends = [v[y].astype(F32) for y in (3, 4, 3 + ROWS, 4 + ROWS)]
    windows = (inner + ends[0] + ends[1], inner + ends[1] + ends[2], inner + ends[2] + ends[3])
    columns = []
    for dz in range(3):
        for dy in range(3):
            values = windows[dy]
            if dz == 0:
                values = jnp.where(lane == 127, 0.0, values)
            if dz == 2:
                values = jnp.where(lane == 0, 0.0, values)
            column = total(values)
            columns.append(column + jnp.concatenate([column[C:], column[:C]], axis=0))
    return jnp.transpose(jnp.concatenate(columns + [jnp.zeros((128, 119), F32)], axis=1))[0:16]


def ones_of(x1):
    return lambda dz, dy: jnp.broadcast_to(x1[dz * 3 + dy : dz * 3 + dy + 1], (C, 128))


def act(z):
    e = jnp.exp2(jnp.abs(z) * (-8.0 / LN2))
    soft = jnp.maximum(z, 0.0) * 0.99 + jnp.log2(1.0 + e) * (0.99 * LN2 / 8.0)
    return 0.01 * z + soft


def act_slope(z):
    return 0.505 + 0.495 * jnp.tanh(4.0 * z)


def kept(place_ref, y, rows, margin):
    low = place_ref[2].astype(F32)
    high = place_ref[3].astype(F32)
    if y < margin:
        edge = place_ref[4].astype(F32)
    elif y >= rows - margin:
        edge = place_ref[5].astype(F32)
    else:
        return low, None, high
    return low * edge, edge, high * edge


def masked(values, factors):
    f_low, f_own, f_high = factors
    own = values[C : 3 * C]
    own = own if f_own is None else own * f_own
    return jnp.concatenate([values[0:C] * f_low, own, values[3 * C :] * f_high], axis=0).astype(
        BF16
    )


def weight_sums(g_ref, v_ref, first, acc_ref):
    step = 4
    for y in range(0, ROWS, step):
        right = jnp.concatenate(
            [v_ref[first + y + k : first + y + k + 3].reshape(384, 128) for k in range(step)], axis=1
        )
        left = g_ref[:, y * 128 : (y + step) * 128]
        product = lax.dot_general(
            left, right, (((1,), (1,)), ((), ())), preferred_element_type=F32
        )
        if y == 0:
            acc_ref[...] = product
        else:
            acc_ref[...] += product


def folded(acc_ref):
    def tile(dz, dy):
        both = acc_ref[dz * 64 : dz * 64 + 64, dy * 128 : dy * 128 + 128]
        return both[0:C] + pltpu.roll(both[C:], 96, 1)

    return tile


def put_shifted(g_ref, y, values, lane):
    at = slice(y * 128, (y + 1) * 128)
    g_ref[0:64, at] = from_above(values, lane).astype(BF16)
    g_ref[64:128, at] = values.astype(BF16)
    g_ref[128:192, at] = from_below(values, lane).astype(BF16)


def pack_kernel(need, send, own, cot, up_ref, down_ref):
    need(own, cot)
    up_ref[0:4] = own[ROWS - 4 : ROWS]
    up_ref[4:6] = cot[ROWS - 2 : ROWS]
    down_ref[0:4] = own[0:4]
    down_ref[4:6] = cot[0:2]


def corner_kernel(need, send, y_low, y_high, rows):
    need(y_low, y_high)
    rows[0:4] = y_low[0:4]
    rows[4:8] = y_high[0:4]


def weights_kernel(need, send, k1, k2, w1, w2):
    need(k1, k2)
    row = lax.broadcasted_iota(jnp.int32, (C, 128), 0)
    col = lax.broadcasted_iota(jnp.int32, (C, 128), 1)
    for k_ref, w_ref in ((k1, w1), (k2, w2)):
        lined = jnp.zeros((9 * C, 128), F32)
        for dx in range(3):
            spot = jnp.where(row + dx * C == col, 1.0, 0.0).astype(BF16)
            lined = lined + jnp.dot(
                k_ref[dx * 9 : dx * 9 + 9].reshape(9 * C, C), spot, preferred_element_type=F32
            )
        for dy in range(3):
            for dz in range(3):
                t = dy * 3 + dz
                put_tile(w_ref, dz, dy, lined[t * C : t * C + C])


def flipped_kernel(need, send, k1, k2, b1, b2):
    need(k1, k2)
    row = lax.broadcasted_iota(jnp.int32, (C, 128), 0)
    col = lax.broadcasted_iota(jnp.int32, (C, 128), 1)
    eye = jnp.where(row == col, 1.0, 0.0)[:, 0:C].astype(BF16)
    zero = jnp.zeros((C, C), BF16)
    for k_ref, b_ref in ((k1, b1), (k2, b2)):
        stack = []
        for t in range(9):
            stack += [k_ref[18 + t], k_ref[9 + t], k_ref[t], zero]
        turned = lax.dot_general(
            eye,
            jnp.concatenate(stack, axis=0),
            (((1,), (1,)), ((), ())),
            preferred_element_type=F32,
        )
        for dy in range(3):
            for dz in range(3):
                t = 8 - dy * 3 - dz
                put_tile(b_ref, dz, dy, turned[:, t * 128 : t * 128 + 128])


def put_tile(ref, dz, dy, tile):
    here = slice(dy * 128, dy * 128 + 128)
    ref[dz * 64 : dz * 64 + C, here] = tile.astype(BF16)
    ref[dz * 64 + C : dz * 64 + 64, here] = pltpu.roll(tile, C, 1).astype(BF16)


def first_kernel(
    need, send, own, x_low, x_high, y_low, y_high, c_low, c_high, w, v, h, msg, x1, center_out
):
    need(own, x_low, x_high, y_low, y_high, c_low, c_high, w)
    low = joined(4, x_low, c_low, c_low, 4)
    high = joined(4, x_high, c_high, c_high, 4)
    own = joined(4, own, y_low, y_high, 0)
    acc = [jnp.zeros((64, 128), F32), jnp.zeros((64, 128), F32)]
    for k, pair in enumerate(((low, own), (own, high))):

        def emit(y, values, k=k):
            h[y, 64 * k : 64 * k + 64] = values
            if k == 1:
                send(h, row=y)
            if 3 <= y < 3 + ROWS:
                acc[k] = acc[k] + values

        conv_rows(windows_of(*pair), w, ROWS + 6, emit)
    send(h)
    for y in range(ROWS + 8):
        v[y] = jnp.concatenate([low(y)[C:], own(y), high(y)[0:C]], axis=0)
        send(v, row=y)
    send(v)
    center = center_of(jnp.concatenate([acc[0][C:], acc[1][0:C]], axis=0))
    both = twice(center)
    spread = jnp.zeros((64, 128), F32)
    for y in range(3, 3 + ROWS):
        off = h[y, C : 3 * C] - both
        spread = spread + off * off
    center_out[...] = jnp.broadcast_to(center, (C, 128))
    x1[...] = feature_sums(v)
    send(center_out, x1)
    rows_message((center, fold(total(spread))), (ones_of(x1),), msg)


def second_kernel(
    cells, need, send, place, r1, gb, h1, cot, y_low, y_high, w, v, h, low, high, msg, st1, x1
):
    need(gb)
    mean, inverse, _, _ = stats_of(r1[:, 0, :], place, cells, st1)
    x1[...] = jnp.sum(r1[...], axis=0)
    send(st1, x1)
    mean4, scale4 = fourfold(mean), fourfold(inverse * gb[:, 0:1])
    shift4 = fourfold(gb[:, 1:2])
    rows = ROWS + 6
    for y in range(rows):
        need(h1, row=y)
        v[y] = masked(act((h1[y] - mean4) * scale4 + shift4), kept(place, y, rows, 3))
        send(v, row=y)
    need(w, cot, y_low, y_high)
    acc = [jnp.zeros((64, 128), F32)]

    def emit(y, values):
        h[y] = values
        send(h, row=y)
        if 2 <= y < 2 + ROWS:
            acc[0] = acc[0] + values

    rows = ROWS + 4
    conv_rows(windows_of(v), w, rows, emit)
    send(h)
    center = center_of(acc[0])
    both = twice(center)
    spread = jnp.zeros((64, 128), F32)
    for y in range(rows):
        off = h[y] - both
        if 2 <= y < 2 + ROWS:
            spread = spread + off * off
        low[2 * y] = off[0:C].astype(BF16)
        high[2 * y] = off[C:].astype(BF16)
        values = cot_row(cot, y_low, y_high, y)
        low[2 * y + 1] = values[0:C]
        high[2 * y + 1] = values[C:]
        send(low, high, row=2 * y + 1)
    message((center, fold(total(spread))), msg)


def side_kernel(need, send, center, h1, v1, xh, g, acc):
    need(center)
    both = twice(center[...])
    lane = lanes(64)
    for y in range(ROWS):
        need(h1, row=y + 3)
        put_shifted(g, y, h1[y + 3] - both, lane)
    need(v1)
    weight_sums(g, v1, 3, acc)
    tile = folded(acc)
    for dz in range(3):
        for dy in range(3):
            xh[dz * 3 + dy] = tile(dz, dy)


def cot_row(cot, y_low, y_high, y):
    if y < 2:
        return y_low[4 + y]
    if y < 2 + ROWS:
        return cot[y - 2]
    return y_high[2 + y - ROWS]


def third_kernel(cells, need, send, place, r2, gb, cot, h2, st1, x1, xh, out, msg, st2):
    need(gb)
    mean, inverse, _, _ = stats_of(r2[...], place, cells, st2)
    mean2, inverse2 = twice(mean), twice(inverse)
    gain2, bias2 = twice(gb[:, 2:3]), twice(gb[:, 3:4])
    plain = jnp.zeros((64, 128), F32)
    both = jnp.zeros((64, 128), F32)
    for y in range(ROWS):
        need(h2, row=y + 2)
        need(cot, row=y)
        normed = (h2[y + 2] - mean2) * inverse2
        z = normed * gain2 + bias2
        out[y] = act(z).astype(BF16)
        send(out, row=y)
        slope = cot[y].astype(F32) * act_slope(z)
        plain = plain + slope
        both = both + slope * normed
    send(out)
    need(st1, x1, xh)
    inverse1, own1 = st1[:, 1:2], st1[:, 4:5]
    ones = ones_of(x1)

    def xn(dz, dy):
        return inverse1 * (xh[dz * 3 + dy] + own1 * ones(dz, dy))


    rows_message((fold(total(both)), fold(total(plain))), (xn,), msg)


def fourth_kernel(
    cells, need, send, place, r3, st2, gb, h2, x_low, x_high, cot, y_low, y_high, w, st1, h1, v2, v1, slope1, low, high, msg, t3, v, g, acc, acc1,
):
    need(st2, gb)
    mean, inverse, o_low, o_high = kept_stats(st2)
    t3[...] = jnp.sum(r3[...], axis=0)
    send(t3)
    nsum, plain = sums_of(t3[0:1])
    need(y_low, y_high)
    gain, bias = gb[:, 2:3], gb[:, 3:4]
    lead = gain * inverse
    p_mean, n_mean = plain / cells, nsum / cells

    def grad(normed, c, gain, bias, lead, p_mean, n_mean):
        slope = c.astype(F32) * act_slope(normed * gain + bias)
        return lead * (slope - p_mean - normed * n_mean)

    one = (gain, bias, lead, p_mean, n_mean)
    two = tuple(twice(a) for a in one)
    mean2, inverse2 = twice(mean), twice(inverse)
    lane = lanes(64)
    rows = ROWS + 4
    for y in range(rows):
        need(h2, row=y)
        need(x_low, x_high, row=2 * y + 1)
        need(cot, row=min(max(y - 2, 0), ROWS - 1))
        g_low = grad((x_low[2 * y].astype(F32) + o_low) * inverse, x_low[2 * y + 1], *one)
        g_own = grad((h2[y] - mean2) * inverse2, cot_row(cot, y_low, y_high, y), *two)
        g_high = grad((x_high[2 * y].astype(F32) + o_high) * inverse, x_high[2 * y + 1], *one)
        both = jnp.concatenate([g_low, g_own, g_high], axis=0)
        v[y] = masked(both, kept(place, y, rows, 2))
        if 2 <= y < 2 + ROWS:
            put_shifted(g, y - 2, g_own, lane)
    need(v2)
    weight_sums(g, v2, 2, acc)

    need(h1, st1, w)
    mean, inverse, _, _ = kept_stats(st1)
    mean2, inverse2 = twice(mean), twice(inverse)
    gain2, bias2 = twice(gb[:, 0:1]), twice(gb[:, 1:2])
    sums = [jnp.zeros((64, 128), F32), jnp.zeros((64, 128), F32)]

    def emit(y, values):
        normed = (h1[y + 2] - mean2) * inverse2
        slope = values * act_slope(normed * gain2 + bias2)
        slope1[y] = slope
        low[y] = slope[0:C].astype(BF16)
        high[y] = slope[C:].astype(BF16)
        send(slope1, low, high, row=y)
        if 1 <= y < 1 + ROWS:
            sums[0] = sums[0] + slope * normed
            sums[1] = sums[1] + slope
            put_shifted(g, y - 1, slope, lane)

    conv_rows(windows_of(v), w, ROWS + 2, emit)
    send(slope1, low, high)
    need(v1)
    weight_sums(g, v1, 3, acc1)
    rows_message(
        (fold(total(sums[0])), fold(total(sums[1]))), (folded(acc1), folded(acc)), msg
    )


def owner_kernel(cells, need, send, place, r4, st1, gb, t3, x1, msg, norms, t4):
    need(st1, gb, t3, x1)
    _, inverse, _, _ = kept_stats(st1)
    t4[...] = jnp.sum(r4[...], axis=0)
    nsum, plain = sums_of(t4[0:1])
    mine = lax.broadcasted_iota(jnp.int32, (C, 1), 0) == place[6]

    def picked(column):
        return jnp.sum(jnp.where(mine, column, 0.0), axis=0, keepdims=True)

    scale = cells**-0.5
    lead = picked(gb[:, 0:1] * inverse) * scale
    third, fourth = t3[...], t4[...]
    one = fourth[1:4] - picked(plain) * (x1[1:4] / cells) - picked(nsum) * (third[1:4] / cells)
    one = lead * one
    two = fourth[4:7] * scale
    tile = jnp.concatenate([one, two, jnp.zeros((2, 128), F32)], axis=0)
    msg[...] = jnp.broadcast_to(tile[None], msg.shape)
    for k, row in enumerate((fourth[0:1], third[0:1])):
        norms[2 * k : 2 * k + 1] = row[:, 0:C] * scale
        norms[2 * k + 1 : 2 * k + 2] = row[:, C : 2 * C] * scale


def finish_kernel(need, send, parts, one, two):
    for dz in range(3):
        for dy in range(3):
            for k, out in enumerate((one, two)):
                tile = parts[dz * C : (dz + 1) * C, 3 * k + dy, :]
                for dx in range(3):
                    out[dx * 9 + dy * 3 + dz] = tile[:, dx * C : (dx + 1) * C]


def fifth_kernel(cells, need, send, place, t4, st1, gb, h1, slope1, s_low, s_high, w, out, v):
    need(t4, st1, gb)
    mean, inverse, _, _ = kept_stats(st1)
    nsum, plain = sums_of(t4[0:1])
    mean4, inverse4 = fourfold(mean), fourfold(inverse)
    lead4 = fourfold(gb[:, 0:1] * inverse)
    p_mean4, n_mean4 = fourfold(plain / cells), fourfold(nsum / cells)
    rows = ROWS + 2
    for y in range(rows):
        need(slope1, s_low, s_high, row=y)
        need(h1, row=y + 2)
        slope = jnp.concatenate(
            [s_low[y].astype(F32), slope1[y], s_high[y].astype(F32)], axis=0
        )
        normed = (h1[y + 2] - mean4) * inverse4
        v[y] = masked(lead4 * (slope - p_mean4 - normed * n_mean4), kept(place, y, rows, 1))
    need(w)

    def emit(y, values):
        out[y] = values.astype(BF16)
        send(out, row=y)

    conv_rows(windows_of(v), w, ROWS, emit)


def pieces_of(shape):
    rows = shape[0]
    if len(shape) < 3 or rows < 32 or rows > 100:
        return [(0, rows)]
    cuts = [rows * c // 4 for c in range(5)]
    return list(zip(cuts, cuts[1:]))


def call(
    kernel, ins, outs, name, scratch=(), smem_first=True, after=(), near=0, cut=(), late=0, grant=56
):
    lead = 1 if smem_first else 0
    count_in, count_out = len(ins) - lead - near, len(outs)
    far_ins = ins[lead + near :]
    own = [any(a is b for b in cut) for a in far_ins]
    shapes = [(a.shape[0], 2 * C, 128) if c else a.shape for a, c in zip(far_ins, own)]

    def body(*refs):
        first, rest = refs[: lead + near], refs[lead + near :]
        parts = []
        for size in (count_in, len(after), count_out, count_in, count_out, 2):
            parts.append(rest[:size])
            rest = rest[size:]
        sources, _, targets, in_bufs, out_bufs, (in_sems, out_sems) = parts

        def source(k, a, b):
            return sources[k].at[a:b, C : 3 * C] if own[k] else sources[k].at[a:b]

        arriving = [
            [
                (a, b, pltpu.make_async_copy(source(k, a, b), buf.at[a:b], in_sems.at[k, c]))
                for c, (a, b) in enumerate(pieces_of(buf.shape))
            ]
            for k, buf in enumerate(in_bufs)
        ]
        leaving = [
            [
                (a, b, pltpu.make_async_copy(buf.at[a:b], targets[k].at[a:b], out_sems.at[k, c]))
                for c, (a, b) in enumerate(pieces_of(buf.shape))
            ]
            for k, buf in enumerate(out_bufs)
        ]
        early, later = arriving[: count_in - late], arriving[count_in - late :]
        for group in (early, later):
            for c in range(4):
                for pieces in group:
                    if c < len(pieces):
                        pieces[c][2].start()
        waiting, held = [list(pieces) for pieces in arriving], [list(pieces) for pieces in leaving]

        def need(*wanted, row=None):
            for ref in wanted:
                for k, buf in enumerate(in_bufs):
                    while buf is ref and waiting[k] and (row is None or waiting[k][0][0] <= row):
                        waiting[k].pop(0)[2].wait()

        def send(*ready, row=None):
            for ref in ready:
                for k, buf in enumerate(out_bufs):
                    while buf is ref and held[k] and (row is None or held[k][0][1] <= row + 1):
                        held[k].pop(0)[2].start()

        kernel(need, send, *first, *in_bufs, *out_bufs, *rest)
        send(*out_bufs)
        need(*in_bufs)
        for pieces in leaving:
            for piece in pieces:
                piece[2].wait()

    far = pl.BlockSpec(memory_space=pltpu.HBM)
    return pl.pallas_call(
        body,
        out_shape=outs,
        in_specs=[SM] * lead
        + [pl.BlockSpec(memory_space=pltpu.VMEM)] * near
        + [far] * (count_in + len(after)),
        out_specs=[far] * count_out,
        scratch_shapes=[
            *[pltpu.VMEM(shape, a.dtype) for shape, a in zip(shapes, far_ins)],
            *[pltpu.VMEM(a.shape, a.dtype) for a in outs],
            pltpu.SemaphoreType.DMA((max(count_in, 1), 4)),
            pltpu.SemaphoreType.DMA((count_out, 4)),
            *scratch,
        ],
        compiler_params=pltpu.CompilerParams(vmem_limit_bytes=grant * 1024 * 1024),
        cost_estimate=pl.CostEstimate(
            flops=2_000_000_000, bytes_accessed=6_000_000, transcendentals=0
        ),
        name=name,
    )(*ins, *after)


def up(values, axes):
    count = lax.axis_size(axes)
    return lax.ppermute(values, axes, [(i, i + 1) for i in range(count - 1)])


def down(values, axes):
    count = lax.axis_size(axes)
    return lax.ppermute(values, axes, [(i + 1, i) for i in range(count - 1)])


def share(msg):
    return lax.all_to_all(msg, ALL, 0, 0, tiled=True)


def local(features, kernel_one, gain_one, bias_one, kernel_two, gain_two, bias_two, cotangent):
    count_x, count_y = lax.axis_size(GX), lax.axis_size(GY)
    count = count_x * count_y
    cells = float(count * 2 * ROWS * 128)
    gx, gy = lax.axis_index(GX), lax.axis_index(GY)
    at = gx * count_y + gy
    place = jnp.stack(
        [at - count_y, at + count_y, gx > 0, gx < count_x - 1, gy > 0, gy < count_y - 1, at % C, at]
    ).astype(jnp.int32)
    gb = jnp.stack([gain_one, bias_one, gain_two, bias_two], axis=1)

    own = jnp.transpose(features, (2, 1, 0, 3)).reshape(ROWS, 64, 128)
    cot = jnp.transpose(cotangent, (2, 1, 0, 3)).reshape(ROWS, 64, 128)

    def rims(rows):
        return [sh((rows, C, 128), BF16)] * 2

    msg, four, wide = (sh((count, *tile), F32) for tile in ((128,), (4, 128), (8, 128)))
    stats = sh((C, 128), F32)
    corr = (pltpu.VMEM((192, ROWS * 128), BF16), pltpu.VMEM((192, 384), F32))

    x_low, x_high = up(own, GX), down(own, GX)
    y_up, y_down = call(
        pack_kernel, (own, cot), [sh((6, 64, 128), BF16)] * 2, "pack", smem_first=False
    )
    y_low, y_high = up(y_up, GY), down(y_down, GY)
    (corner,) = call(
        corner_kernel, (y_low, y_high), [sh((8, 64, 128), BF16)], "corner", smem_first=False
    )
    c_low, c_high = up(corner, GX), down(corner, GX)
    taps = [
        jnp.transpose(k, (2, 3, 4, 0, 1)).reshape(27, C, C) for k in (kernel_one, kernel_two)
    ]
    matrices = [sh((192, 384), BF16)] * 2
    w1, w2 = call(weights_kernel, taps, matrices, "weights", smem_first=False)

    v1, h1, m1, x1_own, center = call(
        first_kernel,
        (own, x_low, x_high, y_low, y_high, c_low, c_high, w1),
        [sh((40, 128, 128), BF16), sh((38, 128, 128), F32), four, sh((16, 128), F32), stats],
        "conv_one",
        smem_first=False,
    )
    r1 = share(m1)

    (xh,) = call(
        side_kernel,
        (center, h1, v1),
        [sh((9, C, 128), F32)],
        "hidden_features",
        scratch=corr,
        smem_first=False,
        cut=(h1,),
    )

    v2, h2, low, high, m2, st1, x1 = call(
        lambda *refs: second_kernel(cells, *refs),
        (place, r1, gb, h1, cot, y_low, y_high, w2),
        [
            sh((38, 128, 128), BF16), sh((36, 64, 128), F32), *rims(72), msg, stats,
            sh((4, 128), F32),
        ],
        "conv_two",
        near=1,
        after=(xh,),
    )
    h2_low, h2_high = up(high, GX), down(low, GX)
    r2 = share(m2)
    b1, b2 = call(flipped_kernel, taps, matrices, "flipped", smem_first=False, after=(h2,))
    output, m3, st2 = call(
        lambda *refs: third_kernel(cells, *refs),
        (place, r2, gb, cot, h2, st1, x1_own, xh),
        [sh((ROWS, 64, 128), BF16), four, stats],
        "slope_two",
        near=1,
        after=(b1,),
    )
    r3 = share(m3)

    def back(rows):
        return jnp.transpose(rows.reshape(ROWS, 2, C, 128), (2, 1, 0, 3))

    output = back(output)

    slope1, low, high, m4, t3 = call(
        lambda *refs: fourth_kernel(cells, *refs),
        (
            place, r3, st2, gb, h2, h2_low, h2_high, cot, y_low, y_high,
            b2, st1, h1, v2, v1,
        ),
        [sh((34, 64, 128), F32), *rims(34), wide, sh((4, 128), F32)],
        "back_two",
        near=1,
        late=5,
        cut=(h1,),
        scratch=(pltpu.VMEM((36, 128, 128), BF16), *corr, corr[1]),
    )
    s_low, s_high = up(high, GX), down(low, GX)
    r4 = share(m4)

    m5, norm_grads, t4 = call(
        lambda *refs: owner_kernel(cells, *refs),
        (place, r4, st1, gb, t3, x1),
        [wide, sh((4, C), F32), sh((8, 128), F32)],
        "own_rows",
        near=1,
        after=(s_low, s_high, output),
    )
    r5 = share(m5)
    (grad,) = call(
        lambda *refs: fifth_kernel(cells, *refs),
        (place, t4, st1, gb, h1, slope1, s_low, s_high, b1),
        [sh((ROWS, 64, 128), BF16)],
        "back_one",
        scratch=(pltpu.VMEM((34, 128, 128), BF16),),
    )
    grads = call(finish_kernel, (r5,), [sh((27, C, C), F32)] * 2, "finish", smem_first=False, near=1, grant=16)
    one, two = [jnp.transpose(k.reshape(3, 3, 3, C, C), (3, 4, 0, 1, 2)) for k in grads]

    return output, back(grad), one, two, norm_grads


def solution(mesh):
    nx, ny = mesh.devices.shape
    parts = (4, nx // 4, ny // 2, 2)
    split = Mesh(mesh.devices.reshape(parts), ALL)
    spec = P(None, GX, GY, None)
    in_specs = (spec, P(), P(), P(), P(), P(), P(), spec)
    out_specs = (spec, spec, P(), P(), P())
    return jax.shard_map(local, mesh=split, in_specs=in_specs, out_specs=out_specs, check_vma=False)
```

```python
import jax
import jax.numpy as jnp
from jax import lax
from jax.experimental import pallas as pl
from jax.experimental.pallas import tpu as pltpu
from jax.sharding import Mesh
from jax.sharding import PartitionSpec as P

GX = ("gx_0", "gx_1")
GY = ("gy_0", "gy_1")
ALL = GX + GY

EPSILON = 1e-05
C = 32
ROWS = 32
F32 = jnp.float32
BF16 = jnp.bfloat16
LN2 = 0.6931471805599453
SM = pl.BlockSpec(memory_space=pltpu.SMEM)


def sh(shape, kind):
    return jax.ShapeDtypeStruct(shape, kind)


def from_below(values, lane):
    return jnp.where(lane == 0, 0.0, pltpu.roll(values, 1, 1))


def from_above(values, lane):
    return jnp.where(lane == 127, 0.0, pltpu.roll(values, 127, 1))


def lanes(rows):
    return lax.broadcasted_iota(jnp.int32, (rows, 128), 1)


def windows_of(*refs):
    if len(refs) == 1:
        return lambda y: refs[0][y : y + 3].reshape(384, 128)
    return lambda y: jnp.concatenate([rows(y + k) for k in range(3) for rows in refs], axis=0)


def joined(margin, middle, below, above, first):
    def row(y):
        if y < margin:
            return below[y]
        if y < margin + ROWS:
            return middle[y - margin]
        return above[first + y - margin - ROWS]

    return row


def conv_rows(window, w_ref, rows, emit):
    lane = lanes(64)
    weights = w_ref[...]
    for y in range(0, rows, 2):
        both = jnp.concatenate([window(y), window(y + 1)], axis=1)
        product = jnp.dot(weights, both, preferred_element_type=F32)
        for k in range(2):
            part = product[:, k * 128 : (k + 1) * 128]
            emit(
                y + k,
                part[64:128] + from_below(part[0:64], lane) + from_above(part[128:192], lane),
            )


def fold(column):
    return column[0:C] + column[C : 2 * C]


def total(values):
    return jnp.sum(values, axis=1, keepdims=True)


def twice(column):
    return jnp.concatenate([column, column], axis=0)


def fourfold(column):
    return twice(twice(column))


def message(columns, msg_ref):
    count = msg_ref.shape[0]
    spare = jnp.zeros((128 - C * len(columns), 1), F32)
    column = jnp.concatenate([*columns, spare], axis=0)
    msg_ref[...] = jnp.transpose(jnp.broadcast_to(column, (128, count)))


def as_row(column):
    return jnp.transpose(jnp.broadcast_to(column, (128, 128)))[0:1]


def rows_message(columns, groups, msg_ref):
    spare = jnp.zeros((128 - C * len(columns), 1), F32)
    row = as_row(jnp.concatenate([*columns, spare], axis=0))
    height = msg_ref.shape[1]
    at = lax.broadcasted_iota(jnp.int32, (height, 128), 0)
    tile = jnp.where(at == 0, jnp.broadcast_to(row, (height, 128)), 0.0)
    msg_ref[...] = jnp.broadcast_to(tile[None], msg_ref.shape)
    for k, group in enumerate(groups):
        for dz in range(3):
            for dy in range(3):
                msg_ref[dz * C : (dz + 1) * C, 1 + 3 * k + dy, :] = group(dz, dy)


def center_of(acc):
    return fold(total(acc)) / (2 * ROWS * 128)


def stats_of(rows, place_ref, cells, st_ref):
    parts = jnp.transpose(rows)
    centers = parts[0:C]
    count = parts.shape[1]
    mean = total(centers) / count
    off = centers - mean
    spread = (total(parts[C : 2 * C]) + (2 * ROWS * 128) * total(off * off)) / cells
    at = lax.broadcasted_iota(jnp.int32, centers.shape, 1)
    low = total(jnp.where(at == place_ref[0], off, 0.0))
    high = total(jnp.where(at == place_ref[1], off, 0.0))
    own = total(jnp.where(at == place_ref[7], off, 0.0))
    found = (mean, lax.rsqrt(spread + EPSILON), low, high)
    st_ref[...] = jnp.concatenate([*found, own, jnp.zeros((C, 123), F32)], axis=1)
    return found


def kept_stats(st_ref):
    return tuple(st_ref[:, k : k + 1] for k in range(4))


def sums_of(row):
    parts = jnp.transpose(jnp.broadcast_to(row, (128, 128)))[:, 0:1]
    return parts[0:C], parts[C : 2 * C]


def feature_sums(v):
    lane = lanes(128)
    inner = v[5].astype(F32)
    for y in range(6, 3 + ROWS):
        inner = inner + v[y].astype(F32)
    ends = [v[y].astype(F32) for y in (3, 4, 3 + ROWS, 4 + ROWS)]
    windows = (inner + ends[0] + ends[1], inner + ends[1] + ends[2], inner + ends[2] + ends[3])
    columns = []
    for dz in range(3):
        for dy in range(3):
            values = windows[dy]
            if dz == 0:
                values = jnp.where(lane == 127, 0.0, values)
            if dz == 2:
                values = jnp.where(lane == 0, 0.0, values)
            column = total(values)
            columns.append(column + jnp.concatenate([column[C:], column[:C]], axis=0))
    return jnp.transpose(jnp.concatenate(columns + [jnp.zeros((128, 119), F32)], axis=1))[0:16]


def ones_of(x1):
    return lambda dz, dy: jnp.broadcast_to(x1[dz * 3 + dy : dz * 3 + dy + 1], (C, 128))


def act(z):
    e = jnp.exp2(jnp.abs(z) * (-8.0 / LN2))
    soft = jnp.maximum(z, 0.0) * 0.99 + jnp.log2(1.0 + e) * (0.99 * LN2 / 8.0)
    return 0.01 * z + soft


def act_slope(z):
    return 0.505 + 0.495 * jnp.tanh(4.0 * z)


def kept(place_ref, y, rows, margin):
    low = place_ref[2].astype(F32)
    high = place_ref[3].astype(F32)
    if y < margin:
        edge = place_ref[4].astype(F32)
    elif y >= rows - margin:
        edge = place_ref[5].astype(F32)
    else:
        return low, None, high
    return low * edge, edge, high * edge


def masked(values, factors):
    f_low, f_own, f_high = factors
    own = values[C : 3 * C]
    own = own if f_own is None else own * f_own
    return jnp.concatenate([values[0:C] * f_low, own, values[3 * C :] * f_high], axis=0).astype(
        BF16
    )


def weight_sums(g_ref, v_ref, first, acc_ref):
    step = 4
    for y in range(0, ROWS, step):
        right = jnp.concatenate(
            [v_ref[first + y + k : first + y + k + 3].reshape(384, 128) for k in range(step)], axis=1
        )
        left = g_ref[:, y * 128 : (y + step) * 128]
        product = lax.dot_general(
            left, right, (((1,), (1,)), ((), ())), preferred_element_type=F32
        )
        if y == 0:
            acc_ref[...] = product
        else:
            acc_ref[...] += product


def folded(acc_ref):
    def tile(dz, dy):
        both = acc_ref[dz * 64 : dz * 64 + 64, dy * 128 : dy * 128 + 128]
        return both[0:C] + pltpu.roll(both[C:], 96, 1)

    return tile


def put_shifted(g_ref, y, values, lane):
    at = slice(y * 128, (y + 1) * 128)
    g_ref[0:64, at] = from_above(values, lane).astype(BF16)
    g_ref[64:128, at] = values.astype(BF16)
    g_ref[128:192, at] = from_below(values, lane).astype(BF16)


def pack_kernel(need, send, own, cot, up_ref, down_ref):
    need(own, cot)
    up_ref[0:4] = own[ROWS - 4 : ROWS]
    up_ref[4:6] = cot[ROWS - 2 : ROWS]
    down_ref[0:4] = own[0:4]
    down_ref[4:6] = cot[0:2]


def corner_kernel(need, send, y_low, y_high, rows):
    need(y_low, y_high)
    rows[0:4] = y_low[0:4]
    rows[4:8] = y_high[0:4]


def weights_kernel(need, send, k1, k2, w1, w2):
    need(k1, k2)
    row = lax.broadcasted_iota(jnp.int32, (C, 128), 0)
    col = lax.broadcasted_iota(jnp.int32, (C, 128), 1)
    for k_ref, w_ref in ((k1, w1), (k2, w2)):
        lined = jnp.zeros((9 * C, 128), F32)
        for dx in range(3):
            spot = jnp.where(row + dx * C == col, 1.0, 0.0).astype(BF16)
            lined = lined + jnp.dot(
                k_ref[dx * 9 : dx * 9 + 9].reshape(9 * C, C), spot, preferred_element_type=F32
            )
        for dy in range(3):
            for dz in range(3):
                t = dy * 3 + dz
                put_tile(w_ref, dz, dy, lined[t * C : t * C + C])


def flipped_kernel(need, send, k1, k2, b1, b2):
    need(k1, k2)
    row = lax.broadcasted_iota(jnp.int32, (C, 128), 0)
    col = lax.broadcasted_iota(jnp.int32, (C, 128), 1)
    eye = jnp.where(row == col, 1.0, 0.0)[:, 0:C].astype(BF16)
    zero = jnp.zeros((C, C), BF16)
    for k_ref, b_ref in ((k1, b1), (k2, b2)):
        stack = []
        for t in range(9):
            stack += [k_ref[18 + t], k_ref[9 + t], k_ref[t], zero]
        turned = lax.dot_general(
            eye,
            jnp.concatenate(stack, axis=0),
            (((1,), (1,)), ((), ())),
            preferred_element_type=F32,
        )
        for dy in range(3):
            for dz in range(3):
                t = 8 - dy * 3 - dz
                put_tile(b_ref, dz, dy, turned[:, t * 128 : t * 128 + 128])


def put_tile(ref, dz, dy, tile):
    here = slice(dy * 128, dy * 128 + 128)
    ref[dz * 64 : dz * 64 + C, here] = tile.astype(BF16)
    ref[dz * 64 + C : dz * 64 + 64, here] = pltpu.roll(tile, C, 1).astype(BF16)


def first_kernel(
    need, send, own, x_low, x_high, y_low, y_high, c_low, c_high, w, v, h, msg, x1, center_out
):
    need(own, x_low, x_high, y_low, y_high, c_low, c_high, w)
    low = joined(4, x_low, c_low, c_low, 4)
    high = joined(4, x_high, c_high, c_high, 4)
    own = joined(4, own, y_low, y_high, 0)
    acc = [jnp.zeros((64, 128), F32), jnp.zeros((64, 128), F32)]
    for k, pair in enumerate(((low, own), (own, high))):

        def emit(y, values, k=k):
            h[y, 64 * k : 64 * k + 64] = values
            if k == 1:
                send(h, row=y)
            if 3 <= y < 3 + ROWS:
                acc[k] = acc[k] + values

        conv_rows(windows_of(*pair), w, ROWS + 6, emit)
    send(h)
    for y in range(ROWS + 8):
        v[y] = jnp.concatenate([low(y)[C:], own(y), high(y)[0:C]], axis=0)
        send(v, row=y)
    send(v)
    center = center_of(jnp.concatenate([acc[0][C:], acc[1][0:C]], axis=0))
    both = twice(center)
    spread = jnp.zeros((64, 128), F32)
    for y in range(3, 3 + ROWS):
        off = h[y, C : 3 * C] - both
        spread = spread + off * off
    center_out[...] = jnp.broadcast_to(center, (C, 128))
    x1[...] = feature_sums(v)
    send(center_out, x1)
    rows_message((center, fold(total(spread))), (ones_of(x1),), msg)


def second_kernel(
    cells, need, send, place, r1, gb, h1, cot, y_low, y_high, w, v, h, low, high, msg, st1
):
    need(gb)
    mean, inverse, _, _ = stats_of(r1[:, 0, :], place, cells, st1)
    send(st1)
    mean4, scale4 = fourfold(mean), fourfold(inverse * gb[:, 0:1])
    shift4 = fourfold(gb[:, 1:2])
    rows = ROWS + 6
    for y in range(rows):
        need(h1, row=y)
        v[y] = masked(act((h1[y] - mean4) * scale4 + shift4), kept(place, y, rows, 3))
        send(v, row=y)
    need(w, cot, y_low, y_high)
    acc = [jnp.zeros((64, 128), F32)]

    def emit(y, values):
        h[y] = values
        send(h, row=y)
        if 2 <= y < 2 + ROWS:
            acc[0] = acc[0] + values

    rows = ROWS + 4
    conv_rows(windows_of(v), w, rows, emit)
    send(h)
    center = center_of(acc[0])
    both = twice(center)
    spread = jnp.zeros((64, 128), F32)
    for y in range(rows):
        off = h[y] - both
        if 2 <= y < 2 + ROWS:
            spread = spread + off * off
        low[2 * y] = off[0:C].astype(BF16)
        high[2 * y] = off[C:].astype(BF16)
        values = cot_row(cot, y_low, y_high, y)
        low[2 * y + 1] = values[0:C]
        high[2 * y + 1] = values[C:]
        send(low, high, row=2 * y + 1)
    message((center, fold(total(spread))), msg)


def total_kernel(need, send, parts, whole):
    need(parts)
    whole[...] = jnp.sum(parts[...], axis=0)


def side_kernel(need, send, center, h1, v1, xh, g, acc):
    need(center)
    both = twice(center[...])
    lane = lanes(64)
    for y in range(ROWS):
        need(h1, row=y + 3)
        put_shifted(g, y, h1[y + 3] - both, lane)
    need(v1)
    weight_sums(g, v1, 3, acc)
    tile = folded(acc)
    for dz in range(3):
        for dy in range(3):
            xh[dz * 3 + dy] = tile(dz, dy)


def cot_row(cot, y_low, y_high, y):
    if y < 2:
        return y_low[4 + y]
    if y < 2 + ROWS:
        return cot[y - 2]
    return y_high[2 + y - ROWS]


def third_kernel(cells, need, send, place, r2, gb, cot, h2, st1, x1, xh, out, msg, st2):
    need(gb)
    mean, inverse, _, _ = stats_of(r2[...], place, cells, st2)
    mean2, inverse2 = twice(mean), twice(inverse)
    gain2, bias2 = twice(gb[:, 2:3]), twice(gb[:, 3:4])
    plain = jnp.zeros((64, 128), F32)
    both = jnp.zeros((64, 128), F32)
    for y in range(ROWS):
        need(h2, row=y + 2)
        need(cot, row=y)
        normed = (h2[y + 2] - mean2) * inverse2
        z = normed * gain2 + bias2
        out[y] = act(z).astype(BF16)
        send(out, row=y)
        slope = cot[y].astype(F32) * act_slope(z)
        plain = plain + slope
        both = both + slope * normed
    send(out)
    need(st1, x1, xh)
    inverse1, own1 = st1[:, 1:2], st1[:, 4:5]
    ones = ones_of(x1)

    def xn(dz, dy):
        return inverse1 * (xh[dz * 3 + dy] + own1 * ones(dz, dy))


    rows_message((fold(total(both)), fold(total(plain))), (xn,), msg)


def fourth_kernel(
    cells, need, send, place, r3, st2, gb, h2, x_low, x_high, cot, y_low, y_high, w, st1, h1, v2, v1, slope1, low, high, msg, t3, v, g, acc, acc1,
):
    need(st2, gb)
    mean, inverse, o_low, o_high = kept_stats(st2)
    t3[...] = jnp.sum(r3[...], axis=0)
    send(t3)
    nsum, plain = sums_of(t3[0:1])
    need(y_low, y_high)
    gain, bias = gb[:, 2:3], gb[:, 3:4]
    lead = gain * inverse
    p_mean, n_mean = plain / cells, nsum / cells

    def grad(normed, c, gain, bias, lead, p_mean, n_mean):
        slope = c.astype(F32) * act_slope(normed * gain + bias)
        return lead * (slope - p_mean - normed * n_mean)

    one = (gain, bias, lead, p_mean, n_mean)
    two = tuple(twice(a) for a in one)
    mean2, inverse2 = twice(mean), twice(inverse)
    lane = lanes(64)
    rows = ROWS + 4
    for y in range(rows):
        need(h2, row=y)
        need(x_low, x_high, row=2 * y + 1)
        need(cot, row=min(max(y - 2, 0), ROWS - 1))
        g_low = grad((x_low[2 * y].astype(F32) + o_low) * inverse, x_low[2 * y + 1], *one)
        g_own = grad((h2[y] - mean2) * inverse2, cot_row(cot, y_low, y_high, y), *two)
        g_high = grad((x_high[2 * y].astype(F32) + o_high) * inverse, x_high[2 * y + 1], *one)
        both = jnp.concatenate([g_low, g_own, g_high], axis=0)
        v[y] = masked(both, kept(place, y, rows, 2))
        if 2 <= y < 2 + ROWS:
            put_shifted(g, y - 2, g_own, lane)
    need(v2)
    weight_sums(g, v2, 2, acc)

    need(h1, st1, w)
    mean, inverse, _, _ = kept_stats(st1)
    mean2, inverse2 = twice(mean), twice(inverse)
    gain2, bias2 = twice(gb[:, 0:1]), twice(gb[:, 1:2])
    sums = [jnp.zeros((64, 128), F32), jnp.zeros((64, 128), F32)]

    def emit(y, values):
        normed = (h1[y + 2] - mean2) * inverse2
        slope = values * act_slope(normed * gain2 + bias2)
        slope1[y] = slope
        low[y] = slope[0:C].astype(BF16)
        high[y] = slope[C:].astype(BF16)
        send(slope1, low, high, row=y)
        if 1 <= y < 1 + ROWS:
            sums[0] = sums[0] + slope * normed
            sums[1] = sums[1] + slope
            put_shifted(g, y - 1, slope, lane)

    conv_rows(windows_of(v), w, ROWS + 2, emit)
    send(slope1, low, high)
    need(v1)
    weight_sums(g, v1, 3, acc1)
    rows_message(
        (fold(total(sums[0])), fold(total(sums[1]))), (folded(acc1), folded(acc)), msg
    )


def owner_kernel(cells, need, send, place, r4, st1, gb, t3, x1, msg, norms, t4):
    need(st1, gb, t3, x1)
    _, inverse, _, _ = kept_stats(st1)
    t4[...] = jnp.sum(r4[...], axis=0)
    nsum, plain = sums_of(t4[0:1])
    mine = lax.broadcasted_iota(jnp.int32, (C, 1), 0) == place[6]

    def picked(column):
        return jnp.sum(jnp.where(mine, column, 0.0), axis=0, keepdims=True)

    scale = cells**-0.5
    lead = picked(gb[:, 0:1] * inverse) * scale
    third, fourth = t3[...], t4[...]
    one = fourth[1:4] - picked(plain) * (x1[1:4] / cells) - picked(nsum) * (third[1:4] / cells)
    one = lead * one
    two = fourth[4:7] * scale
    tile = jnp.concatenate([one, two, jnp.zeros((2, 128), F32)], axis=0)
    pair = twice(tile).astype(BF16)
    for k in range(0, msg.shape[0], 16):
        msg[k : k + 16] = pair
    for k, row in enumerate((fourth[0:1], third[0:1])):
        norms[2 * k : 2 * k + 1] = row[:, 0:C] * scale
        norms[2 * k + 1 : 2 * k + 2] = row[:, C : 2 * C] * scale


def finish_kernel(need, send, parts, one, two, rows):
    rows[...] = parts[0 : 3 * C * 8].astype(F32)
    for dz in range(3):
        for dy in range(3):
            for k, out in enumerate((one, two)):
                tile = rows[pl.ds(dz * C * 8 + 3 * k + dy, C, stride=8), :]
                for dx in range(3):
                    out[dx * 9 + dy * 3 + dz] = tile[:, dx * C : (dx + 1) * C]


def fifth_kernel(cells, need, send, place, t4, st1, gb, h1, slope1, s_low, s_high, w, out, v):
    need(t4, st1, gb)
    mean, inverse, _, _ = kept_stats(st1)
    nsum, plain = sums_of(t4[0:1])
    mean4, inverse4 = fourfold(mean), fourfold(inverse)
    lead4 = fourfold(gb[:, 0:1] * inverse)
    p_mean4, n_mean4 = fourfold(plain / cells), fourfold(nsum / cells)
    rows = ROWS + 2
    for y in range(rows):
        need(slope1, s_low, s_high, row=y)
        need(h1, row=y + 2)
        slope = jnp.concatenate(
            [s_low[y].astype(F32), slope1[y], s_high[y].astype(F32)], axis=0
        )
        normed = (h1[y + 2] - mean4) * inverse4
        v[y] = masked(lead4 * (slope - p_mean4 - normed * n_mean4), kept(place, y, rows, 1))
    need(w)

    def emit(y, values):
        out[y] = values.astype(BF16)
        send(out, row=y)

    conv_rows(windows_of(v), w, ROWS, emit)


def pieces_of(shape):
    rows = shape[0]
    if len(shape) < 3 or rows < 32 or rows > 100:
        return [(0, rows)]
    cuts = [rows * c // 4 for c in range(5)]
    return list(zip(cuts, cuts[1:]))


def call(
    kernel, ins, outs, name, scratch=(), smem_first=True, after=(), near=0, cut=(), late=0, grant=56
):
    lead = 1 if smem_first else 0
    count_in, count_out = len(ins) - lead - near, len(outs)
    far_ins = ins[lead + near :]
    own = [any(a is b for b in cut) for a in far_ins]
    shapes = [(a.shape[0], 2 * C, 128) if c else a.shape for a, c in zip(far_ins, own)]

    def body(*refs):
        first, rest = refs[: lead + near], refs[lead + near :]
        parts = []
        for size in (count_in, len(after), count_out, count_in, count_out, 2):
            parts.append(rest[:size])
            rest = rest[size:]
        sources, _, targets, in_bufs, out_bufs, (in_sems, out_sems) = parts

        def source(k, a, b):
            return sources[k].at[a:b, C : 3 * C] if own[k] else sources[k].at[a:b]

        arriving = [
            [
                (a, b, pltpu.make_async_copy(source(k, a, b), buf.at[a:b], in_sems.at[k, c]))
                for c, (a, b) in enumerate(pieces_of(buf.shape))
            ]
            for k, buf in enumerate(in_bufs)
        ]
        leaving = [
            [
                (a, b, pltpu.make_async_copy(buf.at[a:b], targets[k].at[a:b], out_sems.at[k, c]))
                for c, (a, b) in enumerate(pieces_of(buf.shape))
            ]
            for k, buf in enumerate(out_bufs)
        ]
        early, later = arriving[: count_in - late], arriving[count_in - late :]
        for group in (early, later):
            for c in range(4):
                for pieces in group:
                    if c < len(pieces):
                        pieces[c][2].start()
        waiting, held = [list(pieces) for pieces in arriving], [list(pieces) for pieces in leaving]

        def need(*wanted, row=None):
            for ref in wanted:
                for k, buf in enumerate(in_bufs):
                    while buf is ref and waiting[k] and (row is None or waiting[k][0][0] <= row):
                        waiting[k].pop(0)[2].wait()

        def send(*ready, row=None):
            for ref in ready:
                for k, buf in enumerate(out_bufs):
                    while buf is ref and held[k] and (row is None or held[k][0][1] <= row + 1):
                        held[k].pop(0)[2].start()

        kernel(need, send, *first, *in_bufs, *out_bufs, *rest)
        send(*out_bufs)
        need(*in_bufs)
        for pieces in leaving:
            for piece in pieces:
                piece[2].wait()

    far = pl.BlockSpec(memory_space=pltpu.HBM)
    return pl.pallas_call(
        body,
        out_shape=outs,
        in_specs=[SM] * lead
        + [pl.BlockSpec(memory_space=pltpu.VMEM)] * near
        + [far] * (count_in + len(after)),
        out_specs=[far] * count_out,
        scratch_shapes=[
            *[pltpu.VMEM(shape, a.dtype) for shape, a in zip(shapes, far_ins)],
            *[pltpu.VMEM(a.shape, a.dtype) for a in outs],
            pltpu.SemaphoreType.DMA((max(count_in, 1), 4)),
            pltpu.SemaphoreType.DMA((count_out, 4)),
            *scratch,
        ],
        compiler_params=pltpu.CompilerParams(vmem_limit_bytes=grant * 1024 * 1024),
        cost_estimate=pl.CostEstimate(
            flops=2_000_000_000, bytes_accessed=6_000_000, transcendentals=0
        ),
        name=name,
    )(*ins, *after)


def up(values, axes):
    count = lax.axis_size(axes)
    return lax.ppermute(values, axes, [(i, i + 1) for i in range(count - 1)])


def down(values, axes):
    count = lax.axis_size(axes)
    return lax.ppermute(values, axes, [(i + 1, i) for i in range(count - 1)])


def share(msg):
    return lax.all_to_all(msg, ALL, 0, 0, tiled=True)


def local(features, kernel_one, gain_one, bias_one, kernel_two, gain_two, bias_two, cotangent):
    count_x, count_y = lax.axis_size(GX), lax.axis_size(GY)
    count = count_x * count_y
    cells = float(count * 2 * ROWS * 128)
    gx, gy = lax.axis_index(GX), lax.axis_index(GY)
    at = gx * count_y + gy
    place = jnp.stack(
        [at - count_y, at + count_y, gx > 0, gx < count_x - 1, gy > 0, gy < count_y - 1, at % C, at]
    ).astype(jnp.int32)
    gb = jnp.stack([gain_one, bias_one, gain_two, bias_two], axis=1)

    own = jnp.transpose(features, (2, 1, 0, 3)).reshape(ROWS, 64, 128)
    cot = jnp.transpose(cotangent, (2, 1, 0, 3)).reshape(ROWS, 64, 128)

    def rims(rows):
        return [sh((rows, C, 128), BF16)] * 2

    msg, four, wide = (sh((count, *tile), F32) for tile in ((128,), (4, 128), (8, 128)))
    stats = sh((C, 128), F32)
    corr = (pltpu.VMEM((192, ROWS * 128), BF16), pltpu.VMEM((192, 384), F32))

    x_low, x_high = up(own, GX), down(own, GX)
    y_up, y_down = call(
        pack_kernel, (own, cot), [sh((6, 64, 128), BF16)] * 2, "pack", smem_first=False
    )
    y_low, y_high = up(y_up, GY), down(y_down, GY)
    (corner,) = call(
        corner_kernel, (y_low, y_high), [sh((8, 64, 128), BF16)], "corner", smem_first=False
    )
    c_low, c_high = up(corner, GX), down(corner, GX)
    taps = [
        jnp.transpose(k, (2, 3, 4, 0, 1)).reshape(27, C, C) for k in (kernel_one, kernel_two)
    ]
    matrices = [sh((192, 384), BF16)] * 2
    w1, w2 = call(weights_kernel, taps, matrices, "weights", smem_first=False)

    v1, h1, m1, x1_own, center = call(
        first_kernel,
        (own, x_low, x_high, y_low, y_high, c_low, c_high, w1),
        [sh((40, 128, 128), BF16), sh((38, 128, 128), F32), four, sh((16, 128), F32), stats],
        "conv_one",
        smem_first=False,
    )
    r1 = share(m1)

    (xh,) = call(
        side_kernel,
        (center, h1, v1),
        [sh((9, C, 128), F32)],
        "hidden_features",
        scratch=corr,
        smem_first=False,
        cut=(h1,),
    )

    b1, b2 = call(flipped_kernel, taps, matrices, "flipped", smem_first=False, after=(center,))
    v2, h2, low, high, m2, st1 = call(
        lambda *refs: second_kernel(cells, *refs),
        (place, r1, gb, h1, cot, y_low, y_high, w2),
        [
            sh((38, 128, 128), BF16), sh((36, 64, 128), F32), *rims(72), msg, stats,
        ],
        "conv_two",
        near=1,
        after=(xh, b1),
    )
    h2_low, h2_high = up(high, GX), down(low, GX)
    r2 = share(m2)
    (x1,) = call(
        total_kernel, (r1,), [sh((4, 128), F32)], "total", smem_first=False, after=(st1,)
    )
    output, m3, st2 = call(
        lambda *refs: third_kernel(cells, *refs),
        (place, r2, gb, cot, h2, st1, x1_own, xh),
        [sh((ROWS, 64, 128), BF16), four, stats],
        "slope_two",
        near=1,
        after=(x1,),
    )
    r3 = share(m3)

    def back(rows):
        return jnp.transpose(rows.reshape(ROWS, 2, C, 128), (2, 1, 0, 3))

    output = back(output)

    slope1, low, high, m4, t3 = call(
        lambda *refs: fourth_kernel(cells, *refs),
        (
            place, r3, st2, gb, h2, h2_low, h2_high, cot, y_low, y_high,
            b2, st1, h1, v2, v1,
        ),
        [sh((34, 64, 128), F32), *rims(34), wide, sh((4, 128), F32)],
        "back_two",
        near=1,
        late=5,
        cut=(h1,),
        scratch=(pltpu.VMEM((36, 128, 128), BF16), *corr, corr[1]),
    )
    s_low, s_high = up(high, GX), down(low, GX)
    r4 = share(m4)

    m5, norm_grads, t4 = call(
        lambda *refs: owner_kernel(cells, *refs),
        (place, r4, st1, gb, t3, x1),
        [sh((count * 8, 128), BF16), sh((4, C), F32), sh((8, 128), F32)],
        "own_rows",
        near=1,
        grant=16,
        after=(s_low, s_high, output),
    )
    r5 = share(m5.reshape(count, 8, 128)).reshape(count * 8, 128)
    (grad,) = call(
        lambda *refs: fifth_kernel(cells, *refs),
        (place, t4, st1, gb, h1, slope1, s_low, s_high, b1),
        [sh((ROWS, 64, 128), BF16)],
        "back_one",
        scratch=(pltpu.VMEM((34, 128, 128), BF16),),
    )
    grads = call(
        finish_kernel,
        (r5,),
        [sh((27, C, C), F32)] * 2,
        "finish",
        scratch=(pltpu.VMEM((3 * C * 8, 128), F32),),
        smem_first=False,
        near=1,
        grant=16,
    )
    one, two = [jnp.transpose(k.reshape(3, 3, 3, C, C), (3, 4, 0, 1, 2)) for k in grads]

    return output, back(grad), one, two, norm_grads


def solution(mesh):
    nx, ny = mesh.devices.shape
    parts = (4, nx // 4, ny // 2, 2)
    split = Mesh(mesh.devices.reshape(parts), ALL)
    spec = P(None, GX, GY, None)
    in_specs = (spec, P(), P(), P(), P(), P(), P(), spec)
    out_specs = (spec, spec, P(), P(), P())
    return jax.shard_map(local, mesh=split, in_specs=in_specs, out_specs=out_specs, check_vma=False)
```

```python
import jax
import jax.numpy as jnp
from jax import lax
from jax.experimental import pallas as pl
from jax.experimental.pallas import tpu as pltpu
from jax.sharding import Mesh
from jax.sharding import PartitionSpec as P

GX = ("gx_0", "gx_1")
GY = ("gy_0", "gy_1")
ALL = GX + GY

EPSILON = 1e-05
C = 32
ROWS = 32
F32 = jnp.float32
BF16 = jnp.bfloat16
LN2 = 0.6931471805599453
SM = pl.BlockSpec(memory_space=pltpu.SMEM)


def sh(shape, kind):
    return jax.ShapeDtypeStruct(shape, kind)


def from_below(values, lane):
    return jnp.where(lane == 0, 0.0, pltpu.roll(values, 1, 1))


def from_above(values, lane):
    return jnp.where(lane == 127, 0.0, pltpu.roll(values, 127, 1))


def lanes(rows):
    return lax.broadcasted_iota(jnp.int32, (rows, 128), 1)


def windows_of(*refs):
    if len(refs) == 1:
        return lambda y: refs[0][y : y + 3].reshape(384, 128)
    return lambda y: jnp.concatenate([rows(y + k) for k in range(3) for rows in refs], axis=0)


def joined(k, middle, below, above):
    def row(y):
        if y < 4:
            return below[3 * y + k]
        if y < 4 + ROWS:
            return middle[y - 4]
        return above[3 * (y - 4 - ROWS) + k]

    return row


def conv_rows(window, w_ref, rows, emit):
    lane = lanes(64)
    weights = w_ref[...]
    for y in range(0, rows, 2):
        both = jnp.concatenate([window(y), window(y + 1)], axis=1)
        product = jnp.dot(weights, both, preferred_element_type=F32)
        for k in range(2):
            part = product[:, k * 128 : (k + 1) * 128]
            emit(
                y + k,
                part[64:128] + from_below(part[0:64], lane) + from_above(part[128:192], lane),
            )


def fold(column):
    return column[0:C] + column[C : 2 * C]


def total(values):
    return jnp.sum(values, axis=1, keepdims=True)


def twice(column):
    return jnp.concatenate([column, column], axis=0)


def fourfold(column):
    return twice(twice(column))


def message(columns, msg_ref):
    count = msg_ref.shape[0]
    spare = jnp.zeros((128 - C * len(columns), 1), F32)
    column = jnp.concatenate([*columns, spare], axis=0)
    msg_ref[...] = jnp.transpose(jnp.broadcast_to(column, (128, count)))


def as_row(column):
    return jnp.transpose(jnp.broadcast_to(column, (128, 128)))[0:1]


def rows_message(columns, groups, msg_ref):
    spare = jnp.zeros((128 - C * len(columns), 1), F32)
    row = as_row(jnp.concatenate([*columns, spare], axis=0))
    height = msg_ref.shape[1]
    at = lax.broadcasted_iota(jnp.int32, (height, 128), 0)
    tile = jnp.where(at == 0, jnp.broadcast_to(row, (height, 128)), 0.0)
    msg_ref[...] = jnp.broadcast_to(tile[None], msg_ref.shape)
    for k, group in enumerate(groups):
        for dz in range(3):
            for dy in range(3):
                msg_ref[dz * C : (dz + 1) * C, 1 + 3 * k + dy, :] = group(dz, dy)


def center_of(acc):
    return fold(total(acc)) / (2 * ROWS * 128)


def stats_of(rows, place_ref, cells, st_ref):
    parts = jnp.transpose(rows)
    centers = parts[0:C]
    count = parts.shape[1]
    mean = total(centers) / count
    off = centers - mean
    spread = (total(parts[C : 2 * C]) + (2 * ROWS * 128) * total(off * off)) / cells
    at = lax.broadcasted_iota(jnp.int32, centers.shape, 1)
    low = total(jnp.where(at == place_ref[0], off, 0.0))
    high = total(jnp.where(at == place_ref[1], off, 0.0))
    own = total(jnp.where(at == place_ref[7], off, 0.0))
    found = (mean, lax.rsqrt(spread + EPSILON), low, high)
    st_ref[...] = jnp.concatenate([*found, own, jnp.zeros((C, 123), F32)], axis=1)
    return found


def kept_stats(st_ref):
    return tuple(st_ref[:, k : k + 1] for k in range(4))


def sums_of(row):
    parts = jnp.transpose(jnp.broadcast_to(row, (128, 128)))[:, 0:1]
    return parts[0:C], parts[C : 2 * C]


def feature_sums(v):
    lane = lanes(128)
    inner = v[5].astype(F32)
    for y in range(6, 3 + ROWS):
        inner = inner + v[y].astype(F32)
    ends = [v[y].astype(F32) for y in (3, 4, 3 + ROWS, 4 + ROWS)]
    windows = (inner + ends[0] + ends[1], inner + ends[1] + ends[2], inner + ends[2] + ends[3])
    columns = []
    for dz in range(3):
        for dy in range(3):
            values = windows[dy]
            if dz == 0:
                values = jnp.where(lane == 127, 0.0, values)
            if dz == 2:
                values = jnp.where(lane == 0, 0.0, values)
            column = total(values)
            columns.append(column + jnp.concatenate([column[C:], column[:C]], axis=0))
    return jnp.transpose(jnp.concatenate(columns + [jnp.zeros((128, 119), F32)], axis=1))[0:16]


def ones_of(x1):
    return lambda dz, dy: jnp.broadcast_to(x1[dz * 3 + dy : dz * 3 + dy + 1], (C, 128))


def act(z):
    e = jnp.exp2(jnp.abs(z) * (-8.0 / LN2))
    soft = jnp.maximum(z, 0.0) * 0.99 + jnp.log2(1.0 + e) * (0.99 * LN2 / 8.0)
    return 0.01 * z + soft


def act_slope(z):
    return 0.505 + 0.495 * jnp.tanh(4.0 * z)


def kept(place_ref, y, rows, margin):
    low = place_ref[2].astype(F32)
    high = place_ref[3].astype(F32)
    if y < margin:
        edge = place_ref[4].astype(F32)
    elif y >= rows - margin:
        edge = place_ref[5].astype(F32)
    else:
        return low, None, high
    return low * edge, edge, high * edge


def masked(values, factors):
    f_low, f_own, f_high = factors
    own = values[C : 3 * C]
    own = own if f_own is None else own * f_own
    return jnp.concatenate([values[0:C] * f_low, own, values[3 * C :] * f_high], axis=0).astype(
        BF16
    )


def weight_sums(g_ref, v_ref, first, acc_ref):
    step = 4
    for y in range(0, ROWS, step):
        right = jnp.concatenate(
            [v_ref[first + y + k : first + y + k + 3].reshape(384, 128) for k in range(step)], axis=1
        )
        left = g_ref[:, y * 128 : (y + step) * 128]
        product = lax.dot_general(
            left, right, (((1,), (1,)), ((), ())), preferred_element_type=F32
        )
        if y == 0:
            acc_ref[...] = product
        else:
            acc_ref[...] += product


def folded(acc_ref):
    def tile(dz, dy):
        both = acc_ref[dz * 64 : dz * 64 + 64, dy * 128 : dy * 128 + 128]
        return both[0:C] + pltpu.roll(both[C:], 96, 1)

    return tile


def put_shifted(g_ref, y, values, lane):
    at = slice(y * 128, (y + 1) * 128)
    g_ref[0:64, at] = from_above(values, lane).astype(BF16)
    g_ref[64:128, at] = values.astype(BF16)
    g_ref[128:192, at] = from_below(values, lane).astype(BF16)


def pack_kernel(need, send, x_low, x_high, own, cot, up_ref, down_ref):
    need(x_low, x_high, own, cot)
    for y in range(4):
        for k, part in enumerate((x_low, own, x_high)):
            up_ref[3 * y + k] = part[ROWS - 4 + y]
            down_ref[3 * y + k] = part[y]
    up_ref[12:14] = cot[ROWS - 2 : ROWS]
    down_ref[12:14] = cot[0:2]


def weights_kernel(need, send, k1, k2, w1, w2):
    need(k1, k2)
    row = lax.broadcasted_iota(jnp.int32, (C, 128), 0)
    col = lax.broadcasted_iota(jnp.int32, (C, 128), 1)
    for k_ref, w_ref in ((k1, w1), (k2, w2)):
        lined = jnp.zeros((9 * C, 128), F32)
        for dx in range(3):
            spot = jnp.where(row + dx * C == col, 1.0, 0.0).astype(BF16)
            lined = lined + jnp.dot(
                k_ref[dx * 9 : dx * 9 + 9].reshape(9 * C, C), spot, preferred_element_type=F32
            )
        for dy in range(3):
            for dz in range(3):
                t = dy * 3 + dz
                put_tile(w_ref, dz, dy, lined[t * C : t * C + C])


def flipped_kernel(need, send, k1, k2, b1, b2):
    need(k1, k2)
    row = lax.broadcasted_iota(jnp.int32, (C, 128), 0)
    col = lax.broadcasted_iota(jnp.int32, (C, 128), 1)
    eye = jnp.where(row == col, 1.0, 0.0)[:, 0:C].astype(BF16)
    zero = jnp.zeros((C, C), BF16)
    for k_ref, b_ref in ((k1, b1), (k2, b2)):
        stack = []
        for t in range(9):
            stack += [k_ref[18 + t], k_ref[9 + t], k_ref[t], zero]
        turned = lax.dot_general(
            eye,
            jnp.concatenate(stack, axis=0),
            (((1,), (1,)), ((), ())),
            preferred_element_type=F32,
        )
        for dy in range(3):
            for dz in range(3):
                t = 8 - dy * 3 - dz
                put_tile(b_ref, dz, dy, turned[:, t * 128 : t * 128 + 128])


def put_tile(ref, dz, dy, tile):
    here = slice(dy * 128, dy * 128 + 128)
    ref[dz * 64 : dz * 64 + C, here] = tile.astype(BF16)
    ref[dz * 64 + C : dz * 64 + 64, here] = pltpu.roll(tile, C, 1).astype(BF16)


def first_kernel(
    need, send, y_low, y_high, w, own, x_low, x_high, v, h, msg, x1, center_out
):
    need(own, x_low, x_high, y_low, y_high, w)
    low = joined(0, x_low, y_low, y_high)
    own = joined(1, own, y_low, y_high)
    high = joined(2, x_high, y_low, y_high)
    acc = [jnp.zeros((64, 128), F32), jnp.zeros((64, 128), F32)]
    for k, pair in enumerate(((low, own), (own, high))):

        def emit(y, values, k=k):
            h[y, 64 * k : 64 * k + 64] = values
            if k == 1:
                send(h, row=y)
            if 3 <= y < 3 + ROWS:
                acc[k] = acc[k] + values

        conv_rows(windows_of(*pair), w, ROWS + 6, emit)
    send(h)
    for y in range(ROWS + 8):
        v[y] = jnp.concatenate([low(y)[C:], own(y), high(y)[0:C]], axis=0)
        send(v, row=y)
    send(v)
    center = center_of(jnp.concatenate([acc[0][C:], acc[1][0:C]], axis=0))
    both = twice(center)
    spread = jnp.zeros((64, 128), F32)
    for y in range(3, 3 + ROWS):
        off = h[y, C : 3 * C] - both
        spread = spread + off * off
    center_out[...] = jnp.broadcast_to(center, (C, 128))
    x1[...] = feature_sums(v)
    send(center_out, x1)
    rows_message((center, fold(total(spread))), (ones_of(x1),), msg)


def second_kernel(
    cells, need, send, place, r1, gb, h1, cot, y_low, y_high, w, v, h, low, high, msg, st1
):
    need(r1, gb)
    mean, inverse, _, _ = stats_of(r1[:, 0, :], place, cells, st1)
    send(st1)
    mean4, scale4 = fourfold(mean), fourfold(inverse * gb[:, 0:1])
    shift4 = fourfold(gb[:, 1:2])
    rows = ROWS + 6
    for y in range(rows):
        need(h1, row=y)
        v[y] = masked(act((h1[y] - mean4) * scale4 + shift4), kept(place, y, rows, 3))
        send(v, row=y)
    need(w, cot, y_low, y_high)
    acc = [jnp.zeros((64, 128), F32)]

    def emit(y, values):
        h[y] = values
        send(h, row=y)
        if 2 <= y < 2 + ROWS:
            acc[0] = acc[0] + values

    rows = ROWS + 4
    conv_rows(windows_of(v), w, rows, emit)
    send(h)
    center = center_of(acc[0])
    both = twice(center)
    spread = jnp.zeros((64, 128), F32)
    for y in range(rows):
        off = h[y] - both
        if 2 <= y < 2 + ROWS:
            spread = spread + off * off
        low[2 * y] = off[0:C].astype(BF16)
        high[2 * y] = off[C:].astype(BF16)
        values = cot_row(cot, y_low, y_high, y)
        low[2 * y + 1] = values[0:C]
        high[2 * y + 1] = values[C:]
        send(low, high, row=2 * y + 1)
    message((center, fold(total(spread))), msg)


def total_kernel(need, send, parts, whole):
    need(parts)
    whole[...] = jnp.sum(parts[...], axis=0)


def side_kernel(need, send, center, h1, v1, xh, g, acc):
    need(center)
    both = twice(center[...])
    lane = lanes(64)
    for y in range(ROWS):
        need(h1, row=y + 3)
        put_shifted(g, y, h1[y + 3] - both, lane)
    need(v1)
    weight_sums(g, v1, 3, acc)
    tile = folded(acc)
    for dz in range(3):
        for dy in range(3):
            xh[dz * 3 + dy] = tile(dz, dy)


def cot_row(cot, y_low, y_high, y):
    if y < 2:
        return y_low[12 + y]
    if y < 2 + ROWS:
        return cot[y - 2]
    return y_high[10 + y - ROWS]


def third_kernel(cells, need, send, place, r2, gb, cot, h2, st1, x1, xh, out, msg, st2):
    need(r2, gb)
    mean, inverse, _, _ = stats_of(r2[...], place, cells, st2)
    mean2, inverse2 = twice(mean), twice(inverse)
    gain2, bias2 = twice(gb[:, 2:3]), twice(gb[:, 3:4])
    plain = jnp.zeros((64, 128), F32)
    both = jnp.zeros((64, 128), F32)
    for y in range(ROWS):
        need(h2, row=y + 2)
        need(cot, row=y)
        normed = (h2[y + 2] - mean2) * inverse2
        z = normed * gain2 + bias2
        out[y] = act(z).astype(BF16)
        send(out, row=y)
        slope = cot[y].astype(F32) * act_slope(z)
        plain = plain + slope
        both = both + slope * normed
    send(out)
    need(st1, x1, xh)
    inverse1, own1 = st1[:, 1:2], st1[:, 4:5]
    ones = ones_of(x1)

    def xn(dz, dy):
        return inverse1 * (xh[dz * 3 + dy] + own1 * ones(dz, dy))


    rows_message((fold(total(both)), fold(total(plain))), (xn,), msg)


def fourth_kernel(
    cells, need, send, place, r3, st2, gb, h2, x_low, x_high, cot, y_low, y_high, w, st1, h1, v2, v1, slope1, low, high, msg, t3, v, g, acc, acc1,
):
    need(r3, st2, gb)
    mean, inverse, o_low, o_high = kept_stats(st2)
    t3[...] = jnp.sum(r3[...], axis=0)
    send(t3)
    nsum, plain = sums_of(t3[0:1])
    need(y_low, y_high)
    gain, bias = gb[:, 2:3], gb[:, 3:4]
    lead = gain * inverse
    p_mean, n_mean = plain / cells, nsum / cells

    def grad(normed, c, gain, bias, lead, p_mean, n_mean):
        slope = c.astype(F32) * act_slope(normed * gain + bias)
        return lead * (slope - p_mean - normed * n_mean)

    one = (gain, bias, lead, p_mean, n_mean)
    two = tuple(twice(a) for a in one)
    mean2, inverse2 = twice(mean), twice(inverse)
    lane = lanes(64)
    rows = ROWS + 4
    for y in range(rows):
        need(h2, row=y)
        need(x_low, x_high, row=2 * y + 1)
        need(cot, row=min(max(y - 2, 0), ROWS - 1))
        g_low = grad((x_low[2 * y].astype(F32) + o_low) * inverse, x_low[2 * y + 1], *one)
        g_own = grad((h2[y] - mean2) * inverse2, cot_row(cot, y_low, y_high, y), *two)
        g_high = grad((x_high[2 * y].astype(F32) + o_high) * inverse, x_high[2 * y + 1], *one)
        both = jnp.concatenate([g_low, g_own, g_high], axis=0)
        v[y] = masked(both, kept(place, y, rows, 2))
        if 2 <= y < 2 + ROWS:
            put_shifted(g, y - 2, g_own, lane)
    need(v2)
    weight_sums(g, v2, 2, acc)

    need(h1, st1, w)
    mean, inverse, _, _ = kept_stats(st1)
    mean2, inverse2 = twice(mean), twice(inverse)
    gain2, bias2 = twice(gb[:, 0:1]), twice(gb[:, 1:2])
    sums = [jnp.zeros((64, 128), F32), jnp.zeros((64, 128), F32)]

    def emit(y, values):
        normed = (h1[y + 2] - mean2) * inverse2
        slope = values * act_slope(normed * gain2 + bias2)
        slope1[y] = slope
        low[y] = slope[0:C].astype(BF16)
        high[y] = slope[C:].astype(BF16)
        send(slope1, low, high, row=y)
        if 1 <= y < 1 + ROWS:
            sums[0] = sums[0] + slope * normed
            sums[1] = sums[1] + slope
            put_shifted(g, y - 1, slope, lane)

    conv_rows(windows_of(v), w, ROWS + 2, emit)
    send(slope1, low, high)
    need(v1)
    weight_sums(g, v1, 3, acc1)
    rows_message(
        (fold(total(sums[0])), fold(total(sums[1]))), (folded(acc1), folded(acc)), msg
    )


def owner_kernel(cells, need, send, place, r4, st1, gb, t3, x1, msg, norms, t4):
    need(st1, gb, t3, x1)
    _, inverse, _, _ = kept_stats(st1)
    t4[...] = jnp.sum(r4[...], axis=0)
    nsum, plain = sums_of(t4[0:1])
    mine = lax.broadcasted_iota(jnp.int32, (C, 1), 0) == place[6]

    def picked(column):
        return jnp.sum(jnp.where(mine, column, 0.0), axis=0, keepdims=True)

    scale = cells**-0.5
    lead = picked(gb[:, 0:1] * inverse) * scale
    third, fourth = t3[...], t4[...]
    one = fourth[1:4] - picked(plain) * (x1[1:4] / cells) - picked(nsum) * (third[1:4] / cells)
    one = lead * one
    two = fourth[4:7] * scale
    tile = jnp.concatenate([one, two, jnp.zeros((2, 128), F32)], axis=0)
    pair = twice(tile).astype(BF16)
    for k in range(0, msg.shape[0], 16):
        msg[k : k + 16] = pair
    for k, row in enumerate((fourth[0:1], third[0:1])):
        norms[2 * k : 2 * k + 1] = row[:, 0:C] * scale
        norms[2 * k + 1 : 2 * k + 2] = row[:, C : 2 * C] * scale


def finish_kernel(need, send, parts, one, two, rows):
    rows[...] = parts[0 : 3 * C * 8].astype(F32)
    for dz in range(3):
        for dy in range(3):
            for k, out in enumerate((one, two)):
                tile = rows[pl.ds(dz * C * 8 + 3 * k + dy, C, stride=8), :]
                for dx in range(3):
                    out[dx * 9 + dy * 3 + dz] = tile[:, dx * C : (dx + 1) * C]


def fifth_kernel(cells, need, send, place, t4, st1, gb, h1, slope1, s_low, s_high, w, out, v):
    need(t4, st1, gb)
    mean, inverse, _, _ = kept_stats(st1)
    nsum, plain = sums_of(t4[0:1])
    mean4, inverse4 = fourfold(mean), fourfold(inverse)
    lead4 = fourfold(gb[:, 0:1] * inverse)
    p_mean4, n_mean4 = fourfold(plain / cells), fourfold(nsum / cells)
    rows = ROWS + 2
    for y in range(rows):
        need(slope1, s_low, s_high, row=y)
        need(h1, row=y + 2)
        slope = jnp.concatenate(
            [s_low[y].astype(F32), slope1[y], s_high[y].astype(F32)], axis=0
        )
        normed = (h1[y + 2] - mean4) * inverse4
        v[y] = masked(lead4 * (slope - p_mean4 - normed * n_mean4), kept(place, y, rows, 1))
    need(w)

    def emit(y, values):
        out[y] = values.astype(BF16)
        send(out, row=y)

    conv_rows(windows_of(v), w, ROWS, emit)


def pieces_of(shape):
    rows = shape[0]
    if len(shape) < 3 or rows < 32 or rows > 100:
        return [(0, rows)]
    cuts = [rows * c // 4 for c in range(5)]
    return list(zip(cuts, cuts[1:]))


def call(
    kernel, ins, outs, name, scratch=(), smem_first=True, after=(), near=0, cut=(), late=0, grant=56
):
    lead = 1 if smem_first else 0
    count_in, count_out = len(ins) - lead - near, len(outs)
    far_ins = ins[lead + near :]
    own = [any(a is b for b in cut) for a in far_ins]
    shapes = [(a.shape[0], 2 * C, 128) if c else a.shape for a, c in zip(far_ins, own)]

    def body(*refs):
        first, rest = refs[: lead + near], refs[lead + near :]
        parts = []
        for size in (count_in, len(after), count_out, count_in, count_out, 2):
            parts.append(rest[:size])
            rest = rest[size:]
        sources, _, targets, in_bufs, out_bufs, (in_sems, out_sems) = parts

        def source(k, a, b):
            return sources[k].at[a:b, C : 3 * C] if own[k] else sources[k].at[a:b]

        arriving = [
            [
                (a, b, pltpu.make_async_copy(source(k, a, b), buf.at[a:b], in_sems.at[k, c]))
                for c, (a, b) in enumerate(pieces_of(buf.shape))
            ]
            for k, buf in enumerate(in_bufs)
        ]
        leaving = [
            [
                (a, b, pltpu.make_async_copy(buf.at[a:b], targets[k].at[a:b], out_sems.at[k, c]))
                for c, (a, b) in enumerate(pieces_of(buf.shape))
            ]
            for k, buf in enumerate(out_bufs)
        ]
        early, later = arriving[: count_in - late], arriving[count_in - late :]
        for group in (early, later):
            for c in range(4):
                for pieces in group:
                    if c < len(pieces):
                        pieces[c][2].start()
        waiting, held = [list(pieces) for pieces in arriving], [list(pieces) for pieces in leaving]

        def need(*wanted, row=None):
            for ref in wanted:
                for k, buf in enumerate(in_bufs):
                    while buf is ref and waiting[k] and (row is None or waiting[k][0][0] <= row):
                        waiting[k].pop(0)[2].wait()

        def send(*ready, row=None):
            for ref in ready:
                for k, buf in enumerate(out_bufs):
                    while buf is ref and held[k] and (row is None or held[k][0][1] <= row + 1):
                        held[k].pop(0)[2].start()

        kernel(need, send, *first, *in_bufs, *out_bufs, *rest)
        send(*out_bufs)
        need(*in_bufs)
        for pieces in leaving:
            for piece in pieces:
                piece[2].wait()

    far = pl.BlockSpec(memory_space=pltpu.HBM)
    return pl.pallas_call(
        body,
        out_shape=outs,
        in_specs=[SM] * lead
        + [pl.BlockSpec(memory_space=pltpu.VMEM)] * near
        + [far] * (count_in + len(after)),
        out_specs=[far] * count_out,
        scratch_shapes=[
            *[pltpu.VMEM(shape, a.dtype) for shape, a in zip(shapes, far_ins)],
            *[pltpu.VMEM(a.shape, a.dtype) for a in outs],
            pltpu.SemaphoreType.DMA((max(count_in, 1), 4)),
            pltpu.SemaphoreType.DMA((count_out, 4)),
            *scratch,
        ],
        compiler_params=pltpu.CompilerParams(vmem_limit_bytes=grant * 1024 * 1024),
        cost_estimate=pl.CostEstimate(
            flops=2_000_000_000, bytes_accessed=6_000_000, transcendentals=0
        ),
        name=name,
    )(*ins, *after)


def up(values, axes):
    count = lax.axis_size(axes)
    return lax.ppermute(values, axes, [(i, i + 1) for i in range(count - 1)])


def down(values, axes):
    count = lax.axis_size(axes)
    return lax.ppermute(values, axes, [(i + 1, i) for i in range(count - 1)])


def share(msg):
    return lax.all_to_all(msg, ALL[::-1], 0, 0, tiled=True)


def rank_of(gx, gy):
    rank = gy % lax.axis_size(GY[1])
    for part, axis in (
        (gy // lax.axis_size(GY[1]), GY[0]),
        (gx % lax.axis_size(GX[1]), GX[1]),
        (gx // lax.axis_size(GX[1]), GX[0]),
    ):
        rank = rank * lax.axis_size(axis) + part
    return rank


def local(features, kernel_one, gain_one, bias_one, kernel_two, gain_two, bias_two, cotangent):
    count_x, count_y = lax.axis_size(GX), lax.axis_size(GY)
    count = count_x * count_y
    cells = float(count * 2 * ROWS * 128)
    gx, gy = lax.axis_index(GX), lax.axis_index(GY)
    at = rank_of(gx, gy)
    beside = [rank_of(jnp.clip(gx + k, 0, count_x - 1), gy) for k in (-1, 1)]
    edges = [gx > 0, gx < count_x - 1, gy > 0, gy < count_y - 1]
    place = jnp.stack([*beside, *edges, at % C, at]).astype(jnp.int32)
    gb = jnp.stack([gain_one, bias_one, gain_two, bias_two], axis=1)

    own = jnp.transpose(features, (2, 1, 0, 3)).reshape(ROWS, 64, 128)
    cot = jnp.transpose(cotangent, (2, 1, 0, 3)).reshape(ROWS, 64, 128)

    def rims(rows):
        return [sh((rows, C, 128), BF16)] * 2

    msg, four, wide = (sh((count, *tile), F32) for tile in ((128,), (4, 128), (8, 128)))
    stats = sh((C, 128), F32)
    corr = (pltpu.VMEM((192, ROWS * 128), BF16), pltpu.VMEM((192, 384), F32))

    x_low, x_high = up(own, GX), down(own, GX)
    taps = [
        jnp.transpose(k, (2, 3, 4, 0, 1)).reshape(27, C, C) for k in (kernel_one, kernel_two)
    ]
    matrices = [sh((192, 384), BF16)] * 2
    w1, w2 = call(weights_kernel, taps, matrices, "weights", smem_first=False)
    b1, b2 = call(flipped_kernel, taps, matrices, "flipped", smem_first=False)
    y_up, y_down = call(
        pack_kernel,
        (x_low, x_high, own, cot),
        [sh((14, 64, 128), BF16)] * 2,
        "pack",
        smem_first=False,
        after=(w1, b1),
    )
    y_low, y_high = up(y_up, GY), down(y_down, GY)

    v1, h1, m1, x1_own, center = call(
        first_kernel,
        (y_low, y_high, w1, own, x_low, x_high),
        [sh((40, 128, 128), BF16), sh((38, 128, 128), F32), four, sh((16, 128), F32), stats],
        "conv_one",
        smem_first=False,
    )
    r1 = share(m1)

    (xh,) = call(
        side_kernel,
        (center, h1, v1),
        [sh((9, C, 128), F32)],
        "hidden_features",
        scratch=corr,
        smem_first=False,
        cut=(h1,),
    )

    v2, h2, low, high, m2, st1 = call(
        lambda *refs: second_kernel(cells, *refs),
        (place, r1, gb, h1, cot, y_low, y_high, w2),
        [
            sh((38, 128, 128), BF16), sh((36, 64, 128), F32), *rims(72), msg, stats,
        ],
        "conv_two",
        after=(xh,),
    )
    h2_low, h2_high = up(high, GX), down(low, GX)
    r2 = share(m2)
    (x1,) = call(
        total_kernel, (r1,), [sh((4, 128), F32)], "total", smem_first=False, after=(st1,)
    )
    output, m3, st2 = call(
        lambda *refs: third_kernel(cells, *refs),
        (place, r2, gb, cot, h2, st1, x1_own, xh),
        [sh((ROWS, 64, 128), BF16), four, stats],
        "slope_two",
        after=(x1,),
    )
    r3 = share(m3)

    def back(rows):
        return jnp.transpose(rows.reshape(ROWS, 2, C, 128), (2, 1, 0, 3))

    output = back(output)

    slope1, low, high, m4, t3 = call(
        lambda *refs: fourth_kernel(cells, *refs),
        (
            place, r3, st2, gb, h2, h2_low, h2_high, cot, y_low, y_high,
            b2, st1, h1, v2, v1,
        ),
        [sh((34, 64, 128), F32), *rims(34), wide, sh((4, 128), F32)],
        "back_two",
        late=5,
        cut=(h1,),
        scratch=(pltpu.VMEM((36, 128, 128), BF16), *corr, corr[1]),
    )
    s_low, s_high = up(high, GX), down(low, GX)
    r4 = share(m4)

    m5, norm_grads, t4 = call(
        lambda *refs: owner_kernel(cells, *refs),
        (place, r4, st1, gb, t3, x1),
        [sh((count * 8, 128), BF16), sh((4, C), F32), sh((8, 128), F32)],
        "own_rows",
        near=1,
        grant=16,
        after=(s_low, s_high, output),
    )
    r5 = share(m5.reshape(count, 8, 128)).reshape(count * 8, 128)
    (grad,) = call(
        lambda *refs: fifth_kernel(cells, *refs),
        (place, t4, st1, gb, h1, slope1, s_low, s_high, b1),
        [sh((ROWS, 64, 128), BF16)],
        "back_one",
        scratch=(pltpu.VMEM((34, 128, 128), BF16),),
    )
    grads = call(
        finish_kernel,
        (r5,),
        [sh((27, C, C), F32)] * 2,
        "finish",
        scratch=(pltpu.VMEM((3 * C * 8, 128), F32),),
        smem_first=False,
        near=1,
        grant=16,
    )
    one, two = [jnp.transpose(k.reshape(3, 3, 3, C, C), (3, 4, 0, 1, 2)) for k in grads]

    return output, back(grad), one, two, norm_grads


def solution(mesh):
    nx, ny = mesh.devices.shape
    parts = (4, nx // 4, ny // 2, 2)
    split = Mesh(mesh.devices.reshape(parts), ALL)
    spec = P(None, GX, GY, None)
    in_specs = (spec, P(), P(), P(), P(), P(), P(), spec)
    out_specs = (spec, spec, P(), P(), P())
    return jax.shard_map(local, mesh=split, in_specs=in_specs, out_specs=out_specs, check_vma=False)
```

```python
import jax
import jax.numpy as jnp
from jax import lax
from jax.experimental import pallas as pl
from jax.experimental.pallas import tpu as pltpu
from jax.sharding import Mesh
from jax.sharding import PartitionSpec as P

GX = ("gx_0", "gx_1")
GY = ("gy_0", "gy_1")
ALL = GX + GY

EPSILON = 1e-05
C = 32
ROWS = 32
F32 = jnp.float32
BF16 = jnp.bfloat16
LN2 = 0.6931471805599453
SM = pl.BlockSpec(memory_space=pltpu.SMEM)


def sh(shape, kind):
    return jax.ShapeDtypeStruct(shape, kind)


def from_below(values, lane):
    return jnp.where(lane == 0, 0.0, pltpu.roll(values, 1, 1))


def from_above(values, lane):
    return jnp.where(lane == 127, 0.0, pltpu.roll(values, 127, 1))


def lanes(rows):
    return lax.broadcasted_iota(jnp.int32, (rows, 128), 1)


def windows_of(*refs):
    if len(refs) == 1:
        return lambda y: refs[0][y : y + 3].reshape(384, 128)
    return lambda y: jnp.concatenate([rows(y + k) for k in range(3) for rows in refs], axis=0)


def joined(k, middle, below, above):
    def row(y):
        if y < 4:
            return below[3 * y + k]
        if y < 4 + ROWS:
            return middle[y - 4]
        return above[3 * (y - 4 - ROWS) + k]

    return row


def conv_rows(window, w_ref, rows, emit):
    lane = lanes(64)
    weights = w_ref[...]
    for y in range(0, rows, 2):
        both = jnp.concatenate([window(y), window(y + 1)], axis=1)
        product = jnp.dot(weights, both, preferred_element_type=F32)
        for k in range(2):
            part = product[:, k * 128 : (k + 1) * 128]
            emit(
                y + k,
                part[64:128] + from_below(part[0:64], lane) + from_above(part[128:192], lane),
            )


def fold(column):
    return column[0:C] + column[C : 2 * C]


def total(values):
    return jnp.sum(values, axis=1, keepdims=True)


def twice(column):
    return jnp.concatenate([column, column], axis=0)


def fourfold(column):
    return twice(twice(column))


def message(columns, msg_ref):
    count = msg_ref.shape[0]
    spare = jnp.zeros((128 - C * len(columns), 1), F32)
    column = jnp.concatenate([*columns, spare], axis=0)
    msg_ref[...] = jnp.transpose(jnp.broadcast_to(column, (128, count)))


def as_row(column):
    return jnp.transpose(jnp.broadcast_to(column, (128, 128)))[0:1]


def rows_message(columns, groups, msg_ref):
    spare = jnp.zeros((128 - C * len(columns), 1), F32)
    row = as_row(jnp.concatenate([*columns, spare], axis=0))
    height = msg_ref.shape[1]
    at = lax.broadcasted_iota(jnp.int32, (height, 128), 0)
    tile = jnp.where(at == 0, jnp.broadcast_to(row, (height, 128)), 0.0)
    msg_ref[...] = jnp.broadcast_to(tile[None], msg_ref.shape)
    for k, group in enumerate(groups):
        for dz in range(3):
            for dy in range(3):
                msg_ref[dz * C : (dz + 1) * C, 1 + 3 * k + dy, :] = group(dz, dy)


def center_of(acc):
    return fold(total(acc)) / (2 * ROWS * 128)


def stats_of(rows, place_ref, cells, st_ref):
    parts = jnp.transpose(rows)
    centers = parts[0:C]
    count = parts.shape[1]
    mean = total(centers) / count
    off = centers - mean
    spread = (total(parts[C : 2 * C]) + (2 * ROWS * 128) * total(off * off)) / cells
    at = lax.broadcasted_iota(jnp.int32, centers.shape, 1)
    low = total(jnp.where(at == place_ref[0], off, 0.0))
    high = total(jnp.where(at == place_ref[1], off, 0.0))
    own = total(jnp.where(at == place_ref[7], off, 0.0))
    found = (mean, lax.rsqrt(spread + EPSILON), low, high)
    st_ref[...] = jnp.concatenate([*found, own, jnp.zeros((C, 123), F32)], axis=1)
    return found


def kept_stats(st_ref):
    return tuple(st_ref[:, k : k + 1] for k in range(4))


def sums_of(row):
    parts = jnp.transpose(jnp.broadcast_to(row, (128, 128)))[:, 0:1]
    return parts[0:C], parts[C : 2 * C]


def feature_sums(v):
    lane = lanes(128)
    inner = v[5].astype(F32)
    for y in range(6, 3 + ROWS):
        inner = inner + v[y].astype(F32)
    ends = [v[y].astype(F32) for y in (3, 4, 3 + ROWS, 4 + ROWS)]
    windows = (inner + ends[0] + ends[1], inner + ends[1] + ends[2], inner + ends[2] + ends[3])
    columns = []
    for dz in range(3):
        for dy in range(3):
            values = windows[dy]
            if dz == 0:
                values = jnp.where(lane == 127, 0.0, values)
            if dz == 2:
                values = jnp.where(lane == 0, 0.0, values)
            column = total(values)
            columns.append(column + jnp.concatenate([column[C:], column[:C]], axis=0))
    return jnp.transpose(jnp.concatenate(columns + [jnp.zeros((128, 119), F32)], axis=1))[0:16]


def ones_of(x1):
    return lambda dz, dy: jnp.broadcast_to(x1[dz * 3 + dy : dz * 3 + dy + 1], (C, 128))


def act(z):
    e = jnp.exp2(jnp.abs(z) * (-8.0 / LN2))
    soft = jnp.maximum(z, 0.0) * 0.99 + jnp.log2(1.0 + e) * (0.99 * LN2 / 8.0)
    return 0.01 * z + soft


def act_slope(z):
    return 0.505 + 0.495 * jnp.tanh(4.0 * z)


def kept(place_ref, y, rows, margin):
    low = place_ref[2].astype(F32)
    high = place_ref[3].astype(F32)
    if y < margin:
        edge = place_ref[4].astype(F32)
    elif y >= rows - margin:
        edge = place_ref[5].astype(F32)
    else:
        return low, None, high
    return low * edge, edge, high * edge


def masked(values, factors):
    f_low, f_own, f_high = factors
    own = values[C : 3 * C]
    own = own if f_own is None else own * f_own
    return jnp.concatenate([values[0:C] * f_low, own, values[3 * C :] * f_high], axis=0).astype(
        BF16
    )


def weight_sums(g_ref, v_ref, first, acc_ref):
    step = 4
    for y in range(0, ROWS, step):
        window = jnp.concatenate(
            [v_ref[first + y + k : first + y + k + 3].reshape(384, 128) for k in range(step)], axis=1
        )
        product = lax.dot_general(
            window,
            g_ref[:, y * 128 : (y + step) * 128],
            (((1,), (1,)), ((), ())),
            preferred_element_type=F32,
        )
        if y == 0:
            acc_ref[...] = product
        else:
            acc_ref[...] += product


def folded(acc_ref):
    turned = [jnp.transpose(acc_ref[dy * 128 : dy * 128 + 128]) for dy in range(3)]

    def tile(dz, dy):
        both = turned[dy][dz * 64 : dz * 64 + 64]
        return both[0:C] + pltpu.roll(both[C:], 96, 1)

    return tile


def put_shifted(g_ref, y, values, lane):
    at = slice(y * 128, (y + 1) * 128)
    g_ref[0:64, at] = from_above(values, lane).astype(BF16)
    g_ref[64:128, at] = values.astype(BF16)
    g_ref[128:192, at] = from_below(values, lane).astype(BF16)


def pack_kernel(need, send, x_low, x_high, own, cot, up_ref, down_ref):
    need(own, cot)
    for y in range(4):
        for k, part in enumerate((x_low, own, x_high)):
            up_ref[3 * y + k] = part[ROWS - 4 + y]
            down_ref[3 * y + k] = part[y]
    up_ref[12:14] = cot[ROWS - 2 : ROWS]
    down_ref[12:14] = cot[0:2]


def weights_kernel(need, send, k1, k2, w1, w2):
    need(k1, k2)
    row = lax.broadcasted_iota(jnp.int32, (C, 128), 0)
    col = lax.broadcasted_iota(jnp.int32, (C, 128), 1)
    for k_ref, w_ref in ((k1, w1), (k2, w2)):
        lined = jnp.zeros((9 * C, 128), F32)
        for dx in range(3):
            spot = jnp.where(row + dx * C == col, 1.0, 0.0).astype(BF16)
            lined = lined + jnp.dot(
                k_ref[dx * 9 : dx * 9 + 9].reshape(9 * C, C), spot, preferred_element_type=F32
            )
        for dy in range(3):
            for dz in range(3):
                t = dy * 3 + dz
                put_tile(w_ref, dz, dy, lined[t * C : t * C + C])


def flipped_kernel(need, send, k1, k2, b1, b2):
    need(k1, k2)
    row = lax.broadcasted_iota(jnp.int32, (C, 128), 0)
    col = lax.broadcasted_iota(jnp.int32, (C, 128), 1)
    eye = jnp.where(row == col, 1.0, 0.0)[:, 0:C].astype(BF16)
    zero = jnp.zeros((C, C), BF16)
    for k_ref, b_ref in ((k1, b1), (k2, b2)):
        stack = []
        for t in range(9):
            stack += [k_ref[18 + t], k_ref[9 + t], k_ref[t], zero]
        turned = lax.dot_general(
            eye,
            jnp.concatenate(stack, axis=0),
            (((1,), (1,)), ((), ())),
            preferred_element_type=F32,
        )
        for dy in range(3):
            for dz in range(3):
                t = 8 - dy * 3 - dz
                put_tile(b_ref, dz, dy, turned[:, t * 128 : t * 128 + 128])


def put_tile(ref, dz, dy, tile):
    here = slice(dy * 128, dy * 128 + 128)
    ref[dz * 64 : dz * 64 + C, here] = tile.astype(BF16)
    ref[dz * 64 + C : dz * 64 + 64, here] = pltpu.roll(tile, C, 1).astype(BF16)


def first_kernel(
    need, send, y_low, y_high, w, own, x_low, x_high, v, h, msg, x1, center_out
):
    need(own, x_low, x_high, y_low, y_high, w)
    low = joined(0, x_low, y_low, y_high)
    own = joined(1, own, y_low, y_high)
    high = joined(2, x_high, y_low, y_high)
    acc = [jnp.zeros((64, 128), F32), jnp.zeros((64, 128), F32)]
    for k, pair in enumerate(((low, own), (own, high))):

        def emit(y, values, k=k):
            h[y, 64 * k : 64 * k + 64] = values
            if k == 1:
                send(h, row=y)
            if 3 <= y < 3 + ROWS:
                acc[k] = acc[k] + values

        conv_rows(windows_of(*pair), w, ROWS + 6, emit)
    send(h)
    for y in range(ROWS + 8):
        v[y] = jnp.concatenate([low(y)[C:], own(y), high(y)[0:C]], axis=0)
        send(v, row=y)
    send(v)
    center = center_of(jnp.concatenate([acc[0][C:], acc[1][0:C]], axis=0))
    both = twice(center)
    spread = jnp.zeros((64, 128), F32)
    for y in range(3, 3 + ROWS):
        off = h[y, C : 3 * C] - both
        spread = spread + off * off
    center_out[...] = jnp.broadcast_to(center, (C, 128))
    x1[...] = feature_sums(v)
    send(center_out, x1)
    rows_message((center, fold(total(spread))), (ones_of(x1),), msg)


def second_kernel(
    cells, need, send, place, r1, gb, h1, cot, y_low, y_high, w, v, h, low, high, msg, st1
):
    need(r1, gb)
    mean, inverse, _, _ = stats_of(r1[:, 0, :], place, cells, st1)
    send(st1)
    mean4, scale4 = fourfold(mean), fourfold(inverse * gb[:, 0:1])
    shift4 = fourfold(gb[:, 1:2])
    rows = ROWS + 6
    for y in range(rows):
        need(h1, row=y)
        v[y] = masked(act((h1[y] - mean4) * scale4 + shift4), kept(place, y, rows, 3))
        send(v, row=y)
    need(w, cot, y_low, y_high)
    acc = [jnp.zeros((64, 128), F32)]

    def emit(y, values):
        h[y] = values
        send(h, row=y)
        if 2 <= y < 2 + ROWS:
            acc[0] = acc[0] + values

    rows = ROWS + 4
    conv_rows(windows_of(v), w, rows, emit)
    send(h)
    center = center_of(acc[0])
    both = twice(center)
    spread = jnp.zeros((64, 128), F32)
    for y in range(rows):
        off = h[y] - both
        if 2 <= y < 2 + ROWS:
            spread = spread + off * off
        low[2 * y] = off[0:C].astype(BF16)
        high[2 * y] = off[C:].astype(BF16)
        values = cot_row(cot, y_low, y_high, y)
        low[2 * y + 1] = values[0:C]
        high[2 * y + 1] = values[C:]
        send(low, high, row=2 * y + 1)
    message((center, fold(total(spread))), msg)


def total_kernel(need, send, parts, whole):
    need(parts)
    whole[...] = jnp.sum(parts[...], axis=0)


def side_kernel(need, send, center, h1, v1, xh, g, acc):
    need(center)
    both = twice(center[...])
    lane = lanes(64)
    for y in range(ROWS):
        need(h1, row=y + 3)
        put_shifted(g, y, h1[y + 3] - both, lane)
    need(v1)
    weight_sums(g, v1, 3, acc)
    tile = folded(acc)
    for dz in range(3):
        for dy in range(3):
            xh[dz * 3 + dy] = tile(dz, dy)


def cot_row(cot, y_low, y_high, y):
    if y < 2:
        return y_low[12 + y]
    if y < 2 + ROWS:
        return cot[y - 2]
    return y_high[10 + y - ROWS]


def third_kernel(cells, need, send, place, r2, gb, cot, h2, st1, x1, xh, msg, st2):
    need(r2, gb)
    mean, inverse, _, _ = stats_of(r2[...], place, cells, st2)
    mean2, inverse2 = twice(mean), twice(inverse)
    gain2, bias2 = twice(gb[:, 2:3]), twice(gb[:, 3:4])
    plain = jnp.zeros((64, 128), F32)
    both = jnp.zeros((64, 128), F32)
    for y in range(ROWS):
        need(h2, row=y + 2)
        need(cot, row=y)
        normed = (h2[y + 2] - mean2) * inverse2
        z = normed * gain2 + bias2
        slope = cot[y].astype(F32) * act_slope(z)
        plain = plain + slope
        both = both + slope * normed
    need(st1, x1, xh)
    inverse1, own1 = st1[:, 1:2], st1[:, 4:5]
    ones = ones_of(x1)

    def xn(dz, dy):
        return inverse1 * (xh[dz * 3 + dy] + own1 * ones(dz, dy))


    rows_message((fold(total(both)), fold(total(plain))), (xn,), msg)


def output_kernel(need, send, st2, gb, h2, out):
    need(st2, gb)
    mean, inverse, _, _ = kept_stats(st2)
    mean2, scale2 = twice(mean), twice(inverse * gb[:, 2:3])
    shift2 = twice(gb[:, 3:4])
    for y in range(ROWS):
        need(h2, row=y + 2)
        out[y] = act((h2[y + 2] - mean2) * scale2 + shift2).astype(BF16)
        send(out, row=y)


def fourth_kernel(
    cells, need, send, place, r3, st2, gb, h2, x_low, x_high, cot, y_low, y_high, w, st1, h1, v2, v1, slope1, low, high, msg, t3, v, g, acc, acc1,
):
    need(r3, st2, gb)
    mean, inverse, o_low, o_high = kept_stats(st2)
    t3[...] = jnp.sum(r3[...], axis=0)
    send(t3)
    nsum, plain = sums_of(t3[0:1])
    need(y_low, y_high)
    gain, bias = gb[:, 2:3], gb[:, 3:4]
    lead = gain * inverse
    p_mean, n_mean = plain / cells, nsum / cells

    def grad(normed, c, gain, bias, lead, p_mean, n_mean):
        slope = c.astype(F32) * act_slope(normed * gain + bias)
        return lead * (slope - p_mean - normed * n_mean)

    one = (gain, bias, lead, p_mean, n_mean)
    two = tuple(twice(a) for a in one)
    mean2, inverse2 = twice(mean), twice(inverse)
    lane = lanes(64)
    rows = ROWS + 4
    for y in range(rows):
        need(h2, row=y)
        need(x_low, x_high, row=2 * y + 1)
        need(cot, row=min(max(y - 2, 0), ROWS - 1))
        g_low = grad((x_low[2 * y].astype(F32) + o_low) * inverse, x_low[2 * y + 1], *one)
        g_own = grad((h2[y] - mean2) * inverse2, cot_row(cot, y_low, y_high, y), *two)
        g_high = grad((x_high[2 * y].astype(F32) + o_high) * inverse, x_high[2 * y + 1], *one)
        both = jnp.concatenate([g_low, g_own, g_high], axis=0)
        v[y] = masked(both, kept(place, y, rows, 2))
        if 2 <= y < 2 + ROWS:
            put_shifted(g, y - 2, g_own, lane)
    need(v2)
    weight_sums(g, v2, 2, acc)

    need(h1, st1, w)
    mean, inverse, _, _ = kept_stats(st1)
    mean2, inverse2 = twice(mean), twice(inverse)
    gain2, bias2 = twice(gb[:, 0:1]), twice(gb[:, 1:2])
    sums = [jnp.zeros((64, 128), F32), jnp.zeros((64, 128), F32)]

    def emit(y, values):
        normed = (h1[y + 2] - mean2) * inverse2
        slope = values * act_slope(normed * gain2 + bias2)
        slope1[y] = slope
        low[y] = slope[0:C].astype(BF16)
        high[y] = slope[C:].astype(BF16)
        send(slope1, low, high, row=y)
        if 1 <= y < 1 + ROWS:
            sums[0] = sums[0] + slope * normed
            sums[1] = sums[1] + slope
            put_shifted(g, y - 1, slope, lane)

    conv_rows(windows_of(v), w, ROWS + 2, emit)
    send(slope1, low, high)
    need(v1)
    weight_sums(g, v1, 3, acc1)
    rows_message(
        (fold(total(sums[0])), fold(total(sums[1]))), (folded(acc1), folded(acc)), msg
    )


def owner_kernel(cells, need, send, place, r4, st1, gb, t3, x1, msg, norms, t4):
    need(st1, gb, t3, x1)
    _, inverse, _, _ = kept_stats(st1)
    t4[...] = jnp.sum(r4[...], axis=0)
    nsum, plain = sums_of(t4[0:1])
    mine = lax.broadcasted_iota(jnp.int32, (C, 1), 0) == place[6]

    def picked(column):
        return jnp.sum(jnp.where(mine, column, 0.0), axis=0, keepdims=True)

    scale = cells**-0.5
    lead = picked(gb[:, 0:1] * inverse) * scale
    third, fourth = t3[...], t4[...]
    one = fourth[1:4] - picked(plain) * (x1[1:4] / cells) - picked(nsum) * (third[1:4] / cells)
    one = lead * one
    two = fourth[4:7] * scale
    tile = jnp.concatenate([one, two, jnp.zeros((2, 128), F32)], axis=0)
    pair = twice(tile).astype(BF16)
    for k in range(0, msg.shape[0], 16):
        msg[k : k + 16] = pair
    for k, row in enumerate((fourth[0:1], third[0:1])):
        norms[2 * k : 2 * k + 1] = row[:, 0:C] * scale
        norms[2 * k + 1 : 2 * k + 2] = row[:, C : 2 * C] * scale


def finish_kernel(need, send, parts, one, two, rows):
    rows[...] = parts[0 : 3 * C * 8].astype(F32)
    for dz in range(3):
        for dy in range(3):
            for k, out in enumerate((one, two)):
                tile = rows[pl.ds(dz * C * 8 + 3 * k + dy, C, stride=8), :]
                for dx in range(3):
                    out[dx * 9 + dy * 3 + dz] = tile[:, dx * C : (dx + 1) * C]


def fifth_kernel(cells, need, send, place, t4, st1, gb, h1, slope1, s_low, s_high, w, out, v):
    need(t4, st1, gb)
    mean, inverse, _, _ = kept_stats(st1)
    nsum, plain = sums_of(t4[0:1])
    mean4, inverse4 = fourfold(mean), fourfold(inverse)
    lead4 = fourfold(gb[:, 0:1] * inverse)
    p_mean4, n_mean4 = fourfold(plain / cells), fourfold(nsum / cells)
    rows = ROWS + 2
    for y in range(rows):
        need(slope1, s_low, s_high, row=y)
        need(h1, row=y + 2)
        slope = jnp.concatenate(
            [s_low[y].astype(F32), slope1[y], s_high[y].astype(F32)], axis=0
        )
        normed = (h1[y + 2] - mean4) * inverse4
        v[y] = masked(lead4 * (slope - p_mean4 - normed * n_mean4), kept(place, y, rows, 1))
    need(w)

    def emit(y, values):
        out[y] = values.astype(BF16)
        send(out, row=y)

    conv_rows(windows_of(v), w, ROWS, emit)


def pieces_of(shape):
    rows = shape[0]
    if len(shape) < 3 or rows < 32 or rows > 100:
        return [(0, rows)]
    cuts = [rows * c // 4 for c in range(5)]
    return list(zip(cuts, cuts[1:]))


def call(
    kernel, ins, outs, name, scratch=(), smem_first=True, after=(), near=0, cut=(), late=0, grant=56
):
    lead = 1 if smem_first else 0
    count_in, count_out = len(ins) - lead - near, len(outs)
    far_ins = ins[lead + near :]
    own = [any(a is b for b in cut) for a in far_ins]
    shapes = [(a.shape[0], 2 * C, 128) if c else a.shape for a, c in zip(far_ins, own)]

    def body(*refs):
        first, rest = refs[: lead + near], refs[lead + near :]
        parts = []
        for size in (count_in, len(after), count_out, count_in, count_out, 2):
            parts.append(rest[:size])
            rest = rest[size:]
        sources, _, targets, in_bufs, out_bufs, (in_sems, out_sems) = parts

        def source(k, a, b):
            return sources[k].at[a:b, C : 3 * C] if own[k] else sources[k].at[a:b]

        arriving = [
            [
                (a, b, pltpu.make_async_copy(source(k, a, b), buf.at[a:b], in_sems.at[k, c]))
                for c, (a, b) in enumerate(pieces_of(buf.shape))
            ]
            for k, buf in enumerate(in_bufs)
        ]
        leaving = [
            [
                (a, b, pltpu.make_async_copy(buf.at[a:b], targets[k].at[a:b], out_sems.at[k, c]))
                for c, (a, b) in enumerate(pieces_of(buf.shape))
            ]
            for k, buf in enumerate(out_bufs)
        ]
        early, later = arriving[: count_in - late], arriving[count_in - late :]
        for group in (early, later):
            for c in range(4):
                for pieces in group:
                    if c < len(pieces):
                        pieces[c][2].start()
        waiting, held = [list(pieces) for pieces in arriving], [list(pieces) for pieces in leaving]

        def need(*wanted, row=None):
            for ref in wanted:
                for k, buf in enumerate(in_bufs):
                    while buf is ref and waiting[k] and (row is None or waiting[k][0][0] <= row):
                        waiting[k].pop(0)[2].wait()

        def send(*ready, row=None):
            for ref in ready:
                for k, buf in enumerate(out_bufs):
                    while buf is ref and held[k] and (row is None or held[k][0][1] <= row + 1):
                        held[k].pop(0)[2].start()

        kernel(need, send, *first, *in_bufs, *out_bufs, *rest)
        send(*out_bufs)
        need(*in_bufs)
        for pieces in leaving:
            for piece in pieces:
                piece[2].wait()

    far = pl.BlockSpec(memory_space=pltpu.HBM)
    return pl.pallas_call(
        body,
        out_shape=outs,
        in_specs=[SM] * lead
        + [pl.BlockSpec(memory_space=pltpu.VMEM)] * near
        + [far] * (count_in + len(after)),
        out_specs=[far] * count_out,
        scratch_shapes=[
            *[pltpu.VMEM(shape, a.dtype) for shape, a in zip(shapes, far_ins)],
            *[pltpu.VMEM(a.shape, a.dtype) for a in outs],
            pltpu.SemaphoreType.DMA((max(count_in, 1), 4)),
            pltpu.SemaphoreType.DMA((count_out, 4)),
            *scratch,
        ],
        compiler_params=pltpu.CompilerParams(vmem_limit_bytes=grant * 1024 * 1024),
        cost_estimate=pl.CostEstimate(
            flops=2_000_000_000, bytes_accessed=6_000_000, transcendentals=0
        ),
        name=name,
    )(*ins, *after)


def up(values, axes):
    count = lax.axis_size(axes)
    return lax.ppermute(values, axes, [(i, i + 1) for i in range(count - 1)])


def down(values, axes):
    count = lax.axis_size(axes)
    return lax.ppermute(values, axes, [(i + 1, i) for i in range(count - 1)])


def share(msg):
    return lax.all_to_all(msg, ALL[::-1], 0, 0, tiled=True)


def rank_of(gx, gy):
    rank = gy % lax.axis_size(GY[1])
    for part, axis in (
        (gy // lax.axis_size(GY[1]), GY[0]),
        (gx % lax.axis_size(GX[1]), GX[1]),
        (gx // lax.axis_size(GX[1]), GX[0]),
    ):
        rank = rank * lax.axis_size(axis) + part
    return rank


def local(features, kernel_one, gain_one, bias_one, kernel_two, gain_two, bias_two, cotangent):
    count_x, count_y = lax.axis_size(GX), lax.axis_size(GY)
    count = count_x * count_y
    cells = float(count * 2 * ROWS * 128)
    gx, gy = lax.axis_index(GX), lax.axis_index(GY)
    at = rank_of(gx, gy)
    beside = [rank_of(jnp.clip(gx + k, 0, count_x - 1), gy) for k in (-1, 1)]
    edges = [gx > 0, gx < count_x - 1, gy > 0, gy < count_y - 1]
    place = jnp.stack([*beside, *edges, at % C, at]).astype(jnp.int32)
    gb = jnp.stack([gain_one, bias_one, gain_two, bias_two], axis=1)

    own = jnp.transpose(features, (2, 1, 0, 3)).reshape(ROWS, 64, 128)
    cot = jnp.transpose(cotangent, (2, 1, 0, 3)).reshape(ROWS, 64, 128)

    def rims(rows):
        return [sh((rows, C, 128), BF16)] * 2

    msg, four, wide = (sh((count, *tile), F32) for tile in ((128,), (4, 128), (8, 128)))
    stats = sh((C, 128), F32)
    corr = (pltpu.VMEM((192, ROWS * 128), BF16), pltpu.VMEM((384, 192), F32))

    x_low, x_high = up(own, GX), down(own, GX)
    taps = [
        jnp.transpose(k, (2, 3, 4, 0, 1)).reshape(27, C, C) for k in (kernel_one, kernel_two)
    ]
    matrices = [sh((192, 384), BF16)] * 2
    w1, w2 = call(weights_kernel, taps, matrices, "weights", smem_first=False)
    b1, b2 = call(flipped_kernel, taps, matrices, "flipped", smem_first=False)
    y_up, y_down = call(
        pack_kernel,
        (x_low, x_high, own, cot),
        [sh((14, 64, 128), BF16)] * 2,
        "pack",
        smem_first=False,
        after=(w1, b1),
        near=2,
        grant=16,
    )
    y_low, y_high = up(y_up, GY), down(y_down, GY)

    v1, h1, m1, x1_own, center = call(
        first_kernel,
        (y_low, y_high, w1, own, x_low, x_high),
        [sh((40, 128, 128), BF16), sh((38, 128, 128), F32), four, sh((16, 128), F32), stats],
        "conv_one",
        smem_first=False,
    )
    r1 = share(m1)

    (xh,) = call(
        side_kernel,
        (center, h1, v1),
        [sh((9, C, 128), F32)],
        "hidden_features",
        scratch=corr,
        smem_first=False,
        cut=(h1,),
    )

    v2, h2, low, high, m2, st1 = call(
        lambda *refs: second_kernel(cells, *refs),
        (place, r1, gb, h1, cot, y_low, y_high, w2),
        [
            sh((38, 128, 128), BF16), sh((36, 64, 128), F32), *rims(72), msg, stats,
        ],
        "conv_two",
        after=(xh,),
    )
    h2_low, h2_high = up(high, GX), down(low, GX)
    r2 = share(m2)
    (x1,) = call(
        total_kernel, (r1,), [sh((4, 128), F32)], "total", smem_first=False, after=(st1,)
    )
    m3, st2 = call(
        lambda *refs: third_kernel(cells, *refs),
        (place, r2, gb, cot, h2, st1, x1_own, xh),
        [four, stats],
        "slope_two",
        after=(x1,),
    )
    r3 = share(m3)
    (output,) = call(
        output_kernel, (st2, gb, h2), [sh((ROWS, 64, 128), BF16)], "output", smem_first=False
    )

    rows_out = output

    slope1, low, high, m4, t3 = call(
        lambda *refs: fourth_kernel(cells, *refs),
        (
            place, r3, st2, gb, h2, h2_low, h2_high, cot, y_low, y_high,
            b2, st1, h1, v2, v1,
        ),
        [sh((34, 64, 128), F32), *rims(34), wide, sh((4, 128), F32)],
        "back_two",
        after=(rows_out,),
        late=5,
        cut=(h1,),
        scratch=(pltpu.VMEM((36, 128, 128), BF16), *corr, corr[1]),
    )
    s_low, s_high = up(high, GX), down(low, GX)
    r4 = share(m4)

    def back(rows):
        return jnp.transpose(rows.reshape(ROWS, 2, C, 128), (2, 1, 0, 3))

    output = back(rows_out)

    m5, norm_grads, t4 = call(
        lambda *refs: owner_kernel(cells, *refs),
        (place, r4, st1, gb, t3, x1),
        [sh((count * 8, 128), BF16), sh((4, C), F32), sh((8, 128), F32)],
        "own_rows",
        near=1,
        grant=16,
        after=(s_low, s_high, output),
    )
    r5 = share(m5.reshape(count, 8, 128)).reshape(count * 8, 128)
    (grad,) = call(
        lambda *refs: fifth_kernel(cells, *refs),
        (place, t4, st1, gb, h1, slope1, s_low, s_high, b1),
        [sh((ROWS, 64, 128), BF16)],
        "back_one",
        scratch=(pltpu.VMEM((34, 128, 128), BF16),),
    )
    grads = call(
        finish_kernel,
        (r5,),
        [sh((27, C, C), F32)] * 2,
        "finish",
        scratch=(pltpu.VMEM((3 * C * 8, 128), F32),),
        smem_first=False,
        near=1,
        grant=16,
    )
    one, two = [jnp.transpose(k.reshape(3, 3, 3, C, C), (3, 4, 0, 1, 2)) for k in grads]

    return output, back(grad), one, two, norm_grads


def solution(mesh):
    nx, ny = mesh.devices.shape
    parts = (4, nx // 4, ny // 2, 2)
    split = Mesh(mesh.devices.reshape(parts), ALL)
    spec = P(None, GX, GY, None)
    in_specs = (spec, P(), P(), P(), P(), P(), P(), spec)
    out_specs = (spec, spec, P(), P(), P())
    return jax.shard_map(local, mesh=split, in_specs=in_specs, out_specs=out_specs, check_vma=False)
```

```python
import jax
import jax.numpy as jnp
from jax import lax
from jax.experimental import pallas as pl
from jax.experimental.pallas import tpu as pltpu
from jax.sharding import Mesh
from jax.sharding import PartitionSpec as P

GX = ("gx_0", "gx_1")
GY = ("gy_0", "gy_1")
ALL = GX + GY

EPSILON = 1e-05
C = 32
ROWS = 32
F32 = jnp.float32
BF16 = jnp.bfloat16
LN2 = 0.6931471805599453
SM = pl.BlockSpec(memory_space=pltpu.SMEM)


def sh(shape, kind):
    return jax.ShapeDtypeStruct(shape, kind)


def from_below(values, lane):
    return jnp.where(lane == 0, 0.0, pltpu.roll(values, 1, 1))


def from_above(values, lane):
    return jnp.where(lane == 127, 0.0, pltpu.roll(values, 127, 1))


def lanes(rows):
    return lax.broadcasted_iota(jnp.int32, (rows, 128), 1)


def windows_of(*refs):
    if len(refs) == 1:
        return lambda y: refs[0][y : y + 3].reshape(384, 128)
    return lambda y: jnp.concatenate([rows(y + k) for k in range(3) for rows in refs], axis=0)


def joined(k, middle, below, above):
    def row(y):
        if y < 4:
            return below[3 * y + k]
        if y < 4 + ROWS:
            return middle[y - 4]
        return above[3 * (y - 4 - ROWS) + k]

    return row


def conv_rows(window, w_ref, rows, emit):
    lane = lanes(64)
    weights = w_ref[...]
    for y in range(0, rows, 2):
        both = jnp.concatenate([window(y), window(y + 1)], axis=1)
        product = jnp.dot(weights, both, preferred_element_type=F32)
        for k in range(2):
            part = product[:, k * 128 : (k + 1) * 128]
            emit(
                y + k,
                part[64:128] + from_below(part[0:64], lane) + from_above(part[128:192], lane),
            )


def fold(column):
    return column[0:C] + column[C : 2 * C]


def total(values):
    return jnp.sum(values, axis=1, keepdims=True)


def twice(column):
    return jnp.concatenate([column, column], axis=0)


def fourfold(column):
    return twice(twice(column))


def message(columns, msg_ref):
    count = msg_ref.shape[0]
    spare = jnp.zeros((128 - C * len(columns), 1), F32)
    column = jnp.concatenate([*columns, spare], axis=0)
    msg_ref[...] = jnp.transpose(jnp.broadcast_to(column, (128, count)))


def as_row(column):
    return jnp.transpose(jnp.broadcast_to(column, (128, 128)))[0:1]


def rows_message(columns, groups, msg_ref):
    spare = jnp.zeros((128 - C * len(columns), 1), F32)
    row = as_row(jnp.concatenate([*columns, spare], axis=0))
    height = msg_ref.shape[1]
    at = lax.broadcasted_iota(jnp.int32, (height, 128), 0)
    tile = jnp.where(at == 0, jnp.broadcast_to(row, (height, 128)), 0.0)
    msg_ref[...] = jnp.broadcast_to(tile[None], msg_ref.shape)
    for k, group in enumerate(groups):
        for dz in range(3):
            for dy in range(3):
                msg_ref[dz * C : (dz + 1) * C, 1 + 3 * k + dy, :] = group(dz, dy)


def center_of(acc):
    return fold(total(acc)) / (2 * ROWS * 128)


def stats_of(rows, place_ref, cells, st_ref):
    parts = jnp.transpose(rows)
    centers = parts[0:C]
    count = parts.shape[1]
    mean = total(centers) / count
    off = centers - mean
    spread = (total(parts[C : 2 * C]) + (2 * ROWS * 128) * total(off * off)) / cells
    at = lax.broadcasted_iota(jnp.int32, centers.shape, 1)
    low = total(jnp.where(at == place_ref[0], off, 0.0))
    high = total(jnp.where(at == place_ref[1], off, 0.0))
    own = total(jnp.where(at == place_ref[7], off, 0.0))
    found = (mean, lax.rsqrt(spread + EPSILON), low, high)
    st_ref[...] = jnp.concatenate([*found, own, jnp.zeros((C, 123), F32)], axis=1)
    return found


def kept_stats(st_ref):
    return tuple(st_ref[:, k : k + 1] for k in range(4))


def sums_of(row):
    parts = jnp.transpose(jnp.broadcast_to(row, (128, 128)))[:, 0:1]
    return parts[0:C], parts[C : 2 * C]


def feature_sums(v):
    lane = lanes(128)
    inner = v[5].astype(F32)
    for y in range(6, 3 + ROWS):
        inner = inner + v[y].astype(F32)
    ends = [v[y].astype(F32) for y in (3, 4, 3 + ROWS, 4 + ROWS)]
    windows = (inner + ends[0] + ends[1], inner + ends[1] + ends[2], inner + ends[2] + ends[3])
    columns = []
    for dz in range(3):
        for dy in range(3):
            values = windows[dy]
            if dz == 0:
                values = jnp.where(lane == 127, 0.0, values)
            if dz == 2:
                values = jnp.where(lane == 0, 0.0, values)
            column = total(values)
            columns.append(column + jnp.concatenate([column[C:], column[:C]], axis=0))
    return jnp.transpose(jnp.concatenate(columns + [jnp.zeros((128, 119), F32)], axis=1))[0:16]


def ones_of(x1):
    return lambda dz, dy: jnp.broadcast_to(x1[dz * 3 + dy : dz * 3 + dy + 1], (C, 128))


def act(z):
    e = jnp.exp2(jnp.abs(z) * (-8.0 / LN2))
    soft = jnp.maximum(z, 0.0) * 0.99 + jnp.log2(1.0 + e) * (0.99 * LN2 / 8.0)
    return 0.01 * z + soft


def act_slope(z):
    return 0.505 + 0.495 * jnp.tanh(4.0 * z)


def kept(place_ref, y, rows, margin):
    low = place_ref[2].astype(F32)
    high = place_ref[3].astype(F32)
    if y < margin:
        edge = place_ref[4].astype(F32)
    elif y >= rows - margin:
        edge = place_ref[5].astype(F32)
    else:
        return low, None, high
    return low * edge, edge, high * edge


def masked(values, factors):
    f_low, f_own, f_high = factors
    own = values[C : 3 * C]
    own = own if f_own is None else own * f_own
    return jnp.concatenate([values[0:C] * f_low, own, values[3 * C :] * f_high], axis=0).astype(
        BF16
    )


def weight_sums(g_ref, v_ref, first, acc_ref):
    step = 4
    for y in range(0, ROWS, step):
        window = jnp.concatenate(
            [v_ref[first + y + k : first + y + k + 3].reshape(384, 128) for k in range(step)], axis=1
        )
        product = lax.dot_general(
            window,
            g_ref[:, y * 128 : (y + step) * 128],
            (((1,), (1,)), ((), ())),
            preferred_element_type=F32,
        )
        if y == 0:
            acc_ref[...] = product
        else:
            acc_ref[...] += product


def folded(acc_ref):
    turned = [jnp.transpose(acc_ref[dy * 128 : dy * 128 + 128]) for dy in range(3)]

    def tile(dz, dy):
        both = turned[dy][dz * 64 : dz * 64 + 64]
        return both[0:C] + pltpu.roll(both[C:], 96, 1)

    return tile


def put_shifted(g_ref, y, values, lane):
    at = slice(y * 128, (y + 1) * 128)
    g_ref[0:64, at] = from_above(values, lane).astype(BF16)
    g_ref[64:128, at] = values.astype(BF16)
    g_ref[128:192, at] = from_below(values, lane).astype(BF16)


def pack_kernel(need, send, x_low, x_high, own, cot, up_ref, down_ref):
    need(own, cot)
    for y in range(4):
        for k, part in enumerate((x_low, own, x_high)):
            up_ref[3 * y + k] = part[ROWS - 4 + y]
            down_ref[3 * y + k] = part[y]
    up_ref[12:14] = cot[ROWS - 2 : ROWS]
    down_ref[12:14] = cot[0:2]


def weights_kernel(need, send, k1, k2, w1, w2):
    need(k1, k2)
    row = lax.broadcasted_iota(jnp.int32, (C, 128), 0)
    col = lax.broadcasted_iota(jnp.int32, (C, 128), 1)
    for k_ref, w_ref in ((k1, w1), (k2, w2)):
        lined = jnp.zeros((9 * C, 128), F32)
        for dx in range(3):
            spot = jnp.where(row + dx * C == col, 1.0, 0.0).astype(BF16)
            lined = lined + jnp.dot(
                k_ref[dx * 9 : dx * 9 + 9].reshape(9 * C, C), spot, preferred_element_type=F32
            )
        for dy in range(3):
            for dz in range(3):
                t = dy * 3 + dz
                put_tile(w_ref, dz, dy, lined[t * C : t * C + C])


def flipped_kernel(need, send, k1, k2, b1, b2):
    need(k1, k2)
    row = lax.broadcasted_iota(jnp.int32, (C, 128), 0)
    col = lax.broadcasted_iota(jnp.int32, (C, 128), 1)
    eye = jnp.where(row == col, 1.0, 0.0)[:, 0:C].astype(BF16)
    zero = jnp.zeros((C, C), BF16)
    for k_ref, b_ref in ((k1, b1), (k2, b2)):
        stack = []
        for t in range(9):
            stack += [k_ref[18 + t], k_ref[9 + t], k_ref[t], zero]
        turned = lax.dot_general(
            eye,
            jnp.concatenate(stack, axis=0),
            (((1,), (1,)), ((), ())),
            preferred_element_type=F32,
        )
        for dy in range(3):
            for dz in range(3):
                t = 8 - dy * 3 - dz
                put_tile(b_ref, dz, dy, turned[:, t * 128 : t * 128 + 128])


def put_tile(ref, dz, dy, tile):
    here = slice(dy * 128, dy * 128 + 128)
    ref[dz * 64 : dz * 64 + C, here] = tile.astype(BF16)
    ref[dz * 64 + C : dz * 64 + 64, here] = pltpu.roll(tile, C, 1).astype(BF16)


def first_kernel(
    need, send, y_low, y_high, w, own, x_low, x_high, v, h, msg, x1, center_out
):
    need(own, x_low, x_high, y_low, y_high, w)
    low = joined(0, x_low, y_low, y_high)
    own = joined(1, own, y_low, y_high)
    high = joined(2, x_high, y_low, y_high)
    acc = [jnp.zeros((64, 128), F32), jnp.zeros((64, 128), F32)]
    for k, pair in enumerate(((low, own), (own, high))):

        def emit(y, values, k=k):
            h[y, 64 * k : 64 * k + 64] = values
            if k == 1:
                send(h, row=y)
            if 3 <= y < 3 + ROWS:
                acc[k] = acc[k] + values

        conv_rows(windows_of(*pair), w, ROWS + 6, emit)
    send(h)
    for y in range(ROWS + 8):
        v[y] = jnp.concatenate([low(y)[C:], own(y), high(y)[0:C]], axis=0)
        send(v, row=y)
    send(v)
    center = center_of(jnp.concatenate([acc[0][C:], acc[1][0:C]], axis=0))
    both = twice(center)
    spread = jnp.zeros((64, 128), F32)
    for y in range(3, 3 + ROWS):
        off = h[y, C : 3 * C] - both
        spread = spread + off * off
    center_out[...] = jnp.broadcast_to(center, (C, 128))
    x1[...] = feature_sums(v)
    send(center_out, x1)
    rows_message((center, fold(total(spread))), (ones_of(x1),), msg)


def second_kernel(
    cells, need, send, place, r1, gb, h1, cot, y_low, y_high, w, v, h, low, high, msg, st1
):
    need(r1, gb)
    mean, inverse, _, _ = stats_of(r1[:, 0, :], place, cells, st1)
    send(st1)
    mean4, scale4 = fourfold(mean), fourfold(inverse * gb[:, 0:1])
    shift4 = fourfold(gb[:, 1:2])
    rows = ROWS + 6
    for y in range(rows):
        need(h1, row=y)
        v[y] = masked(act((h1[y] - mean4) * scale4 + shift4), kept(place, y, rows, 3))
        send(v, row=y)
    need(w, cot, y_low, y_high)
    acc = [jnp.zeros((64, 128), F32)]

    def emit(y, values):
        h[y] = values
        send(h, row=y)
        if 2 <= y < 2 + ROWS:
            acc[0] = acc[0] + values

    rows = ROWS + 4
    conv_rows(windows_of(v), w, rows, emit)
    send(h)
    center = center_of(acc[0])
    both = twice(center)
    spread = jnp.zeros((64, 128), F32)
    for y in range(rows):
        off = h[y] - both
        if 2 <= y < 2 + ROWS:
            spread = spread + off * off
        low[2 * y] = off[0:C].astype(BF16)
        high[2 * y] = off[C:].astype(BF16)
        values = cot_row(cot, y_low, y_high, y)
        low[2 * y + 1] = values[0:C]
        high[2 * y + 1] = values[C:]
        send(low, high, row=2 * y + 1)
    message((center, fold(total(spread))), msg)


def total_kernel(need, send, parts, whole):
    need(parts)
    whole[...] = jnp.sum(parts[...], axis=0)


def side_kernel(need, send, center, h1, v1, xh, g, acc):
    need(center)
    both = twice(center[...])
    lane = lanes(64)
    for y in range(ROWS):
        need(h1, row=y + 3)
        put_shifted(g, y, h1[y + 3] - both, lane)
    need(v1)
    weight_sums(g, v1, 3, acc)
    tile = folded(acc)
    for dz in range(3):
        for dy in range(3):
            xh[dz * 3 + dy] = tile(dz, dy)


def cot_row(cot, y_low, y_high, y):
    if y < 2:
        return y_low[12 + y]
    if y < 2 + ROWS:
        return cot[y - 2]
    return y_high[10 + y - ROWS]


def third_kernel(cells, need, send, place, r2, gb, cot, h2, st1, x1, xh, msg, st2):
    need(r2, gb)
    mean, inverse, _, _ = stats_of(r2[...], place, cells, st2)
    mean2, inverse2 = twice(mean), twice(inverse)
    gain2, bias2 = twice(gb[:, 2:3]), twice(gb[:, 3:4])
    plain = jnp.zeros((64, 128), F32)
    both = jnp.zeros((64, 128), F32)
    for y in range(ROWS):
        need(h2, row=y + 2)
        need(cot, row=y)
        normed = (h2[y + 2] - mean2) * inverse2
        z = normed * gain2 + bias2
        slope = cot[y].astype(F32) * act_slope(z)
        plain = plain + slope
        both = both + slope * normed
    need(st1, x1, xh)
    inverse1, own1 = st1[:, 1:2], st1[:, 4:5]
    ones = ones_of(x1)

    def xn(dz, dy):
        return inverse1 * (xh[dz * 3 + dy] + own1 * ones(dz, dy))


    rows_message((fold(total(both)), fold(total(plain))), (xn,), msg)


def output_kernel(need, send, st2, gb, h2, out):
    need(st2, gb)
    mean, inverse, _, _ = kept_stats(st2)
    mean2, scale2 = twice(mean), twice(inverse * gb[:, 2:3])
    shift2 = twice(gb[:, 3:4])
    for y in range(ROWS):
        need(h2, row=y + 2)
        out[y] = act((h2[y + 2] - mean2) * scale2 + shift2).astype(BF16)
        send(out, row=y)


def fourth_kernel(
    cells, need, send, place, r3, st2, gb, h2, x_low, x_high, cot, y_low, y_high, w, st1, h1, v2, v1, slope1, low, high, msg, t3, v, g, acc, acc1,
):
    need(r3, st2, gb)
    mean, inverse, o_low, o_high = kept_stats(st2)
    t3[...] = jnp.sum(r3[...], axis=0)
    send(t3)
    nsum, plain = sums_of(t3[0:1])
    need(y_low, y_high)
    gain, bias = gb[:, 2:3], gb[:, 3:4]
    lead = gain * inverse
    p_mean, n_mean = plain / cells, nsum / cells

    def grad(normed, c, gain, bias, lead, p_mean, n_mean):
        slope = c.astype(F32) * act_slope(normed * gain + bias)
        return lead * (slope - p_mean - normed * n_mean)

    one = (gain, bias, lead, p_mean, n_mean)
    two = tuple(twice(a) for a in one)
    mean2, inverse2 = twice(mean), twice(inverse)
    lane = lanes(64)
    rows = ROWS + 4
    for y in range(rows):
        need(h2, row=y)
        need(x_low, x_high, row=2 * y + 1)
        need(cot, row=min(max(y - 2, 0), ROWS - 1))
        g_low = grad((x_low[2 * y].astype(F32) + o_low) * inverse, x_low[2 * y + 1], *one)
        g_own = grad((h2[y] - mean2) * inverse2, cot_row(cot, y_low, y_high, y), *two)
        g_high = grad((x_high[2 * y].astype(F32) + o_high) * inverse, x_high[2 * y + 1], *one)
        both = jnp.concatenate([g_low, g_own, g_high], axis=0)
        v[y] = masked(both, kept(place, y, rows, 2))
        if 2 <= y < 2 + ROWS:
            put_shifted(g, y - 2, g_own, lane)
    need(v2)
    weight_sums(g, v2, 2, acc)

    need(h1, st1, w)
    mean, inverse, _, _ = kept_stats(st1)
    mean2, inverse2 = twice(mean), twice(inverse)
    gain2, bias2 = twice(gb[:, 0:1]), twice(gb[:, 1:2])
    sums = [jnp.zeros((64, 128), F32), jnp.zeros((64, 128), F32)]

    def emit(y, values):
        normed = (h1[y + 2] - mean2) * inverse2
        slope = values * act_slope(normed * gain2 + bias2)
        slope1[y] = slope
        low[y] = slope[0:C].astype(BF16)
        high[y] = slope[C:].astype(BF16)
        send(slope1, low, high, row=y)
        if 1 <= y < 1 + ROWS:
            sums[0] = sums[0] + slope * normed
            sums[1] = sums[1] + slope
            put_shifted(g, y - 1, slope, lane)

    conv_rows(windows_of(v), w, ROWS + 2, emit)
    send(slope1, low, high)
    need(v1)
    weight_sums(g, v1, 3, acc1)
    rows_message(
        (fold(total(sums[0])), fold(total(sums[1]))), (folded(acc1), folded(acc)), msg
    )


def owner_kernel(cells, need, send, place, r4, st1, gb, t3, x1, msg, norms, t4):
    need(st1, gb, t3, x1)
    _, inverse, _, _ = kept_stats(st1)
    t4[...] = jnp.sum(r4[...], axis=0)
    nsum, plain = sums_of(t4[0:1])
    mine = lax.broadcasted_iota(jnp.int32, (C, 1), 0) == place[6]

    def picked(column):
        return jnp.sum(jnp.where(mine, column, 0.0), axis=0, keepdims=True)

    scale = cells**-0.5
    lead = picked(gb[:, 0:1] * inverse) * scale
    third, fourth = t3[...], t4[...]
    one = fourth[1:4] - picked(plain) * (x1[1:4] / cells) - picked(nsum) * (third[1:4] / cells)
    one = lead * one
    two = fourth[4:7] * scale
    tile = jnp.concatenate([one, two, jnp.zeros((2, 128), F32)], axis=0)
    pair = twice(tile).astype(BF16)
    for k in range(0, msg.shape[0], 16):
        msg[k : k + 16] = pair
    for k, row in enumerate((fourth[0:1], third[0:1])):
        norms[2 * k : 2 * k + 1] = row[:, 0:C] * scale
        norms[2 * k + 1 : 2 * k + 2] = row[:, C : 2 * C] * scale


def finish_kernel(need, send, parts, one, two, rows):
    rows[...] = parts[0 : 3 * C * 8].astype(F32)
    for dz in range(3):
        for dy in range(3):
            for k, out in enumerate((one, two)):
                tile = rows[pl.ds(dz * C * 8 + 3 * k + dy, C, stride=8), :]
                for dx in range(3):
                    out[dx * 9 + dy * 3 + dz] = tile[:, dx * C : (dx + 1) * C]


def fifth_kernel(cells, need, send, place, t4, st1, gb, h1, slope1, s_low, s_high, w, out, v, turned):
    need(t4, st1, gb)
    mean, inverse, _, _ = kept_stats(st1)
    nsum, plain = sums_of(t4[0:1])
    mean4, inverse4 = fourfold(mean), fourfold(inverse)
    lead4 = fourfold(gb[:, 0:1] * inverse)
    p_mean4, n_mean4 = fourfold(plain / cells), fourfold(nsum / cells)
    rows = ROWS + 2
    for y in range(rows):
        need(slope1, s_low, s_high, row=y)
        need(h1, row=y + 2)
        slope = jnp.concatenate(
            [s_low[y].astype(F32), slope1[y], s_high[y].astype(F32)], axis=0
        )
        normed = (h1[y + 2] - mean4) * inverse4
        v[y] = masked(lead4 * (slope - p_mean4 - normed * n_mean4), kept(place, y, rows, 1))
    need(w)

    def emit(y, values):
        turned[:, y, :] = values

    conv_rows(windows_of(v), w, ROWS, emit)
    for i in range(C):
        for x in range(2):
            out[i, x] = turned[x * C + i].astype(BF16)
        send(out, row=i)


def pieces_of(shape):
    rows = shape[0]
    if len(shape) < 3 or rows < 32 or rows > 100:
        return [(0, rows)]
    cuts = [rows * c // 4 for c in range(5)]
    return list(zip(cuts, cuts[1:]))


def call(
    kernel, ins, outs, name, scratch=(), smem_first=True, after=(), near=0, cut=(), late=0, grant=56
):
    lead = 1 if smem_first else 0
    count_in, count_out = len(ins) - lead - near, len(outs)
    far_ins = ins[lead + near :]
    own = [any(a is b for b in cut) for a in far_ins]
    shapes = [(a.shape[0], 2 * C, 128) if c else a.shape for a, c in zip(far_ins, own)]

    def body(*refs):
        first, rest = refs[: lead + near], refs[lead + near :]
        parts = []
        for size in (count_in, len(after), count_out, count_in, count_out, 2):
            parts.append(rest[:size])
            rest = rest[size:]
        sources, _, targets, in_bufs, out_bufs, (in_sems, out_sems) = parts

        def source(k, a, b):
            return sources[k].at[a:b, C : 3 * C] if own[k] else sources[k].at[a:b]

        arriving = [
            [
                (a, b, pltpu.make_async_copy(source(k, a, b), buf.at[a:b], in_sems.at[k, c]))
                for c, (a, b) in enumerate(pieces_of(buf.shape))
            ]
            for k, buf in enumerate(in_bufs)
        ]
        leaving = [
            [
                (a, b, pltpu.make_async_copy(buf.at[a:b], targets[k].at[a:b], out_sems.at[k, c]))
                for c, (a, b) in enumerate(pieces_of(buf.shape))
            ]
            for k, buf in enumerate(out_bufs)
        ]
        early, later = arriving[: count_in - late], arriving[count_in - late :]
        for group in (early, later):
            for c in range(4):
                for pieces in group:
                    if c < len(pieces):
                        pieces[c][2].start()
        waiting, held = [list(pieces) for pieces in arriving], [list(pieces) for pieces in leaving]

        def need(*wanted, row=None):
            for ref in wanted:
                for k, buf in enumerate(in_bufs):
                    while buf is ref and waiting[k] and (row is None or waiting[k][0][0] <= row):
                        waiting[k].pop(0)[2].wait()

        def send(*ready, row=None):
            for ref in ready:
                for k, buf in enumerate(out_bufs):
                    while buf is ref and held[k] and (row is None or held[k][0][1] <= row + 1):
                        held[k].pop(0)[2].start()

        kernel(need, send, *first, *in_bufs, *out_bufs, *rest)
        send(*out_bufs)
        need(*in_bufs)
        for pieces in leaving:
            for piece in pieces:
                piece[2].wait()

    far = pl.BlockSpec(memory_space=pltpu.HBM)
    return pl.pallas_call(
        body,
        out_shape=outs,
        in_specs=[SM] * lead
        + [pl.BlockSpec(memory_space=pltpu.VMEM)] * near
        + [far] * (count_in + len(after)),
        out_specs=[far] * count_out,
        scratch_shapes=[
            *[pltpu.VMEM(shape, a.dtype) for shape, a in zip(shapes, far_ins)],
            *[pltpu.VMEM(a.shape, a.dtype) for a in outs],
            pltpu.SemaphoreType.DMA((max(count_in, 1), 4)),
            pltpu.SemaphoreType.DMA((count_out, 4)),
            *scratch,
        ],
        compiler_params=pltpu.CompilerParams(vmem_limit_bytes=grant * 1024 * 1024),
        cost_estimate=pl.CostEstimate(
            flops=2_000_000_000, bytes_accessed=6_000_000, transcendentals=0
        ),
        name=name,
    )(*ins, *after)


def up(values, axes):
    count = lax.axis_size(axes)
    return lax.ppermute(values, axes, [(i, i + 1) for i in range(count - 1)])


def down(values, axes):
    count = lax.axis_size(axes)
    return lax.ppermute(values, axes, [(i + 1, i) for i in range(count - 1)])


def share(msg):
    return lax.all_to_all(msg, ALL[::-1], 0, 0, tiled=True)


def rank_of(gx, gy):
    rank = gy % lax.axis_size(GY[1])
    for part, axis in (
        (gy // lax.axis_size(GY[1]), GY[0]),
        (gx % lax.axis_size(GX[1]), GX[1]),
        (gx // lax.axis_size(GX[1]), GX[0]),
    ):
        rank = rank * lax.axis_size(axis) + part
    return rank


def local(features, kernel_one, gain_one, bias_one, kernel_two, gain_two, bias_two, cotangent):
    count_x, count_y = lax.axis_size(GX), lax.axis_size(GY)
    count = count_x * count_y
    cells = float(count * 2 * ROWS * 128)
    gx, gy = lax.axis_index(GX), lax.axis_index(GY)
    at = rank_of(gx, gy)
    beside = [rank_of(jnp.clip(gx + k, 0, count_x - 1), gy) for k in (-1, 1)]
    edges = [gx > 0, gx < count_x - 1, gy > 0, gy < count_y - 1]
    place = jnp.stack([*beside, *edges, at % C, at]).astype(jnp.int32)
    gb = jnp.stack([gain_one, bias_one, gain_two, bias_two], axis=1)

    own = jnp.transpose(features, (2, 1, 0, 3)).reshape(ROWS, 64, 128)
    cot = jnp.transpose(cotangent, (2, 1, 0, 3)).reshape(ROWS, 64, 128)

    def rims(rows):
        return [sh((rows, C, 128), BF16)] * 2

    msg, four, wide = (sh((count, *tile), F32) for tile in ((128,), (4, 128), (8, 128)))
    stats = sh((C, 128), F32)
    corr = (pltpu.VMEM((192, ROWS * 128), BF16), pltpu.VMEM((384, 192), F32))

    x_low, x_high = up(own, GX), down(own, GX)
    taps = [
        jnp.transpose(k, (2, 3, 4, 0, 1)).reshape(27, C, C) for k in (kernel_one, kernel_two)
    ]
    matrices = [sh((192, 384), BF16)] * 2
    w1, w2 = call(weights_kernel, taps, matrices, "weights", smem_first=False)
    b1, b2 = call(flipped_kernel, taps, matrices, "flipped", smem_first=False)
    y_up, y_down = call(
        pack_kernel,
        (x_low, x_high, own, cot),
        [sh((14, 64, 128), BF16)] * 2,
        "pack",
        smem_first=False,
        after=(w1, b1),
        near=2,
        grant=16,
    )
    y_low, y_high = up(y_up, GY), down(y_down, GY)

    v1, h1, m1, x1_own, center = call(
        first_kernel,
        (y_low, y_high, w1, own, x_low, x_high),
        [sh((40, 128, 128), BF16), sh((38, 128, 128), F32), four, sh((16, 128), F32), stats],
        "conv_one",
        smem_first=False,
    )
    r1 = share(m1)

    (xh,) = call(
        side_kernel,
        (center, h1, v1),
        [sh((9, C, 128), F32)],
        "hidden_features",
        scratch=corr,
        smem_first=False,
        cut=(h1,),
    )

    v2, h2, low, high, m2, st1 = call(
        lambda *refs: second_kernel(cells, *refs),
        (place, r1, gb, h1, cot, y_low, y_high, w2),
        [
            sh((38, 128, 128), BF16), sh((36, 64, 128), F32), *rims(72), msg, stats,
        ],
        "conv_two",
        after=(xh,),
    )
    h2_low, h2_high = up(high, GX), down(low, GX)
    r2 = share(m2)
    (x1,) = call(
        total_kernel, (r1,), [sh((4, 128), F32)], "total", smem_first=False, after=(st1,)
    )
    m3, st2 = call(
        lambda *refs: third_kernel(cells, *refs),
        (place, r2, gb, cot, h2, st1, x1_own, xh),
        [four, stats],
        "slope_two",
        after=(x1,),
    )
    r3 = share(m3)
    (output,) = call(
        output_kernel, (st2, gb, h2), [sh((ROWS, 64, 128), BF16)], "output", smem_first=False
    )

    rows_out = output

    slope1, low, high, m4, t3 = call(
        lambda *refs: fourth_kernel(cells, *refs),
        (
            place, r3, st2, gb, h2, h2_low, h2_high, cot, y_low, y_high,
            b2, st1, h1, v2, v1,
        ),
        [sh((34, 64, 128), F32), *rims(34), wide, sh((4, 128), F32)],
        "back_two",
        after=(rows_out,),
        late=5,
        cut=(h1,),
        scratch=(pltpu.VMEM((36, 128, 128), BF16), *corr, corr[1]),
    )
    s_low, s_high = up(high, GX), down(low, GX)
    r4 = share(m4)

    def back(rows):
        return jnp.transpose(rows.reshape(ROWS, 2, C, 128), (2, 1, 0, 3))

    output = back(rows_out)

    m5, norm_grads, t4 = call(
        lambda *refs: owner_kernel(cells, *refs),
        (place, r4, st1, gb, t3, x1),
        [sh((count * 8, 128), BF16), sh((4, C), F32), sh((8, 128), F32)],
        "own_rows",
        near=1,
        grant=16,
        after=(s_low, s_high, output),
    )
    r5 = share(m5.reshape(count, 8, 128)).reshape(count * 8, 128)
    (grad,) = call(
        lambda *refs: fifth_kernel(cells, *refs),
        (place, t4, st1, gb, h1, slope1, s_low, s_high, b1),
        [sh((C, 2, ROWS, 128), BF16)],
        "back_one",
        scratch=(pltpu.VMEM((34, 128, 128), BF16), pltpu.VMEM((64, ROWS, 128), F32)),
    )
    grads = call(
        finish_kernel,
        (r5,),
        [sh((27, C, C), F32)] * 2,
        "finish",
        scratch=(pltpu.VMEM((3 * C * 8, 128), F32),),
        smem_first=False,
        near=1,
        grant=16,
    )
    one, two = [jnp.transpose(k.reshape(3, 3, 3, C, C), (3, 4, 0, 1, 2)) for k in grads]

    return output, grad, one, two, norm_grads


def solution(mesh):
    nx, ny = mesh.devices.shape
    parts = (4, nx // 4, ny // 2, 2)
    split = Mesh(mesh.devices.reshape(parts), ALL)
    spec = P(None, GX, GY, None)
    in_specs = (spec, P(), P(), P(), P(), P(), P(), spec)
    out_specs = (spec, spec, P(), P(), P())
    return jax.shard_map(local, mesh=split, in_specs=in_specs, out_specs=out_specs, check_vma=False)
```

```python
import jax
import jax.numpy as jnp
from jax import lax
from jax.experimental import pallas as pl
from jax.experimental.pallas import tpu as pltpu
from jax.sharding import Mesh
from jax.sharding import PartitionSpec as P

GX = ("gx_0", "gx_1")
GY = ("gy_0", "gy_1")
ALL = GX + GY

EPSILON = 1e-05
C = 32
ROWS = 32
F32 = jnp.float32
BF16 = jnp.bfloat16
LN2 = 0.6931471805599453
SM = pl.BlockSpec(memory_space=pltpu.SMEM)


def sh(shape, kind):
    return jax.ShapeDtypeStruct(shape, kind)


def from_below(values, lane):
    return jnp.where(lane == 0, 0.0, pltpu.roll(values, 1, 1))


def from_above(values, lane):
    return jnp.where(lane == 127, 0.0, pltpu.roll(values, 127, 1))


def lanes(rows):
    return lax.broadcasted_iota(jnp.int32, (rows, 128), 1)


def windows_of(*refs):
    if len(refs) == 1:
        return lambda y: refs[0][y : y + 3].reshape(384, 128)
    return lambda y: jnp.concatenate([rows(y + k) for k in range(3) for rows in refs], axis=0)


def joined(k, middle, below, above):
    def row(y):
        if y < 4:
            return below[3 * y + k]
        if y < 4 + ROWS:
            return middle[y - 4]
        return above[3 * (y - 4 - ROWS) + k]

    return row


def conv_rows(window, w_ref, rows, emit):
    lane = lanes(64)
    weights = w_ref[...]
    for y in range(0, rows, 2):
        both = jnp.concatenate([window(y), window(y + 1)], axis=1)
        product = jnp.dot(weights, both, preferred_element_type=F32)
        for k in range(2):
            part = product[:, k * 128 : (k + 1) * 128]
            emit(
                y + k,
                part[64:128] + from_below(part[0:64], lane) + from_above(part[128:192], lane),
            )


def fold(column):
    return column[0:C] + column[C : 2 * C]


def total(values):
    return jnp.sum(values, axis=1, keepdims=True)


def twice(column):
    return jnp.concatenate([column, column], axis=0)


def fourfold(column):
    return twice(twice(column))


def message(columns, msg_ref):
    count = msg_ref.shape[0]
    spare = jnp.zeros((128 - C * len(columns), 1), F32)
    column = jnp.concatenate([*columns, spare], axis=0)
    msg_ref[...] = jnp.transpose(jnp.broadcast_to(column, (128, count)))


def as_row(column):
    return jnp.transpose(jnp.broadcast_to(column, (128, 128)))[0:1]


def rows_message(columns, groups, msg_ref):
    spare = jnp.zeros((128 - C * len(columns), 1), F32)
    row = as_row(jnp.concatenate([*columns, spare], axis=0))
    height = msg_ref.shape[1]
    at = lax.broadcasted_iota(jnp.int32, (height, 128), 0)
    tile = jnp.where(at == 0, jnp.broadcast_to(row, (height, 128)), 0.0)
    msg_ref[...] = jnp.broadcast_to(tile[None], msg_ref.shape)
    for k, group in enumerate(groups):
        for dz in range(3):
            for dy in range(3):
                msg_ref[dz * C : (dz + 1) * C, 1 + 3 * k + dy, :] = group(dz, dy)


def center_of(acc):
    return fold(total(acc)) / (2 * ROWS * 128)


def stats_of(rows, place_ref, cells, st_ref):
    parts = jnp.transpose(rows)
    centers = parts[0:C]
    count = parts.shape[1]
    mean = total(centers) / count
    off = centers - mean
    spread = (total(parts[C : 2 * C]) + (2 * ROWS * 128) * total(off * off)) / cells
    at = lax.broadcasted_iota(jnp.int32, centers.shape, 1)
    low = total(jnp.where(at == place_ref[0], off, 0.0))
    high = total(jnp.where(at == place_ref[1], off, 0.0))
    own = total(jnp.where(at == place_ref[7], off, 0.0))
    found = (mean, lax.rsqrt(spread + EPSILON), low, high)
    st_ref[...] = jnp.concatenate([*found, own, jnp.zeros((C, 123), F32)], axis=1)
    return found


def kept_stats(st_ref):
    return tuple(st_ref[:, k : k + 1] for k in range(4))


def sums_of(row):
    parts = jnp.transpose(jnp.broadcast_to(row, (128, 128)))[:, 0:1]
    return parts[0:C], parts[C : 2 * C]


def feature_sums(v):
    lane = lanes(128)
    inner = v[5].astype(F32)
    for y in range(6, 3 + ROWS):
        inner = inner + v[y].astype(F32)
    ends = [v[y].astype(F32) for y in (3, 4, 3 + ROWS, 4 + ROWS)]
    windows = (inner + ends[0] + ends[1], inner + ends[1] + ends[2], inner + ends[2] + ends[3])
    columns = []
    for dz in range(3):
        for dy in range(3):
            values = windows[dy]
            if dz == 0:
                values = jnp.where(lane == 127, 0.0, values)
            if dz == 2:
                values = jnp.where(lane == 0, 0.0, values)
            column = total(values)
            columns.append(column + jnp.concatenate([column[C:], column[:C]], axis=0))
    return jnp.transpose(jnp.concatenate(columns + [jnp.zeros((128, 119), F32)], axis=1))[0:16]


def ones_of(x1):
    return lambda dz, dy: jnp.broadcast_to(x1[dz * 3 + dy : dz * 3 + dy + 1], (C, 128))


def act(z):
    e = jnp.exp2(jnp.abs(z) * (-8.0 / LN2))
    soft = jnp.maximum(z, 0.0) * 0.99 + jnp.log2(1.0 + e) * (0.99 * LN2 / 8.0)
    return 0.01 * z + soft


def act_slope(z):
    return 0.505 + 0.495 * jnp.tanh(4.0 * z)


def kept(place_ref, y, rows, margin):
    low = place_ref[2].astype(F32)
    high = place_ref[3].astype(F32)
    if y < margin:
        edge = place_ref[4].astype(F32)
    elif y >= rows - margin:
        edge = place_ref[5].astype(F32)
    else:
        return low, None, high
    return low * edge, edge, high * edge


def masked(values, factors):
    f_low, f_own, f_high = factors
    own = values[C : 3 * C]
    own = own if f_own is None else own * f_own
    return jnp.concatenate([values[0:C] * f_low, own, values[3 * C :] * f_high], axis=0).astype(
        BF16
    )


def weight_sums(g_ref, v_ref, first, acc_ref):
    step = 4
    for y in range(0, ROWS, step):
        window = jnp.concatenate(
            [v_ref[first + y + k : first + y + k + 3].reshape(384, 128) for k in range(step)], axis=1
        )
        product = lax.dot_general(
            window,
            g_ref[:, y * 128 : (y + step) * 128],
            (((1,), (1,)), ((), ())),
            preferred_element_type=F32,
        )
        if y == 0:
            acc_ref[...] = product
        else:
            acc_ref[...] += product


def folded(acc_ref):
    turned = [jnp.transpose(acc_ref[dy * 128 : dy * 128 + 128]) for dy in range(3)]

    def tile(dz, dy):
        both = turned[dy][dz * 64 : dz * 64 + 64]
        return both[0:C] + pltpu.roll(both[C:], 96, 1)

    return tile


def put_shifted(g_ref, y, values, lane):
    at = slice(y * 128, (y + 1) * 128)
    g_ref[0:64, at] = from_above(values, lane).astype(BF16)
    g_ref[64:128, at] = values.astype(BF16)
    g_ref[128:192, at] = from_below(values, lane).astype(BF16)


def pack_kernel(need, send, x_low, x_high, own, cot, up_ref, down_ref):
    need(own, cot)
    for y in range(4):
        for k, part in enumerate((x_low, own, x_high)):
            up_ref[3 * y + k] = part[ROWS - 4 + y]
            down_ref[3 * y + k] = part[y]
    up_ref[12:14] = cot[ROWS - 2 : ROWS]
    down_ref[12:14] = cot[0:2]


def weights_kernel(need, send, k1, k2, w1, w2):
    need(k1, k2)
    row = lax.broadcasted_iota(jnp.int32, (C, 128), 0)
    col = lax.broadcasted_iota(jnp.int32, (C, 128), 1)
    for k_ref, w_ref in ((k1, w1), (k2, w2)):
        lined = jnp.zeros((9 * C, 128), F32)
        for dx in range(3):
            spot = jnp.where(row + dx * C == col, 1.0, 0.0).astype(BF16)
            lined = lined + jnp.dot(
                k_ref[dx * 9 : dx * 9 + 9].reshape(9 * C, C), spot, preferred_element_type=F32
            )
        for dy in range(3):
            for dz in range(3):
                t = dy * 3 + dz
                put_tile(w_ref, dz, dy, lined[t * C : t * C + C])


def flipped_kernel(need, send, k1, k2, b1, b2):
    need(k1, k2)
    row = lax.broadcasted_iota(jnp.int32, (C, 128), 0)
    col = lax.broadcasted_iota(jnp.int32, (C, 128), 1)
    eye = jnp.where(row == col, 1.0, 0.0)[:, 0:C].astype(BF16)
    zero = jnp.zeros((C, C), BF16)
    for k_ref, b_ref in ((k1, b1), (k2, b2)):
        stack = []
        for t in range(9):
            stack += [k_ref[18 + t], k_ref[9 + t], k_ref[t], zero]
        turned = lax.dot_general(
            eye,
            jnp.concatenate(stack, axis=0),
            (((1,), (1,)), ((), ())),
            preferred_element_type=F32,
        )
        for dy in range(3):
            for dz in range(3):
                t = 8 - dy * 3 - dz
                put_tile(b_ref, dz, dy, turned[:, t * 128 : t * 128 + 128])


def put_tile(ref, dz, dy, tile):
    here = slice(dy * 128, dy * 128 + 128)
    ref[dz * 64 : dz * 64 + C, here] = tile.astype(BF16)
    ref[dz * 64 + C : dz * 64 + 64, here] = pltpu.roll(tile, C, 1).astype(BF16)


def first_kernel(
    need, send, y_low, y_high, w, own, x_low, x_high, v, h, msg, x1, center_out
):
    need(own, x_low, x_high, y_low, y_high, w)
    low = joined(0, x_low, y_low, y_high)
    own = joined(1, own, y_low, y_high)
    high = joined(2, x_high, y_low, y_high)
    acc = [jnp.zeros((64, 128), F32), jnp.zeros((64, 128), F32)]
    for k, pair in enumerate(((low, own), (own, high))):

        def emit(y, values, k=k):
            h[y, 64 * k : 64 * k + 64] = values
            if k == 1:
                send(h, row=y)
            if 3 <= y < 3 + ROWS:
                acc[k] = acc[k] + values

        conv_rows(windows_of(*pair), w, ROWS + 6, emit)
    send(h)
    for y in range(ROWS + 8):
        v[y] = jnp.concatenate([low(y)[C:], own(y), high(y)[0:C]], axis=0)
        send(v, row=y)
    send(v)
    center = center_of(jnp.concatenate([acc[0][C:], acc[1][0:C]], axis=0))
    both = twice(center)
    spread = jnp.zeros((64, 128), F32)
    for y in range(3, 3 + ROWS):
        off = h[y, C : 3 * C] - both
        spread = spread + off * off
    center_out[...] = jnp.broadcast_to(center, (C, 128))
    x1[...] = feature_sums(v)
    send(center_out, x1)
    rows_message((center, fold(total(spread))), (ones_of(x1),), msg)


def second_kernel(
    cells, need, send, place, r1, gb, h1, cot, y_low, y_high, w, v, h, low, high, msg, st1
):
    need(r1, gb)
    mean, inverse, _, _ = stats_of(r1[:, 0, :], place, cells, st1)
    send(st1)
    mean4, scale4 = fourfold(mean), fourfold(inverse * gb[:, 0:1])
    shift4 = fourfold(gb[:, 1:2])
    rows = ROWS + 6
    for y in range(rows):
        need(h1, row=y)
        v[y] = masked(act((h1[y] - mean4) * scale4 + shift4), kept(place, y, rows, 3))
        send(v, row=y)
    need(w, cot, y_low, y_high)
    acc = [jnp.zeros((64, 128), F32)]

    def emit(y, values):
        h[y] = values
        send(h, row=y)
        if 2 <= y < 2 + ROWS:
            acc[0] = acc[0] + values

    rows = ROWS + 4
    conv_rows(windows_of(v), w, rows, emit)
    send(h)
    center = center_of(acc[0])
    both = twice(center)
    spread = jnp.zeros((64, 128), F32)
    for y in range(rows):
        off = h[y] - both
        if 2 <= y < 2 + ROWS:
            spread = spread + off * off
        low[2 * y] = off[0:C].astype(BF16)
        high[2 * y] = off[C:].astype(BF16)
        values = cot_row(cot, y_low, y_high, y)
        low[2 * y + 1] = values[0:C]
        high[2 * y + 1] = values[C:]
        send(low, high, row=2 * y + 1)
    message((center, fold(total(spread))), msg)


def total_kernel(need, send, parts, whole):
    need(parts)
    whole[...] = jnp.sum(parts[...], axis=0)


def side_kernel(need, send, center, h1, v1, xh, g, acc):
    need(center)
    both = twice(center[...])
    lane = lanes(64)
    for y in range(ROWS):
        need(h1, row=y + 3)
        put_shifted(g, y, h1[y + 3] - both, lane)
    need(v1)
    weight_sums(g, v1, 3, acc)
    tile = folded(acc)
    for dz in range(3):
        for dy in range(3):
            xh[dz * 3 + dy] = tile(dz, dy)


def cot_row(cot, y_low, y_high, y):
    if y < 2:
        return y_low[12 + y]
    if y < 2 + ROWS:
        return cot[y - 2]
    return y_high[10 + y - ROWS]


def third_kernel(cells, need, send, place, r2, gb, cot, h2, st1, x1, xh, msg, st2):
    need(r2, gb)
    mean, inverse, _, _ = stats_of(r2[...], place, cells, st2)
    mean2, inverse2 = twice(mean), twice(inverse)
    gain2, bias2 = twice(gb[:, 2:3]), twice(gb[:, 3:4])
    plain = jnp.zeros((64, 128), F32)
    both = jnp.zeros((64, 128), F32)
    for y in range(ROWS):
        need(h2, row=y + 2)
        need(cot, row=y)
        normed = (h2[y + 2] - mean2) * inverse2
        z = normed * gain2 + bias2
        slope = cot[y].astype(F32) * act_slope(z)
        plain = plain + slope
        both = both + slope * normed
    need(st1, x1, xh)
    inverse1, own1 = st1[:, 1:2], st1[:, 4:5]
    ones = ones_of(x1)

    def xn(dz, dy):
        return inverse1 * (xh[dz * 3 + dy] + own1 * ones(dz, dy))


    rows_message((fold(total(both)), fold(total(plain))), (xn,), msg)


def output_kernel(need, send, st2, gb, h2, out):
    need(st2, gb)
    mean, inverse, _, _ = kept_stats(st2)
    mean2, scale2 = twice(mean), twice(inverse * gb[:, 2:3])
    shift2 = twice(gb[:, 3:4])
    for y in range(ROWS):
        need(h2, row=y + 2)
        out[y] = act((h2[y + 2] - mean2) * scale2 + shift2).astype(BF16)
        send(out, row=y)


def fourth_kernel(
    cells, need, send, place, r3, st2, gb, h2, x_low, x_high, cot, y_low, y_high, w, st1, h1, v2, v1, slope1, low, high, msg, t3, v, g, acc, acc1,
):
    need(r3, st2, gb)
    mean, inverse, o_low, o_high = kept_stats(st2)
    t3[...] = jnp.sum(r3[...], axis=0)
    send(t3)
    nsum, plain = sums_of(t3[0:1])
    need(y_low, y_high)
    gain, bias = gb[:, 2:3], gb[:, 3:4]
    lead = gain * inverse
    p_mean, n_mean = plain / cells, nsum / cells

    def grad(normed, c, gain, bias, lead, p_mean, n_mean):
        slope = c.astype(F32) * act_slope(normed * gain + bias)
        return lead * (slope - p_mean - normed * n_mean)

    one = (gain, bias, lead, p_mean, n_mean)
    two = tuple(twice(a) for a in one)
    mean2, inverse2 = twice(mean), twice(inverse)
    lane = lanes(64)
    rows = ROWS + 4
    for y in range(rows):
        need(h2, row=y)
        need(x_low, x_high, row=2 * y + 1)
        need(cot, row=min(max(y - 2, 0), ROWS - 1))
        g_low = grad((x_low[2 * y].astype(F32) + o_low) * inverse, x_low[2 * y + 1], *one)
        g_own = grad((h2[y] - mean2) * inverse2, cot_row(cot, y_low, y_high, y), *two)
        g_high = grad((x_high[2 * y].astype(F32) + o_high) * inverse, x_high[2 * y + 1], *one)
        both = jnp.concatenate([g_low, g_own, g_high], axis=0)
        v[y] = masked(both, kept(place, y, rows, 2))
        if 2 <= y < 2 + ROWS:
            put_shifted(g, y - 2, g_own, lane)
    need(v2)
    weight_sums(g, v2, 2, acc)

    need(h1, st1, w)
    mean, inverse, _, _ = kept_stats(st1)
    mean2, inverse2 = twice(mean), twice(inverse)
    gain2, bias2 = twice(gb[:, 0:1]), twice(gb[:, 1:2])
    sums = [jnp.zeros((64, 128), F32), jnp.zeros((64, 128), F32)]

    def emit(y, values):
        normed = (h1[y + 2] - mean2) * inverse2
        slope = values * act_slope(normed * gain2 + bias2)
        slope1[y] = slope
        low[y] = slope[0:C].astype(BF16)
        high[y] = slope[C:].astype(BF16)
        send(slope1, low, high, row=y)
        if 1 <= y < 1 + ROWS:
            sums[0] = sums[0] + slope * normed
            sums[1] = sums[1] + slope
            put_shifted(g, y - 1, slope, lane)

    conv_rows(windows_of(v), w, ROWS + 2, emit)
    send(slope1, low, high)
    need(v1)
    weight_sums(g, v1, 3, acc1)
    rows_message(
        (fold(total(sums[0])), fold(total(sums[1]))), (folded(acc1), folded(acc)), msg
    )


def owner_kernel(cells, need, send, place, r4, st1, gb, t3, x1, msg, norms, t4):
    need(st1, gb, t3, x1)
    _, inverse, _, _ = kept_stats(st1)
    t4[...] = jnp.sum(r4[...], axis=0)
    nsum, plain = sums_of(t4[0:1])
    mine = lax.broadcasted_iota(jnp.int32, (C, 1), 0) == place[6]

    def picked(column):
        return jnp.sum(jnp.where(mine, column, 0.0), axis=0, keepdims=True)

    scale = cells**-0.5
    lead = picked(gb[:, 0:1] * inverse) * scale
    third, fourth = t3[...], t4[...]
    one = fourth[1:4] - picked(plain) * (x1[1:4] / cells) - picked(nsum) * (third[1:4] / cells)
    one = lead * one
    two = fourth[4:7] * scale
    tile = jnp.concatenate([one, two, jnp.zeros((2, 128), F32)], axis=0)
    pair = twice(tile).astype(BF16)
    for k in range(0, msg.shape[0], 16):
        msg[k : k + 16] = pair
    for k, row in enumerate((fourth[0:1], third[0:1])):
        norms[2 * k : 2 * k + 1] = row[:, 0:C] * scale
        norms[2 * k + 1 : 2 * k + 2] = row[:, C : 2 * C] * scale


def finish_kernel(need, send, parts, one, two, rows):
    rows[...] = parts[0 : 3 * C * 8].astype(F32)
    for dz in range(3):
        for dy in range(3):
            for k, out in enumerate((one, two)):
                tile = rows[pl.ds(dz * C * 8 + 3 * k + dy, C, stride=8), :]
                for dx in range(3):
                    out[dx * 9 + dy * 3 + dz] = tile[:, dx * C : (dx + 1) * C]


def fifth_kernel(cells, need, send, place, t4, st1, gb, h1, slope1, s_low, s_high, w, out, v, turned):
    need(t4, st1, gb)
    mean, inverse, _, _ = kept_stats(st1)
    nsum, plain = sums_of(t4[0:1])
    mean4, inverse4 = fourfold(mean), fourfold(inverse)
    lead4 = fourfold(gb[:, 0:1] * inverse)
    p_mean4, n_mean4 = fourfold(plain / cells), fourfold(nsum / cells)
    rows = ROWS + 2
    for y in range(rows):
        need(slope1, s_low, s_high, row=y)
        need(h1, row=y + 2)
        slope = jnp.concatenate(
            [s_low[y].astype(F32), slope1[y], s_high[y].astype(F32)], axis=0
        )
        normed = (h1[y + 2] - mean4) * inverse4
        v[y] = masked(lead4 * (slope - p_mean4 - normed * n_mean4), kept(place, y, rows, 1))
    need(w)

    def emit(y, values):
        turned[:, y, :] = values

    conv_rows(windows_of(v), w, ROWS, emit)
    for i in range(C):
        for x in range(2):
            out[i, x] = turned[x * C + i].astype(BF16)
        send(out, row=i)


def pieces_of(shape):
    rows = shape[0]
    if len(shape) < 3 or rows < 32 or rows > 100:
        return [(0, rows)]
    cuts = [rows * c // 4 for c in range(5)]
    return list(zip(cuts, cuts[1:]))


def call(
    kernel, ins, outs, name, scratch=(), smem_first=True, after=(), near=0, cut=(), late=0, grant=56
):
    lead = 1 if smem_first else 0
    count_in, count_out = len(ins) - lead - near, len(outs)
    far_ins = ins[lead + near :]
    own = [any(a is b for b in cut) for a in far_ins]
    shapes = [(a.shape[0], 2 * C, 128) if c else a.shape for a, c in zip(far_ins, own)]

    def body(*refs):
        first, rest = refs[: lead + near], refs[lead + near :]
        parts = []
        for size in (count_in, len(after), count_out, count_in, count_out, 2):
            parts.append(rest[:size])
            rest = rest[size:]
        sources, _, targets, in_bufs, out_bufs, (in_sems, out_sems) = parts

        def source(k, a, b):
            return sources[k].at[a:b, C : 3 * C] if own[k] else sources[k].at[a:b]

        arriving = [
            [
                (a, b, pltpu.make_async_copy(source(k, a, b), buf.at[a:b], in_sems.at[k, c]))
                for c, (a, b) in enumerate(pieces_of(buf.shape))
            ]
            for k, buf in enumerate(in_bufs)
        ]
        leaving = [
            [
                (a, b, pltpu.make_async_copy(buf.at[a:b], targets[k].at[a:b], out_sems.at[k, c]))
                for c, (a, b) in enumerate(pieces_of(buf.shape))
            ]
            for k, buf in enumerate(out_bufs)
        ]
        early, later = arriving[: count_in - late], arriving[count_in - late :]
        for group in (early, later):
            for c in range(4):
                for pieces in group:
                    if c < len(pieces):
                        pieces[c][2].start()
        waiting, held = [list(pieces) for pieces in arriving], [list(pieces) for pieces in leaving]

        def need(*wanted, row=None):
            for ref in wanted:
                for k, buf in enumerate(in_bufs):
                    while buf is ref and waiting[k] and (row is None or waiting[k][0][0] <= row):
                        waiting[k].pop(0)[2].wait()

        def send(*ready, row=None):
            for ref in ready:
                for k, buf in enumerate(out_bufs):
                    while buf is ref and held[k] and (row is None or held[k][0][1] <= row + 1):
                        held[k].pop(0)[2].start()

        kernel(need, send, *first, *in_bufs, *out_bufs, *rest)
        send(*out_bufs)
        need(*in_bufs)
        for pieces in leaving:
            for piece in pieces:
                piece[2].wait()

    far = pl.BlockSpec(memory_space=pltpu.HBM)
    return pl.pallas_call(
        body,
        out_shape=outs,
        in_specs=[SM] * lead
        + [pl.BlockSpec(memory_space=pltpu.VMEM)] * near
        + [far] * (count_in + len(after)),
        out_specs=[far] * count_out,
        scratch_shapes=[
            *[pltpu.VMEM(shape, a.dtype) for shape, a in zip(shapes, far_ins)],
            *[pltpu.VMEM(a.shape, a.dtype) for a in outs],
            pltpu.SemaphoreType.DMA((max(count_in, 1), 4)),
            pltpu.SemaphoreType.DMA((count_out, 4)),
            *scratch,
        ],
        compiler_params=pltpu.CompilerParams(vmem_limit_bytes=grant * 1024 * 1024),
        cost_estimate=pl.CostEstimate(
            flops=2_000_000_000, bytes_accessed=6_000_000, transcendentals=0
        ),
        name=name,
    )(*ins, *after)


def up(values, axes):
    count = lax.axis_size(axes)
    return lax.ppermute(values, axes, [(i, i + 1) for i in range(count - 1)])


def down(values, axes):
    count = lax.axis_size(axes)
    return lax.ppermute(values, axes, [(i + 1, i) for i in range(count - 1)])


def share(msg):
    return lax.all_to_all(msg, ALL[::-1], 0, 0, tiled=True)


def rank_of(gx, gy):
    rank = gy % lax.axis_size(GY[1])
    for part, axis in (
        (gy // lax.axis_size(GY[1]), GY[0]),
        (gx % lax.axis_size(GX[1]), GX[1]),
        (gx // lax.axis_size(GX[1]), GX[0]),
    ):
        rank = rank * lax.axis_size(axis) + part
    return rank


def local(features, kernel_one, gain_one, bias_one, kernel_two, gain_two, bias_two, cotangent):
    count_x, count_y = lax.axis_size(GX), lax.axis_size(GY)
    count = count_x * count_y
    cells = float(count * 2 * ROWS * 128)
    gx, gy = lax.axis_index(GX), lax.axis_index(GY)
    at = rank_of(gx, gy)
    beside = [rank_of(jnp.clip(gx + k, 0, count_x - 1), gy) for k in (-1, 1)]
    edges = [gx > 0, gx < count_x - 1, gy > 0, gy < count_y - 1]
    place = jnp.stack([*beside, *edges, at % C, at]).astype(jnp.int32)
    gb = jnp.stack([gain_one, bias_one, gain_two, bias_two], axis=1)

    own = jnp.transpose(features, (2, 1, 0, 3)).reshape(ROWS, 64, 128)
    cot = jnp.transpose(cotangent, (2, 1, 0, 3)).reshape(ROWS, 64, 128)

    def rims(rows):
        return [sh((rows, C, 128), BF16)] * 2

    msg, four, wide = (sh((count, *tile), F32) for tile in ((128,), (4, 128), (8, 128)))
    stats = sh((C, 128), F32)
    corr = (pltpu.VMEM((192, ROWS * 128), BF16), pltpu.VMEM((384, 192), F32))

    x_low, x_high = up(own, GX), down(own, GX)
    taps = [
        jnp.transpose(k, (2, 3, 4, 0, 1)).reshape(27, C, C) for k in (kernel_one, kernel_two)
    ]
    matrices = [sh((192, 384), BF16)] * 2
    w1, w2 = call(weights_kernel, taps, matrices, "weights", smem_first=False)
    b1, b2 = call(flipped_kernel, taps, matrices, "flipped", smem_first=False)
    y_up, y_down = call(
        pack_kernel,
        (x_low, x_high, own, cot),
        [sh((14, 64, 128), BF16)] * 2,
        "pack",
        smem_first=False,
        after=(w1,),
        near=2,
        grant=16,
    )
    y_low, y_high = up(y_up, GY), down(y_down, GY)

    v1, h1, m1, x1_own, center = call(
        first_kernel,
        (y_low, y_high, w1, own, x_low, x_high),
        [sh((40, 128, 128), BF16), sh((38, 128, 128), F32), four, sh((16, 128), F32), stats],
        "conv_one",
        smem_first=False,
    )
    r1 = share(m1)

    (xh,) = call(
        side_kernel,
        (center, h1, v1),
        [sh((9, C, 128), F32)],
        "hidden_features",
        scratch=corr,
        smem_first=False,
        cut=(h1,),
    )

    v2, h2, low, high, m2, st1 = call(
        lambda *refs: second_kernel(cells, *refs),
        (place, r1, gb, h1, cot, y_low, y_high, w2),
        [
            sh((38, 128, 128), BF16), sh((36, 64, 128), F32), *rims(72), msg, stats,
        ],
        "conv_two",
        after=(xh,),
    )
    h2_low, h2_high = up(high, GX), down(low, GX)
    r2 = share(m2)
    (x1,) = call(
        total_kernel, (r1,), [sh((4, 128), F32)], "total", smem_first=False, after=(st1,)
    )
    m3, st2 = call(
        lambda *refs: third_kernel(cells, *refs),
        (place, r2, gb, cot, h2, st1, x1_own, xh),
        [four, stats],
        "slope_two",
        after=(x1,),
    )
    r3 = share(m3)
    (output,) = call(
        output_kernel, (st2, gb, h2), [sh((ROWS, 64, 128), BF16)], "output", smem_first=False
    )

    rows_out = output

    slope1, low, high, m4, t3 = call(
        lambda *refs: fourth_kernel(cells, *refs),
        (
            place, r3, st2, gb, h2, h2_low, h2_high, cot, y_low, y_high,
            b2, st1, h1, v2, v1,
        ),
        [sh((34, 64, 128), F32), *rims(34), wide, sh((4, 128), F32)],
        "back_two",
        after=(rows_out,),
        late=5,
        cut=(h1,),
        scratch=(pltpu.VMEM((36, 128, 128), BF16), *corr, corr[1]),
    )
    s_low, s_high = up(high, GX), down(low, GX)
    r4 = share(m4)

    def back(rows):
        return jnp.transpose(rows.reshape(ROWS, 2, C, 128), (2, 1, 0, 3))

    output = back(rows_out)

    m5, norm_grads, t4 = call(
        lambda *refs: owner_kernel(cells, *refs),
        (place, r4, st1, gb, t3, x1),
        [sh((count * 8, 128), BF16), sh((4, C), F32), sh((8, 128), F32)],
        "own_rows",
        near=1,
        grant=16,
        after=(s_low, s_high, output),
    )
    r5 = share(m5.reshape(count, 8, 128)).reshape(count * 8, 128)
    (grad,) = call(
        lambda *refs: fifth_kernel(cells, *refs),
        (place, t4, st1, gb, h1, slope1, s_low, s_high, b1),
        [sh((C, 2, ROWS, 128), BF16)],
        "back_one",
        scratch=(pltpu.VMEM((34, 128, 128), BF16), pltpu.VMEM((64, ROWS, 128), F32)),
    )
    grads = call(
        finish_kernel,
        (r5,),
        [sh((27, C, C), F32)] * 2,
        "finish",
        scratch=(pltpu.VMEM((3 * C * 8, 128), F32),),
        smem_first=False,
        near=1,
        grant=16,
    )
    one, two = [jnp.transpose(k.reshape(3, 3, 3, C, C), (3, 4, 0, 1, 2)) for k in grads]

    return output, grad, one, two, norm_grads


def solution(mesh):
    nx, ny = mesh.devices.shape
    parts = (4, nx // 4, ny // 2, 2)
    split = Mesh(mesh.devices.reshape(parts), ALL)
    spec = P(None, GX, GY, None)
    in_specs = (spec, P(), P(), P(), P(), P(), P(), spec)
    out_specs = (spec, spec, P(), P(), P())
    return jax.shard_map(local, mesh=split, in_specs=in_specs, out_specs=out_specs, check_vma=False)
```

```python
import jax
import jax.numpy as jnp
from jax import lax
from jax.experimental import pallas as pl
from jax.experimental.pallas import tpu as pltpu
from jax.sharding import Mesh
from jax.sharding import PartitionSpec as P

GX = ("gx_0", "gx_1")
GY = ("gy_0", "gy_1")
ALL = GX + GY

EPSILON = 1e-05
C = 32
ROWS = 32
F32 = jnp.float32
BF16 = jnp.bfloat16
LN2 = 0.6931471805599453
SM = pl.BlockSpec(memory_space=pltpu.SMEM)


def sh(shape, kind):
    return jax.ShapeDtypeStruct(shape, kind)


def from_below(values, lane):
    return jnp.where(lane == 0, 0.0, pltpu.roll(values, 1, 1))


def from_above(values, lane):
    return jnp.where(lane == 127, 0.0, pltpu.roll(values, 127, 1))


def lanes(rows):
    return lax.broadcasted_iota(jnp.int32, (rows, 128), 1)


def windows_of(*refs):
    if len(refs) == 1:
        return lambda y: refs[0][y : y + 3].reshape(384, 128)
    return lambda y: jnp.concatenate([rows(y + k) for k in range(3) for rows in refs], axis=0)


def joined(k, middle, below, above):
    def row(y):
        if y < 4:
            return below[3 * y + k]
        if y < 4 + ROWS:
            return middle[y - 4]
        return above[3 * (y - 4 - ROWS) + k]

    return row


def conv_rows(window, w_ref, rows, emit):
    lane = lanes(64)
    weights = w_ref[...]
    for y in range(0, rows, 2):
        both = jnp.concatenate([window(y), window(y + 1)], axis=1)
        product = jnp.dot(weights, both, preferred_element_type=F32)
        for k in range(2):
            part = product[:, k * 128 : (k + 1) * 128]
            emit(
                y + k,
                part[64:128] + from_below(part[0:64], lane) + from_above(part[128:192], lane),
            )


def fold(column):
    return column[0:C] + column[C : 2 * C]


def total(values):
    return jnp.sum(values, axis=1, keepdims=True)


def twice(column):
    return jnp.concatenate([column, column], axis=0)


def fourfold(column):
    return twice(twice(column))


def message(columns, msg_ref):
    count = msg_ref.shape[0]
    spare = jnp.zeros((128 - C * len(columns), 1), F32)
    column = jnp.concatenate([*columns, spare], axis=0)
    msg_ref[...] = jnp.transpose(jnp.broadcast_to(column, (128, count)))


def as_row(column):
    return jnp.transpose(jnp.broadcast_to(column, (128, 128)))[0:1]


def rows_message(columns, groups, msg_ref):
    spare = jnp.zeros((128 - C * len(columns), 1), F32)
    row = as_row(jnp.concatenate([*columns, spare], axis=0))
    height = msg_ref.shape[1]
    at = lax.broadcasted_iota(jnp.int32, (height, 128), 0)
    tile = jnp.where(at == 0, jnp.broadcast_to(row, (height, 128)), 0.0)
    msg_ref[...] = jnp.broadcast_to(tile[None], msg_ref.shape)
    for k, group in enumerate(groups):
        for dz in range(3):
            for dy in range(3):
                msg_ref[dz * C : (dz + 1) * C, 1 + 3 * k + dy, :] = group(dz, dy)


def center_of(acc):
    return fold(total(acc)) / (2 * ROWS * 128)


def stats_of(rows, place_ref, cells, st_ref):
    parts = jnp.transpose(rows)
    centers = parts[0:C]
    count = parts.shape[1]
    mean = total(centers) / count
    off = centers - mean
    spread = (total(parts[C : 2 * C]) + (2 * ROWS * 128) * total(off * off)) / cells
    at = lax.broadcasted_iota(jnp.int32, centers.shape, 1)
    low = total(jnp.where(at == place_ref[0], off, 0.0))
    high = total(jnp.where(at == place_ref[1], off, 0.0))
    own = total(jnp.where(at == place_ref[7], off, 0.0))
    found = (mean, lax.rsqrt(spread + EPSILON), low, high)
    st_ref[...] = jnp.concatenate([*found, own, jnp.zeros((C, 123), F32)], axis=1)
    return found


def kept_stats(st_ref):
    return tuple(st_ref[:, k : k + 1] for k in range(4))


def sums_of(row):
    parts = jnp.transpose(jnp.broadcast_to(row, (128, 128)))[:, 0:1]
    return parts[0:C], parts[C : 2 * C]


def feature_sums(v, first):
    lane = lanes(128)
    inner = v[first + 2].astype(F32)
    for y in range(first + 3, first + ROWS):
        inner = inner + v[y].astype(F32)
    ends = [v[first + y].astype(F32) for y in (0, 1, ROWS, ROWS + 1)]
    windows = (inner + ends[0] + ends[1], inner + ends[1] + ends[2], inner + ends[2] + ends[3])
    columns = []
    for dz in range(3):
        for dy in range(3):
            values = windows[dy]
            if dz == 0:
                values = jnp.where(lane == 127, 0.0, values)
            if dz == 2:
                values = jnp.where(lane == 0, 0.0, values)
            column = total(values)
            columns.append(column + jnp.concatenate([column[C:], column[:C]], axis=0))
    return jnp.transpose(jnp.concatenate(columns + [jnp.zeros((128, 119), F32)], axis=1))[0:16]


def ones_of(x1):
    return lambda dz, dy: jnp.broadcast_to(x1[dz * 3 + dy : dz * 3 + dy + 1], (C, 128))


def act(z):
    e = jnp.exp2(jnp.abs(z) * (-8.0 / LN2))
    soft = jnp.maximum(z, 0.0) * 0.99 + jnp.log2(1.0 + e) * (0.99 * LN2 / 8.0)
    return 0.01 * z + soft


def act_slope(z):
    return 0.505 + 0.495 * jnp.tanh(4.0 * z)


def kept(place_ref, y, rows, margin):
    low = place_ref[2].astype(F32)
    high = place_ref[3].astype(F32)
    if y < margin:
        edge = place_ref[4].astype(F32)
    elif y >= rows - margin:
        edge = place_ref[5].astype(F32)
    else:
        return low, None, high
    return low * edge, edge, high * edge


def masked(values, factors):
    f_low, f_own, f_high = factors
    own = values[C : 3 * C]
    own = own if f_own is None else own * f_own
    return jnp.concatenate([values[0:C] * f_low, own, values[3 * C :] * f_high], axis=0).astype(
        BF16
    )


def weight_sums(g_ref, v_ref, first, acc_ref):
    step = 4
    for y in range(0, ROWS, step):
        window = jnp.concatenate(
            [v_ref[first + y + k : first + y + k + 3].reshape(384, 128) for k in range(step)], axis=1
        )
        product = lax.dot_general(
            window,
            g_ref[:, y * 128 : (y + step) * 128],
            (((1,), (1,)), ((), ())),
            preferred_element_type=F32,
        )
        if y == 0:
            acc_ref[...] = product
        else:
            acc_ref[...] += product


def folded(acc_ref):
    turned = [jnp.transpose(acc_ref[dy * 128 : dy * 128 + 128]) for dy in range(3)]

    def tile(dz, dy):
        both = turned[dy][dz * 64 : dz * 64 + 64]
        return both[0:C] + pltpu.roll(both[C:], 96, 1)

    return tile


def put_shifted(g_ref, y, values, lane):
    at = slice(y * 128, (y + 1) * 128)
    g_ref[0:64, at] = from_above(values, lane).astype(BF16)
    g_ref[64:128, at] = values.astype(BF16)
    g_ref[128:192, at] = from_below(values, lane).astype(BF16)


def pack_kernel(need, send, x_low, x_high, own, cot, up_ref, down_ref):
    need(own, cot)
    for y in range(4):
        for k, part in enumerate((x_low, own, x_high)):
            up_ref[3 * y + k] = part[ROWS - 4 + y]
            down_ref[3 * y + k] = part[y]
    up_ref[12:14] = cot[ROWS - 2 : ROWS]
    down_ref[12:14] = cot[0:2]


def weights_kernel(need, send, k1, k2, w1, w2):
    need(k1, k2)
    row = lax.broadcasted_iota(jnp.int32, (C, 128), 0)
    col = lax.broadcasted_iota(jnp.int32, (C, 128), 1)
    for k_ref, w_ref in ((k1, w1), (k2, w2)):
        lined = jnp.zeros((9 * C, 128), F32)
        for dx in range(3):
            spot = jnp.where(row + dx * C == col, 1.0, 0.0).astype(BF16)
            lined = lined + jnp.dot(
                k_ref[dx * 9 : dx * 9 + 9].reshape(9 * C, C), spot, preferred_element_type=F32
            )
        for dy in range(3):
            for dz in range(3):
                t = dy * 3 + dz
                put_tile(w_ref, dz, dy, lined[t * C : t * C + C])


def flipped_kernel(need, send, k1, k2, b1, b2):
    need(k1, k2)
    row = lax.broadcasted_iota(jnp.int32, (C, 128), 0)
    col = lax.broadcasted_iota(jnp.int32, (C, 128), 1)
    eye = jnp.where(row == col, 1.0, 0.0)[:, 0:C].astype(BF16)
    zero = jnp.zeros((C, C), BF16)
    for k_ref, b_ref in ((k1, b1), (k2, b2)):
        stack = []
        for t in range(9):
            stack += [k_ref[18 + t], k_ref[9 + t], k_ref[t], zero]
        turned = lax.dot_general(
            eye,
            jnp.concatenate(stack, axis=0),
            (((1,), (1,)), ((), ())),
            preferred_element_type=F32,
        )
        for dy in range(3):
            for dz in range(3):
                t = 8 - dy * 3 - dz
                put_tile(b_ref, dz, dy, turned[:, t * 128 : t * 128 + 128])


def put_tile(ref, dz, dy, tile):
    here = slice(dy * 128, dy * 128 + 128)
    ref[dz * 64 : dz * 64 + C, here] = tile.astype(BF16)
    ref[dz * 64 + C : dz * 64 + 64, here] = pltpu.roll(tile, C, 1).astype(BF16)


def first_kernel(
    need, send, y_low, y_high, w, own, x_low, x_high, v, h, msg, x1, center_out
):
    need(own, x_low, x_high, y_low, y_high, w)
    low = joined(0, x_low, y_low, y_high)
    own = joined(1, own, y_low, y_high)
    high = joined(2, x_high, y_low, y_high)
    acc = [jnp.zeros((64, 128), F32), jnp.zeros((64, 128), F32)]
    for k, pair in enumerate(((low, own), (own, high))):

        def emit(y, values, k=k):
            h[y, 64 * k : 64 * k + 64] = values
            if k == 1:
                send(h, row=y)
            if 3 <= y < 3 + ROWS:
                acc[k] = acc[k] + values

        conv_rows(windows_of(*pair), w, ROWS + 6, emit)
    send(h)
    for y in range(ROWS + 8):
        v[y] = jnp.concatenate([low(y)[C:], own(y), high(y)[0:C]], axis=0)
        send(v, row=y)
    send(v)
    center = center_of(jnp.concatenate([acc[0][C:], acc[1][0:C]], axis=0))
    both = twice(center)
    spread = jnp.zeros((64, 128), F32)
    for y in range(3, 3 + ROWS):
        off = h[y, C : 3 * C] - both
        spread = spread + off * off
    center_out[...] = jnp.broadcast_to(center, (C, 128))
    x1[...] = feature_sums(v, 3)
    send(center_out, x1)
    rows_message((center, fold(total(spread))), (ones_of(x1),), msg)


def second_kernel(
    cells, need, send, place, r1, gb, h1, cot, y_low, y_high, w, v, h, low, high, msg, st1
):
    need(r1, gb)
    mean, inverse, _, _ = stats_of(r1[:, 0, :], place, cells, st1)
    send(st1)
    mean4, scale4 = fourfold(mean), fourfold(inverse * gb[:, 0:1])
    shift4 = fourfold(gb[:, 1:2])
    rows = ROWS + 6
    for y in range(rows):
        need(h1, row=y)
        v[y] = masked(act((h1[y] - mean4) * scale4 + shift4), kept(place, y, rows, 3))
        send(v, row=y)
    need(w, cot, y_low, y_high)
    acc = [jnp.zeros((64, 128), F32)]

    def emit(y, values):
        h[y] = values
        send(h, row=y)
        if 2 <= y < 2 + ROWS:
            acc[0] = acc[0] + values

    rows = ROWS + 4
    conv_rows(windows_of(v), w, rows, emit)
    send(h)
    center = center_of(acc[0])
    both = twice(center)
    spread = jnp.zeros((64, 128), F32)
    for y in range(rows):
        off = h[y] - both
        if 2 <= y < 2 + ROWS:
            spread = spread + off * off
        low[2 * y] = off[0:C].astype(BF16)
        high[2 * y] = off[C:].astype(BF16)
        values = cot_row(cot, y_low, y_high, y)
        low[2 * y + 1] = values[0:C]
        high[2 * y + 1] = values[C:]
        send(low, high, row=2 * y + 1)
    message((center, fold(total(spread))), msg)


def total_kernel(need, send, parts, whole):
    need(parts)
    whole[...] = jnp.sum(parts[...], axis=0)


def side_kernel(need, send, center, h1, v1, xh, g, acc):
    need(center)
    both = twice(center[...])
    lane = lanes(64)
    for y in range(ROWS):
        need(h1, row=y + 3)
        put_shifted(g, y, h1[y + 3] - both, lane)
    need(v1)
    weight_sums(g, v1, 3, acc)
    tile = folded(acc)
    for dz in range(3):
        for dy in range(3):
            xh[dz * 3 + dy] = tile(dz, dy)


def cot_row(cot, y_low, y_high, y):
    if y < 2:
        return y_low[12 + y]
    if y < 2 + ROWS:
        return cot[y - 2]
    return y_high[10 + y - ROWS]


def third_kernel(cells, need, send, place, r2, gb, cot, h2, st1, x1, xh, msg, st2):
    need(r2, gb)
    mean, inverse, _, _ = stats_of(r2[...], place, cells, st2)
    mean2, inverse2 = twice(mean), twice(inverse)
    gain2, bias2 = twice(gb[:, 2:3]), twice(gb[:, 3:4])
    plain = jnp.zeros((64, 128), F32)
    both = jnp.zeros((64, 128), F32)
    for y in range(ROWS):
        need(h2, row=y + 2)
        need(cot, row=y)
        normed = (h2[y + 2] - mean2) * inverse2
        z = normed * gain2 + bias2
        slope = cot[y].astype(F32) * act_slope(z)
        plain = plain + slope
        both = both + slope * normed
    need(st1, x1, xh)
    inverse1, own1 = st1[:, 1:2], st1[:, 4:5]
    ones = ones_of(x1)

    def xn(dz, dy):
        return inverse1 * (xh[dz * 3 + dy] + own1 * ones(dz, dy))


    rows_message((fold(total(both)), fold(total(plain))), (xn,), msg)


def active_kernel(need, send, st2, gb, h2, cot, v2, s2, n2, a1, g, acc):
    need(st2, gb)
    mean, inverse, _, _ = kept_stats(st2)
    mean2, inverse2 = twice(mean), twice(inverse)
    gain2, bias2 = twice(gb[:, 2:3]), twice(gb[:, 3:4])
    lane = lanes(64)

    def sums_to(out):
        weight_sums(g, v2, 2, acc)
        tile = folded(acc)
        for dz in range(3):
            for dy in range(3):
                out[dz * 3 + dy] = tile(dz, dy)
        send(out)

    for y in range(ROWS):
        need(h2, row=y + 2)
        put_shifted(g, y, (h2[y + 2] - mean2) * inverse2, lane)
    need(v2)
    sums_to(n2)
    for y in range(ROWS):
        need(cot, row=y)
        normed = (h2[y + 2] - mean2) * inverse2
        put_shifted(g, y, cot[y].astype(F32) * act_slope(normed * gain2 + bias2), lane)
    sums_to(s2)
    a1[...] = feature_sums(v2, 2)


def output_kernel(need, send, st2, gb, h2, out):
    need(st2, gb)
    mean, inverse, _, _ = kept_stats(st2)
    mean2, scale2 = twice(mean), twice(inverse * gb[:, 2:3])
    shift2 = twice(gb[:, 3:4])
    for y in range(ROWS):
        need(h2, row=y + 2)
        out[y] = act((h2[y + 2] - mean2) * scale2 + shift2).astype(BF16)
        send(out, row=y)


def fourth_kernel(
    cells, need, send, place, r3, st2, gb, h2, x_low, x_high, cot, y_low, y_high, w, st1, h1, v1, s2, n2, a1,
    slope1, low, high, msg, t3, v, g, acc,
):
    need(r3, st2, gb)
    mean, inverse, o_low, o_high = kept_stats(st2)
    t3[...] = jnp.sum(r3[...], axis=0)
    send(t3)
    nsum, plain = sums_of(t3[0:1])
    need(y_low, y_high)
    gain, bias = gb[:, 2:3], gb[:, 3:4]
    lead = gain * inverse
    p_mean, n_mean = plain / cells, nsum / cells

    def grad(normed, c, gain, bias, lead, p_mean, n_mean):
        slope = c.astype(F32) * act_slope(normed * gain + bias)
        return lead * (slope - p_mean - normed * n_mean)

    one = (gain, bias, lead, p_mean, n_mean)
    both = tuple(twice(a) for a in one)
    mean2, inverse2 = twice(mean), twice(inverse)
    lane = lanes(64)
    rows = ROWS + 4
    for y in range(rows):
        need(h2, row=y)
        need(x_low, x_high, row=2 * y + 1)
        need(cot, row=min(max(y - 2, 0), ROWS - 1))
        g_low = grad((x_low[2 * y].astype(F32) + o_low) * inverse, x_low[2 * y + 1], *one)
        g_own = grad((h2[y] - mean2) * inverse2, cot_row(cot, y_low, y_high, y), *both)
        g_high = grad((x_high[2 * y].astype(F32) + o_high) * inverse, x_high[2 * y + 1], *one)
        planes = jnp.concatenate([g_low, g_own, g_high], axis=0)
        v[y] = masked(planes, kept(place, y, rows, 2))
    need(h1, st1, w)
    mean, inverse, _, _ = kept_stats(st1)
    mean2, inverse2 = twice(mean), twice(inverse)
    gain2, bias2 = twice(gb[:, 0:1]), twice(gb[:, 1:2])
    sums = [jnp.zeros((64, 128), F32), jnp.zeros((64, 128), F32)]

    def emit(y, values):
        normed = (h1[y + 2] - mean2) * inverse2
        slope = values * act_slope(normed * gain2 + bias2)
        slope1[y] = slope
        low[y] = slope[0:C].astype(BF16)
        high[y] = slope[C:].astype(BF16)
        send(slope1, low, high, row=y)
        if 1 <= y < 1 + ROWS:
            sums[0] = sums[0] + slope * normed
            sums[1] = sums[1] + slope
            put_shifted(g, y - 1, slope, lane)

    conv_rows(windows_of(v), w, ROWS + 2, emit)
    send(slope1, low, high)
    need(v1)
    weight_sums(g, v1, 3, acc)
    need(s2, n2, a1)
    ones = ones_of(a1)

    def two(dz, dy):
        k = dz * 3 + dy
        return lead * (s2[k] - p_mean * ones(dz, dy) - n_mean * n2[k])

    rows_message(
        (fold(total(sums[0])), fold(total(sums[1]))), (folded(acc), two), msg
    )


def owner_kernel(cells, need, send, place, r4, st1, gb, t3, x1, msg, norms, t4):
    need(st1, gb, t3, x1)
    _, inverse, _, _ = kept_stats(st1)
    t4[...] = jnp.sum(r4[...], axis=0)
    nsum, plain = sums_of(t4[0:1])
    mine = lax.broadcasted_iota(jnp.int32, (C, 1), 0) == place[6]

    def picked(column):
        return jnp.sum(jnp.where(mine, column, 0.0), axis=0, keepdims=True)

    scale = cells**-0.5
    lead = picked(gb[:, 0:1] * inverse) * scale
    third, fourth = t3[...], t4[...]
    one = fourth[1:4] - picked(plain) * (x1[1:4] / cells) - picked(nsum) * (third[1:4] / cells)
    one = lead * one
    two = fourth[4:7] * scale
    tile = jnp.concatenate([one, two, jnp.zeros((2, 128), F32)], axis=0)
    pair = twice(tile).astype(BF16)
    for k in range(0, msg.shape[0], 16):
        msg[k : k + 16] = pair
    for k, row in enumerate((fourth[0:1], third[0:1])):
        norms[2 * k : 2 * k + 1] = row[:, 0:C] * scale
        norms[2 * k + 1 : 2 * k + 2] = row[:, C : 2 * C] * scale


def finish_kernel(need, send, parts, one, two, rows):
    rows[...] = parts[0 : 3 * C * 8].astype(F32)
    for dz in range(3):
        for dy in range(3):
            for k, out in enumerate((one, two)):
                tile = rows[pl.ds(dz * C * 8 + 3 * k + dy, C, stride=8), :]
                for dx in range(3):
                    out[dx * 9 + dy * 3 + dz] = tile[:, dx * C : (dx + 1) * C]


def fifth_kernel(cells, need, send, place, t4, st1, gb, h1, slope1, s_low, s_high, w, out, v, turned):
    need(t4, st1, gb)
    mean, inverse, _, _ = kept_stats(st1)
    nsum, plain = sums_of(t4[0:1])
    mean4, inverse4 = fourfold(mean), fourfold(inverse)
    lead4 = fourfold(gb[:, 0:1] * inverse)
    p_mean4, n_mean4 = fourfold(plain / cells), fourfold(nsum / cells)
    rows = ROWS + 2
    for y in range(rows):
        need(slope1, s_low, s_high, row=y)
        need(h1, row=y + 2)
        slope = jnp.concatenate(
            [s_low[y].astype(F32), slope1[y], s_high[y].astype(F32)], axis=0
        )
        normed = (h1[y + 2] - mean4) * inverse4
        v[y] = masked(lead4 * (slope - p_mean4 - normed * n_mean4), kept(place, y, rows, 1))
    need(w)

    def emit(y, values):
        turned[:, y, :] = values

    conv_rows(windows_of(v), w, ROWS, emit)
    for i in range(C):
        for x in range(2):
            out[i, x] = turned[x * C + i].astype(BF16)
        send(out, row=i)


def pieces_of(shape):
    rows = shape[0]
    if len(shape) < 3 or rows < 32 or rows > 100:
        return [(0, rows)]
    cuts = [rows * c // 4 for c in range(5)]
    return list(zip(cuts, cuts[1:]))


def call(
    kernel, ins, outs, name, scratch=(), smem_first=True, after=(), near=0, cut=(), late=0, grant=56
):
    lead = 1 if smem_first else 0
    count_in, count_out = len(ins) - lead - near, len(outs)
    far_ins = ins[lead + near :]
    own = [any(a is b for b in cut) for a in far_ins]
    shapes = [(a.shape[0], 2 * C, 128) if c else a.shape for a, c in zip(far_ins, own)]

    def body(*refs):
        first, rest = refs[: lead + near], refs[lead + near :]
        parts = []
        for size in (count_in, len(after), count_out, count_in, count_out, 2):
            parts.append(rest[:size])
            rest = rest[size:]
        sources, _, targets, in_bufs, out_bufs, (in_sems, out_sems) = parts

        def source(k, a, b):
            return sources[k].at[a:b, C : 3 * C] if own[k] else sources[k].at[a:b]

        arriving = [
            [
                (a, b, pltpu.make_async_copy(source(k, a, b), buf.at[a:b], in_sems.at[k, c]))
                for c, (a, b) in enumerate(pieces_of(buf.shape))
            ]
            for k, buf in enumerate(in_bufs)
        ]
        leaving = [
            [
                (a, b, pltpu.make_async_copy(buf.at[a:b], targets[k].at[a:b], out_sems.at[k, c]))
                for c, (a, b) in enumerate(pieces_of(buf.shape))
            ]
            for k, buf in enumerate(out_bufs)
        ]
        early, later = arriving[: count_in - late], arriving[count_in - late :]
        for group in (early, later):
            for c in range(4):
                for pieces in group:
                    if c < len(pieces):
                        pieces[c][2].start()
        waiting, held = [list(pieces) for pieces in arriving], [list(pieces) for pieces in leaving]

        def need(*wanted, row=None):
            for ref in wanted:
                for k, buf in enumerate(in_bufs):
                    while buf is ref and waiting[k] and (row is None or waiting[k][0][0] <= row):
                        waiting[k].pop(0)[2].wait()

        def send(*ready, row=None):
            for ref in ready:
                for k, buf in enumerate(out_bufs):
                    while buf is ref and held[k] and (row is None or held[k][0][1] <= row + 1):
                        held[k].pop(0)[2].start()

        kernel(need, send, *first, *in_bufs, *out_bufs, *rest)
        send(*out_bufs)
        need(*in_bufs)
        for pieces in leaving:
            for piece in pieces:
                piece[2].wait()

    far = pl.BlockSpec(memory_space=pltpu.HBM)
    return pl.pallas_call(
        body,
        out_shape=outs,
        in_specs=[SM] * lead
        + [pl.BlockSpec(memory_space=pltpu.VMEM)] * near
        + [far] * (count_in + len(after)),
        out_specs=[far] * count_out,
        scratch_shapes=[
            *[pltpu.VMEM(shape, a.dtype) for shape, a in zip(shapes, far_ins)],
            *[pltpu.VMEM(a.shape, a.dtype) for a in outs],
            pltpu.SemaphoreType.DMA((max(count_in, 1), 4)),
            pltpu.SemaphoreType.DMA((count_out, 4)),
            *scratch,
        ],
        compiler_params=pltpu.CompilerParams(vmem_limit_bytes=grant * 1024 * 1024),
        cost_estimate=pl.CostEstimate(
            flops=2_000_000_000, bytes_accessed=6_000_000, transcendentals=0
        ),
        name=name,
    )(*ins, *after)


def up(values, axes):
    count = lax.axis_size(axes)
    return lax.ppermute(values, axes, [(i, i + 1) for i in range(count - 1)])


def down(values, axes):
    count = lax.axis_size(axes)
    return lax.ppermute(values, axes, [(i + 1, i) for i in range(count - 1)])


def share(msg):
    return lax.all_to_all(msg, ALL[::-1], 0, 0, tiled=True)


def rank_of(gx, gy):
    rank = gy % lax.axis_size(GY[1])
    for part, axis in (
        (gy // lax.axis_size(GY[1]), GY[0]),
        (gx % lax.axis_size(GX[1]), GX[1]),
        (gx // lax.axis_size(GX[1]), GX[0]),
    ):
        rank = rank * lax.axis_size(axis) + part
    return rank


def local(features, kernel_one, gain_one, bias_one, kernel_two, gain_two, bias_two, cotangent):
    count_x, count_y = lax.axis_size(GX), lax.axis_size(GY)
    count = count_x * count_y
    cells = float(count * 2 * ROWS * 128)
    gx, gy = lax.axis_index(GX), lax.axis_index(GY)
    at = rank_of(gx, gy)
    beside = [rank_of(jnp.clip(gx + k, 0, count_x - 1), gy) for k in (-1, 1)]
    edges = [gx > 0, gx < count_x - 1, gy > 0, gy < count_y - 1]
    place = jnp.stack([*beside, *edges, at % C, at]).astype(jnp.int32)
    gb = jnp.stack([gain_one, bias_one, gain_two, bias_two], axis=1)

    own = jnp.transpose(features, (2, 1, 0, 3)).reshape(ROWS, 64, 128)
    cot = jnp.transpose(cotangent, (2, 1, 0, 3)).reshape(ROWS, 64, 128)

    def rims(rows):
        return [sh((rows, C, 128), BF16)] * 2

    msg, four, wide = (sh((count, *tile), F32) for tile in ((128,), (4, 128), (8, 128)))
    stats = sh((C, 128), F32)
    corr = (pltpu.VMEM((192, ROWS * 128), BF16), pltpu.VMEM((384, 192), F32))

    x_low, x_high = up(own, GX), down(own, GX)
    taps = [
        jnp.transpose(k, (2, 3, 4, 0, 1)).reshape(27, C, C) for k in (kernel_one, kernel_two)
    ]
    matrices = [sh((192, 384), BF16)] * 2
    w1, w2 = call(weights_kernel, taps, matrices, "weights", smem_first=False)
    b1, b2 = call(flipped_kernel, taps, matrices, "flipped", smem_first=False)
    y_up, y_down = call(
        pack_kernel,
        (x_low, x_high, own, cot),
        [sh((14, 64, 128), BF16)] * 2,
        "pack",
        smem_first=False,
        after=(w1, b1),
        near=2,
        grant=16,
    )
    y_low, y_high = up(y_up, GY), down(y_down, GY)

    v1, h1, m1, x1_own, center = call(
        first_kernel,
        (y_low, y_high, w1, own, x_low, x_high),
        [sh((40, 128, 128), BF16), sh((38, 128, 128), F32), four, sh((16, 128), F32), stats],
        "conv_one",
        smem_first=False,
    )
    r1 = share(m1)

    (xh,) = call(
        side_kernel,
        (center, h1, v1),
        [sh((9, C, 128), F32)],
        "hidden_features",
        scratch=corr,
        smem_first=False,
        cut=(h1,),
    )

    v2, h2, low, high, m2, st1 = call(
        lambda *refs: second_kernel(cells, *refs),
        (place, r1, gb, h1, cot, y_low, y_high, w2),
        [
            sh((38, 128, 128), BF16), sh((36, 64, 128), F32), *rims(72), msg, stats,
        ],
        "conv_two",
        after=(xh,),
    )
    h2_low, h2_high = up(high, GX), down(low, GX)
    r2 = share(m2)
    (x1,) = call(
        total_kernel, (r1,), [sh((4, 128), F32)], "total", smem_first=False, after=(st1,)
    )
    m3, st2 = call(
        lambda *refs: third_kernel(cells, *refs),
        (place, r2, gb, cot, h2, st1, x1_own, xh),
        [four, stats],
        "slope_two",
        after=(x1,),
    )
    r3 = share(m3)
    s2, n2, a1 = call(
        active_kernel,
        (st2, gb, h2, cot, v2),
        [sh((9, C, 128), F32), sh((9, C, 128), F32), sh((16, 128), F32)],
        "active_sums",
        scratch=corr,
        smem_first=False,
    )

    slope1, low, high, m4, t3 = call(
        lambda *refs: fourth_kernel(cells, *refs),
        (
            place, r3, st2, gb, h2, h2_low, h2_high, cot, y_low, y_high,
            b2, st1, h1, v1, s2, n2, a1,
        ),
        [sh((34, 64, 128), F32), *rims(34), wide, sh((4, 128), F32)],
        "back_two",
        late=7,
        cut=(h1,),
        scratch=(pltpu.VMEM((36, 128, 128), BF16), *corr),
    )
    s_low, s_high = up(high, GX), down(low, GX)
    r4 = share(m4)

    (rows_out,) = call(
        output_kernel,
        (st2, gb, h2),
        [sh((ROWS, 64, 128), BF16)],
        "output",
        smem_first=False,
        after=(slope1,),
    )

    def back(rows):
        return jnp.transpose(rows.reshape(ROWS, 2, C, 128), (2, 1, 0, 3))

    output = back(rows_out)

    m5, norm_grads, t4 = call(
        lambda *refs: owner_kernel(cells, *refs),
        (place, r4, st1, gb, t3, x1),
        [sh((count * 8, 128), BF16), sh((4, C), F32), sh((8, 128), F32)],
        "own_rows",
        near=1,
        grant=16,
        after=(s_low, s_high, output),
    )
    r5 = share(m5.reshape(count, 8, 128)).reshape(count * 8, 128)
    (grad,) = call(
        lambda *refs: fifth_kernel(cells, *refs),
        (place, t4, st1, gb, h1, slope1, s_low, s_high, b1),
        [sh((C, 2, ROWS, 128), BF16)],
        "back_one",
        scratch=(pltpu.VMEM((34, 128, 128), BF16), pltpu.VMEM((64, ROWS, 128), F32)),
    )
    grads = call(
        finish_kernel,
        (r5,),
        [sh((27, C, C), F32)] * 2,
        "finish",
        scratch=(pltpu.VMEM((3 * C * 8, 128), F32),),
        smem_first=False,
        near=1,
        grant=16,
    )
    one, two = [jnp.transpose(k.reshape(3, 3, 3, C, C), (3, 4, 0, 1, 2)) for k in grads]

    return output, grad, one, two, norm_grads


def solution(mesh):
    nx, ny = mesh.devices.shape
    parts = (4, nx // 4, ny // 2, 2)
    split = Mesh(mesh.devices.reshape(parts), ALL)
    spec = P(None, GX, GY, None)
    in_specs = (spec, P(), P(), P(), P(), P(), P(), spec)
    out_specs = (spec, spec, P(), P(), P())
    return jax.shard_map(local, mesh=split, in_specs=in_specs, out_specs=out_specs, check_vma=False)
```

```python
import jax
import jax.numpy as jnp
from jax import lax
from jax.experimental import pallas as pl
from jax.experimental.pallas import tpu as pltpu
from jax.sharding import Mesh
from jax.sharding import PartitionSpec as P

GX = ("gx_0", "gx_1")
GY = ("gy_0", "gy_1")
ALL = GX + GY

EPSILON = 1e-05
C = 32
ROWS = 32
F32 = jnp.float32
BF16 = jnp.bfloat16
LN2 = 0.6931471805599453
SM = pl.BlockSpec(memory_space=pltpu.SMEM)


def sh(shape, kind):
    return jax.ShapeDtypeStruct(shape, kind)


def from_below(values, lane):
    return jnp.where(lane == 0, 0.0, pltpu.roll(values, 1, 1))


def from_above(values, lane):
    return jnp.where(lane == 127, 0.0, pltpu.roll(values, 127, 1))


def lanes(rows):
    return lax.broadcasted_iota(jnp.int32, (rows, 128), 1)


def windows_of(*refs):
    if len(refs) == 1:
        return lambda y: refs[0][y : y + 3].reshape(384, 128)
    return lambda y: jnp.concatenate([rows(y + k) for k in range(3) for rows in refs], axis=0)


def joined(k, middle, below, above):
    def row(y):
        if y < 4:
            return below[3 * y + k]
        if y < 4 + ROWS:
            return middle[y - 4]
        return above[3 * (y - 4 - ROWS) + k]

    return row


def conv_rows(window, w_ref, rows, emit):
    lane = lanes(64)
    weights = w_ref[...]
    for y in range(0, rows, 2):
        both = jnp.concatenate([window(y), window(y + 1)], axis=1)
        product = jnp.dot(weights, both, preferred_element_type=F32)
        for k in range(2):
            part = product[:, k * 128 : (k + 1) * 128]
            emit(
                y + k,
                part[64:128] + from_below(part[0:64], lane) + from_above(part[128:192], lane),
            )


def fold(column):
    return column[0:C] + column[C : 2 * C]


def total(values):
    return jnp.sum(values, axis=1, keepdims=True)


def twice(column):
    return jnp.concatenate([column, column], axis=0)


def fourfold(column):
    return twice(twice(column))


def message(columns, msg_ref):
    count = msg_ref.shape[0]
    spare = jnp.zeros((128 - C * len(columns), 1), F32)
    column = jnp.concatenate([*columns, spare], axis=0)
    msg_ref[...] = jnp.transpose(jnp.broadcast_to(column, (128, count)))


def as_row(column):
    return jnp.transpose(jnp.broadcast_to(column, (128, 128)))[0:1]


def rows_message(columns, groups, msg_ref):
    spare = jnp.zeros((128 - C * len(columns), 1), F32)
    row = as_row(jnp.concatenate([*columns, spare], axis=0))
    height = msg_ref.shape[1]
    at = lax.broadcasted_iota(jnp.int32, (height, 128), 0)
    tile = jnp.where(at == 0, jnp.broadcast_to(row, (height, 128)), 0.0)
    msg_ref[...] = jnp.broadcast_to(tile[None], msg_ref.shape)
    for k, group in enumerate(groups):
        for dz in range(3):
            for dy in range(3):
                msg_ref[dz * C : (dz + 1) * C, 1 + 3 * k + dy, :] = group(dz, dy)


def center_of(acc):
    return fold(total(acc)) / (2 * ROWS * 128)


def stats_of(rows, place_ref, cells, st_ref):
    parts = jnp.transpose(rows)
    centers = parts[0:C]
    count = parts.shape[1]
    mean = total(centers) / count
    off = centers - mean
    spread = (total(parts[C : 2 * C]) + (2 * ROWS * 128) * total(off * off)) / cells
    at = lax.broadcasted_iota(jnp.int32, centers.shape, 1)
    low = total(jnp.where(at == place_ref[0], off, 0.0))
    high = total(jnp.where(at == place_ref[1], off, 0.0))
    own = total(jnp.where(at == place_ref[7], off, 0.0))
    found = (mean, lax.rsqrt(spread + EPSILON), low, high)
    st_ref[...] = jnp.concatenate([*found, own, jnp.zeros((C, 123), F32)], axis=1)
    return found


def kept_stats(st_ref):
    return tuple(st_ref[:, k : k + 1] for k in range(4))


def sums_of(row):
    parts = jnp.transpose(jnp.broadcast_to(row, (128, 128)))[:, 0:1]
    return parts[0:C], parts[C : 2 * C]


def feature_sums(v, first):
    lane = lanes(128)
    inner = v[first + 2].astype(F32)
    for y in range(first + 3, first + ROWS):
        inner = inner + v[y].astype(F32)
    ends = [v[first + y].astype(F32) for y in (0, 1, ROWS, ROWS + 1)]
    windows = (inner + ends[0] + ends[1], inner + ends[1] + ends[2], inner + ends[2] + ends[3])
    columns = []
    for dz in range(3):
        for dy in range(3):
            values = windows[dy]
            if dz == 0:
                values = jnp.where(lane == 127, 0.0, values)
            if dz == 2:
                values = jnp.where(lane == 0, 0.0, values)
            column = total(values)
            columns.append(column + jnp.concatenate([column[C:], column[:C]], axis=0))
    return jnp.transpose(jnp.concatenate(columns + [jnp.zeros((128, 119), F32)], axis=1))[0:16]


def ones_of(x1):
    return lambda dz, dy: jnp.broadcast_to(x1[dz * 3 + dy : dz * 3 + dy + 1], (C, 128))


def act(z):
    e = jnp.exp2(jnp.abs(z) * (-8.0 / LN2))
    soft = jnp.maximum(z, 0.0) * 0.99 + jnp.log2(1.0 + e) * (0.99 * LN2 / 8.0)
    return 0.01 * z + soft


def act_slope(z):
    return 0.505 + 0.495 * jnp.tanh(4.0 * z)


def kept(place_ref, y, rows, margin):
    low = place_ref[2].astype(F32)
    high = place_ref[3].astype(F32)
    if y < margin:
        edge = place_ref[4].astype(F32)
    elif y >= rows - margin:
        edge = place_ref[5].astype(F32)
    else:
        return low, None, high
    return low * edge, edge, high * edge


def masked(values, factors):
    f_low, f_own, f_high = factors
    own = values[C : 3 * C]
    own = own if f_own is None else own * f_own
    return jnp.concatenate([values[0:C] * f_low, own, values[3 * C :] * f_high], axis=0).astype(
        BF16
    )


def weight_sums(g_ref, v_ref, first, acc_ref):
    step = 4
    for y in range(0, ROWS, step):
        window = jnp.concatenate(
            [v_ref[first + y + k : first + y + k + 3].reshape(384, 128) for k in range(step)], axis=1
        )
        product = lax.dot_general(
            window,
            g_ref[:, y * 128 : (y + step) * 128],
            (((1,), (1,)), ((), ())),
            preferred_element_type=F32,
        )
        if y == 0:
            acc_ref[...] = product
        else:
            acc_ref[...] += product


def folded(acc_ref):
    turned = [jnp.transpose(acc_ref[dy * 128 : dy * 128 + 128]) for dy in range(3)]

    def tile(dz, dy):
        both = turned[dy][dz * 64 : dz * 64 + 64]
        return both[0:C] + pltpu.roll(both[C:], 96, 1)

    return tile


def put_shifted(g_ref, y, values, lane):
    at = slice(y * 128, (y + 1) * 128)
    g_ref[0:64, at] = from_above(values, lane).astype(BF16)
    g_ref[64:128, at] = values.astype(BF16)
    g_ref[128:192, at] = from_below(values, lane).astype(BF16)


def pack_kernel(need, send, x_low, x_high, own, cot, up_ref, down_ref):
    need(own, cot)
    for y in range(4):
        for k, part in enumerate((x_low, own, x_high)):
            up_ref[3 * y + k] = part[ROWS - 4 + y]
            down_ref[3 * y + k] = part[y]
    up_ref[12:14] = cot[ROWS - 2 : ROWS]
    down_ref[12:14] = cot[0:2]


def weights_kernel(need, send, k1, k2, w1, w2):
    need(k1, k2)
    row = lax.broadcasted_iota(jnp.int32, (C, 128), 0)
    col = lax.broadcasted_iota(jnp.int32, (C, 128), 1)
    for k_ref, w_ref in ((k1, w1), (k2, w2)):
        lined = jnp.zeros((9 * C, 128), F32)
        for dx in range(3):
            spot = jnp.where(row + dx * C == col, 1.0, 0.0).astype(BF16)
            lined = lined + jnp.dot(
                k_ref[dx * 9 : dx * 9 + 9].reshape(9 * C, C), spot, preferred_element_type=F32
            )
        for dy in range(3):
            for dz in range(3):
                t = dy * 3 + dz
                put_tile(w_ref, dz, dy, lined[t * C : t * C + C])


def flipped_kernel(need, send, k_ref, b_ref):
    need(k_ref)
    row = lax.broadcasted_iota(jnp.int32, (C, 128), 0)
    col = lax.broadcasted_iota(jnp.int32, (C, 128), 1)
    eye = jnp.where(row == col, 1.0, 0.0)[:, 0:C].astype(BF16)
    zero = jnp.zeros((C, C), BF16)
    stack = []
    for t in range(9):
        stack += [k_ref[18 + t], k_ref[9 + t], k_ref[t], zero]
    turned = lax.dot_general(
        eye,
        jnp.concatenate(stack, axis=0),
        (((1,), (1,)), ((), ())),
        preferred_element_type=F32,
    )
    for dy in range(3):
        for dz in range(3):
            t = 8 - dy * 3 - dz
            put_tile(b_ref, dz, dy, turned[:, t * 128 : t * 128 + 128])


def put_tile(ref, dz, dy, tile):
    here = slice(dy * 128, dy * 128 + 128)
    ref[dz * 64 : dz * 64 + C, here] = tile.astype(BF16)
    ref[dz * 64 + C : dz * 64 + 64, here] = pltpu.roll(tile, C, 1).astype(BF16)


def first_kernel(
    need, send, y_low, y_high, w, own, x_low, x_high, v, h, msg, x1, center_out
):
    need(own, x_low, x_high, y_low, y_high, w)
    low = joined(0, x_low, y_low, y_high)
    own = joined(1, own, y_low, y_high)
    high = joined(2, x_high, y_low, y_high)
    acc = [jnp.zeros((64, 128), F32), jnp.zeros((64, 128), F32)]
    for k, pair in enumerate(((low, own), (own, high))):

        def emit(y, values, k=k):
            h[y, 64 * k : 64 * k + 64] = values
            if k == 1:
                send(h, row=y)
            if 3 <= y < 3 + ROWS:
                acc[k] = acc[k] + values

        conv_rows(windows_of(*pair), w, ROWS + 6, emit)
    send(h)
    for y in range(ROWS + 8):
        v[y] = jnp.concatenate([low(y)[C:], own(y), high(y)[0:C]], axis=0)
        send(v, row=y)
    send(v)
    center = center_of(jnp.concatenate([acc[0][C:], acc[1][0:C]], axis=0))
    both = twice(center)
    spread = jnp.zeros((64, 128), F32)
    for y in range(3, 3 + ROWS):
        off = h[y, C : 3 * C] - both
        spread = spread + off * off
    center_out[...] = jnp.broadcast_to(center, (C, 128))
    x1[...] = feature_sums(v, 3)
    send(center_out, x1)
    rows_message((center, fold(total(spread))), (ones_of(x1),), msg)


def second_kernel(
    cells, need, send, place, r1, gb, h1, cot, y_low, y_high, w, v, h, low, high, msg, st1
):
    need(r1, gb)
    mean, inverse, _, _ = stats_of(r1[:, 0, :], place, cells, st1)
    send(st1)
    mean4, scale4 = fourfold(mean), fourfold(inverse * gb[:, 0:1])
    shift4 = fourfold(gb[:, 1:2])
    rows = ROWS + 6
    for y in range(rows):
        need(h1, row=y)
        v[y] = masked(act((h1[y] - mean4) * scale4 + shift4), kept(place, y, rows, 3))
        send(v, row=y)
    need(w, cot, y_low, y_high)
    acc = [jnp.zeros((64, 128), F32)]

    def emit(y, values):
        h[y] = values
        send(h, row=y)
        if 2 <= y < 2 + ROWS:
            acc[0] = acc[0] + values

    rows = ROWS + 4
    conv_rows(windows_of(v), w, rows, emit)
    send(h)
    center = center_of(acc[0])
    both = twice(center)
    spread = jnp.zeros((64, 128), F32)
    for y in range(rows):
        off = h[y] - both
        if 2 <= y < 2 + ROWS:
            spread = spread + off * off
        low[2 * y] = off[0:C].astype(BF16)
        high[2 * y] = off[C:].astype(BF16)
        values = cot_row(cot, y_low, y_high, y)
        low[2 * y + 1] = values[0:C]
        high[2 * y + 1] = values[C:]
        send(low, high, row=2 * y + 1)
    message((center, fold(total(spread))), msg)


def total_kernel(need, send, parts, whole):
    need(parts)
    whole[...] = jnp.sum(parts[...], axis=0)


def side_kernel(need, send, center, h1, v1, xh, g, acc):
    need(center)
    both = twice(center[...])
    lane = lanes(64)
    for y in range(ROWS):
        need(h1, row=y + 3)
        put_shifted(g, y, h1[y + 3] - both, lane)
    need(v1)
    weight_sums(g, v1, 3, acc)
    tile = folded(acc)
    for dz in range(3):
        for dy in range(3):
            xh[dz * 3 + dy] = tile(dz, dy)


def cot_row(cot, y_low, y_high, y):
    if y < 2:
        return y_low[12 + y]
    if y < 2 + ROWS:
        return cot[y - 2]
    return y_high[10 + y - ROWS]


def third_kernel(cells, need, send, place, r2, gb, cot, h2, st1, x1, xh, msg, st2):
    need(r2, gb)
    mean, inverse, _, _ = stats_of(r2[...], place, cells, st2)
    mean2, inverse2 = twice(mean), twice(inverse)
    gain2, bias2 = twice(gb[:, 2:3]), twice(gb[:, 3:4])
    plain = jnp.zeros((64, 128), F32)
    both = jnp.zeros((64, 128), F32)
    for y in range(ROWS):
        need(h2, row=y + 2)
        need(cot, row=y)
        normed = (h2[y + 2] - mean2) * inverse2
        z = normed * gain2 + bias2
        slope = cot[y].astype(F32) * act_slope(z)
        plain = plain + slope
        both = both + slope * normed
    need(st1, x1, xh)
    inverse1, own1 = st1[:, 1:2], st1[:, 4:5]
    ones = ones_of(x1)

    def xn(dz, dy):
        return inverse1 * (xh[dz * 3 + dy] + own1 * ones(dz, dy))


    rows_message((fold(total(both)), fold(total(plain))), (xn,), msg)


def active_kernel(need, send, st2, gb, h2, cot, v2, s2, n2, a1, g, acc):
    need(st2, gb)
    mean, inverse, _, _ = kept_stats(st2)
    mean2, inverse2 = twice(mean), twice(inverse)
    gain2, bias2 = twice(gb[:, 2:3]), twice(gb[:, 3:4])
    lane = lanes(64)

    def sums_to(out):
        weight_sums(g, v2, 2, acc)
        tile = folded(acc)
        for dz in range(3):
            for dy in range(3):
                out[dz * 3 + dy] = tile(dz, dy)
        send(out)

    for y in range(ROWS):
        need(h2, row=y + 2)
        put_shifted(g, y, (h2[y + 2] - mean2) * inverse2, lane)
    need(v2)
    sums_to(n2)
    for y in range(ROWS):
        need(cot, row=y)
        normed = (h2[y + 2] - mean2) * inverse2
        put_shifted(g, y, cot[y].astype(F32) * act_slope(normed * gain2 + bias2), lane)
    sums_to(s2)
    a1[...] = feature_sums(v2, 2)


def output_kernel(need, send, st2, gb, h2, out):
    need(st2, gb)
    mean, inverse, _, _ = kept_stats(st2)
    mean2, scale2 = twice(mean), twice(inverse * gb[:, 2:3])
    shift2 = twice(gb[:, 3:4])
    for y in range(ROWS):
        need(h2, row=y + 2)
        out[y] = act((h2[y + 2] - mean2) * scale2 + shift2).astype(BF16)
        send(out, row=y)


def fourth_kernel(
    cells, need, send, place, r3, st2, gb, h2, x_low, x_high, cot, y_low, y_high, w, st1, h1, v1, s2, n2, a1,
    slope1, low, high, msg, t3, v, g, acc,
):
    need(r3, st2, gb)
    mean, inverse, o_low, o_high = kept_stats(st2)
    t3[...] = jnp.sum(r3[...], axis=0)
    send(t3)
    nsum, plain = sums_of(t3[0:1])
    need(y_low, y_high)
    gain, bias = gb[:, 2:3], gb[:, 3:4]
    lead = gain * inverse
    p_mean, n_mean = plain / cells, nsum / cells

    def grad(normed, c, gain, bias, lead, p_mean, n_mean):
        slope = c.astype(F32) * act_slope(normed * gain + bias)
        return lead * (slope - p_mean - normed * n_mean)

    one = (gain, bias, lead, p_mean, n_mean)
    both = tuple(twice(a) for a in one)
    mean2, inverse2 = twice(mean), twice(inverse)
    lane = lanes(64)
    rows = ROWS + 4
    for y in range(rows):
        need(h2, row=y)
        need(x_low, x_high, row=2 * y + 1)
        need(cot, row=min(max(y - 2, 0), ROWS - 1))
        g_low = grad((x_low[2 * y].astype(F32) + o_low) * inverse, x_low[2 * y + 1], *one)
        g_own = grad((h2[y] - mean2) * inverse2, cot_row(cot, y_low, y_high, y), *both)
        g_high = grad((x_high[2 * y].astype(F32) + o_high) * inverse, x_high[2 * y + 1], *one)
        planes = jnp.concatenate([g_low, g_own, g_high], axis=0)
        v[y] = masked(planes, kept(place, y, rows, 2))
    need(h1, st1, w)
    mean, inverse, _, _ = kept_stats(st1)
    mean2, inverse2 = twice(mean), twice(inverse)
    gain2, bias2 = twice(gb[:, 0:1]), twice(gb[:, 1:2])
    sums = [jnp.zeros((64, 128), F32), jnp.zeros((64, 128), F32)]

    def emit(y, values):
        normed = (h1[y + 2] - mean2) * inverse2
        slope = values * act_slope(normed * gain2 + bias2)
        slope1[y] = slope
        low[y] = slope[0:C].astype(BF16)
        high[y] = slope[C:].astype(BF16)
        send(slope1, low, high, row=y)
        if 1 <= y < 1 + ROWS:
            sums[0] = sums[0] + slope * normed
            sums[1] = sums[1] + slope
            put_shifted(g, y - 1, slope, lane)

    conv_rows(windows_of(v), w, ROWS + 2, emit)
    send(slope1, low, high)
    need(v1)
    weight_sums(g, v1, 3, acc)
    need(s2, n2, a1)
    ones = ones_of(a1)

    def two(dz, dy):
        k = dz * 3 + dy
        return lead * (s2[k] - p_mean * ones(dz, dy) - n_mean * n2[k])

    rows_message(
        (fold(total(sums[0])), fold(total(sums[1]))), (folded(acc), two), msg
    )


def owner_kernel(cells, need, send, place, r4, st1, gb, t3, x1, msg, norms, t4):
    need(st1, gb, t3, x1)
    _, inverse, _, _ = kept_stats(st1)
    t4[...] = jnp.sum(r4[...], axis=0)
    nsum, plain = sums_of(t4[0:1])
    mine = lax.broadcasted_iota(jnp.int32, (C, 1), 0) == place[6]

    def picked(column):
        return jnp.sum(jnp.where(mine, column, 0.0), axis=0, keepdims=True)

    scale = cells**-0.5
    lead = picked(gb[:, 0:1] * inverse) * scale
    third, fourth = t3[...], t4[...]
    one = fourth[1:4] - picked(plain) * (x1[1:4] / cells) - picked(nsum) * (third[1:4] / cells)
    one = lead * one
    two = fourth[4:7] * scale
    tile = jnp.concatenate([one, two, jnp.zeros((2, 128), F32)], axis=0)
    pair = twice(tile).astype(BF16)
    for k in range(0, msg.shape[0], 16):
        msg[k : k + 16] = pair
    for k, row in enumerate((fourth[0:1], third[0:1])):
        norms[2 * k : 2 * k + 1] = row[:, 0:C] * scale
        norms[2 * k + 1 : 2 * k + 2] = row[:, C : 2 * C] * scale


def finish_kernel(need, send, parts, one, two, rows):
    rows[...] = parts[0 : 3 * C * 8].astype(F32)
    for dz in range(3):
        for dy in range(3):
            for k, out in enumerate((one, two)):
                tile = rows[pl.ds(dz * C * 8 + 3 * k + dy, C, stride=8), :]
                for dx in range(3):
                    out[dx * 9 + dy * 3 + dz] = tile[:, dx * C : (dx + 1) * C]


def fifth_kernel(cells, need, send, place, t4, st1, gb, h1, slope1, s_low, s_high, w, out, v, turned):
    need(t4, st1, gb)
    mean, inverse, _, _ = kept_stats(st1)
    nsum, plain = sums_of(t4[0:1])
    mean4, inverse4 = fourfold(mean), fourfold(inverse)
    lead4 = fourfold(gb[:, 0:1] * inverse)
    p_mean4, n_mean4 = fourfold(plain / cells), fourfold(nsum / cells)
    rows = ROWS + 2
    for y in range(rows):
        need(slope1, s_low, s_high, row=y)
        need(h1, row=y + 2)
        slope = jnp.concatenate(
            [s_low[y].astype(F32), slope1[y], s_high[y].astype(F32)], axis=0
        )
        normed = (h1[y + 2] - mean4) * inverse4
        v[y] = masked(lead4 * (slope - p_mean4 - normed * n_mean4), kept(place, y, rows, 1))
    need(w)

    def emit(y, values):
        turned[:, y, :] = values

    conv_rows(windows_of(v), w, ROWS, emit)
    for i in range(C):
        for x in range(2):
            out[i, x] = turned[x * C + i].astype(BF16)
        send(out, row=i)


def pieces_of(shape):
    rows = shape[0]
    if len(shape) < 3 or rows < 32 or rows > 100:
        return [(0, rows)]
    cuts = [rows * c // 4 for c in range(5)]
    return list(zip(cuts, cuts[1:]))


def call(
    kernel, ins, outs, name, scratch=(), smem_first=True, after=(), near=0, cut=(), late=0, grant=56
):
    lead = 1 if smem_first else 0
    count_in, count_out = len(ins) - lead - near, len(outs)
    far_ins = ins[lead + near :]
    own = [any(a is b for b in cut) for a in far_ins]
    shapes = [(a.shape[0], 2 * C, 128) if c else a.shape for a, c in zip(far_ins, own)]

    def body(*refs):
        first, rest = refs[: lead + near], refs[lead + near :]
        parts = []
        for size in (count_in, len(after), count_out, count_in, count_out, 2):
            parts.append(rest[:size])
            rest = rest[size:]
        sources, _, targets, in_bufs, out_bufs, (in_sems, out_sems) = parts

        def source(k, a, b):
            return sources[k].at[a:b, C : 3 * C] if own[k] else sources[k].at[a:b]

        arriving = [
            [
                (a, b, pltpu.make_async_copy(source(k, a, b), buf.at[a:b], in_sems.at[k, c]))
                for c, (a, b) in enumerate(pieces_of(buf.shape))
            ]
            for k, buf in enumerate(in_bufs)
        ]
        leaving = [
            [
                (a, b, pltpu.make_async_copy(buf.at[a:b], targets[k].at[a:b], out_sems.at[k, c]))
                for c, (a, b) in enumerate(pieces_of(buf.shape))
            ]
            for k, buf in enumerate(out_bufs)
        ]
        early, later = arriving[: count_in - late], arriving[count_in - late :]
        for group in (early, later):
            for c in range(4):
                for pieces in group:
                    if c < len(pieces):
                        pieces[c][2].start()
        waiting, held = [list(pieces) for pieces in arriving], [list(pieces) for pieces in leaving]

        def need(*wanted, row=None):
            for ref in wanted:
                for k, buf in enumerate(in_bufs):
                    while buf is ref and waiting[k] and (row is None or waiting[k][0][0] <= row):
                        waiting[k].pop(0)[2].wait()

        def send(*ready, row=None):
            for ref in ready:
                for k, buf in enumerate(out_bufs):
                    while buf is ref and held[k] and (row is None or held[k][0][1] <= row + 1):
                        held[k].pop(0)[2].start()

        kernel(need, send, *first, *in_bufs, *out_bufs, *rest)
        send(*out_bufs)
        need(*in_bufs)
        for pieces in leaving:
            for piece in pieces:
                piece[2].wait()

    far = pl.BlockSpec(memory_space=pltpu.HBM)
    return pl.pallas_call(
        body,
        out_shape=outs,
        in_specs=[SM] * lead
        + [pl.BlockSpec(memory_space=pltpu.VMEM)] * near
        + [far] * (count_in + len(after)),
        out_specs=[far] * count_out,
        scratch_shapes=[
            *[pltpu.VMEM(shape, a.dtype) for shape, a in zip(shapes, far_ins)],
            *[pltpu.VMEM(a.shape, a.dtype) for a in outs],
            pltpu.SemaphoreType.DMA((max(count_in, 1), 4)),
            pltpu.SemaphoreType.DMA((count_out, 4)),
            *scratch,
        ],
        compiler_params=pltpu.CompilerParams(vmem_limit_bytes=grant * 1024 * 1024),
        cost_estimate=pl.CostEstimate(
            flops=2_000_000_000, bytes_accessed=6_000_000, transcendentals=0
        ),
        name=name,
    )(*ins, *after)


def up(values, axes):
    count = lax.axis_size(axes)
    return lax.ppermute(values, axes, [(i, i + 1) for i in range(count - 1)])


def down(values, axes):
    count = lax.axis_size(axes)
    return lax.ppermute(values, axes, [(i + 1, i) for i in range(count - 1)])


def share(msg):
    return lax.all_to_all(msg, ALL[::-1], 0, 0, tiled=True)


def rank_of(gx, gy):
    rank = gy % lax.axis_size(GY[1])
    for part, axis in (
        (gy // lax.axis_size(GY[1]), GY[0]),
        (gx % lax.axis_size(GX[1]), GX[1]),
        (gx // lax.axis_size(GX[1]), GX[0]),
    ):
        rank = rank * lax.axis_size(axis) + part
    return rank


def local(features, kernel_one, gain_one, bias_one, kernel_two, gain_two, bias_two, cotangent):
    count_x, count_y = lax.axis_size(GX), lax.axis_size(GY)
    count = count_x * count_y
    cells = float(count * 2 * ROWS * 128)
    gx, gy = lax.axis_index(GX), lax.axis_index(GY)
    at = rank_of(gx, gy)
    beside = [rank_of(jnp.clip(gx + k, 0, count_x - 1), gy) for k in (-1, 1)]
    edges = [gx > 0, gx < count_x - 1, gy > 0, gy < count_y - 1]
    place = jnp.stack([*beside, *edges, at % C, at]).astype(jnp.int32)
    gb = jnp.stack([gain_one, bias_one, gain_two, bias_two], axis=1)

    own = jnp.transpose(features, (2, 1, 0, 3)).reshape(ROWS, 64, 128)
    cot = jnp.transpose(cotangent, (2, 1, 0, 3)).reshape(ROWS, 64, 128)

    def rims(rows):
        return [sh((rows, C, 128), BF16)] * 2

    msg, four, wide = (sh((count, *tile), F32) for tile in ((128,), (4, 128), (8, 128)))
    stats = sh((C, 128), F32)
    corr = (pltpu.VMEM((192, ROWS * 128), BF16), pltpu.VMEM((384, 192), F32))

    x_low, x_high = up(own, GX), down(own, GX)
    taps = [
        jnp.transpose(k, (2, 3, 4, 0, 1)).reshape(27, C, C) for k in (kernel_one, kernel_two)
    ]
    matrices = [sh((192, 384), BF16)] * 2
    w1, w2 = call(weights_kernel, taps, matrices, "weights", smem_first=False)
    y_up, y_down = call(
        pack_kernel,
        (x_low, x_high, own, cot),
        [sh((14, 64, 128), BF16)] * 2,
        "pack",
        smem_first=False,
        after=(w1,),
        near=2,
        grant=16,
    )
    y_low, y_high = up(y_up, GY), down(y_down, GY)

    v1, h1, m1, x1_own, center = call(
        first_kernel,
        (y_low, y_high, w1, own, x_low, x_high),
        [sh((40, 128, 128), BF16), sh((38, 128, 128), F32), four, sh((16, 128), F32), stats],
        "conv_one",
        smem_first=False,
    )
    r1 = share(m1)

    (xh,) = call(
        side_kernel,
        (center, h1, v1),
        [sh((9, C, 128), F32)],
        "hidden_features",
        scratch=corr,
        smem_first=False,
        cut=(h1,),
    )

    v2, h2, low, high, m2, st1 = call(
        lambda *refs: second_kernel(cells, *refs),
        (place, r1, gb, h1, cot, y_low, y_high, w2),
        [
            sh((38, 128, 128), BF16), sh((36, 64, 128), F32), *rims(72), msg, stats,
        ],
        "conv_two",
        after=(xh,),
    )
    h2_low, h2_high = up(high, GX), down(low, GX)
    r2 = share(m2)
    (b2,) = call(
        flipped_kernel, taps[1:], matrices[1:], "flipped_two", smem_first=False, after=(st1,)
    )
    m3, st2 = call(
        lambda *refs: third_kernel(cells, *refs),
        (place, r2, gb, cot, h2, st1, x1_own, xh),
        [four, stats],
        "slope_two",
        after=(b2,),
    )
    r3 = share(m3)
    s2, n2, a1 = call(
        active_kernel,
        (st2, gb, h2, cot, v2),
        [sh((9, C, 128), F32), sh((9, C, 128), F32), sh((16, 128), F32)],
        "active_sums",
        scratch=corr,
        smem_first=False,
    )

    slope1, low, high, m4, t3 = call(
        lambda *refs: fourth_kernel(cells, *refs),
        (
            place, r3, st2, gb, h2, h2_low, h2_high, cot, y_low, y_high,
            b2, st1, h1, v1, s2, n2, a1,
        ),
        [sh((34, 64, 128), F32), *rims(34), wide, sh((4, 128), F32)],
        "back_two",
        late=7,
        cut=(h1,),
        scratch=(pltpu.VMEM((36, 128, 128), BF16), *corr),
    )
    s_low, s_high = up(high, GX), down(low, GX)
    r4 = share(m4)

    (b1,) = call(
        flipped_kernel, taps[:1], matrices[1:], "flipped_one", smem_first=False, after=(slope1,)
    )
    (x1,) = call(total_kernel, (r1,), [sh((4, 128), F32)], "total", smem_first=False, after=(b1,))
    (rows_out,) = call(
        output_kernel,
        (st2, gb, h2),
        [sh((ROWS, 64, 128), BF16)],
        "output",
        smem_first=False,
        after=(slope1,),
    )

    def back(rows):
        return jnp.transpose(rows.reshape(ROWS, 2, C, 128), (2, 1, 0, 3))

    output = back(rows_out)

    m5, norm_grads, t4 = call(
        lambda *refs: owner_kernel(cells, *refs),
        (place, r4, st1, gb, t3, x1),
        [sh((count * 8, 128), BF16), sh((4, C), F32), sh((8, 128), F32)],
        "own_rows",
        near=1,
        grant=16,
        after=(s_low, s_high, output),
    )
    r5 = share(m5.reshape(count, 8, 128)).reshape(count * 8, 128)
    (grad,) = call(
        lambda *refs: fifth_kernel(cells, *refs),
        (place, t4, st1, gb, h1, slope1, s_low, s_high, b1),
        [sh((C, 2, ROWS, 128), BF16)],
        "back_one",
        scratch=(pltpu.VMEM((34, 128, 128), BF16), pltpu.VMEM((64, ROWS, 128), F32)),
    )
    grads = call(
        finish_kernel,
        (r5,),
        [sh((27, C, C), F32)] * 2,
        "finish",
        scratch=(pltpu.VMEM((3 * C * 8, 128), F32),),
        smem_first=False,
        near=1,
        grant=16,
    )
    one, two = [jnp.transpose(k.reshape(3, 3, 3, C, C), (3, 4, 0, 1, 2)) for k in grads]

    return output, grad, one, two, norm_grads


def solution(mesh):
    nx, ny = mesh.devices.shape
    parts = (4, nx // 4, ny // 2, 2)
    split = Mesh(mesh.devices.reshape(parts), ALL)
    spec = P(None, GX, GY, None)
    in_specs = (spec, P(), P(), P(), P(), P(), P(), spec)
    out_specs = (spec, spec, P(), P(), P())
    return jax.shard_map(local, mesh=split, in_specs=in_specs, out_specs=out_specs, check_vma=False)
```

```python
import jax
import jax.numpy as jnp
from jax import lax
from jax.experimental import pallas as pl
from jax.experimental.pallas import tpu as pltpu
from jax.sharding import Mesh
from jax.sharding import PartitionSpec as P

GX = ("gx_0", "gx_1")
GY = ("gy_0", "gy_1")
ALL = GX + GY

EPSILON = 1e-05
C = 32
ROWS = 32
F32 = jnp.float32
BF16 = jnp.bfloat16
LN2 = 0.6931471805599453
SM = pl.BlockSpec(memory_space=pltpu.SMEM)


def sh(shape, kind):
    return jax.ShapeDtypeStruct(shape, kind)


def from_below(values, lane):
    return jnp.where(lane == 0, 0.0, pltpu.roll(values, 1, 1))


def from_above(values, lane):
    return jnp.where(lane == 127, 0.0, pltpu.roll(values, 127, 1))


def lanes(rows):
    return lax.broadcasted_iota(jnp.int32, (rows, 128), 1)


def windows_of(*refs):
    if len(refs) == 1:
        return lambda y: refs[0][y : y + 3].reshape(384, 128)
    return lambda y: jnp.concatenate([rows(y + k) for k in range(3) for rows in refs], axis=0)


def joined(k, middle, below, above):
    def row(y):
        if y < 4:
            return below[3 * y + k]
        if y < 4 + ROWS:
            return middle[y - 4]
        return above[3 * (y - 4 - ROWS) + k]

    return row


def conv_rows(window, w_ref, rows, emit):
    lane = lanes(64)
    weights = w_ref[...]
    for y in range(0, rows, 2):
        both = jnp.concatenate([window(y), window(y + 1)], axis=1)
        product = jnp.dot(weights, both, preferred_element_type=F32)
        for k in range(2):
            part = product[:, k * 128 : (k + 1) * 128]
            emit(
                y + k,
                part[64:128] + from_below(part[0:64], lane) + from_above(part[128:192], lane),
            )


def fold(column):
    return column[0:C] + column[C : 2 * C]


def total(values):
    return jnp.sum(values, axis=1, keepdims=True)


def twice(column):
    return jnp.concatenate([column, column], axis=0)


def fourfold(column):
    return twice(twice(column))


def message(columns, msg_ref):
    count = msg_ref.shape[0]
    spare = jnp.zeros((128 - C * len(columns), 1), F32)
    column = jnp.concatenate([*columns, spare], axis=0)
    msg_ref[...] = jnp.transpose(jnp.broadcast_to(column, (128, count)))


def as_row(column):
    return jnp.transpose(jnp.broadcast_to(column, (128, 128)))[0:1]


def rows_message(columns, groups, msg_ref):
    spare = jnp.zeros((128 - C * len(columns), 1), F32)
    row = as_row(jnp.concatenate([*columns, spare], axis=0))
    height = msg_ref.shape[1]
    at = lax.broadcasted_iota(jnp.int32, (height, 128), 0)
    tile = jnp.where(at == 0, jnp.broadcast_to(row, (height, 128)), 0.0)
    msg_ref[...] = jnp.broadcast_to(tile[None], msg_ref.shape)
    for k, group in enumerate(groups):
        for dz in range(3):
            for dy in range(3):
                msg_ref[dz * C : (dz + 1) * C, 1 + 3 * k + dy, :] = group(dz, dy)


def center_of(acc):
    return fold(total(acc)) / (2 * ROWS * 128)


def stats_of(rows, place_ref, cells, st_ref):
    parts = jnp.transpose(rows)
    centers = parts[0:C]
    count = parts.shape[1]
    mean = total(centers) / count
    off = centers - mean
    spread = (total(parts[C : 2 * C]) + (2 * ROWS * 128) * total(off * off)) / cells
    at = lax.broadcasted_iota(jnp.int32, centers.shape, 1)
    low = total(jnp.where(at == place_ref[0], off, 0.0))
    high = total(jnp.where(at == place_ref[1], off, 0.0))
    own = total(jnp.where(at == place_ref[7], off, 0.0))
    found = (mean, lax.rsqrt(spread + EPSILON), low, high)
    st_ref[...] = jnp.concatenate([*found, own, jnp.zeros((C, 123), F32)], axis=1)
    return found


def kept_stats(st_ref):
    return tuple(st_ref[:, k : k + 1] for k in range(4))


def sums_of(row):
    parts = jnp.transpose(jnp.broadcast_to(row, (128, 128)))[:, 0:1]
    return parts[0:C], parts[C : 2 * C]


def feature_sums(v, first):
    lane = lanes(128)
    inner = v[first + 2].astype(F32)
    for y in range(first + 3, first + ROWS):
        inner = inner + v[y].astype(F32)
    ends = [v[first + y].astype(F32) for y in (0, 1, ROWS, ROWS + 1)]
    windows = (inner + ends[0] + ends[1], inner + ends[1] + ends[2], inner + ends[2] + ends[3])
    columns = []
    for dz in range(3):
        for dy in range(3):
            values = windows[dy]
            if dz == 0:
                values = jnp.where(lane == 127, 0.0, values)
            if dz == 2:
                values = jnp.where(lane == 0, 0.0, values)
            column = total(values)
            columns.append(column + jnp.concatenate([column[C:], column[:C]], axis=0))
    return jnp.transpose(jnp.concatenate(columns + [jnp.zeros((128, 119), F32)], axis=1))[0:16]


def ones_of(x1):
    return lambda dz, dy: jnp.broadcast_to(x1[dz * 3 + dy : dz * 3 + dy + 1], (C, 128))


def act(z):
    e = jnp.exp2(jnp.abs(z) * (-8.0 / LN2))
    soft = jnp.maximum(z, 0.0) * 0.99 + jnp.log2(1.0 + e) * (0.99 * LN2 / 8.0)
    return 0.01 * z + soft


def act_slope(z):
    return 0.505 + 0.495 * jnp.tanh(4.0 * z)


def kept(place_ref, y, rows, margin):
    low = place_ref[2].astype(F32)
    high = place_ref[3].astype(F32)
    if y < margin:
        edge = place_ref[4].astype(F32)
    elif y >= rows - margin:
        edge = place_ref[5].astype(F32)
    else:
        return low, None, high
    return low * edge, edge, high * edge


def masked(values, factors):
    f_low, f_own, f_high = factors
    own = values[C : 3 * C]
    own = own if f_own is None else own * f_own
    return jnp.concatenate([values[0:C] * f_low, own, values[3 * C :] * f_high], axis=0).astype(
        BF16
    )


def weight_sums(g_ref, v_ref, first, acc_ref):
    step = 4
    for y in range(0, ROWS, step):
        window = jnp.concatenate(
            [v_ref[first + y + k : first + y + k + 3].reshape(384, 128) for k in range(step)], axis=1
        )
        product = lax.dot_general(
            window,
            g_ref[:, y * 128 : (y + step) * 128],
            (((1,), (1,)), ((), ())),
            preferred_element_type=F32,
        )
        if y == 0:
            acc_ref[...] = product
        else:
            acc_ref[...] += product


def folded(acc_ref):
    turned = [jnp.transpose(acc_ref[dy * 128 : dy * 128 + 128]) for dy in range(3)]

    def tile(dz, dy):
        both = turned[dy][dz * 64 : dz * 64 + 64]
        return both[0:C] + pltpu.roll(both[C:], 96, 1)

    return tile


def put_shifted(g_ref, y, values, lane):
    at = slice(y * 128, (y + 1) * 128)
    g_ref[0:64, at] = from_above(values, lane).astype(BF16)
    g_ref[64:128, at] = values.astype(BF16)
    g_ref[128:192, at] = from_below(values, lane).astype(BF16)


def pack_kernel(need, send, x_low, x_high, own, cot, up_ref, down_ref):
    need(own, cot)
    for y in range(4):
        for k, part in enumerate((x_low, own, x_high)):
            up_ref[3 * y + k] = part[ROWS - 4 + y]
            down_ref[3 * y + k] = part[y]
    up_ref[12:14] = cot[ROWS - 2 : ROWS]
    down_ref[12:14] = cot[0:2]


def weights_kernel(need, send, k1, k2, w1, w2):
    need(k1, k2)
    row = lax.broadcasted_iota(jnp.int32, (C, 128), 0)
    col = lax.broadcasted_iota(jnp.int32, (C, 128), 1)
    for k_ref, w_ref in ((k1, w1), (k2, w2)):
        lined = jnp.zeros((9 * C, 128), F32)
        for dx in range(3):
            spot = jnp.where(row + dx * C == col, 1.0, 0.0).astype(BF16)
            lined = lined + jnp.dot(
                k_ref[dx * 9 : dx * 9 + 9].reshape(9 * C, C), spot, preferred_element_type=F32
            )
        for dy in range(3):
            for dz in range(3):
                t = dy * 3 + dz
                put_tile(w_ref, dz, dy, lined[t * C : t * C + C])


def flipped_kernel(need, send, k_ref, b_ref):
    need(k_ref)
    row = lax.broadcasted_iota(jnp.int32, (C, 128), 0)
    col = lax.broadcasted_iota(jnp.int32, (C, 128), 1)
    eye = jnp.where(row == col, 1.0, 0.0)[:, 0:C].astype(BF16)
    zero = jnp.zeros((C, C), BF16)
    stack = []
    for t in range(9):
        stack += [k_ref[18 + t], k_ref[9 + t], k_ref[t], zero]
    turned = lax.dot_general(
        eye,
        jnp.concatenate(stack, axis=0),
        (((1,), (1,)), ((), ())),
        preferred_element_type=F32,
    )
    for dy in range(3):
        for dz in range(3):
            t = 8 - dy * 3 - dz
            put_tile(b_ref, dz, dy, turned[:, t * 128 : t * 128 + 128])


def put_tile(ref, dz, dy, tile):
    here = slice(dy * 128, dy * 128 + 128)
    ref[dz * 64 : dz * 64 + C, here] = tile.astype(BF16)
    ref[dz * 64 + C : dz * 64 + 64, here] = pltpu.roll(tile, C, 1).astype(BF16)


def first_kernel(
    need, send, y_low, y_high, w, own, x_low, x_high, v, h, msg, x1, center_out
):
    need(own, x_low, x_high, y_low, y_high, w)
    low = joined(0, x_low, y_low, y_high)
    own = joined(1, own, y_low, y_high)
    high = joined(2, x_high, y_low, y_high)
    acc = [jnp.zeros((64, 128), F32), jnp.zeros((64, 128), F32)]
    for k, pair in enumerate(((low, own), (own, high))):

        def emit(y, values, k=k):
            h[y, 64 * k : 64 * k + 64] = values
            if k == 1:
                send(h, row=y)
            if 3 <= y < 3 + ROWS:
                acc[k] = acc[k] + values

        conv_rows(windows_of(*pair), w, ROWS + 6, emit)
    send(h)
    for y in range(ROWS + 8):
        v[y] = jnp.concatenate([low(y)[C:], own(y), high(y)[0:C]], axis=0)
        send(v, row=y)
    send(v)
    center = center_of(jnp.concatenate([acc[0][C:], acc[1][0:C]], axis=0))
    both = twice(center)
    spread = jnp.zeros((64, 128), F32)
    for y in range(3, 3 + ROWS):
        off = h[y, C : 3 * C] - both
        spread = spread + off * off
    center_out[...] = jnp.broadcast_to(center, (C, 128))
    x1[...] = feature_sums(v, 3)
    send(center_out, x1)
    rows_message((center, fold(total(spread))), (ones_of(x1),), msg)


def second_kernel(
    cells, need, send, place, r1, gb, h1, cot, y_low, y_high, w, v, h, low, high, msg, st1
):
    need(r1, gb)
    mean, inverse, _, _ = stats_of(r1[:, 0, :], place, cells, st1)
    send(st1)
    mean4, scale4 = fourfold(mean), fourfold(inverse * gb[:, 0:1])
    shift4 = fourfold(gb[:, 1:2])
    rows = ROWS + 6
    for y in range(rows):
        need(h1, row=y)
        v[y] = masked(act((h1[y] - mean4) * scale4 + shift4), kept(place, y, rows, 3))
        send(v, row=y)
    need(w, cot, y_low, y_high)
    acc = [jnp.zeros((64, 128), F32)]

    def emit(y, values):
        h[y] = values
        send(h, row=y)
        if 2 <= y < 2 + ROWS:
            acc[0] = acc[0] + values

    rows = ROWS + 4
    conv_rows(windows_of(v), w, rows, emit)
    send(h)
    center = center_of(acc[0])
    both = twice(center)
    spread = jnp.zeros((64, 128), F32)
    for y in range(rows):
        off = h[y] - both
        if 2 <= y < 2 + ROWS:
            spread = spread + off * off
        low[2 * y] = off[0:C].astype(BF16)
        high[2 * y] = off[C:].astype(BF16)
        values = cot_row(cot, y_low, y_high, y)
        low[2 * y + 1] = values[0:C]
        high[2 * y + 1] = values[C:]
        send(low, high, row=2 * y + 1)
    message((center, fold(total(spread))), msg)


def total_kernel(need, send, parts, whole):
    need(parts)
    whole[...] = jnp.sum(parts[...], axis=0)


def side_kernel(need, send, center, h1, v1, xh, g, acc):
    need(center)
    both = twice(center[...])
    lane = lanes(64)
    for y in range(ROWS):
        need(h1, row=y + 3)
        put_shifted(g, y, h1[y + 3] - both, lane)
    need(v1)
    weight_sums(g, v1, 3, acc)
    tile = folded(acc)
    for dz in range(3):
        for dy in range(3):
            xh[dz * 3 + dy] = tile(dz, dy)


def cot_row(cot, y_low, y_high, y):
    if y < 2:
        return y_low[12 + y]
    if y < 2 + ROWS:
        return cot[y - 2]
    return y_high[10 + y - ROWS]


def third_kernel(cells, need, send, place, r2, gb, cot, h2, st1, x1, xh, msg, st2):
    need(r2, gb)
    mean, inverse, _, _ = stats_of(r2[...], place, cells, st2)
    mean2, inverse2 = twice(mean), twice(inverse)
    gain2, bias2 = twice(gb[:, 2:3]), twice(gb[:, 3:4])
    plain = jnp.zeros((64, 128), F32)
    both = jnp.zeros((64, 128), F32)
    for y in range(ROWS):
        need(h2, row=y + 2)
        need(cot, row=y)
        normed = (h2[y + 2] - mean2) * inverse2
        z = normed * gain2 + bias2
        slope = cot[y].astype(F32) * act_slope(z)
        plain = plain + slope
        both = both + slope * normed
    need(st1, x1, xh)
    inverse1, own1 = st1[:, 1:2], st1[:, 4:5]
    ones = ones_of(x1)

    def xn(dz, dy):
        return inverse1 * (xh[dz * 3 + dy] + own1 * ones(dz, dy))


    rows_message((fold(total(both)), fold(total(plain))), (xn,), msg)


def active_kernel(need, send, st2, gb, h2, cot, v2, s2, n2, a1, g, acc):
    need(st2, gb)
    mean, inverse, _, _ = kept_stats(st2)
    mean2, inverse2 = twice(mean), twice(inverse)
    gain2, bias2 = twice(gb[:, 2:3]), twice(gb[:, 3:4])
    lane = lanes(64)

    def sums_to(out):
        weight_sums(g, v2, 2, acc)
        tile = folded(acc)
        for dz in range(3):
            for dy in range(3):
                out[dz * 3 + dy] = tile(dz, dy)
        send(out)

    for y in range(ROWS):
        need(h2, row=y + 2)
        put_shifted(g, y, (h2[y + 2] - mean2) * inverse2, lane)
    need(v2)
    sums_to(n2)
    for y in range(ROWS):
        need(cot, row=y)
        normed = (h2[y + 2] - mean2) * inverse2
        put_shifted(g, y, cot[y].astype(F32) * act_slope(normed * gain2 + bias2), lane)
    sums_to(s2)
    a1[...] = feature_sums(v2, 2)


def output_kernel(need, send, st2, gb, h2, out):
    need(st2, gb)
    mean, inverse, _, _ = kept_stats(st2)
    mean2, scale2 = twice(mean), twice(inverse * gb[:, 2:3])
    shift2 = twice(gb[:, 3:4])
    for y in range(ROWS):
        need(h2, row=y + 2)
        out[y] = act((h2[y + 2] - mean2) * scale2 + shift2).astype(BF16)
        send(out, row=y)


def fourth_kernel(
    cells, need, send, place, r3, st2, gb, h2, x_low, x_high, cot, y_low, y_high, w, st1, h1, v1, s2, n2, a1,
    slope1, low, high, msg, t3, v, g, acc,
):
    need(r3, st2, gb)
    mean, inverse, o_low, o_high = kept_stats(st2)
    t3[...] = jnp.sum(r3[...], axis=0)
    send(t3)
    nsum, plain = sums_of(t3[0:1])
    need(y_low, y_high)
    gain, bias = gb[:, 2:3], gb[:, 3:4]
    lead = gain * inverse
    p_mean, n_mean = plain / cells, nsum / cells

    def grad(normed, c, gain, bias, lead, p_mean, n_mean):
        slope = c.astype(F32) * act_slope(normed * gain + bias)
        return lead * (slope - p_mean - normed * n_mean)

    one = (gain, bias, lead, p_mean, n_mean)
    both = tuple(twice(a) for a in one)
    mean2, inverse2 = twice(mean), twice(inverse)
    lane = lanes(64)
    rows = ROWS + 4
    for y in range(rows):
        need(h2, row=y)
        need(x_low, x_high, row=2 * y + 1)
        need(cot, row=min(max(y - 2, 0), ROWS - 1))
        g_low = grad((x_low[2 * y].astype(F32) + o_low) * inverse, x_low[2 * y + 1], *one)
        g_own = grad((h2[y] - mean2) * inverse2, cot_row(cot, y_low, y_high, y), *both)
        g_high = grad((x_high[2 * y].astype(F32) + o_high) * inverse, x_high[2 * y + 1], *one)
        planes = jnp.concatenate([g_low, g_own, g_high], axis=0)
        v[y] = masked(planes, kept(place, y, rows, 2))
    need(h1, st1, w)
    mean, inverse, _, _ = kept_stats(st1)
    mean2, inverse2 = twice(mean), twice(inverse)
    gain2, bias2 = twice(gb[:, 0:1]), twice(gb[:, 1:2])
    sums = [jnp.zeros((64, 128), F32), jnp.zeros((64, 128), F32)]

    def emit(y, values):
        normed = (h1[y + 2] - mean2) * inverse2
        slope = values * act_slope(normed * gain2 + bias2)
        slope1[y] = slope
        low[y] = slope[0:C].astype(BF16)
        high[y] = slope[C:].astype(BF16)
        send(slope1, low, high, row=y)
        if 1 <= y < 1 + ROWS:
            sums[0] = sums[0] + slope * normed
            sums[1] = sums[1] + slope
            put_shifted(g, y - 1, slope, lane)

    conv_rows(windows_of(v), w, ROWS + 2, emit)
    send(slope1, low, high)
    need(v1)
    weight_sums(g, v1, 3, acc)
    need(s2, n2, a1)
    ones = ones_of(a1)

    def two(dz, dy):
        k = dz * 3 + dy
        return lead * (s2[k] - p_mean * ones(dz, dy) - n_mean * n2[k])

    rows_message(
        (fold(total(sums[0])), fold(total(sums[1]))), (folded(acc), two), msg
    )


def owner_kernel(cells, need, send, place, r4, st1, gb, t3, x1, msg, norms, t4):
    need(st1, gb, t3, x1)
    _, inverse, _, _ = kept_stats(st1)
    t4[...] = jnp.sum(r4[...], axis=0)
    nsum, plain = sums_of(t4[0:1])
    mine = lax.broadcasted_iota(jnp.int32, (C, 1), 0) == place[6]

    def picked(column):
        return jnp.sum(jnp.where(mine, column, 0.0), axis=0, keepdims=True)

    scale = cells**-0.5
    lead = picked(gb[:, 0:1] * inverse) * scale
    third, fourth = t3[...], t4[...]
    one = fourth[1:4] - picked(plain) * (x1[1:4] / cells) - picked(nsum) * (third[1:4] / cells)
    one = lead * one
    two = fourth[4:7] * scale
    tile = jnp.concatenate([one, two, jnp.zeros((2, 128), F32)], axis=0)
    pair = twice(tile).astype(BF16)
    for k in range(0, msg.shape[0], 16):
        msg[k : k + 16] = pair
    for k, row in enumerate((fourth[0:1], third[0:1])):
        norms[2 * k : 2 * k + 1] = row[:, 0:C] * scale
        norms[2 * k + 1 : 2 * k + 2] = row[:, C : 2 * C] * scale


def finish_kernel(need, send, parts, one, two, rows):
    rows[...] = parts[0 : 3 * C * 8].astype(F32)
    for dz in range(3):
        for dy in range(3):
            for k, out in enumerate((one, two)):
                tile = rows[pl.ds(dz * C * 8 + 3 * k + dy, C, stride=8), :]
                for dx in range(3):
                    out[dx * 9 + dy * 3 + dz] = tile[:, dx * C : (dx + 1) * C]


def fifth_kernel(cells, need, send, place, t4, st1, gb, h1, slope1, s_low, s_high, w, out, v, turned):
    need(t4, st1, gb)
    mean, inverse, _, _ = kept_stats(st1)
    nsum, plain = sums_of(t4[0:1])
    mean4, inverse4 = fourfold(mean), fourfold(inverse)
    lead4 = fourfold(gb[:, 0:1] * inverse)
    p_mean4, n_mean4 = fourfold(plain / cells), fourfold(nsum / cells)
    rows = ROWS + 2
    for y in range(rows):
        need(slope1, s_low, s_high, row=y)
        need(h1, row=y + 2)
        slope = jnp.concatenate(
            [s_low[y].astype(F32), slope1[y], s_high[y].astype(F32)], axis=0
        )
        normed = (h1[y + 2] - mean4) * inverse4
        v[y] = masked(lead4 * (slope - p_mean4 - normed * n_mean4), kept(place, y, rows, 1))
    need(w)

    def emit(y, values):
        turned[:, y, :] = values

    conv_rows(windows_of(v), w, ROWS, emit)
    for i in range(C):
        for x in range(2):
            out[i, x] = turned[x * C + i].astype(BF16)
        send(out, row=i)


def pieces_of(shape):
    rows = shape[0]
    if len(shape) < 3 or rows < 32 or rows > 100:
        return [(0, rows)]
    cuts = [rows * c // 4 for c in range(5)]
    return list(zip(cuts, cuts[1:]))


def call(
    kernel, ins, outs, name, scratch=(), smem_first=True, after=(), near=0, cut=(), late=0, grant=56
):
    lead = 1 if smem_first else 0
    count_in, count_out = len(ins) - lead - near, len(outs)
    far_ins = ins[lead + near :]
    own = [any(a is b for b in cut) for a in far_ins]
    shapes = [(a.shape[0], 2 * C, 128) if c else a.shape for a, c in zip(far_ins, own)]

    def body(*refs):
        first, rest = refs[: lead + near], refs[lead + near :]
        parts = []
        for size in (count_in, len(after), count_out, count_in, count_out, 2):
            parts.append(rest[:size])
            rest = rest[size:]
        sources, _, targets, in_bufs, out_bufs, (in_sems, out_sems) = parts

        def source(k, a, b):
            return sources[k].at[a:b, C : 3 * C] if own[k] else sources[k].at[a:b]

        arriving = [
            [
                (a, b, pltpu.make_async_copy(source(k, a, b), buf.at[a:b], in_sems.at[k, c]))
                for c, (a, b) in enumerate(pieces_of(buf.shape))
            ]
            for k, buf in enumerate(in_bufs)
        ]
        leaving = [
            [
                (a, b, pltpu.make_async_copy(buf.at[a:b], targets[k].at[a:b], out_sems.at[k, c]))
                for c, (a, b) in enumerate(pieces_of(buf.shape))
            ]
            for k, buf in enumerate(out_bufs)
        ]
        early, later = arriving[: count_in - late], arriving[count_in - late :]
        for group in (early, later):
            for c in range(4):
                for pieces in group:
                    if c < len(pieces):
                        pieces[c][2].start()
        waiting, held = [list(pieces) for pieces in arriving], [list(pieces) for pieces in leaving]

        def need(*wanted, row=None):
            for ref in wanted:
                for k, buf in enumerate(in_bufs):
                    while buf is ref and waiting[k] and (row is None or waiting[k][0][0] <= row):
                        waiting[k].pop(0)[2].wait()

        def send(*ready, row=None):
            for ref in ready:
                for k, buf in enumerate(out_bufs):
                    while buf is ref and held[k] and (row is None or held[k][0][1] <= row + 1):
                        held[k].pop(0)[2].start()

        kernel(need, send, *first, *in_bufs, *out_bufs, *rest)
        send(*out_bufs)
        need(*in_bufs)
        for pieces in leaving:
            for piece in pieces:
                piece[2].wait()

    far = pl.BlockSpec(memory_space=pltpu.HBM)
    return pl.pallas_call(
        body,
        out_shape=outs,
        in_specs=[SM] * lead
        + [pl.BlockSpec(memory_space=pltpu.VMEM)] * near
        + [far] * (count_in + len(after)),
        out_specs=[far] * count_out,
        scratch_shapes=[
            *[pltpu.VMEM(shape, a.dtype) for shape, a in zip(shapes, far_ins)],
            *[pltpu.VMEM(a.shape, a.dtype) for a in outs],
            pltpu.SemaphoreType.DMA((max(count_in, 1), 4)),
            pltpu.SemaphoreType.DMA((count_out, 4)),
            *scratch,
        ],
        compiler_params=pltpu.CompilerParams(vmem_limit_bytes=grant * 1024 * 1024),
        cost_estimate=pl.CostEstimate(
            flops=2_000_000_000, bytes_accessed=6_000_000, transcendentals=0
        ),
        name=name,
    )(*ins, *after)


def up(values, axes):
    count = lax.axis_size(axes)
    return lax.ppermute(values, axes, [(i, i + 1) for i in range(count - 1)])


def down(values, axes):
    count = lax.axis_size(axes)
    return lax.ppermute(values, axes, [(i + 1, i) for i in range(count - 1)])


def share(msg):
    return lax.all_to_all(msg, ALL[::-1], 0, 0, tiled=True)


def rank_of(gx, gy):
    rank = gy % lax.axis_size(GY[1])
    for part, axis in (
        (gy // lax.axis_size(GY[1]), GY[0]),
        (gx % lax.axis_size(GX[1]), GX[1]),
        (gx // lax.axis_size(GX[1]), GX[0]),
    ):
        rank = rank * lax.axis_size(axis) + part
    return rank


def local(features, kernel_one, gain_one, bias_one, kernel_two, gain_two, bias_two, cotangent):
    count_x, count_y = lax.axis_size(GX), lax.axis_size(GY)
    count = count_x * count_y
    cells = float(count * 2 * ROWS * 128)
    gx, gy = lax.axis_index(GX), lax.axis_index(GY)
    at = rank_of(gx, gy)
    beside = [rank_of(jnp.clip(gx + k, 0, count_x - 1), gy) for k in (-1, 1)]
    edges = [gx > 0, gx < count_x - 1, gy > 0, gy < count_y - 1]
    place = jnp.stack([*beside, *edges, at % C, at]).astype(jnp.int32)
    gb = jnp.stack([gain_one, bias_one, gain_two, bias_two], axis=1)

    own = jnp.transpose(features, (2, 1, 0, 3)).reshape(ROWS, 64, 128)
    cot = jnp.transpose(cotangent, (2, 1, 0, 3)).reshape(ROWS, 64, 128)

    def rims(rows):
        return [sh((rows, C, 128), BF16)] * 2

    msg, four, wide = (sh((count, *tile), F32) for tile in ((128,), (4, 128), (8, 128)))
    stats = sh((C, 128), F32)
    corr = (pltpu.VMEM((192, ROWS * 128), BF16), pltpu.VMEM((384, 192), F32))

    x_low, x_high = up(own, GX), down(own, GX)
    taps = [
        jnp.transpose(k, (2, 3, 4, 0, 1)).reshape(27, C, C) for k in (kernel_one, kernel_two)
    ]
    matrices = [sh((192, 384), BF16)] * 2
    w1, w2 = call(weights_kernel, taps, matrices, "weights", smem_first=False)
    y_up, y_down = call(
        pack_kernel,
        (x_low, x_high, own, cot),
        [sh((14, 64, 128), BF16)] * 2,
        "pack",
        smem_first=False,
        near=2,
        grant=16,
    )
    y_low, y_high = up(y_up, GY), down(y_down, GY)

    v1, h1, m1, x1_own, center = call(
        first_kernel,
        (y_low, y_high, w1, own, x_low, x_high),
        [sh((40, 128, 128), BF16), sh((38, 128, 128), F32), four, sh((16, 128), F32), stats],
        "conv_one",
        smem_first=False,
    )
    r1 = share(m1)

    (xh,) = call(
        side_kernel,
        (center, h1, v1),
        [sh((9, C, 128), F32)],
        "hidden_features",
        scratch=corr,
        smem_first=False,
        cut=(h1,),
    )

    v2, h2, low, high, m2, st1 = call(
        lambda *refs: second_kernel(cells, *refs),
        (place, r1, gb, h1, cot, y_low, y_high, w2),
        [
            sh((38, 128, 128), BF16), sh((36, 64, 128), F32), *rims(72), msg, stats,
        ],
        "conv_two",
        after=(xh,),
    )
    h2_low, h2_high = up(high, GX), down(low, GX)
    r2 = share(m2)
    (b2,) = call(
        flipped_kernel, taps[1:], matrices[1:], "flipped_two", smem_first=False, after=(st1,)
    )
    m3, st2 = call(
        lambda *refs: third_kernel(cells, *refs),
        (place, r2, gb, cot, h2, st1, x1_own, xh),
        [four, stats],
        "slope_two",
        after=(b2,),
    )
    r3 = share(m3)
    s2, n2, a1 = call(
        active_kernel,
        (st2, gb, h2, cot, v2),
        [sh((9, C, 128), F32), sh((9, C, 128), F32), sh((16, 128), F32)],
        "active_sums",
        scratch=corr,
        smem_first=False,
    )

    slope1, low, high, m4, t3 = call(
        lambda *refs: fourth_kernel(cells, *refs),
        (
            place, r3, st2, gb, h2, h2_low, h2_high, cot, y_low, y_high,
            b2, st1, h1, v1, s2, n2, a1,
        ),
        [sh((34, 64, 128), F32), *rims(34), wide, sh((4, 128), F32)],
        "back_two",
        late=7,
        cut=(h1,),
        scratch=(pltpu.VMEM((36, 128, 128), BF16), *corr),
    )
    s_low, s_high = up(high, GX), down(low, GX)
    r4 = share(m4)

    (b1,) = call(
        flipped_kernel, taps[:1], matrices[1:], "flipped_one", smem_first=False, after=(slope1,)
    )
    (x1,) = call(total_kernel, (r1,), [sh((4, 128), F32)], "total", smem_first=False, after=(b1,))
    (rows_out,) = call(
        output_kernel,
        (st2, gb, h2),
        [sh((ROWS, 64, 128), BF16)],
        "output",
        smem_first=False,
        after=(slope1,),
    )

    def back(rows):
        return jnp.transpose(rows.reshape(ROWS, 2, C, 128), (2, 1, 0, 3))

    output = back(rows_out)

    m5, norm_grads, t4 = call(
        lambda *refs: owner_kernel(cells, *refs),
        (place, r4, st1, gb, t3, x1),
        [sh((count * 8, 128), BF16), sh((4, C), F32), sh((8, 128), F32)],
        "own_rows",
        near=1,
        grant=16,
        after=(s_low, s_high, output),
    )
    r5 = share(m5.reshape(count, 8, 128)).reshape(count * 8, 128)
    (grad,) = call(
        lambda *refs: fifth_kernel(cells, *refs),
        (place, t4, st1, gb, h1, slope1, s_low, s_high, b1),
        [sh((C, 2, ROWS, 128), BF16)],
        "back_one",
        scratch=(pltpu.VMEM((34, 128, 128), BF16), pltpu.VMEM((64, ROWS, 128), F32)),
    )
    grads = call(
        finish_kernel,
        (r5,),
        [sh((27, C, C), F32)] * 2,
        "finish",
        scratch=(pltpu.VMEM((3 * C * 8, 128), F32),),
        smem_first=False,
        near=1,
        grant=16,
    )
    one, two = [jnp.transpose(k.reshape(3, 3, 3, C, C), (3, 4, 0, 1, 2)) for k in grads]

    return output, grad, one, two, norm_grads


def solution(mesh):
    nx, ny = mesh.devices.shape
    parts = (4, nx // 4, ny // 2, 2)
    split = Mesh(mesh.devices.reshape(parts), ALL)
    spec = P(None, GX, GY, None)
    in_specs = (spec, P(), P(), P(), P(), P(), P(), spec)
    out_specs = (spec, spec, P(), P(), P())
    return jax.shard_map(local, mesh=split, in_specs=in_specs, out_specs=out_specs, check_vma=False)
```
